32 devices in a mesh: dp: 8 (over z, core), tensor: 4 (over y, x).
Axes of the slice: x: 2, y: 2, z: 4, core: 2. Of those that a mesh axis runs over, the one named last changes fastest.
Arguments:
- tokens: bfloat16 [4096, 2048], P(('dp', 'tensor')), may hold values from -6 to 6
- gain_attn: bfloat16 [2048], replicated, may hold values from 0.5 to 1.5
- gain_mlp: bfloat16 [2048], replicated, may hold values from 0.5 to 1.5
- w_qkv: bfloat16 [3, 2048, 2048], P(None, None, 'tensor'), may hold values from -0.125 to 0.125
- w_out: bfloat16 [2048, 2048], P('tensor'), may hold values from -1.5 to 1.5
- w_gate_up: bfloat16 [2, 2048, 5632], P(None, None, 'tensor'), may hold values from -0.125 to 0.125
- w_down: bfloat16 [5632, 2048], P('tensor'), may hold values from -0.078125 to 0.078125
- cotangent: bfloat16 [4096, 2048], P(('dp', 'tensor')), may hold values from -6 to 6
- segment_ids: int32 [4096], P('dp'), may hold values from 0 to 512, as said below
- valid_mask: int32 [4096], P('dp'), may hold values from 0 to 1, as said below
Outputs:
- output: bfloat16 [4096, 2048], P(('dp', 'tensor'))
- grad_tokens: float32 [4096, 2048], P(('dp', 'tensor'))
- grad_gain_attn: float32 [2048], replicated
- grad_gain_mlp: float32 [2048], replicated
- grad_w_qkv: float32 [3, 2048, 2048], P(None, 'dp', 'tensor')
- grad_w_out: float32 [2048, 2048], P('tensor', 'dp')
- grad_w_gate_up: float32 [2, 2048, 5632], P(None, 'dp', 'tensor')
- grad_w_down: float32 [5632, 2048], P('tensor', 'dp')
The draws below stay inside these ranges and needn't reach their ends.
Inputs may be any that keep to these rules, and one draw needn't show every extreme that they name: `segment_ids`: within each sequence of 512 tokens the ids never fall and begin at 0; one document of each sequence begins within its first 128 tokens and ends within its last 128; the padding at a sequence's end carries the id 512, which no document has. `valid_mask`: zeros form the tail of each sequence, 2 or more tokens, and match the last id of segment_ids.
All inputs are finite; a program needn't handle non-finite values.
Results may differ from the reference program's by a relative error of at most 0.023.
Values may be sent and summed in bfloat16 or wider, within the bound.
No kernel may reach another device: no remote copies, remote signals or barrier semaphores. Data moves between devices by JAX's collectives and lax.ppermute only.
A program may use at most 128 MiB of HBM per device.

```python
import jax
import jax.numpy as jnp
from jax import lax

D = 2048
HEADS = 16
HD = 128
FF = 5632
TOK_DEV = 128
SEQ = 512
TOKENS = 4096


def layout(key):
    groups = TOKENS // SEQ
    keys_all = jax.random.split(key, groups)

    def one_group(group_key):
        key_a, key_b, key_c, key_d = jax.random.split(group_key, 4)
        head = jax.random.randint(key_a, (), 1, max(2, TOK_DEV // 2))
        padding = jax.random.randint(key_b, (), 2, max(5, TOK_DEV // 4))
        tail = jax.random.randint(key_c, (), 1, max(2, TOK_DEV // 2))
        flags = jax.random.randint(key_d, (SEQ,), 0, 8) == 0
        positions = jnp.arange(SEQ)
        finish = SEQ - padding
        tail_start = finish - tail
        bounds = (positions == head) | (positions == tail_start) | flags & (positions > tail_start) & (positions < finish)
        counted = jnp.cumsum(bounds.astype(jnp.int32)).astype(jnp.int32)
        segments = jnp.where(positions >= finish, SEQ, counted).astype(jnp.int32)
        valid = (positions < finish).astype(jnp.int32)
        return (segments, valid)
    segments, valid = jax.vmap(one_group)(keys_all)
    return (segments.reshape(-1), valid.reshape(-1))


def draw_segment_ids(key, part):
    shared = layout(key)
    return shared[0]


def draw_valid_mask(key, part):
    shared = layout(key)
    return shared[1]


def strengthened(values, own_key, source, target, shards_of, factor):
    def block_of(axis_at):
        return (jnp.arange(values.shape[axis_at]) // (values.shape[axis_at] // shards_of)).reshape((-1,) + (1,) * (values.ndim - 1 - axis_at))

    near = jax.random.permutation(own_key, shards_of)[block_of(target)]
    second = (block_of(target) + shards_of // 2) % shards_of
    return jnp.where((block_of(source) == near) | (block_of(source) == second), factor * values, values)


def levels(stream_key, dims, cuts, low, high):
    loudness, own = 1.0, jax.random.fold_in(stream_key, 6)
    for position, shards_of in cuts:
        steps = jnp.exp(jax.random.uniform(jax.random.fold_in(own, position), (shards_of,), jnp.float32, low / len(cuts), high / len(cuts)))
        loudness = loudness * jnp.repeat(steps, dims[position] // shards_of).reshape([-1 if axis == position else 1 for axis in range(len(dims))])
    return loudness


def scatter_about(own_key, shape, deviation, most, pieces=(), kind=jnp.bfloat16):
    entries = deviation * jax.random.normal(own_key, shape, jnp.float32)
    if pieces:
        entries = entries * levels(own_key, shape, pieces, -0.22, 0.18)
    return jnp.clip(entries, -most, most).astype(kind)


def bell_draw_with(own_key, extent, spread, reach, cuts, heavy, kind=jnp.bfloat16):
    values = spread * jax.random.normal(own_key, extent, jnp.float32)
    if cuts:
        values = values * levels(own_key, extent, cuts, -0.22, 0.18)
    return jnp.clip(strengthened(values, jax.random.fold_in(own_key, 3), *heavy), -reach, reach).astype(kind)


def setup_inputs(seed: int = 0) -> dict:
    splits = jax.random.split(jax.random.key(seed), 11)
    return {
        "tokens": scatter_about(splits[0], (TOKENS, D), 1.0, 6.0, ((0, 32),)),
        "gain_attn": jnp.clip(1.0 + 0.1 * jax.random.normal(splits[1], (D,), jnp.float32), 0.5, 1.5).astype(jnp.bfloat16),
        "gain_mlp": jnp.clip(1.0 + 0.1 * jax.random.normal(splits[2], (D,), jnp.float32), 0.5, 1.5).astype(jnp.bfloat16),
        "w_qkv": scatter_about(splits[3], (3, D, D), D ** -0.5, 0.125, ((2, 4),)),
        "w_out": scatter_about(splits[4], (D, D), (max(2, (4 * D) // SEQ)) ** -0.5, 1.5, ((0, 4),)),
        "w_gate_up": scatter_about(splits[5], (2, D, FF), D ** -0.5, 0.125, ((2, 4),)),
        "w_down": scatter_about(splits[6], (FF, D), FF ** -0.5, 0.078125, ((0, 4),)),
        "cotangent": bell_draw_with(splits[7], (TOKENS, D), 1.0, 6.0, ((0, 32),), (0, 1, 32, 2.75)),
        "segment_ids": draw_segment_ids(jax.random.fold_in(splits[10], 71), 0),
        "valid_mask": draw_valid_mask(jax.random.fold_in(splits[10], 71), 0),
    }


EPS = 1e-06
THETA = 10000.0
HIGH = lax.Precision.HIGHEST

@jax.custom_vjp
def low(v):
    return lax.optimization_barrier(v.astype(jnp.bfloat16)).astype(jnp.float32)

@jax.custom_vjp
def low_back(v):
    return v

def low_keep(v):
    return (low(v), None)

def low_pass(kept, grad):
    return (grad,)

def back_keep(v):
    return (v, None)

def back_low(kept, grad):
    return (low(grad),)
low.defvjp(low_keep, low_pass)
low_back.defvjp(back_keep, back_low)

def tables():
    positions = jnp.arange(SEQ).astype(jnp.float32)
    freqs = THETA ** (-(jnp.arange(HD // 2).astype(jnp.float32) * 2.0 / HD))
    angles = positions[:, None] * freqs[None, :]
    return (jnp.cos(angles), jnp.sin(angles))

def rotate(values, cosine, sine):
    half = values.shape[-1] // 2
    first = values[..., :half]
    second = values[..., half:]
    cosine = cosine[:, None, :]
    sine = sine[:, None, :]
    return jnp.concatenate([first * cosine - second * sine, second * cosine + first * sine], axis=-1)

def attention(queries, keys_rot, values, segments, valid):
    block_rows = min(512, SEQ)
    count = SEQ // block_rows
    scale = HD ** (-0.5)
    key_pos = jnp.arange(SEQ).astype(jnp.int32)

    def one_block(index):
        start = index * block_rows
        q_block = lax.dynamic_slice_in_dim(queries, start, block_rows, 0)
        row_pos = start + jnp.arange(block_rows).astype(jnp.int32)
        row_seg = lax.dynamic_slice_in_dim(segments, start, block_rows, 0)
        scores = low_back(jnp.einsum('qhd,khd->hqk', q_block, keys_rot, precision=HIGH) * scale)
        allowed = (key_pos[None, :] <= row_pos[:, None]) & (row_seg[:, None] == segments[None, :]) & ((valid[None, :] == 1) | (key_pos[None, :] == row_pos[:, None]))
        scores = jnp.where(allowed[None], scores, -1e+30)
        top = lax.optimization_barrier(jnp.max(scores, axis=-1, keepdims=True))
        expo = jnp.exp(scores - top)
        probs = low(expo / lax.optimization_barrier(jnp.sum(expo, axis=-1, keepdims=True)))
        return jnp.einsum('hqk,khd->qhd', probs, values, precision=HIGH)
    blocks = lax.map(jax.checkpoint(one_block), jnp.arange(count).astype(jnp.int32))
    return blocks.reshape(SEQ, HEADS * HD)

def forward(incoming, gain_one, gain_two, w_qkv, w_out, w_gate_up, w_down, segments, valid, cosine, sine):
    inv_one = lax.rsqrt(lax.optimization_barrier(jnp.mean(incoming * incoming, axis=-1, keepdims=True)) + EPS)
    normed = low(incoming * inv_one * gain_one)
    project = jnp.einsum('td,cde->cte', normed, w_qkv, precision=HIGH)
    shape3 = (SEQ, HEADS, HD)
    queries = low(rotate(low_back(project[0]).reshape(shape3), cosine, sine))
    keys_rot = low(rotate(low_back(project[1]).reshape(shape3), cosine, sine))
    values = low(low_back(project[2])).reshape(shape3)
    mixed = low_back(low(attention(queries, keys_rot, values, segments, valid)))
    middle = incoming + low_back(jnp.dot(mixed, w_out, precision=HIGH))
    inv_two = lax.rsqrt(lax.optimization_barrier(jnp.mean(middle * middle, axis=-1, keepdims=True)) + EPS)
    normed_two = low(middle * inv_two * gain_two)
    gate = low_back(jnp.dot(normed_two, w_gate_up[0], precision=HIGH))
    upper = low_back(jnp.dot(normed_two, w_gate_up[1], precision=HIGH))
    hidden = low(jax.nn.silu(gate) * upper)
    return middle + low_back(jnp.dot(hidden, w_down, precision=HIGH))

def reference(tokens, gain_attn, gain_mlp, w_qkv, w_out, w_gate_up, w_down, cotangent, segment_ids, valid_mask):
    groups = TOKENS // SEQ
    weights = tuple((item.astype(jnp.float32) for item in (gain_attn, gain_mlp, w_qkv, w_out, w_gate_up, w_down)))
    cosine, sine = tables()
    inputs_all = tokens.astype(jnp.float32).reshape(groups, SEQ, D)
    cots_all = cotangent.astype(jnp.float32).reshape(groups, SEQ, D)
    segs_all = segment_ids.reshape(groups, SEQ)
    valid_all = valid_mask.reshape(groups, SEQ)

    def step(totals, item):
        incoming, cot, segments, valid = item

        def local(inputs_in, *params):
            return forward(inputs_in, *params, segments, valid, cosine, sine)
        result, pull = jax.vjp(local, incoming, *weights)
        grads = pull(cot)
        totals = tuple((total + grad for total, grad in zip(totals, grads[1:])))
        return (totals, (result.astype(jnp.bfloat16), grads[0]))
    init = tuple((jnp.zeros(weight.shape, jnp.float32) for weight in weights))
    totals, (results, d_inputs) = lax.scan(step, init, (inputs_all, cots_all, segs_all, valid_all))
    return (results.reshape(TOKENS, D), d_inputs.reshape(TOKENS, D), totals[0], totals[1], totals[2], totals[3], totals[4], totals[5])
```

```python
import jax
import jax.numpy as jnp
from jax import lax
from jax.sharding import PartitionSpec as P

HD = 128


EPS = 1e-06
THETA = 10000.0


def rope_tables(positions):
    freqs = THETA ** (-(jnp.arange(HD // 2).astype(jnp.float32) * 2.0 / HD))
    angles = positions.astype(jnp.float32)[:, None] * freqs[None, :]
    return (jnp.cos(angles), jnp.sin(angles))


def rotate(values, cosine, sine):
    half = values.shape[-1] // 2
    first = values[..., :half]
    second = values[..., half:]
    cosine = cosine[:, None, :]
    sine = sine[:, None, :]
    return jnp.concatenate(
        [first * cosine - second * sine, second * cosine + first * sine], axis=-1
    )


def block_scores(q_block, keys_rot, start, places, segments, valid):
    block_rows = q_block.shape[0]
    row_pos = lax.dynamic_slice_in_dim(places, start, block_rows, 0)
    row_seg = lax.dynamic_slice_in_dim(segments, start, block_rows, 0)
    scores = jnp.einsum(
        "qhd,khd->hqk", q_block, keys_rot, preferred_element_type=jnp.float32
    ) * HD ** (-0.5)
    allowed = (
        (places[None, :] <= row_pos[:, None])
        & (row_seg[:, None] == segments[None, :])
        & ((valid[None, :] == 1) | (places[None, :] == row_pos[:, None]))
    )
    return jnp.where(allowed[None], scores, -1e30)


def attend(queries, keys_rot, values, places, segments, valid):
    length = queries.shape[0]
    block_rows = min(512, length)
    count = length // block_rows

    def one_block(index):
        start = index * block_rows
        q_block = lax.dynamic_slice_in_dim(queries, start, block_rows, 0)
        scores = block_scores(q_block, keys_rot, start, places, segments, valid)
        top = jnp.max(scores, axis=-1, keepdims=True)
        expo = jnp.exp(scores - top)
        total = jnp.sum(expo, axis=-1, keepdims=True)
        probs = (expo / total).astype(jnp.bfloat16)
        result = jnp.einsum("hqk,khd->qhd", probs, values, preferred_element_type=jnp.float32)
        return (result, top[..., 0] + jnp.log(total[..., 0]))

    blocks, log_sums = lax.map(one_block, jnp.arange(count))
    return (blocks.reshape(length, -1), log_sums)


def attend_back(queries, keys_rot, values, d_mixed, log_sums, places, segments, valid):
    length = queries.shape[0]
    block_rows = min(512, length)
    count = length // block_rows
    scale = HD ** (-0.5)

    def one_block(carry, index):
        d_keys, d_values = carry
        start = index * block_rows
        q_block = lax.dynamic_slice_in_dim(queries, start, block_rows, 0)
        d_block = lax.dynamic_slice_in_dim(d_mixed, start, block_rows, 0)
        scores = block_scores(q_block, keys_rot, start, places, segments, valid)
        probs = jnp.exp(scores - log_sums[index][..., None])
        d_values = d_values + jnp.einsum(
            "hqk,qhd->khd", probs.astype(jnp.bfloat16), d_block, preferred_element_type=jnp.float32
        )
        d_probs = jnp.einsum("qhd,khd->hqk", d_block, values, preferred_element_type=jnp.float32)
        delta = jnp.sum(d_probs * probs, axis=-1, keepdims=True)
        d_scores = (probs * (d_probs - delta)).astype(jnp.bfloat16)
        d_query = scale * jnp.einsum(
            "hqk,khd->qhd", d_scores, keys_rot, preferred_element_type=jnp.float32
        )
        d_keys = d_keys + scale * jnp.einsum(
            "hqk,qhd->khd", d_scores, q_block, preferred_element_type=jnp.float32
        )
        return ((d_keys, d_values), d_query)

    empty = jnp.zeros(keys_rot.shape, jnp.float32)
    (d_keys, d_values), d_queries = lax.scan(one_block, (empty, empty), jnp.arange(count))
    return (d_queries.reshape(queries.shape), d_keys, d_values)


def flips(size, bit):
    return [(i, i ^ bit) for i in range(size)]


class Square:
    def __init__(self, size):
        self.size = size
        self.square = size == 4

    def places(self, rows):
        if not self.square:
            return jnp.arange(self.size * rows)
        me = lax.axis_index("tensor")
        order = jnp.stack([me, me ^ 1, me ^ 2, me ^ 3])
        return (order[:, None] * rows + jnp.arange(rows)[None, :]).reshape(-1)

    def move(self, values, bit):
        return lax.ppermute(values, "tensor", flips(4, bit))

    def gather(self, own):
        if not self.square:
            return lax.all_gather(own, "tensor", axis=0, tiled=True)
        half = own.shape[0] // 2
        from_x = self.move(own, 1)
        from_y = self.move(own, 2)
        low = self.move(from_y[:half], 1)
        high = self.move(from_x[half:], 2)
        return jnp.concatenate([own, from_x, from_y, low, high], axis=0)

    def scatter(self, part):
        if not self.square:
            return lax.psum_scatter(
                part.astype(jnp.bfloat16), "tensor", scatter_dimension=0, tiled=True
            ).astype(jnp.float32)
        rows = part.shape[0] // 4
        half = rows // 2
        low = jnp.bfloat16
        via_x = self.move(part[3 * rows : 3 * rows + half].astype(low), 1)
        via_y = self.move(part[3 * rows + half :].astype(low), 2)
        wide = part.astype(jnp.float32)
        to_x = jnp.concatenate(
            [wide[rows : rows + half], wide[rows + half : 2 * rows] + via_y.astype(jnp.float32)]
        ).astype(low)
        to_y = jnp.concatenate(
            [wide[2 * rows : 2 * rows + half] + via_x.astype(jnp.float32), wide[2 * rows + half : 3 * rows]]
        ).astype(low)
        got_x = self.move(to_x, 1).astype(jnp.float32)
        got_y = self.move(to_y, 2).astype(jnp.float32)
        return wide[:rows] + got_x + got_y


class Line:
    def __init__(self, size):
        self.size = size
        self.line = size == 8
        self.chips = size // 2

    def sibling(self, values):
        return lax.ppermute(values, "dp", flips(self.size, 1))

    def with_sibling(self, values):
        return jnp.concatenate([values, self.sibling(values)], axis=0)

    def columns(self, values):
        core = lax.axis_index("dp") % 2
        cut = values.reshape(values.shape[0], self.chips, 2, -1)
        keep = lax.dynamic_index_in_dim(cut, core, 2, keepdims=False)
        send = lax.dynamic_index_in_dim(cut, 1 - core, 2, keepdims=False)
        return jnp.concatenate([keep, self.sibling(send)], axis=0)

    def reduce(self, pieces):
        chips = self.chips
        low = jnp.bfloat16
        place = lax.axis_index("dp") // 2
        up = down = None
        for turn in range(1, chips):
            ups = [
                (2 * z + core, 2 * z + 2 + core)
                for z in range(min(turn, chips - 1))
                for core in range(2)
            ]
            downs = [(self.size - 1 - a, self.size - 1 - b) for a, b in ups]
            up_piece = lax.dynamic_index_in_dim(
                pieces, jnp.clip(place + chips - turn, 0, chips - 1), 0, keepdims=False
            ).astype(jnp.float32)
            down_piece = lax.dynamic_index_in_dim(
                pieces, jnp.clip(place - chips + turn, 0, chips - 1), 0, keepdims=False
            ).astype(jnp.float32)
            if up is not None:
                up_piece = up_piece + up
                down_piece = down_piece + down
            up = lax.ppermute(up_piece.astype(low), "dp", ups).astype(jnp.float32)
            down = lax.ppermute(down_piece.astype(low), "dp", downs).astype(jnp.float32)
        own = lax.dynamic_index_in_dim(pieces, place, 0, keepdims=False).astype(jnp.float32)
        return own + up + down

    def left(self, split, other):
        if not self.line:
            full = jnp.einsum("tf,td->fd", other, split, preferred_element_type=jnp.float32)
            return lax.psum_scatter(
                full.astype(jnp.bfloat16), "dp", scatter_dimension=1, tiled=True
            ).astype(jnp.float32)
        pieces = jnp.einsum(
            "tzd,tf->zfd",
            self.columns(split),
            self.with_sibling(other),
            preferred_element_type=jnp.float32,
        ).astype(jnp.bfloat16)
        return self.reduce(pieces)

    def right(self, split, other):
        if not self.line:
            full = jnp.einsum("td,tf->df", split, other, preferred_element_type=jnp.float32)
            return lax.psum_scatter(
                full.astype(jnp.bfloat16), "dp", scatter_dimension=0, tiled=True
            ).astype(jnp.float32)
        pieces = jnp.einsum(
            "tzd,tf->zdf",
            self.columns(split),
            self.with_sibling(other),
            preferred_element_type=jnp.float32,
        ).astype(jnp.bfloat16)
        return self.reduce(pieces)


def sum_all(values, dp_size, tensor_size):
    if dp_size != 8 or tensor_size != 4:
        return lax.psum(values, ("dp", "tensor"))
    for axis, size, bit in (
        ("dp", 8, 1),
        ("tensor", 4, 1),
        ("tensor", 4, 2),
        ("dp", 8, 2),
        ("dp", 8, 4),
    ):
        values = values + lax.ppermute(values, axis, flips(size, bit))
    return values


def per_device(
    dp_size,
    tensor_size,
    tokens,
    gain_attn,
    gain_mlp,
    w_qkv,
    w_out,
    w_gate_up,
    w_down,
    cotangent,
    segment_ids,
    valid_mask,
):
    square = Square(tensor_size)
    line = Line(dp_size)
    length = segment_ids.shape[0]
    heads_here = w_qkv.shape[2] // HD
    shape3 = (length, heads_here, HD)
    places = square.places(tokens.shape[0])
    segments = segment_ids[places]
    valid = valid_mask[places]
    incoming = tokens.astype(jnp.float32)
    gain_one = gain_attn.astype(jnp.float32)
    gain_two = gain_mlp.astype(jnp.float32)
    cosine, sine = rope_tables(places)
    inv_one = lax.rsqrt(jnp.mean(incoming * incoming, axis=-1, keepdims=True) + EPS)
    normed = (incoming * inv_one * gain_one).astype(jnp.bfloat16)
    normed_all = square.gather(normed)
    project = jnp.einsum("td,cde->cte", normed_all, w_qkv, preferred_element_type=jnp.float32)
    queries = rotate(project[0].reshape(shape3), cosine, sine).astype(jnp.bfloat16)
    keys_rot = rotate(project[1].reshape(shape3), cosine, sine).astype(jnp.bfloat16)
    values = project[2].reshape(shape3).astype(jnp.bfloat16)
    mixed, log_sums = attend(queries, keys_rot, values, places, segments, valid)
    mixed = mixed.astype(jnp.bfloat16)
    middle = incoming + square.scatter(
        jnp.dot(mixed, w_out, preferred_element_type=jnp.float32).astype(jnp.bfloat16)
    )
    inv_two = lax.rsqrt(jnp.mean(middle * middle, axis=-1, keepdims=True) + EPS)
    normed_two = (middle * inv_two * gain_two).astype(jnp.bfloat16)
    normed_two_all = square.gather(normed_two)
    gate = jnp.dot(normed_two_all, w_gate_up[0], preferred_element_type=jnp.float32)
    upper = jnp.dot(normed_two_all, w_gate_up[1], preferred_element_type=jnp.float32)
    sigma = jax.nn.sigmoid(gate)
    hidden = (gate * sigma * upper).astype(jnp.bfloat16)
    cot_all = square.gather(cotangent)
    grad_down = line.left(cot_all, hidden)
    d_hidden = jnp.einsum("td,fd->tf", cot_all, w_down, preferred_element_type=jnp.float32)
    d_upper = (d_hidden * gate * sigma).astype(jnp.bfloat16)
    d_gate = (d_hidden * upper * sigma * (1.0 + gate * (1.0 - sigma))).astype(jnp.bfloat16)
    d_normed_two = square.scatter(
        (
            jnp.einsum("tf,df->td", d_gate, w_gate_up[0], preferred_element_type=jnp.float32)
            + jnp.einsum("tf,df->td", d_upper, w_gate_up[1], preferred_element_type=jnp.float32)
        ).astype(jnp.bfloat16)
    )
    grad_gate = line.right(normed_two_all, d_gate)
    grad_up = line.right(normed_two_all, d_upper)
    scaled_two = gain_two * d_normed_two
    d_middle = (
        cotangent.astype(jnp.float32)
        + inv_two * scaled_two
        - middle * inv_two**3 * jnp.mean(scaled_two * middle, axis=-1, keepdims=True)
    )
    grad_gain_two = jnp.sum(d_normed_two * middle * inv_two, axis=0)
    d_middle_all = square.gather(d_middle.astype(jnp.bfloat16))
    d_mixed = jnp.einsum(
        "td,ed->te", d_middle_all, w_out, preferred_element_type=jnp.float32
    ).astype(jnp.bfloat16)
    grad_out = line.left(d_middle_all, mixed)
    result = middle + square.scatter(
        jnp.dot(hidden, w_down, preferred_element_type=jnp.float32).astype(jnp.bfloat16)
    )
    output = result.astype(jnp.bfloat16)
    d_queries, d_keys, d_values = attend_back(
        queries, keys_rot, values, d_mixed.reshape(shape3), log_sums, places, segments, valid
    )
    d_project = jnp.concatenate(
        [
            rotate(d_queries, cosine, -sine).reshape(length, -1),
            rotate(d_keys, cosine, -sine).reshape(length, -1),
            d_values.reshape(length, -1),
        ],
        axis=1,
    ).astype(jnp.bfloat16)
    wide = d_project.shape[1] // 3
    grad_qkv = line.right(normed_all, d_project)
    grad_qkv = jnp.stack([grad_qkv[:, c * wide : (c + 1) * wide] for c in range(3)])
    d_normed = square.scatter(
        sum(
            jnp.einsum(
                "te,de->td",
                d_project[:, c * wide : (c + 1) * wide],
                w_qkv[c],
                preferred_element_type=jnp.float32,
            )
            for c in range(3)
        ).astype(jnp.bfloat16)
    )
    scaled_one = gain_one * d_normed
    d_inputs = (
        d_middle
        + inv_one * scaled_one
        - incoming * inv_one**3 * jnp.mean(scaled_one * incoming, axis=-1, keepdims=True)
    )
    grad_gain_one = jnp.sum(d_normed * incoming * inv_one, axis=0)
    grad_gain_two = sum_all(grad_gain_two, dp_size, tensor_size)
    grad_gain_one = sum_all(grad_gain_one, dp_size, tensor_size)
    return (
        output,
        d_inputs,
        grad_gain_one,
        grad_gain_two,
        grad_qkv,
        grad_out,
        jnp.stack([grad_gate, grad_up]),
        grad_down,
    )


def solution(mesh):
    placed = (
        P(("dp", "tensor"), None),
        P(),
        P(),
        P(None, None, "tensor"),
        P("tensor", None),
        P(None, None, "tensor"),
        P("tensor", None),
        P(("dp", "tensor"), None),
        P("dp"),
        P("dp"),
    )

    def body(*arrays):
        return per_device(mesh.shape["dp"], mesh.shape["tensor"], *arrays)

    return jax.shard_map(
        body,
        mesh=mesh,
        in_specs=placed,
        out_specs=(
            P(("dp", "tensor"), None),
            P(("dp", "tensor"), None),
            P(),
            P(),
            P(None, "dp", "tensor"),
            P("tensor", "dp"),
            P(None, "dp", "tensor"),
            P("tensor", "dp"),
        ),
        check_vma=False,
    )
```

```python
import jax
import jax.numpy as jnp
from jax import lax
from jax.sharding import PartitionSpec as P

HD = 128


EPS = 1e-06
THETA = 10000.0


def rope_tables(positions):
    freqs = THETA ** (-(jnp.arange(HD // 2).astype(jnp.float32) * 2.0 / HD))
    angles = positions.astype(jnp.float32)[:, None] * freqs[None, :]
    return (jnp.cos(angles), jnp.sin(angles))


def rotate(values, cosine, sine):
    half = values.shape[-1] // 2
    first = values[..., :half]
    second = values[..., half:]
    cosine = cosine[:, None, :]
    sine = sine[:, None, :]
    return jnp.concatenate(
        [first * cosine - second * sine, second * cosine + first * sine], axis=-1
    )


def block_scores(q_block, keys_rot, start, places, segments, valid):
    block_rows = q_block.shape[0]
    row_pos = lax.dynamic_slice_in_dim(places, start, block_rows, 0)
    row_seg = lax.dynamic_slice_in_dim(segments, start, block_rows, 0)
    scores = jnp.einsum(
        "qhd,khd->hqk", q_block, keys_rot, preferred_element_type=jnp.float32
    ) * HD ** (-0.5)
    allowed = (
        (places[None, :] <= row_pos[:, None])
        & (row_seg[:, None] == segments[None, :])
        & ((valid[None, :] == 1) | (places[None, :] == row_pos[:, None]))
    )
    return jnp.where(allowed[None], scores, -1e30)


def attend(queries, keys_rot, values, places, segments, valid):
    length = queries.shape[0]
    block_rows = min(512, length)
    count = length // block_rows

    def one_block(index):
        start = index * block_rows
        q_block = lax.dynamic_slice_in_dim(queries, start, block_rows, 0)
        scores = block_scores(q_block, keys_rot, start, places, segments, valid)
        top = jnp.max(scores, axis=-1, keepdims=True)
        expo = jnp.exp(scores - top)
        total = jnp.sum(expo, axis=-1, keepdims=True)
        probs = (expo / total).astype(jnp.bfloat16)
        result = jnp.einsum("hqk,khd->qhd", probs, values, preferred_element_type=jnp.float32)
        return (result, top[..., 0] + jnp.log(total[..., 0]))

    blocks, log_sums = lax.map(one_block, jnp.arange(count))
    return (blocks.reshape(length, -1), log_sums)


def attend_back(queries, keys_rot, values, d_mixed, log_sums, places, segments, valid):
    length = queries.shape[0]
    block_rows = min(512, length)
    count = length // block_rows
    scale = HD ** (-0.5)

    def one_block(carry, index):
        d_keys, d_values = carry
        start = index * block_rows
        q_block = lax.dynamic_slice_in_dim(queries, start, block_rows, 0)
        d_block = lax.dynamic_slice_in_dim(d_mixed, start, block_rows, 0)
        scores = block_scores(q_block, keys_rot, start, places, segments, valid)
        probs = jnp.exp(scores - log_sums[index][..., None])
        d_values = d_values + jnp.einsum(
            "hqk,qhd->khd", probs.astype(jnp.bfloat16), d_block, preferred_element_type=jnp.float32
        )
        d_probs = jnp.einsum("qhd,khd->hqk", d_block, values, preferred_element_type=jnp.float32)
        delta = jnp.sum(d_probs * probs, axis=-1, keepdims=True)
        d_scores = (probs * (d_probs - delta)).astype(jnp.bfloat16)
        d_query = scale * jnp.einsum(
            "hqk,khd->qhd", d_scores, keys_rot, preferred_element_type=jnp.float32
        )
        d_keys = d_keys + scale * jnp.einsum(
            "hqk,qhd->khd", d_scores, q_block, preferred_element_type=jnp.float32
        )
        return ((d_keys, d_values), d_query)

    empty = jnp.zeros(keys_rot.shape, jnp.float32)
    (d_keys, d_values), d_queries = lax.scan(one_block, (empty, empty), jnp.arange(count))
    return (d_queries.reshape(queries.shape), d_keys, d_values)


def flips(size, bit):
    return [(i, i ^ bit) for i in range(size)]


class Square:
    def __init__(self, size):
        self.size = size
        self.square = size == 4

    def places(self, rows):
        if not self.square:
            return jnp.arange(self.size * rows)
        me = lax.axis_index("tensor")
        order = jnp.stack([me, me ^ 1, me ^ 2, me ^ 3])
        return (order[:, None] * rows + jnp.arange(rows)[None, :]).reshape(-1)

    def move(self, values, bit):
        return lax.ppermute(values, "tensor", flips(4, bit))

    def gather(self, own):
        if not self.square:
            return lax.all_gather(own, "tensor", axis=0, tiled=True)
        half = own.shape[0] // 2
        from_x = self.move(own, 1)
        from_y = self.move(own, 2)
        low = self.move(from_y[:half], 1)
        high = self.move(from_x[half:], 2)
        return jnp.concatenate([own, from_x, from_y, low, high], axis=0)

    def scatter(self, part):
        if not self.square:
            return lax.psum_scatter(
                part.astype(jnp.bfloat16), "tensor", scatter_dimension=0, tiled=True
            ).astype(jnp.float32)
        rows = part.shape[0] // 4
        half = rows // 2
        low = jnp.bfloat16
        via_x = self.move(part[3 * rows : 3 * rows + half].astype(low), 1)
        via_y = self.move(part[3 * rows + half :].astype(low), 2)
        wide = part.astype(jnp.float32)
        to_x = jnp.concatenate(
            [wide[rows : rows + half], wide[rows + half : 2 * rows] + via_y.astype(jnp.float32)]
        ).astype(low)
        to_y = jnp.concatenate(
            [wide[2 * rows : 2 * rows + half] + via_x.astype(jnp.float32), wide[2 * rows + half : 3 * rows]]
        ).astype(low)
        got_x = self.move(to_x, 1).astype(jnp.float32)
        got_y = self.move(to_y, 2).astype(jnp.float32)
        return wide[:rows] + got_x + got_y


class Line:
    def __init__(self, size):
        self.size = size
        self.line = False
        self.chips = size // 2

    def sibling(self, values):
        return lax.ppermute(values, "dp", flips(self.size, 1))

    def with_sibling(self, values):
        return jnp.concatenate([values, self.sibling(values)], axis=0)

    def columns(self, values):
        core = lax.axis_index("dp") % 2
        cut = values.reshape(values.shape[0], self.chips, 2, -1)
        keep = lax.dynamic_index_in_dim(cut, core, 2, keepdims=False)
        send = lax.dynamic_index_in_dim(cut, 1 - core, 2, keepdims=False)
        return jnp.concatenate([keep, self.sibling(send)], axis=0)

    def reduce(self, pieces):
        chips = self.chips
        low = jnp.bfloat16
        place = lax.axis_index("dp") // 2
        up = down = None
        for turn in range(1, chips):
            ups = [
                (2 * z + core, 2 * z + 2 + core)
                for z in range(min(turn, chips - 1))
                for core in range(2)
            ]
            downs = [(self.size - 1 - a, self.size - 1 - b) for a, b in ups]
            up_piece = lax.dynamic_index_in_dim(
                pieces, jnp.clip(place + chips - turn, 0, chips - 1), 0, keepdims=False
            ).astype(jnp.float32)
            down_piece = lax.dynamic_index_in_dim(
                pieces, jnp.clip(place - chips + turn, 0, chips - 1), 0, keepdims=False
            ).astype(jnp.float32)
            if up is not None:
                up_piece = up_piece + up
                down_piece = down_piece + down
            up = lax.ppermute(up_piece.astype(low), "dp", ups).astype(jnp.float32)
            down = lax.ppermute(down_piece.astype(low), "dp", downs).astype(jnp.float32)
        own = lax.dynamic_index_in_dim(pieces, place, 0, keepdims=False).astype(jnp.float32)
        return own + up + down

    def left(self, split, other):
        if not self.line:
            full = jnp.einsum("tf,td->fd", other, split, preferred_element_type=jnp.float32)
            return lax.psum_scatter(
                full.astype(jnp.bfloat16), "dp", scatter_dimension=1, tiled=True
            ).astype(jnp.float32)
        pieces = jnp.einsum(
            "tzd,tf->zfd",
            self.columns(split),
            self.with_sibling(other),
            preferred_element_type=jnp.float32,
        ).astype(jnp.bfloat16)
        return self.reduce(pieces)

    def right(self, split, other):
        if not self.line:
            full = jnp.einsum("td,tf->df", split, other, preferred_element_type=jnp.float32)
            return lax.psum_scatter(
                full.astype(jnp.bfloat16), "dp", scatter_dimension=0, tiled=True
            ).astype(jnp.float32)
        pieces = jnp.einsum(
            "tzd,tf->zdf",
            self.columns(split),
            self.with_sibling(other),
            preferred_element_type=jnp.float32,
        ).astype(jnp.bfloat16)
        return self.reduce(pieces)


def sum_all(values, dp_size, tensor_size):
    if dp_size != 8 or tensor_size != 4:
        return lax.psum(values, ("dp", "tensor"))
    for axis, size, bit in (
        ("dp", 8, 1),
        ("tensor", 4, 1),
        ("tensor", 4, 2),
        ("dp", 8, 2),
        ("dp", 8, 4),
    ):
        values = values + lax.ppermute(values, axis, flips(size, bit))
    return values


def per_device(
    dp_size,
    tensor_size,
    tokens,
    gain_attn,
    gain_mlp,
    w_qkv,
    w_out,
    w_gate_up,
    w_down,
    cotangent,
    segment_ids,
    valid_mask,
):
    square = Square(tensor_size)
    line = Line(dp_size)
    length = segment_ids.shape[0]
    heads_here = w_qkv.shape[2] // HD
    shape3 = (length, heads_here, HD)
    places = square.places(tokens.shape[0])
    segments = segment_ids[places]
    valid = valid_mask[places]
    incoming = tokens.astype(jnp.float32)
    gain_one = gain_attn.astype(jnp.float32)
    gain_two = gain_mlp.astype(jnp.float32)
    cosine, sine = rope_tables(places)
    inv_one = lax.rsqrt(jnp.mean(incoming * incoming, axis=-1, keepdims=True) + EPS)
    normed = (incoming * inv_one * gain_one).astype(jnp.bfloat16)
    normed_all = square.gather(normed)
    project = jnp.einsum("td,cde->cte", normed_all, w_qkv, preferred_element_type=jnp.float32)
    queries = rotate(project[0].reshape(shape3), cosine, sine).astype(jnp.bfloat16)
    keys_rot = rotate(project[1].reshape(shape3), cosine, sine).astype(jnp.bfloat16)
    values = project[2].reshape(shape3).astype(jnp.bfloat16)
    mixed, log_sums = attend(queries, keys_rot, values, places, segments, valid)
    mixed = mixed.astype(jnp.bfloat16)
    middle = incoming + square.scatter(
        jnp.dot(mixed, w_out, preferred_element_type=jnp.float32).astype(jnp.bfloat16)
    )
    inv_two = lax.rsqrt(jnp.mean(middle * middle, axis=-1, keepdims=True) + EPS)
    normed_two = (middle * inv_two * gain_two).astype(jnp.bfloat16)
    normed_two_all = square.gather(normed_two)
    gate = jnp.dot(normed_two_all, w_gate_up[0], preferred_element_type=jnp.float32)
    upper = jnp.dot(normed_two_all, w_gate_up[1], preferred_element_type=jnp.float32)
    sigma = jax.nn.sigmoid(gate)
    hidden = (gate * sigma * upper).astype(jnp.bfloat16)
    cot_all = square.gather(cotangent)
    grad_down = line.left(cot_all, hidden)
    d_hidden = jnp.einsum("td,fd->tf", cot_all, w_down, preferred_element_type=jnp.float32)
    d_upper = (d_hidden * gate * sigma).astype(jnp.bfloat16)
    d_gate = (d_hidden * upper * sigma * (1.0 + gate * (1.0 - sigma))).astype(jnp.bfloat16)
    d_normed_two = square.scatter(
        (
            jnp.einsum("tf,df->td", d_gate, w_gate_up[0], preferred_element_type=jnp.float32)
            + jnp.einsum("tf,df->td", d_upper, w_gate_up[1], preferred_element_type=jnp.float32)
        ).astype(jnp.bfloat16)
    )
    grad_gate = line.right(normed_two_all, d_gate)
    grad_up = line.right(normed_two_all, d_upper)
    scaled_two = gain_two * d_normed_two
    d_middle = (
        cotangent.astype(jnp.float32)
        + inv_two * scaled_two
        - middle * inv_two**3 * jnp.mean(scaled_two * middle, axis=-1, keepdims=True)
    )
    grad_gain_two = jnp.sum(d_normed_two * middle * inv_two, axis=0)
    d_middle_all = square.gather(d_middle.astype(jnp.bfloat16))
    d_mixed = jnp.einsum(
        "td,ed->te", d_middle_all, w_out, preferred_element_type=jnp.float32
    ).astype(jnp.bfloat16)
    grad_out = line.left(d_middle_all, mixed)
    result = middle + square.scatter(
        jnp.dot(hidden, w_down, preferred_element_type=jnp.float32).astype(jnp.bfloat16)
    )
    output = result.astype(jnp.bfloat16)
    d_queries, d_keys, d_values = attend_back(
        queries, keys_rot, values, d_mixed.reshape(shape3), log_sums, places, segments, valid
    )
    d_project = jnp.concatenate(
        [
            rotate(d_queries, cosine, -sine).reshape(length, -1),
            rotate(d_keys, cosine, -sine).reshape(length, -1),
            d_values.reshape(length, -1),
        ],
        axis=1,
    ).astype(jnp.bfloat16)
    wide = d_project.shape[1] // 3
    grad_qkv = line.right(normed_all, d_project)
    grad_qkv = jnp.stack([grad_qkv[:, c * wide : (c + 1) * wide] for c in range(3)])
    d_normed = square.scatter(
        sum(
            jnp.einsum(
                "te,de->td",
                d_project[:, c * wide : (c + 1) * wide],
                w_qkv[c],
                preferred_element_type=jnp.float32,
            )
            for c in range(3)
        ).astype(jnp.bfloat16)
    )
    scaled_one = gain_one * d_normed
    d_inputs = (
        d_middle
        + inv_one * scaled_one
        - incoming * inv_one**3 * jnp.mean(scaled_one * incoming, axis=-1, keepdims=True)
    )
    grad_gain_one = jnp.sum(d_normed * incoming * inv_one, axis=0)
    grad_gain_two = sum_all(grad_gain_two, dp_size, tensor_size)
    grad_gain_one = sum_all(grad_gain_one, dp_size, tensor_size)
    return (
        output,
        d_inputs,
        grad_gain_one,
        grad_gain_two,
        grad_qkv,
        grad_out,
        jnp.stack([grad_gate, grad_up]),
        grad_down,
    )


def solution(mesh):
    placed = (
        P(("dp", "tensor"), None),
        P(),
        P(),
        P(None, None, "tensor"),
        P("tensor", None),
        P(None, None, "tensor"),
        P("tensor", None),
        P(("dp", "tensor"), None),
        P("dp"),
        P("dp"),
    )

    def body(*arrays):
        return per_device(mesh.shape["dp"], mesh.shape["tensor"], *arrays)

    return jax.shard_map(
        body,
        mesh=mesh,
        in_specs=placed,
        out_specs=(
            P(("dp", "tensor"), None),
            P(("dp", "tensor"), None),
            P(),
            P(),
            P(None, "dp", "tensor"),
            P("tensor", "dp"),
            P(None, "dp", "tensor"),
            P("tensor", "dp"),
        ),
        check_vma=False,
    )
```

```python
import functools

import jax
import jax.numpy as jnp
from jax import lax
from jax.experimental import pallas as pl
from jax.experimental.pallas import tpu as pltpu
from jax.sharding import PartitionSpec as P

HD = 128


EPS = 1e-06
THETA = 10000.0


def rope_tables(length):
    positions = jnp.arange(length).astype(jnp.float32)
    freqs = THETA ** (-(jnp.arange(HD // 2).astype(jnp.float32) * 2.0 / HD))
    angles = positions[:, None] * freqs[None, :]
    return (jnp.cos(angles), jnp.sin(angles))


def rotate(values, cosine, sine):
    half = values.shape[-1] // 2
    first = values[..., :half]
    second = values[..., half:]
    cosine = cosine[:, None, :]
    sine = sine[:, None, :]
    return jnp.concatenate(
        [first * cosine - second * sine, second * cosine + first * sine], axis=-1
    )


def block_scores(q_block, keys_rot, start, segments, valid):
    block_rows = q_block.shape[0]
    length = keys_rot.shape[0]
    key_pos = jnp.arange(length)
    row_pos = start + jnp.arange(block_rows)
    row_seg = lax.dynamic_slice_in_dim(segments, start, block_rows, 0)
    scores = jnp.einsum(
        "qhd,khd->hqk", q_block, keys_rot, preferred_element_type=jnp.float32
    ) * HD ** (-0.5)
    allowed = (
        (key_pos[None, :] <= row_pos[:, None])
        & (row_seg[:, None] == segments[None, :])
        & ((valid[None, :] == 1) | (key_pos[None, :] == row_pos[:, None]))
    )
    return jnp.where(allowed[None], scores, -1e30)


def attend(queries, keys_rot, values, segments, valid):
    length = queries.shape[0]
    block_rows = min(512, length)
    count = length // block_rows

    def one_block(index):
        start = index * block_rows
        q_block = lax.dynamic_slice_in_dim(queries, start, block_rows, 0)
        scores = block_scores(q_block, keys_rot, start, segments, valid)
        top = jnp.max(scores, axis=-1, keepdims=True)
        expo = jnp.exp(scores - top)
        total = jnp.sum(expo, axis=-1, keepdims=True)
        probs = (expo / total).astype(jnp.bfloat16)
        result = jnp.einsum("hqk,khd->qhd", probs, values, preferred_element_type=jnp.float32)
        return (result, top[..., 0] + jnp.log(total[..., 0]))

    blocks, log_sums = lax.map(one_block, jnp.arange(count))
    return (blocks.reshape(length, -1), log_sums)


def attend_back(queries, keys_rot, values, d_mixed, log_sums, segments, valid):
    length = queries.shape[0]
    block_rows = min(512, length)
    count = length // block_rows
    scale = HD ** (-0.5)

    def one_block(carry, index):
        d_keys, d_values = carry
        start = index * block_rows
        q_block = lax.dynamic_slice_in_dim(queries, start, block_rows, 0)
        d_block = lax.dynamic_slice_in_dim(d_mixed, start, block_rows, 0)
        scores = block_scores(q_block, keys_rot, start, segments, valid)
        probs = jnp.exp(scores - log_sums[index][..., None])
        d_values = d_values + jnp.einsum(
            "hqk,qhd->khd", probs.astype(jnp.bfloat16), d_block, preferred_element_type=jnp.float32
        )
        d_probs = jnp.einsum("qhd,khd->hqk", d_block, values, preferred_element_type=jnp.float32)
        delta = jnp.sum(d_probs * probs, axis=-1, keepdims=True)
        d_scores = (probs * (d_probs - delta)).astype(jnp.bfloat16)
        d_query = scale * jnp.einsum(
            "hqk,khd->qhd", d_scores, keys_rot, preferred_element_type=jnp.float32
        )
        d_keys = d_keys + scale * jnp.einsum(
            "hqk,qhd->khd", d_scores, q_block, preferred_element_type=jnp.float32
        )
        return ((d_keys, d_values), d_query)

    empty = jnp.zeros(keys_rot.shape, jnp.float32)
    (d_keys, d_values), d_queries = lax.scan(one_block, (empty, empty), jnp.arange(count))
    return (d_queries.reshape(queries.shape), d_keys, d_values)


def per_device(
    tokens, gain_attn, gain_mlp, w_qkv, w_out, w_gate_up, w_down, cotangent, segment_ids, valid_mask
):
    length = segment_ids.shape[0]
    heads_here = w_qkv.shape[2] // HD
    shape3 = (length, heads_here, HD)
    incoming = tokens.astype(jnp.float32)
    gain_one = gain_attn.astype(jnp.float32)
    gain_two = gain_mlp.astype(jnp.float32)
    cosine, sine = rope_tables(length)
    inv_one = lax.rsqrt(jnp.mean(incoming * incoming, axis=-1, keepdims=True) + EPS)
    normed = (incoming * inv_one * gain_one).astype(jnp.bfloat16)
    normed_all = lax.all_gather(normed, "tensor", axis=0, tiled=True)
    project = jnp.einsum("td,cde->cte", normed_all, w_qkv, preferred_element_type=jnp.float32)
    queries = rotate(project[0].reshape(shape3), cosine, sine).astype(jnp.bfloat16)
    keys_rot = rotate(project[1].reshape(shape3), cosine, sine).astype(jnp.bfloat16)
    values = project[2].reshape(shape3).astype(jnp.bfloat16)
    mixed, log_sums = attend(queries, keys_rot, values, segment_ids, valid_mask)
    mixed = mixed.astype(jnp.bfloat16)
    middle = incoming + lax.psum_scatter(
        jnp.dot(mixed, w_out, preferred_element_type=jnp.float32).astype(jnp.bfloat16),
        "tensor",
        scatter_dimension=0,
        tiled=True,
    ).astype(jnp.float32)
    inv_two = lax.rsqrt(jnp.mean(middle * middle, axis=-1, keepdims=True) + EPS)
    normed_two = (middle * inv_two * gain_two).astype(jnp.bfloat16)
    normed_two_all = lax.all_gather(normed_two, "tensor", axis=0, tiled=True)
    gate = jnp.dot(normed_two_all, w_gate_up[0], preferred_element_type=jnp.float32)
    upper = jnp.dot(normed_two_all, w_gate_up[1], preferred_element_type=jnp.float32)
    sigma = jax.nn.sigmoid(gate)
    hidden = (gate * sigma * upper).astype(jnp.bfloat16)
    result = middle + lax.psum_scatter(
        jnp.dot(hidden, w_down, preferred_element_type=jnp.float32).astype(jnp.bfloat16),
        "tensor",
        scatter_dimension=0,
        tiled=True,
    ).astype(jnp.float32)
    output = result.astype(jnp.bfloat16)
    cot_all = lax.all_gather(cotangent, "tensor", axis=0, tiled=True)
    d_hidden = jnp.einsum("td,fd->tf", cot_all, w_down, preferred_element_type=jnp.float32)
    grad_down = jnp.einsum("tf,td->fd", hidden, cot_all, preferred_element_type=jnp.float32)
    d_upper = (d_hidden * gate * sigma).astype(jnp.bfloat16)
    d_gate = (d_hidden * upper * sigma * (1.0 + gate * (1.0 - sigma))).astype(jnp.bfloat16)
    grad_gate_up = jnp.stack(
        [
            jnp.einsum("td,tf->df", normed_two_all, d_gate, preferred_element_type=jnp.float32),
            jnp.einsum("td,tf->df", normed_two_all, d_upper, preferred_element_type=jnp.float32),
        ]
    )
    d_normed_two = lax.psum_scatter(
        (
            jnp.einsum("tf,df->td", d_gate, w_gate_up[0], preferred_element_type=jnp.float32)
            + jnp.einsum("tf,df->td", d_upper, w_gate_up[1], preferred_element_type=jnp.float32)
        ).astype(jnp.bfloat16),
        "tensor",
        scatter_dimension=0,
        tiled=True,
    ).astype(jnp.float32)
    scaled_two = gain_two * d_normed_two
    d_middle = (
        cotangent.astype(jnp.float32)
        + inv_two * scaled_two
        - middle * inv_two**3 * jnp.mean(scaled_two * middle, axis=-1, keepdims=True)
    )
    grad_gain_two = jnp.sum(d_normed_two * middle * inv_two, axis=0)
    d_middle_all = lax.all_gather(d_middle.astype(jnp.bfloat16), "tensor", axis=0, tiled=True)
    d_mixed = jnp.einsum(
        "td,ed->te", d_middle_all, w_out, preferred_element_type=jnp.float32
    ).astype(jnp.bfloat16)
    grad_out = jnp.einsum("te,td->ed", mixed, d_middle_all, preferred_element_type=jnp.float32)
    d_queries, d_keys, d_values = attend_back(
        queries, keys_rot, values, d_mixed.reshape(shape3), log_sums, segment_ids, valid_mask
    )
    d_project = jnp.stack(
        [
            rotate(d_queries, cosine, -sine).reshape(length, -1),
            rotate(d_keys, cosine, -sine).reshape(length, -1),
            d_values.reshape(length, -1),
        ]
    ).astype(jnp.bfloat16)
    grad_qkv = jnp.einsum("td,cte->cde", normed_all, d_project, preferred_element_type=jnp.float32)
    d_normed = lax.psum_scatter(
        jnp.einsum("cte,cde->td", d_project, w_qkv, preferred_element_type=jnp.float32).astype(
            jnp.bfloat16
        ),
        "tensor",
        scatter_dimension=0,
        tiled=True,
    ).astype(jnp.float32)
    scaled_one = gain_one * d_normed
    d_inputs = (
        d_middle
        + inv_one * scaled_one
        - incoming * inv_one**3 * jnp.mean(scaled_one * incoming, axis=-1, keepdims=True)
    )
    grad_gain_one = jnp.sum(d_normed * incoming * inv_one, axis=0)
    grad_gain_one, grad_gain_two = lax.psum((grad_gain_one, grad_gain_two), ("dp", "tensor"))
    grad_qkv, grad_out, grad_gate_up, grad_down = (
        lax.psum_scatter(
            grad_qkv.astype(jnp.bfloat16), "dp", scatter_dimension=1, tiled=True
        ).astype(jnp.float32),
        lax.psum_scatter(
            grad_out.astype(jnp.bfloat16), "dp", scatter_dimension=1, tiled=True
        ).astype(jnp.float32),
        lax.psum_scatter(
            grad_gate_up.astype(jnp.bfloat16), "dp", scatter_dimension=1, tiled=True
        ).astype(jnp.float32),
        lax.psum_scatter(
            grad_down.astype(jnp.bfloat16), "dp", scatter_dimension=1, tiled=True
        ).astype(jnp.float32),
    )
    return (
        output,
        d_inputs,
        grad_gain_one,
        grad_gain_two,
        grad_qkv,
        grad_out,
        grad_gate_up,
        grad_down,
    )


NT = (((1,), (1,)), ((), ()))
TN = (((0,), (0,)), ((), ()))
SPARE = 100 * 1024 * 1024 // 2


def chunks(total, step):
    return [(at, min(step, total - at)) for at in range(0, total, step)]


def dot(left, right, dims=None):
    if dims is None:
        return jnp.dot(left, right, preferred_element_type=jnp.float32)
    return lax.dot_general(left, right, dims, preferred_element_type=jnp.float32)


def in_vmem(count):
    return [pl.BlockSpec(memory_space=pltpu.VMEM)] * count


def anywhere(count):
    return [pl.BlockSpec(memory_space=pl.ANY)] * count


def like(shape, kind=jnp.bfloat16):
    return jax.ShapeDtypeStruct(shape, kind)


class Copies:
    def __init__(self, sems):
        self.sems = sems
        self.used = 0

    def start(self, source, target):
        copy = pltpu.make_async_copy(source, target, self.sems.at[self.used])
        self.used += 1
        copy.start()
        return copy


def block_starts(blocks):
    at, starts = 0, []
    for block in blocks:
        starts.append((at, block.shape[0]))
        at += block.shape[0]
    return starts


def send_specs(rows, width):
    half = rows // 2
    return [
        like((rows, width), jnp.float32),
        like((rows, width)),
        like((rows, width)),
        like((half, width)),
        like((half, width)),
    ]


def attend_kernel(
    rows_at, own, from_x, from_y, low, high, w_qkv, w_out, cosine, sine, seg_row, seg_col, valid_col,
    keep, to_x, to_y, far_low, far_high, normed_all, queries, keys, values, probs, mixed,
    w_qkv_v, w_out_v, bias, normed_v, q_v, k_v, v_v, probs_v, joined_v, mixed_v, sems,
):
    copies = Copies(sems)
    length = normed_v.shape[0]
    wide = q_v.shape[1]
    step = 2 * HD
    arrive = {}
    for c in range(3):
        for at, size in chunks(wide, step):
            arrive[c, at] = copies.start(
                w_qkv.at[c, :, pl.ds(at, size)], w_qkv_v.at[c, :, pl.ds(at, size)]
            )
    out_arrive = copies.start(w_out, w_out_v)
    blocks = [own, from_x, from_y, low, high]
    starts = block_starts(blocks)
    for i, block in enumerate(blocks):
        place = pl.multiple_of(rows_at[i], 64)
        normed_v[pl.ds(place, block.shape[0]), :] = block[...]
    leave = [copies.start(normed_v, normed_all)]
    key_at = lax.broadcasted_iota(jnp.int32, (length, length), 0)
    query_at = lax.broadcasted_iota(jnp.int32, (length, length), 1)
    allowed = (
        (key_at <= query_at)
        & (seg_col[...] == seg_row[...])
        & ((valid_col[...] == 1) | (key_at == query_at))
    )
    bias[...] = jnp.where(allowed, 0.0, -1e30)
    for c, target in enumerate((q_v, k_v, v_v)):
        for at, size in chunks(wide, step):
            arrive[c, at].wait()
            part = dot(normed_v[...], w_qkv_v[c, :, at : at + size])
            for head in range(0, size, HD):
                piece = part[:, head : head + HD]
                if c < 2:
                    piece = piece * cosine[...] + pltpu.roll(piece, HD // 2, 1) * sine[...]
                target[:, at + head : at + head + HD] = piece.astype(jnp.bfloat16)
    leave += [copies.start(q_v, queries), copies.start(k_v, keys), copies.start(v_v, values)]
    block_rows = 256
    for at in range(0, wide, HD):
        head = at // HD
        for q_at, q_size in chunks(length, block_rows):
            seen = q_at + q_size
            scores = dot(k_v[0:seen, at : at + HD], q_v[q_at:seen, at : at + HD], NT)
            scores = scores * HD ** (-0.5) + bias[0:seen, q_at:seen]
            top = jnp.max(scores, axis=0, keepdims=True)
            expo = jnp.exp(scores - top)
            total = jnp.sum(expo, axis=0, keepdims=True)
            chance = (expo * (1.0 / total)).astype(jnp.bfloat16)
            probs_v[head, 0:seen, q_at:seen] = chance
            result = dot(v_v[0:seen, at : at + HD], chance, TN)
            joined_v[q_at:seen, at : at + HD] = result.T.astype(jnp.bfloat16)
    leave.append(copies.start(probs_v, probs))
    for i, (start, size) in enumerate(starts):
        place = pl.multiple_of(rows_at[i], 64)
        mixed_v[start : start + size, :] = joined_v[pl.ds(place, size), :]
    leave.append(copies.start(mixed_v, mixed))
    out_arrive.wait()
    targets = [keep, to_x, to_y, far_low, far_high]
    for at, size in chunks(w_out.shape[1], 512):
        part = dot(mixed_v[...], w_out_v[:, at : at + size])
        for (start, rows), target in zip(starts, targets):
            target[:, at : at + size] = part[start : start + rows].astype(target.dtype)
    for copy in leave:
        copy.wait()


def attend_square(rows_at, blocks, w_qkv, w_out, cosine, sine, seg_row, seg_col, valid_col):
    rows, width = blocks[0].shape
    length = 4 * rows
    wide = w_qkv.shape[2]
    heads = wide // HD
    return pl.pallas_call(
        attend_kernel,
        name="attend",
        out_shape=send_specs(rows, width)
        + [
            like((length, width)),
            like((length, wide)),
            like((length, wide)),
            like((length, wide)),
            like((heads, length, length)),
            like((length, wide)),
        ],
        in_specs=[pl.BlockSpec(memory_space=pltpu.SMEM)] + in_vmem(5) + anywhere(2) + in_vmem(5),
        out_specs=in_vmem(5) + anywhere(6),
        scratch_shapes=[
            pltpu.VMEM(w_qkv.shape, jnp.bfloat16),
            pltpu.VMEM(w_out.shape, jnp.bfloat16),
            pltpu.VMEM((length, length), jnp.float32),
            pltpu.VMEM((length, width), jnp.bfloat16),
            pltpu.VMEM((length, wide), jnp.bfloat16),
            pltpu.VMEM((length, wide), jnp.bfloat16),
            pltpu.VMEM((length, wide), jnp.bfloat16),
            pltpu.VMEM((heads, length, length), jnp.bfloat16),
            pltpu.VMEM((length, wide), jnp.bfloat16),
            pltpu.VMEM((length, wide), jnp.bfloat16),
            pltpu.SemaphoreType.DMA((3 * (wide // (2 * HD)) + 8,)),
        ],
        compiler_params=pltpu.CompilerParams(vmem_limit_bytes=SPARE),
    )(rows_at, *blocks, w_qkv, w_out, cosine, sine, seg_row, seg_col, valid_col)


def d_hidden_kernel(count, *refs):
    blocks = refs[:count]
    w_down, d_hidden, cot_all, w_down_v, cot_v, d_hidden_v, sems = refs[count:]
    copies = Copies(sems)
    parts = chunks(w_down.shape[0], 256)
    arrive = [
        copies.start(w_down.at[pl.ds(at, size), :], w_down_v.at[pl.ds(at, size), :])
        for at, size in parts
    ]
    for (start, size), block in zip(block_starts(blocks), blocks):
        cot_v[start : start + size, :] = block[...]
    leave = [copies.start(cot_v, cot_all)]
    for (at, size), copy in zip(parts, arrive):
        copy.wait()
        d_hidden_v[:, at : at + size] = dot(cot_v[...], w_down_v[at : at + size, :], NT)
        leave.append(
            copies.start(d_hidden_v.at[:, pl.ds(at, size)], d_hidden.at[:, pl.ds(at, size)])
        )
    for copy in leave:
        copy.wait()


def back_through_down(blocks, w_down):
    width = blocks[0].shape[1]
    length = sum(block.shape[0] for block in blocks)
    units = w_down.shape[0]
    return pl.pallas_call(
        functools.partial(d_hidden_kernel, len(blocks)),
        name="back_through_down",
        out_shape=[like((length, units), jnp.float32), like((length, width))],
        in_specs=in_vmem(len(blocks)) + anywhere(1),
        out_specs=anywhere(2),
        scratch_shapes=[
            pltpu.VMEM(w_down.shape, jnp.bfloat16),
            pltpu.VMEM((length, width), jnp.bfloat16),
            pltpu.VMEM((length, units), jnp.float32),
            pltpu.SemaphoreType.DMA((2 * len(chunks(units, 256)) + 1,)),
        ],
        compiler_params=pltpu.CompilerParams(vmem_limit_bytes=SPARE),
    )(*blocks, w_down)


def mlp_kernel(
    sends, own, from_x, from_y, low, high, d_hidden, w_gate_up, *rest
):
    outs, scratch = rest[: 3 + 5 * sends], rest[3 + 5 * sends :]
    normed_all, hidden, d_gate_up = outs[:3]
    targets = outs[3:]
    w_v, normed_v, d_hidden_v, hidden_v, d_gate_up_v, sems = scratch
    copies = Copies(sems)
    units = w_gate_up.shape[2]
    parts = chunks(units, 256)
    arrive = []
    for at, size in parts:
        arrive.append(
            [
                copies.start(w_gate_up.at[c, :, pl.ds(at, size)], w_v.at[c, :, pl.ds(at, size)])
                for c in range(2)
            ]
            + [copies.start(d_hidden.at[:, pl.ds(at, size)], d_hidden_v.at[:, pl.ds(at, size)])]
        )
    blocks = [own, from_x, from_y, low, high]
    starts = block_starts(blocks)
    for (start, size), block in zip(starts, blocks):
        normed_v[start : start + size, :] = block[...]
    leave = [copies.start(normed_v, normed_all)]
    for (at, size), pending in zip(parts, arrive):
        for copy in pending:
            copy.wait()
        here = slice(at, at + size)
        gate = dot(normed_v[...], w_v[0, :, here])
        upper = dot(normed_v[...], w_v[1, :, here])
        incoming = d_hidden_v[:, here]
        sigma = 1.0 / (1.0 + jnp.exp(-gate))
        silu = gate * sigma
        hidden_v[:, here] = (silu * upper).astype(jnp.bfloat16)
        d_gate_up_v[:, here] = (incoming * upper * sigma * (1.0 + gate * (1.0 - sigma))).astype(
            jnp.bfloat16
        )
        d_gate_up_v[:, units + at : units + at + size] = (incoming * silu).astype(jnp.bfloat16)
    leave += [copies.start(hidden_v, hidden), copies.start(d_gate_up_v, d_gate_up)]
    if sends:
        for at, size in chunks(normed_v.shape[1], 256):
            part = dot(d_gate_up_v[:, 0:units], w_v[0, at : at + size, :], NT) + dot(
                d_gate_up_v[:, units : 2 * units], w_v[1, at : at + size, :], NT
            )
            for (start, rows), target in zip(starts, targets):
                target[:, at : at + size] = part[start : start + rows].astype(target.dtype)
    for copy in leave:
        copy.wait()


def mlp(blocks, d_hidden, w_gate_up, sends):
    rows, width = blocks[0].shape
    length = 4 * rows
    units = w_gate_up.shape[2]
    return pl.pallas_call(
        functools.partial(mlp_kernel, sends),
        name="mlp" if sends else "mlp_guest",
        out_shape=[like((length, width)), like((length, units)), like((length, 2 * units))]
        + (send_specs(rows, width) if sends else []),
        in_specs=in_vmem(5) + anywhere(2),
        out_specs=anywhere(3) + in_vmem(5 * sends),
        scratch_shapes=[
            pltpu.VMEM(w_gate_up.shape, jnp.bfloat16),
            pltpu.VMEM((length, width), jnp.bfloat16),
            pltpu.VMEM((length, units), jnp.float32),
            pltpu.VMEM((length, units), jnp.bfloat16),
            pltpu.VMEM((length, 2 * units), jnp.bfloat16),
            pltpu.SemaphoreType.DMA((3 * len(chunks(units, 256)) + 3,)),
        ],
        compiler_params=pltpu.CompilerParams(vmem_limit_bytes=SPARE),
    )(*blocks, d_hidden, w_gate_up)


def attend_back_kernel(
    rows_at, own, from_x, from_y, low, high, w_out, w_qkv, probs, queries, keys, values, cosine, sine,
    keep, to_x, to_y, far_low, far_high, d_middle_all, d_project,
    w_out_v, w_qkv_v, probs_v, q_v, k_v, v_v, d_middle_v, d_mixed_v, d_project_v, turned_v, sems,
):
    copies = Copies(sems)
    length = d_middle_v.shape[0]
    wide = q_v.shape[1]
    out_arrive = copies.start(w_out, w_out_v)
    arrive = [
        copies.start(probs, probs_v),
        copies.start(queries, q_v),
        copies.start(keys, k_v),
        copies.start(values, v_v),
    ]
    qkv_arrive = copies.start(w_qkv, w_qkv_v)
    blocks = [own, from_x, from_y, low, high]
    starts = block_starts(blocks)
    for (start, size), block in zip(starts, blocks):
        d_middle_v[start : start + size, :] = block[...]
    leave = [copies.start(d_middle_v, d_middle_all)]
    out_arrive.wait()
    for at, size in chunks(wide, 256):
        part = dot(d_middle_v[...], w_out_v[at : at + size, :], NT).astype(jnp.bfloat16)
        for i, (start, rows) in enumerate(starts):
            place = pl.multiple_of(rows_at[i], 64)
            d_mixed_v[pl.ds(place, rows), at : at + size] = part[start : start + rows]
    for copy in arrive:
        copy.wait()
    scale = HD ** (-0.5)

    def back(turned, rows):
        return turned * cosine[rows, :] - pltpu.roll(turned, HD // 2, 1) * sine[rows, :]

    block_rows = 256
    for at in range(0, wide, HD):
        head = at // HD
        cols = slice(at, at + HD)
        d_keys = d_values = None
        for q_at, q_size in reversed(chunks(length, block_rows)):
            seen = q_at + q_size
            rows = slice(q_at, seen)
            chance = probs_v[head, 0:seen, rows]
            d_out = d_mixed_v[rows, cols]
            d_chance = dot(v_v[0:seen, cols], d_out, NT)
            exact = chance.astype(jnp.float32)
            delta = jnp.sum(d_chance * exact, axis=0, keepdims=True)
            d_scores = (exact * (d_chance - delta)).astype(jnp.bfloat16)
            more_values = dot(chance, d_out)
            more_keys = dot(d_scores, q_v[rows, cols])
            d_queries = dot(k_v[0:seen, cols], d_scores, TN).T
            d_project_v[rows, cols] = back(d_queries * scale, rows).astype(jnp.bfloat16)
            if d_keys is None:
                d_keys, d_values = more_keys, more_values
            else:
                d_keys = jnp.concatenate([d_keys[:seen] + more_keys, d_keys[seen:]], axis=0)
                d_values = jnp.concatenate([d_values[:seen] + more_values, d_values[seen:]], axis=0)
        everything = slice(0, length)
        d_project_v[:, wide + at : wide + at + HD] = back(d_keys * scale, everything).astype(
            jnp.bfloat16
        )
        d_project_v[:, 2 * wide + at : 2 * wide + at + HD] = d_values.astype(jnp.bfloat16)
    leave.append(copies.start(d_project_v, d_project))
    for i, (start, size) in enumerate(starts):
        place = pl.multiple_of(rows_at[i], 64)
        turned_v[start : start + size, :] = d_project_v[pl.ds(place, size), :]
    qkv_arrive.wait()
    targets = [keep, to_x, to_y, far_low, far_high]
    for at, size in chunks(d_middle_v.shape[1], 256):
        part = sum(
            dot(turned_v[:, c * wide : (c + 1) * wide], w_qkv_v[c, at : at + size, :], NT)
            for c in range(3)
        )
        for (start, rows), target in zip(starts, targets):
            target[:, at : at + size] = part[start : start + rows].astype(target.dtype)
    for copy in leave:
        copy.wait()


def attend_back_square(rows_at, blocks, w_out, w_qkv, probs, queries, keys, values, cosine, sine):
    rows, width = blocks[0].shape
    length = 4 * rows
    wide = w_qkv.shape[2]
    return pl.pallas_call(
        attend_back_kernel,
        name="attend_back",
        out_shape=send_specs(rows, width) + [like((length, width)), like((length, 3 * wide))],
        in_specs=[pl.BlockSpec(memory_space=pltpu.SMEM)] + in_vmem(5) + anywhere(6) + in_vmem(2),
        out_specs=in_vmem(5) + anywhere(2),
        scratch_shapes=[
            pltpu.VMEM(w_out.shape, jnp.bfloat16),
            pltpu.VMEM(w_qkv.shape, jnp.bfloat16),
            pltpu.VMEM(probs.shape, jnp.bfloat16),
            pltpu.VMEM(queries.shape, jnp.bfloat16),
            pltpu.VMEM(queries.shape, jnp.bfloat16),
            pltpu.VMEM(queries.shape, jnp.bfloat16),
            pltpu.VMEM((length, width), jnp.bfloat16),
            pltpu.VMEM((length, wide), jnp.bfloat16),
            pltpu.VMEM((length, 3 * wide), jnp.bfloat16),
            pltpu.VMEM((length, 3 * wide), jnp.bfloat16),
            pltpu.SemaphoreType.DMA((8,)),
        ],
        compiler_params=pltpu.CompilerParams(vmem_limit_bytes=SPARE),
    )(rows_at, *blocks, w_out, w_qkv, probs, queries, keys, values, cosine, sine)


def weight_kernel(count, which, *refs):
    splits, others = refs[:count], refs[count : 2 * count]
    rest = refs[2 * count :]
    turned = rest[-1]
    out = rest[-2]
    more = rest[0] if len(rest) == 3 else None
    length = splits[0].shape[0]
    for i, split in enumerate(splits):
        turned[:, i * length : (i + 1) * length] = split[...].T
    for at, size in chunks(out.shape[2], 256):
        part = None
        for i, other in enumerate(others):
            piece = dot(turned[:, i * length : (i + 1) * length], other[:, at : at + size])
            part = piece if part is None else part + piece
        if more is not None:
            part = part + more[0, :, at : at + size].astype(jnp.float32)
        out[0, :, at : at + size] = part.astype(out.dtype)


def weight_pieces(which, splits, others, more=None, base=0):
    count = which.shape[0]
    length, width = splits[0].shape
    across = others[0].shape[1]
    piece = 256
    step = [pl.BlockSpec((length, piece), lambda i, which: (0, which[i]))] * len(splits)
    whole = [pl.BlockSpec((length, across), lambda i, which: (0, 0))] * len(others)
    one = pl.BlockSpec((1, piece, across), lambda i, which: (i, 0, 0))
    added = pl.BlockSpec((1, piece, across), lambda i, which: (base + i, 0, 0))
    return pl.pallas_call(
        functools.partial(weight_kernel, len(splits)),
        name="weight_pieces",
        grid_spec=pltpu.PrefetchScalarGridSpec(
            num_scalar_prefetch=1,
            grid=(count,),
            in_specs=step + whole + ([added] if more is not None else []),
            out_specs=one,
            scratch_shapes=[pltpu.VMEM((piece, len(splits) * length), jnp.bfloat16)],
        ),
        out_shape=like((count, piece, across)),
        compiler_params=pltpu.CompilerParams(vmem_limit_bytes=SPARE),
    )(which, *splits, *others, *([more] if more is not None else []))


def flips(size, bit):
    return [(i, i ^ bit) for i in range(size)]


def over_tensor(values, bit):
    return lax.ppermute(values, "tensor", flips(4, bit))


def gather_blocks(own):
    half = own.shape[0] // 2
    from_x = over_tensor(own, 1)
    from_y = over_tensor(own, 2)
    low = over_tensor(from_y[:half], 1)
    high = over_tensor(from_x[half:], 2)
    return [own, from_x, from_y, low, high]


def scatter_blocks(keep, to_x, to_y, far_low, far_high):
    half = far_low.shape[0]
    via_x = over_tensor(far_low, 1)
    via_y = over_tensor(far_high, 2)
    wide = jnp.float32
    to_x = to_x.at[half:].set((to_x[half:].astype(wide) + via_y.astype(wide)).astype(to_x.dtype))
    to_y = to_y.at[:half].set((to_y[:half].astype(wide) + via_x.astype(wide)).astype(to_y.dtype))
    return keep + over_tensor(to_x, 1).astype(wide) + over_tensor(to_y, 2).astype(wide)


def rows_of(blocks):
    return jnp.concatenate(blocks, axis=0)


def over_cores(values):
    return lax.ppermute(values, "dp", flips(8, 1))


def to_inner(values):
    return lax.ppermute(values, "dp", [(0, 2), (1, 3), (6, 4), (7, 5)])


def to_outer(values):
    return lax.ppermute(values, "dp", [(2, 0), (3, 1), (4, 6), (5, 7)])


def over_middle(values):
    return lax.ppermute(values, "dp", [(2, 4), (3, 5), (4, 2), (5, 3)])


def sum_over_chips(splits, others):
    index = lax.axis_index("dp")
    place, core = index // 2, index % 2
    order = jnp.where(place < 2, jnp.array([3, 2, 0, 1]), jnp.array([0, 1, 3, 2])).astype(jnp.int32)
    theirs = over_cores(weight_pieces(2 * order + 1 - core, splits, others))
    mine = 2 * order + core
    far = over_middle(weight_pieces(mine[:2], splits, others, theirs, 0))
    near = weight_pieces(mine[2:], splits, others, theirs, 2)
    total = near.astype(jnp.float32) + far.astype(jnp.float32)
    given = to_outer(total[0].astype(jnp.bfloat16)).astype(jnp.float32)
    return jnp.where((place == 1) | (place == 2), total[1], given)


def sum_everywhere(values):
    for axis, size, bit in (
        ("dp", 8, 1),
        ("tensor", 4, 1),
        ("tensor", 4, 2),
        ("dp", 8, 2),
        ("dp", 8, 4),
    ):
        values = values + lax.ppermute(values, axis, flips(size, bit))
    return values


def per_device_square(
    tokens, gain_attn, gain_mlp, w_qkv, w_out, w_gate_up, w_down, cotangent, segment_ids, valid_mask
):
    rows = tokens.shape[0]
    length = segment_ids.shape[0]
    me = lax.axis_index("tensor")
    order = [me, me ^ 1, me ^ 2, me ^ 3]
    rows_at = jnp.stack([at * rows for at in order] + [order[3] * rows + rows // 2]).astype(jnp.int32)
    cosine, sine = rope_tables(length)
    cosine_full = jnp.concatenate([cosine, cosine], axis=1)
    sine_full = jnp.concatenate([-sine, sine], axis=1)
    incoming = tokens.astype(jnp.float32)
    gain_one = gain_attn.astype(jnp.float32)
    gain_two = gain_mlp.astype(jnp.float32)

    inv_one = lax.rsqrt(jnp.mean(incoming * incoming, axis=-1, keepdims=True) + EPS)
    normed = (incoming * inv_one * gain_one).astype(jnp.bfloat16)
    *sent, normed_all, queries, keys, values, probs, mixed = attend_square(
        rows_at,
        gather_blocks(normed),
        w_qkv,
        w_out,
        cosine_full,
        sine_full,
        segment_ids[None, :],
        segment_ids[:, None],
        valid_mask[:, None],
    )
    middle = incoming + scatter_blocks(*sent)
    inv_two = lax.rsqrt(jnp.mean(middle * middle, axis=-1, keepdims=True) + EPS)
    normed_two = (middle * inv_two * gain_two).astype(jnp.bfloat16)
    d_hidden, cot_all = back_through_down(gather_blocks(cotangent), w_down)
    normed_two_all, hidden, d_gate_up, *sent_back = mlp(
        gather_blocks(normed_two), d_hidden, w_gate_up, True
    )
    d_normed_two = scatter_blocks(*sent_back)

    guest_blocks = gather_blocks(to_inner(normed_two))
    guest_cot = to_inner(cot_all)
    guest_d_hidden, _ = back_through_down([guest_cot], w_down)
    guest_normed_two, guest_hidden, guest_d_gate_up = mlp(
        guest_blocks, guest_d_hidden, w_gate_up, False
    )
    grad_down = sum_over_chips([cot_all, guest_cot], [hidden, guest_hidden])
    grad_gate_up = sum_over_chips(
        [normed_two_all, guest_normed_two], [d_gate_up, guest_d_gate_up]
    )

    scaled_two = gain_two * d_normed_two
    d_middle = (
        cotangent.astype(jnp.float32)
        + inv_two * scaled_two
        - middle * inv_two**3 * jnp.mean(scaled_two * middle, axis=-1, keepdims=True)
    )
    grad_gain_two = jnp.sum(d_normed_two * middle * inv_two, axis=0)
    *sent, d_middle_all, d_project = attend_back_square(
        rows_at,
        gather_blocks(d_middle.astype(jnp.bfloat16)),
        w_out,
        w_qkv,
        probs,
        queries,
        keys,
        values,
        cosine_full,
        sine_full,
    )
    d_normed = scatter_blocks(*sent)
    everything = jnp.arange(8, dtype=jnp.int32)
    grad_out = lax.psum_scatter(
        weight_pieces(everything, [d_middle_all], [mixed]), "dp", scatter_dimension=0
    ).astype(jnp.float32)
    grad_qkv = sum_over_chips(
        [normed_all, to_inner(normed_all)], [d_project, to_inner(d_project)]
    )

    down = jnp.dot(hidden, w_down, preferred_element_type=jnp.float32)
    half = rows // 2
    low = down.astype(jnp.bfloat16)
    result = middle + scatter_blocks(
        down[:rows], low[rows : 2 * rows], low[2 * rows : 3 * rows], low[3 * rows : 3 * rows + half],
        low[3 * rows + half :],
    )
    output = result.astype(jnp.bfloat16)

    scaled_one = gain_one * d_normed
    d_inputs = (
        d_middle
        + inv_one * scaled_one
        - incoming * inv_one**3 * jnp.mean(scaled_one * incoming, axis=-1, keepdims=True)
    )
    grad_gain_one = jnp.sum(d_normed * incoming * inv_one, axis=0)
    wide = w_qkv.shape[2]
    units = w_down.shape[0]
    return (
        output,
        d_inputs,
        sum_everywhere(grad_gain_one),
        sum_everywhere(grad_gain_two),
        jnp.stack([grad_qkv[:, c * wide : (c + 1) * wide] for c in range(3)]),
        grad_out.T,
        jnp.stack([grad_gate_up[:, c * units : (c + 1) * units] for c in range(2)]),
        grad_down.T,
    )


def solution(mesh):
    placed = (
        P(("dp", "tensor"), None),
        P(),
        P(),
        P(None, None, "tensor"),
        P("tensor", None),
        P(None, None, "tensor"),
        P("tensor", None),
        P(("dp", "tensor"), None),
        P("dp"),
        P("dp"),
    )
    square = mesh.shape["tensor"] == 4 and mesh.shape["dp"] == 8
    return jax.shard_map(
        per_device_square if square else per_device,
        mesh=mesh,
        in_specs=placed,
        out_specs=(
            P(("dp", "tensor"), None),
            P(("dp", "tensor"), None),
            P(),
            P(),
            P(None, "dp", "tensor"),
            P("tensor", "dp"),
            P(None, "dp", "tensor"),
            P("tensor", "dp"),
        ),
        check_vma=False,
    )
```

```python
import functools

import jax
import jax.numpy as jnp
from jax import lax
from jax.experimental import pallas as pl
from jax.experimental.pallas import tpu as pltpu
from jax.sharding import PartitionSpec as P

HD = 128


EPS = 1e-06
THETA = 10000.0


def rope_tables(length):
    positions = jnp.arange(length).astype(jnp.float32)
    freqs = THETA ** (-(jnp.arange(HD // 2).astype(jnp.float32) * 2.0 / HD))
    angles = positions[:, None] * freqs[None, :]
    return (jnp.cos(angles), jnp.sin(angles))


def rotate(values, cosine, sine):
    half = values.shape[-1] // 2
    first = values[..., :half]
    second = values[..., half:]
    cosine = cosine[:, None, :]
    sine = sine[:, None, :]
    return jnp.concatenate(
        [first * cosine - second * sine, second * cosine + first * sine], axis=-1
    )


def block_scores(q_block, keys_rot, start, segments, valid):
    block_rows = q_block.shape[0]
    length = keys_rot.shape[0]
    key_pos = jnp.arange(length)
    row_pos = start + jnp.arange(block_rows)
    row_seg = lax.dynamic_slice_in_dim(segments, start, block_rows, 0)
    scores = jnp.einsum(
        "qhd,khd->hqk", q_block, keys_rot, preferred_element_type=jnp.float32
    ) * HD ** (-0.5)
    allowed = (
        (key_pos[None, :] <= row_pos[:, None])
        & (row_seg[:, None] == segments[None, :])
        & ((valid[None, :] == 1) | (key_pos[None, :] == row_pos[:, None]))
    )
    return jnp.where(allowed[None], scores, -1e30)


def attend(queries, keys_rot, values, segments, valid):
    length = queries.shape[0]
    block_rows = min(512, length)
    count = length // block_rows

    def one_block(index):
        start = index * block_rows
        q_block = lax.dynamic_slice_in_dim(queries, start, block_rows, 0)
        scores = block_scores(q_block, keys_rot, start, segments, valid)
        top = jnp.max(scores, axis=-1, keepdims=True)
        expo = jnp.exp(scores - top)
        total = jnp.sum(expo, axis=-1, keepdims=True)
        probs = (expo / total).astype(jnp.bfloat16)
        result = jnp.einsum("hqk,khd->qhd", probs, values, preferred_element_type=jnp.float32)
        return (result, top[..., 0] + jnp.log(total[..., 0]))

    blocks, log_sums = lax.map(one_block, jnp.arange(count))
    return (blocks.reshape(length, -1), log_sums)


def attend_back(queries, keys_rot, values, d_mixed, log_sums, segments, valid):
    length = queries.shape[0]
    block_rows = min(512, length)
    count = length // block_rows
    scale = HD ** (-0.5)

    def one_block(carry, index):
        d_keys, d_values = carry
        start = index * block_rows
        q_block = lax.dynamic_slice_in_dim(queries, start, block_rows, 0)
        d_block = lax.dynamic_slice_in_dim(d_mixed, start, block_rows, 0)
        scores = block_scores(q_block, keys_rot, start, segments, valid)
        probs = jnp.exp(scores - log_sums[index][..., None])
        d_values = d_values + jnp.einsum(
            "hqk,qhd->khd", probs.astype(jnp.bfloat16), d_block, preferred_element_type=jnp.float32
        )
        d_probs = jnp.einsum("qhd,khd->hqk", d_block, values, preferred_element_type=jnp.float32)
        delta = jnp.sum(d_probs * probs, axis=-1, keepdims=True)
        d_scores = (probs * (d_probs - delta)).astype(jnp.bfloat16)
        d_query = scale * jnp.einsum(
            "hqk,khd->qhd", d_scores, keys_rot, preferred_element_type=jnp.float32
        )
        d_keys = d_keys + scale * jnp.einsum(
            "hqk,qhd->khd", d_scores, q_block, preferred_element_type=jnp.float32
        )
        return ((d_keys, d_values), d_query)

    empty = jnp.zeros(keys_rot.shape, jnp.float32)
    (d_keys, d_values), d_queries = lax.scan(one_block, (empty, empty), jnp.arange(count))
    return (d_queries.reshape(queries.shape), d_keys, d_values)


def per_device(
    tokens, gain_attn, gain_mlp, w_qkv, w_out, w_gate_up, w_down, cotangent, segment_ids, valid_mask
):
    length = segment_ids.shape[0]
    heads_here = w_qkv.shape[2] // HD
    shape3 = (length, heads_here, HD)
    incoming = tokens.astype(jnp.float32)
    gain_one = gain_attn.astype(jnp.float32)
    gain_two = gain_mlp.astype(jnp.float32)
    cosine, sine = rope_tables(length)
    inv_one = lax.rsqrt(jnp.mean(incoming * incoming, axis=-1, keepdims=True) + EPS)
    normed = (incoming * inv_one * gain_one).astype(jnp.bfloat16)
    normed_all = lax.all_gather(normed, "tensor", axis=0, tiled=True)
    project = jnp.einsum("td,cde->cte", normed_all, w_qkv, preferred_element_type=jnp.float32)
    queries = rotate(project[0].reshape(shape3), cosine, sine).astype(jnp.bfloat16)
    keys_rot = rotate(project[1].reshape(shape3), cosine, sine).astype(jnp.bfloat16)
    values = project[2].reshape(shape3).astype(jnp.bfloat16)
    mixed, log_sums = attend(queries, keys_rot, values, segment_ids, valid_mask)
    mixed = mixed.astype(jnp.bfloat16)
    middle = incoming + lax.psum_scatter(
        jnp.dot(mixed, w_out, preferred_element_type=jnp.float32).astype(jnp.bfloat16),
        "tensor",
        scatter_dimension=0,
        tiled=True,
    ).astype(jnp.float32)
    inv_two = lax.rsqrt(jnp.mean(middle * middle, axis=-1, keepdims=True) + EPS)
    normed_two = (middle * inv_two * gain_two).astype(jnp.bfloat16)
    normed_two_all = lax.all_gather(normed_two, "tensor", axis=0, tiled=True)
    gate = jnp.dot(normed_two_all, w_gate_up[0], preferred_element_type=jnp.float32)
    upper = jnp.dot(normed_two_all, w_gate_up[1], preferred_element_type=jnp.float32)
    sigma = jax.nn.sigmoid(gate)
    hidden = (gate * sigma * upper).astype(jnp.bfloat16)
    result = middle + lax.psum_scatter(
        jnp.dot(hidden, w_down, preferred_element_type=jnp.float32).astype(jnp.bfloat16),
        "tensor",
        scatter_dimension=0,
        tiled=True,
    ).astype(jnp.float32)
    output = result.astype(jnp.bfloat16)
    cot_all = lax.all_gather(cotangent, "tensor", axis=0, tiled=True)
    d_hidden = jnp.einsum("td,fd->tf", cot_all, w_down, preferred_element_type=jnp.float32)
    grad_down = jnp.einsum("tf,td->fd", hidden, cot_all, preferred_element_type=jnp.float32)
    d_upper = (d_hidden * gate * sigma).astype(jnp.bfloat16)
    d_gate = (d_hidden * upper * sigma * (1.0 + gate * (1.0 - sigma))).astype(jnp.bfloat16)
    grad_gate_up = jnp.stack(
        [
            jnp.einsum("td,tf->df", normed_two_all, d_gate, preferred_element_type=jnp.float32),
            jnp.einsum("td,tf->df", normed_two_all, d_upper, preferred_element_type=jnp.float32),
        ]
    )
    d_normed_two = lax.psum_scatter(
        (
            jnp.einsum("tf,df->td", d_gate, w_gate_up[0], preferred_element_type=jnp.float32)
            + jnp.einsum("tf,df->td", d_upper, w_gate_up[1], preferred_element_type=jnp.float32)
        ).astype(jnp.bfloat16),
        "tensor",
        scatter_dimension=0,
        tiled=True,
    ).astype(jnp.float32)
    scaled_two = gain_two * d_normed_two
    d_middle = (
        cotangent.astype(jnp.float32)
        + inv_two * scaled_two
        - middle * inv_two**3 * jnp.mean(scaled_two * middle, axis=-1, keepdims=True)
    )
    grad_gain_two = jnp.sum(d_normed_two * middle * inv_two, axis=0)
    d_middle_all = lax.all_gather(d_middle.astype(jnp.bfloat16), "tensor", axis=0, tiled=True)
    d_mixed = jnp.einsum(
        "td,ed->te", d_middle_all, w_out, preferred_element_type=jnp.float32
    ).astype(jnp.bfloat16)
    grad_out = jnp.einsum("te,td->ed", mixed, d_middle_all, preferred_element_type=jnp.float32)
    d_queries, d_keys, d_values = attend_back(
        queries, keys_rot, values, d_mixed.reshape(shape3), log_sums, segment_ids, valid_mask
    )
    d_project = jnp.stack(
        [
            rotate(d_queries, cosine, -sine).reshape(length, -1),
            rotate(d_keys, cosine, -sine).reshape(length, -1),
            d_values.reshape(length, -1),
        ]
    ).astype(jnp.bfloat16)
    grad_qkv = jnp.einsum("td,cte->cde", normed_all, d_project, preferred_element_type=jnp.float32)
    d_normed = lax.psum_scatter(
        jnp.einsum("cte,cde->td", d_project, w_qkv, preferred_element_type=jnp.float32).astype(
            jnp.bfloat16
        ),
        "tensor",
        scatter_dimension=0,
        tiled=True,
    ).astype(jnp.float32)
    scaled_one = gain_one * d_normed
    d_inputs = (
        d_middle
        + inv_one * scaled_one
        - incoming * inv_one**3 * jnp.mean(scaled_one * incoming, axis=-1, keepdims=True)
    )
    grad_gain_one = jnp.sum(d_normed * incoming * inv_one, axis=0)
    grad_gain_one, grad_gain_two = lax.psum((grad_gain_one, grad_gain_two), ("dp", "tensor"))
    grad_qkv, grad_out, grad_gate_up, grad_down = (
        lax.psum_scatter(
            grad_qkv.astype(jnp.bfloat16), "dp", scatter_dimension=1, tiled=True
        ).astype(jnp.float32),
        lax.psum_scatter(
            grad_out.astype(jnp.bfloat16), "dp", scatter_dimension=1, tiled=True
        ).astype(jnp.float32),
        lax.psum_scatter(
            grad_gate_up.astype(jnp.bfloat16), "dp", scatter_dimension=1, tiled=True
        ).astype(jnp.float32),
        lax.psum_scatter(
            grad_down.astype(jnp.bfloat16), "dp", scatter_dimension=1, tiled=True
        ).astype(jnp.float32),
    )
    return (
        output,
        d_inputs,
        grad_gain_one,
        grad_gain_two,
        grad_qkv,
        grad_out,
        grad_gate_up,
        grad_down,
    )


NT = (((1,), (1,)), ((), ()))
TN = (((0,), (0,)), ((), ()))
SPARE = 20 * 1024 * 1024


def chunks(total, step):
    return [(at, min(step, total - at)) for at in range(0, total, step)]


def dot(left, right, dims=None):
    if dims is None:
        return jnp.dot(left, right, preferred_element_type=jnp.float32)
    return lax.dot_general(left, right, dims, preferred_element_type=jnp.float32)


def in_vmem(count):
    return [pl.BlockSpec(memory_space=pltpu.VMEM)] * count


def anywhere(count):
    return [pl.BlockSpec(memory_space=pl.ANY)] * count


def like(shape, kind=jnp.bfloat16):
    return jax.ShapeDtypeStruct(shape, kind)


class Copies:
    def __init__(self, sems):
        self.sems = sems
        self.used = 0

    def start(self, source, target):
        copy = pltpu.make_async_copy(source, target, self.sems.at[self.used])
        self.used += 1
        copy.start()
        return copy


def block_starts(blocks):
    at, starts = 0, []
    for block in blocks:
        starts.append((at, block.shape[0]))
        at += block.shape[0]
    return starts


def send_specs(rows, width):
    half = rows // 2
    return [
        like((rows, width), jnp.float32),
        like((rows, width)),
        like((rows, width)),
        like((half, width)),
        like((half, width)),
    ]


def attend_kernel(
    rows_at, own, from_x, from_y, low, high, w_qkv, w_out, cosine, sine, seg_row, seg_col, valid_col,
    keep, to_x, to_y, far_low, far_high, normed_all, queries, keys, values, probs, mixed,
    bias, normed_v, q_v, k_v, v_v, probs_v, joined_v, mixed_v, sems,
):
    copies = Copies(sems)
    length = normed_v.shape[0]
    wide = q_v.shape[1]
    step = 2 * HD
    blocks = [own, from_x, from_y, low, high]
    starts = block_starts(blocks)
    for i, block in enumerate(blocks):
        place = pl.multiple_of(rows_at[i], 64)
        normed_v[pl.ds(place, block.shape[0]), :] = block[...]
    leave = [copies.start(normed_v, normed_all)]
    key_at = lax.broadcasted_iota(jnp.int32, (length, length), 0)
    query_at = lax.broadcasted_iota(jnp.int32, (length, length), 1)
    allowed = (
        (key_at <= query_at)
        & (seg_col[...] == seg_row[...])
        & ((valid_col[...] == 1) | (key_at == query_at))
    )
    bias[...] = jnp.where(allowed, 0.0, -1e30)
    for c, target in enumerate((q_v, k_v, v_v)):
        for at, size in chunks(wide, step):
            part = dot(normed_v[...], w_qkv[c, :, at : at + size])
            for head in range(0, size, HD):
                piece = part[:, head : head + HD]
                if c < 2:
                    piece = piece * cosine[...] + pltpu.roll(piece, HD // 2, 1) * sine[...]
                target[:, at + head : at + head + HD] = piece.astype(jnp.bfloat16)
    leave += [copies.start(q_v, queries), copies.start(k_v, keys), copies.start(v_v, values)]
    block_rows = 256
    for at in range(0, wide, HD):
        head = at // HD
        for q_at, q_size in chunks(length, block_rows):
            seen = q_at + q_size
            scores = dot(k_v[0:seen, at : at + HD], q_v[q_at:seen, at : at + HD], NT)
            scores = scores * HD ** (-0.5) + bias[0:seen, q_at:seen]
            top = jnp.max(scores, axis=0, keepdims=True)
            expo = jnp.exp(scores - top)
            total = jnp.sum(expo, axis=0, keepdims=True)
            chance = (expo * (1.0 / total)).astype(jnp.bfloat16)
            probs_v[head, 0:seen, q_at:seen] = chance
            result = dot(v_v[0:seen, at : at + HD], chance, TN)
            joined_v[q_at:seen, at : at + HD] = result.T.astype(jnp.bfloat16)
    leave.append(copies.start(probs_v, probs))
    for i, (start, size) in enumerate(starts):
        place = pl.multiple_of(rows_at[i], 64)
        mixed_v[start : start + size, :] = joined_v[pl.ds(place, size), :]
    leave.append(copies.start(mixed_v, mixed))
    targets = [keep, to_x, to_y, far_low, far_high]
    for at, size in chunks(w_out.shape[1], 512):
        part = dot(mixed_v[...], w_out[:, at : at + size])
        for (start, rows), target in zip(starts, targets):
            target[:, at : at + size] = part[start : start + rows].astype(target.dtype)
    for copy in leave:
        copy.wait()


def attend_square(rows_at, blocks, w_qkv, w_out, cosine, sine, seg_row, seg_col, valid_col):
    rows, width = blocks[0].shape
    length = 4 * rows
    wide = w_qkv.shape[2]
    heads = wide // HD
    return pl.pallas_call(
        attend_kernel,
        name="attend",
        out_shape=send_specs(rows, width)
        + [
            like((length, width)),
            like((length, wide)),
            like((length, wide)),
            like((length, wide)),
            like((heads, length, length)),
            like((length, wide)),
        ],
        in_specs=[pl.BlockSpec(memory_space=pltpu.SMEM)] + in_vmem(12),
        out_specs=in_vmem(5) + anywhere(6),
        scratch_shapes=[
            pltpu.VMEM((length, length), jnp.float32),
            pltpu.VMEM((length, width), jnp.bfloat16),
            pltpu.VMEM((length, wide), jnp.bfloat16),
            pltpu.VMEM((length, wide), jnp.bfloat16),
            pltpu.VMEM((length, wide), jnp.bfloat16),
            pltpu.VMEM((heads, length, length), jnp.bfloat16),
            pltpu.VMEM((length, wide), jnp.bfloat16),
            pltpu.VMEM((length, wide), jnp.bfloat16),
            pltpu.SemaphoreType.DMA((6,)),
        ],
        compiler_params=pltpu.CompilerParams(vmem_limit_bytes=SPARE),
    )(rows_at, *blocks, w_qkv, w_out, cosine, sine, seg_row, seg_col, valid_col)


def d_hidden_kernel(count, *refs):
    blocks = refs[:count]
    w_down, d_hidden, cot_all, cot_v, sems = refs[count:]
    copies = Copies(sems)
    for (start, size), block in zip(block_starts(blocks), blocks):
        cot_v[start : start + size, :] = block[...]
    leave = [copies.start(cot_v, cot_all)]
    for at, size in chunks(w_down.shape[0], 256):
        d_hidden[:, at : at + size] = dot(cot_v[...], w_down[at : at + size, :], NT)
    for copy in leave:
        copy.wait()


def back_through_down(blocks, w_down):
    width = blocks[0].shape[1]
    length = sum(block.shape[0] for block in blocks)
    units = w_down.shape[0]
    return pl.pallas_call(
        functools.partial(d_hidden_kernel, len(blocks)),
        name="back_through_down",
        out_shape=[like((length, units), jnp.float32), like((length, width))],
        in_specs=in_vmem(len(blocks) + 1),
        out_specs=in_vmem(1) + anywhere(1),
        scratch_shapes=[
            pltpu.VMEM((length, width), jnp.bfloat16),
            pltpu.SemaphoreType.DMA((1,)),
        ],
        compiler_params=pltpu.CompilerParams(vmem_limit_bytes=SPARE),
    )(*blocks, w_down)


def mlp_kernel(
    sends, own, from_x, from_y, low, high, d_hidden, w_gate_up, *rest
):
    outs, scratch = rest[: 3 + 5 * sends], rest[3 + 5 * sends :]
    normed_all, hidden, d_gate_up = outs[:3]
    targets = outs[3:]
    normed_v, hidden_v, d_gate_up_v, sems = scratch
    copies = Copies(sems)
    units = w_gate_up.shape[2]
    blocks = [own, from_x, from_y, low, high]
    starts = block_starts(blocks)
    for (start, size), block in zip(starts, blocks):
        normed_v[start : start + size, :] = block[...]
    leave = [copies.start(normed_v, normed_all)]
    for at, size in chunks(units, 256):
        here = slice(at, at + size)
        gate = dot(normed_v[...], w_gate_up[0, :, here])
        upper = dot(normed_v[...], w_gate_up[1, :, here])
        incoming = d_hidden[:, here]
        sigma = 1.0 / (1.0 + jnp.exp(-gate))
        silu = gate * sigma
        hidden_v[:, here] = (silu * upper).astype(jnp.bfloat16)
        d_gate_up_v[:, here] = (incoming * upper * sigma * (1.0 + gate * (1.0 - sigma))).astype(
            jnp.bfloat16
        )
        d_gate_up_v[:, units + at : units + at + size] = (incoming * silu).astype(jnp.bfloat16)
    leave += [copies.start(hidden_v, hidden), copies.start(d_gate_up_v, d_gate_up)]
    if sends:
        for at, size in chunks(normed_v.shape[1], 256):
            part = dot(d_gate_up_v[:, 0:units], w_gate_up[0, at : at + size, :], NT) + dot(
                d_gate_up_v[:, units : 2 * units], w_gate_up[1, at : at + size, :], NT
            )
            for (start, rows), target in zip(starts, targets):
                target[:, at : at + size] = part[start : start + rows].astype(target.dtype)
    for copy in leave:
        copy.wait()


def mlp(blocks, d_hidden, w_gate_up, sends):
    rows, width = blocks[0].shape
    length = 4 * rows
    units = w_gate_up.shape[2]
    return pl.pallas_call(
        functools.partial(mlp_kernel, sends),
        name="mlp" if sends else "mlp_guest",
        out_shape=[like((length, width)), like((length, units)), like((length, 2 * units))]
        + (send_specs(rows, width) if sends else []),
        in_specs=in_vmem(7),
        out_specs=anywhere(3) + in_vmem(5 * sends),
        scratch_shapes=[
            pltpu.VMEM((length, width), jnp.bfloat16),
            pltpu.VMEM((length, units), jnp.bfloat16),
            pltpu.VMEM((length, 2 * units), jnp.bfloat16),
            pltpu.SemaphoreType.DMA((3,)),
        ],
        compiler_params=pltpu.CompilerParams(vmem_limit_bytes=SPARE),
    )(*blocks, d_hidden, w_gate_up)


def attend_back_kernel(
    rows_at, own, from_x, from_y, low, high, w_out, w_qkv, probs, queries, keys, values, cosine, sine,
    keep, to_x, to_y, far_low, far_high, d_middle_all, d_project,
    probs_v, q_v, k_v, v_v, d_middle_v, d_mixed_v, d_project_v, turned_v, sems,
):
    copies = Copies(sems)
    length = d_middle_v.shape[0]
    wide = q_v.shape[1]
    arrive = [
        copies.start(probs, probs_v),
        copies.start(queries, q_v),
        copies.start(keys, k_v),
        copies.start(values, v_v),
    ]
    blocks = [own, from_x, from_y, low, high]
    starts = block_starts(blocks)
    for (start, size), block in zip(starts, blocks):
        d_middle_v[start : start + size, :] = block[...]
    leave = [copies.start(d_middle_v, d_middle_all)]
    for at, size in chunks(wide, 256):
        part = dot(d_middle_v[...], w_out[at : at + size, :], NT).astype(jnp.bfloat16)
        for i, (start, rows) in enumerate(starts):
            place = pl.multiple_of(rows_at[i], 64)
            d_mixed_v[pl.ds(place, rows), at : at + size] = part[start : start + rows]
    for copy in arrive:
        copy.wait()
    scale = HD ** (-0.5)

    def back(turned, rows):
        return turned * cosine[rows, :] - pltpu.roll(turned, HD // 2, 1) * sine[rows, :]

    block_rows = 256
    for at in range(0, wide, HD):
        head = at // HD
        cols = slice(at, at + HD)
        d_keys = d_values = None
        for q_at, q_size in reversed(chunks(length, block_rows)):
            seen = q_at + q_size
            rows = slice(q_at, seen)
            chance = probs_v[head, 0:seen, rows]
            d_out = d_mixed_v[rows, cols]
            d_chance = dot(v_v[0:seen, cols], d_out, NT)
            exact = chance.astype(jnp.float32)
            delta = jnp.sum(d_chance * exact, axis=0, keepdims=True)
            d_scores = (exact * (d_chance - delta)).astype(jnp.bfloat16)
            more_values = dot(chance, d_out)
            more_keys = dot(d_scores, q_v[rows, cols])
            d_queries = dot(k_v[0:seen, cols], d_scores, TN).T
            d_project_v[rows, cols] = back(d_queries * scale, rows).astype(jnp.bfloat16)
            if d_keys is None:
                d_keys, d_values = more_keys, more_values
            else:
                d_keys = jnp.concatenate([d_keys[:seen] + more_keys, d_keys[seen:]], axis=0)
                d_values = jnp.concatenate([d_values[:seen] + more_values, d_values[seen:]], axis=0)
        everything = slice(0, length)
        d_project_v[:, wide + at : wide + at + HD] = back(d_keys * scale, everything).astype(
            jnp.bfloat16
        )
        d_project_v[:, 2 * wide + at : 2 * wide + at + HD] = d_values.astype(jnp.bfloat16)
    leave.append(copies.start(d_project_v, d_project))
    for i, (start, size) in enumerate(starts):
        place = pl.multiple_of(rows_at[i], 64)
        turned_v[start : start + size, :] = d_project_v[pl.ds(place, size), :]
    targets = [keep, to_x, to_y, far_low, far_high]
    for at, size in chunks(d_middle_v.shape[1], 256):
        part = sum(
            dot(turned_v[:, c * wide : (c + 1) * wide], w_qkv[c, at : at + size, :], NT)
            for c in range(3)
        )
        for (start, rows), target in zip(starts, targets):
            target[:, at : at + size] = part[start : start + rows].astype(target.dtype)
    for copy in leave:
        copy.wait()


def attend_back_square(rows_at, blocks, w_out, w_qkv, probs, queries, keys, values, cosine, sine):
    rows, width = blocks[0].shape
    length = 4 * rows
    wide = w_qkv.shape[2]
    return pl.pallas_call(
        attend_back_kernel,
        name="attend_back",
        out_shape=send_specs(rows, width) + [like((length, width)), like((length, 3 * wide))],
        in_specs=[pl.BlockSpec(memory_space=pltpu.SMEM)] + in_vmem(7) + anywhere(4) + in_vmem(2),
        out_specs=in_vmem(5) + anywhere(2),
        scratch_shapes=[
            pltpu.VMEM(probs.shape, jnp.bfloat16),
            pltpu.VMEM(queries.shape, jnp.bfloat16),
            pltpu.VMEM(queries.shape, jnp.bfloat16),
            pltpu.VMEM(queries.shape, jnp.bfloat16),
            pltpu.VMEM((length, width), jnp.bfloat16),
            pltpu.VMEM((length, wide), jnp.bfloat16),
            pltpu.VMEM((length, 3 * wide), jnp.bfloat16),
            pltpu.VMEM((length, 3 * wide), jnp.bfloat16),
            pltpu.SemaphoreType.DMA((6,)),
        ],
        compiler_params=pltpu.CompilerParams(vmem_limit_bytes=SPARE),
    )(rows_at, *blocks, w_out, w_qkv, probs, queries, keys, values, cosine, sine)


def weight_kernel(count, which, *refs):
    splits, others = refs[:count], refs[count : 2 * count]
    rest = refs[2 * count :]
    turned = rest[-1]
    out = rest[-2]
    more = rest[0] if len(rest) == 3 else None
    length = splits[0].shape[0]
    for i, split in enumerate(splits):
        turned[:, i * length : (i + 1) * length] = split[...].T
    for at, size in chunks(out.shape[2], 256):
        part = None
        for i, other in enumerate(others):
            piece = dot(turned[:, i * length : (i + 1) * length], other[:, at : at + size])
            part = piece if part is None else part + piece
        if more is not None:
            part = part + more[0, :, at : at + size].astype(jnp.float32)
        out[0, :, at : at + size] = part.astype(out.dtype)


def weight_pieces(which, splits, others, more=None, base=0):
    count = which.shape[0]
    length, width = splits[0].shape
    across = others[0].shape[1]
    piece = 256
    step = [pl.BlockSpec((length, piece), lambda i, which: (0, which[i]))] * len(splits)
    whole = [pl.BlockSpec((length, across), lambda i, which: (0, 0))] * len(others)
    one = pl.BlockSpec((1, piece, across), lambda i, which: (i, 0, 0))
    added = pl.BlockSpec((1, piece, across), lambda i, which: (base + i, 0, 0))
    return pl.pallas_call(
        functools.partial(weight_kernel, len(splits)),
        name="weight_pieces",
        grid_spec=pltpu.PrefetchScalarGridSpec(
            num_scalar_prefetch=1,
            grid=(count,),
            in_specs=step + whole + ([added] if more is not None else []),
            out_specs=one,
            scratch_shapes=[pltpu.VMEM((piece, len(splits) * length), jnp.bfloat16)],
        ),
        out_shape=like((count, piece, across)),
        compiler_params=pltpu.CompilerParams(vmem_limit_bytes=SPARE),
    )(which, *splits, *others, *([more] if more is not None else []))


def flips(size, bit):
    return [(i, i ^ bit) for i in range(size)]


def after(value, *earlier):
    return lax.optimization_barrier((value, *earlier))[0]


def over_tensor(values, bit):
    return lax.ppermute(values, "tensor", flips(4, bit))


def gather_near(own):
    return own, over_tensor(own, 1), over_tensor(own, 2)


def gather_far(own, from_x, from_y):
    half = own.shape[0] // 2
    low = over_tensor(from_y[:half], 1)
    high = over_tensor(from_x[half:], 2)
    return [own, from_x, from_y, low, high]


def scatter_far(keep, to_x, to_y, far_low, far_high):
    half = far_low.shape[0]
    via_x = over_tensor(far_low, 1)
    via_y = over_tensor(far_high, 2)
    wide = jnp.float32
    to_x = to_x.at[half:].set((to_x[half:].astype(wide) + via_y.astype(wide)).astype(to_x.dtype))
    to_y = to_y.at[:half].set((to_y[:half].astype(wide) + via_x.astype(wide)).astype(to_y.dtype))
    return keep, to_x, to_y


def scatter_near(keep, to_x, to_y):
    wide = jnp.float32
    return keep + over_tensor(to_x, 1).astype(wide) + over_tensor(to_y, 2).astype(wide)


def over_cores(values):
    return lax.ppermute(values, "dp", flips(8, 1))


def to_inner(values):
    return lax.ppermute(values, "dp", [(0, 2), (1, 3), (6, 4), (7, 5)])


def to_outer(values):
    return lax.ppermute(values, "dp", [(2, 0), (3, 1), (4, 6), (5, 7)])


def over_middle(values):
    return lax.ppermute(values, "dp", [(2, 4), (3, 5), (4, 2), (5, 3)])


class Weight:
    def __init__(self, splits, others):
        self.splits, self.others = splits, others
        index = lax.axis_index("dp")
        place, self.core = index // 2, index % 2
        self.inner = (place == 1) | (place == 2)
        self.order = jnp.where(
            place < 2, jnp.array([3, 2, 0, 1]), jnp.array([0, 1, 3, 2])
        ).astype(jnp.int32)

    def sibling_part(self, *earlier):
        which = after(2 * self.order + 1 - self.core, *earlier)
        self.sibling_sum = weight_pieces(which, self.splits, self.others)
        self.theirs = over_cores(self.sibling_sum)

    def far_part(self, *earlier):
        which = after(2 * self.order[:2] + self.core, *earlier)
        self.far_sum = weight_pieces(which, self.splits, self.others, self.theirs, 0)
        self.far = over_middle(self.far_sum)

    def near_part(self, *earlier):
        which = after(2 * self.order[2:] + self.core, *earlier)
        self.near_sum = weight_pieces(which, self.splits, self.others, self.theirs, 2)

    def finish(self):
        total = self.near_sum.astype(jnp.float32) + self.far.astype(jnp.float32)
        given = to_outer(total[0].astype(jnp.bfloat16)).astype(jnp.float32)
        return jnp.where(self.inner, total[1], given)


def sum_everywhere(values):
    for axis, size, bit in (
        ("dp", 8, 1),
        ("tensor", 4, 1),
        ("tensor", 4, 2),
        ("dp", 8, 2),
        ("dp", 8, 4),
    ):
        values = values + lax.ppermute(values, axis, flips(size, bit))
    return values


def per_device_square(
    tokens, gain_attn, gain_mlp, w_qkv, w_out, w_gate_up, w_down, cotangent, segment_ids, valid_mask
):
    rows = tokens.shape[0]
    length = segment_ids.shape[0]
    low = jnp.bfloat16
    me = lax.axis_index("tensor")
    order = [me, me ^ 1, me ^ 2, me ^ 3]
    rows_at = jnp.stack([at * rows for at in order] + [order[3] * rows + rows // 2]).astype(jnp.int32)
    cosine, sine = rope_tables(length)
    cosine_full = jnp.concatenate([cosine, cosine], axis=1)
    sine_full = jnp.concatenate([-sine, sine], axis=1)
    incoming = tokens.astype(jnp.float32)
    gain_one = gain_attn.astype(jnp.float32)
    gain_two = gain_mlp.astype(jnp.float32)

    inv_one = lax.rsqrt(jnp.mean(incoming * incoming, axis=-1, keepdims=True) + EPS)
    normed = (incoming * inv_one * gain_one).astype(low)
    blocks = gather_far(*gather_near(normed))
    cot_near = gather_near(after(cotangent, *blocks))
    *sent, normed_all, queries, keys, values, probs, mixed = attend_square(
        rows_at,
        blocks,
        w_qkv,
        w_out,
        cosine_full,
        sine_full,
        segment_ids[None, :],
        segment_ids[:, None],
        valid_mask[:, None],
    )
    keep, to_x, to_y = scatter_far(*sent)
    cot_blocks = gather_far(*(after(part, to_x, to_y) for part in cot_near))
    guest_normed = to_inner(after(normed_all, *sent))
    middle_sum = scatter_near(keep, to_x, to_y)
    d_hidden, cot_all = back_through_down(cot_blocks, w_down)
    middle = incoming + after(middle_sum, cot_all)
    inv_two = lax.rsqrt(jnp.mean(middle * middle, axis=-1, keepdims=True) + EPS)
    normed_two = (middle * inv_two * gain_two).astype(low)

    near = gather_near(normed_two)
    guest_rows = to_inner(normed_two)
    guest_cot = to_inner(after(cot_all, normed_two))
    blocks = gather_far(*near)
    guest_near = gather_near(after(guest_rows, *blocks))
    normed_two_all, hidden, d_gate_up, *sent = mlp(blocks, d_hidden, w_gate_up, True)
    keep, to_x, to_y = scatter_far(*sent)
    guest_blocks = gather_far(*(after(part, to_x, to_y) for part in guest_near))
    guest_d_hidden, _ = back_through_down([after(guest_cot, to_x, to_y)], w_down)
    d_normed_two = after(scatter_near(keep, to_x, to_y), guest_d_hidden)
    scaled_two = gain_two * d_normed_two
    d_middle = (
        cotangent.astype(jnp.float32)
        + inv_two * scaled_two
        - middle * inv_two**3 * jnp.mean(scaled_two * middle, axis=-1, keepdims=True)
    )
    d_middle_low = d_middle.astype(low)
    near = gather_near(d_middle_low)
    guest_normed_two, guest_hidden, guest_d_gate_up = mlp(
        guest_blocks, after(guest_d_hidden, d_middle_low), w_gate_up, False
    )
    blocks = gather_far(*near)
    down_weight = Weight([cot_all, guest_cot], [hidden, guest_hidden])
    gate_weight = Weight([normed_two_all, guest_normed_two], [d_gate_up, guest_d_gate_up])
    down_weight.sibling_part(*near)
    gate_weight.sibling_part(down_weight.sibling_sum)

    *sent, d_middle_all, d_project = attend_back_square(
        after(rows_at, gate_weight.sibling_sum),
        blocks,
        w_out,
        w_qkv,
        probs,
        queries,
        keys,
        values,
        cosine_full,
        sine_full,
    )
    guest_d_project = to_inner(d_project)
    down_weight.far_part(d_project)
    gate_weight.far_part(down_weight.far_sum)
    keep, to_x, to_y = scatter_far(*(after(part, gate_weight.far_sum) for part in sent))
    d_normed = scatter_near(keep, to_x, to_y)
    out_sum = weight_pieces(
        after(jnp.arange(8, dtype=jnp.int32), to_x, to_y), [d_middle_all], [mixed]
    )
    grad_out = lax.psum_scatter(out_sum, "dp", scatter_dimension=0).astype(jnp.float32)
    down_weight.near_part(out_sum)
    gate_weight.near_part(down_weight.near_sum)
    qkv_weight = Weight([normed_all, guest_normed], [d_project, guest_d_project])
    qkv_weight.sibling_part(gate_weight.near_sum)
    down = jnp.dot(
        after(hidden, qkv_weight.sibling_sum), w_down, preferred_element_type=jnp.float32
    )
    half = rows // 2
    down_low = down.astype(low)
    down_sent = [
        down[:rows],
        down_low[rows : 2 * rows],
        down_low[2 * rows : 3 * rows],
        down_low[3 * rows : 3 * rows + half],
        down_low[3 * rows + half :],
    ]
    qkv_weight.far_part(*down_sent)
    qkv_weight.near_part(qkv_weight.far_sum)

    result = middle + scatter_near(*scatter_far(*down_sent))
    output = result.astype(low)
    grad_down = down_weight.finish()
    grad_gate_up = gate_weight.finish()
    scaled_one = gain_one * d_normed
    d_inputs = (
        d_middle
        + inv_one * scaled_one
        - incoming * inv_one**3 * jnp.mean(scaled_one * incoming, axis=-1, keepdims=True)
    )
    grad_gains = sum_everywhere(
        jnp.stack(
            [
                jnp.sum(d_normed * incoming * inv_one, axis=0),
                jnp.sum(d_normed_two * middle * inv_two, axis=0),
            ]
        )
    )
    grad_qkv = qkv_weight.finish()
    wide = w_qkv.shape[2]
    units = w_down.shape[0]
    return (
        output,
        d_inputs,
        grad_gains[0],
        grad_gains[1],
        jnp.stack([grad_qkv[:, c * wide : (c + 1) * wide] for c in range(3)]),
        grad_out.T,
        jnp.stack([grad_gate_up[:, c * units : (c + 1) * units] for c in range(2)]),
        grad_down.T,
    )


def solution(mesh):
    placed = (
        P(("dp", "tensor"), None),
        P(),
        P(),
        P(None, None, "tensor"),
        P("tensor", None),
        P(None, None, "tensor"),
        P("tensor", None),
        P(("dp", "tensor"), None),
        P("dp"),
        P("dp"),
    )
    square = mesh.shape["tensor"] == 4 and mesh.shape["dp"] == 8
    return jax.shard_map(
        per_device_square if square else per_device,
        mesh=mesh,
        in_specs=placed,
        out_specs=(
            P(("dp", "tensor"), None),
            P(("dp", "tensor"), None),
            P(),
            P(),
            P(None, "dp", "tensor"),
            P("tensor", "dp"),
            P(None, "dp", "tensor"),
            P("tensor", "dp"),
        ),
        check_vma=False,
    )
```

```python
import functools

import jax
import jax.numpy as jnp
from jax import lax
from jax.experimental import pallas as pl
from jax.experimental.pallas import tpu as pltpu
from jax.sharding import PartitionSpec as P

HD = 128


EPS = 1e-06
THETA = 10000.0


def rope_tables(places):
    positions = places.astype(jnp.float32)
    freqs = THETA ** (-(jnp.arange(HD // 2).astype(jnp.float32) * 2.0 / HD))
    angles = positions[:, None] * freqs[None, :]
    return (jnp.cos(angles), jnp.sin(angles))


def rotate(values, cosine, sine):
    half = values.shape[-1] // 2
    first = values[..., :half]
    second = values[..., half:]
    cosine = cosine[:, None, :]
    sine = sine[:, None, :]
    return jnp.concatenate(
        [first * cosine - second * sine, second * cosine + first * sine], axis=-1
    )


def block_scores(q_block, keys_rot, start, segments, valid):
    block_rows = q_block.shape[0]
    length = keys_rot.shape[0]
    key_pos = jnp.arange(length)
    row_pos = start + jnp.arange(block_rows)
    row_seg = lax.dynamic_slice_in_dim(segments, start, block_rows, 0)
    scores = jnp.einsum(
        "qhd,khd->hqk", q_block, keys_rot, preferred_element_type=jnp.float32
    ) * HD ** (-0.5)
    allowed = (
        (key_pos[None, :] <= row_pos[:, None])
        & (row_seg[:, None] == segments[None, :])
        & ((valid[None, :] == 1) | (key_pos[None, :] == row_pos[:, None]))
    )
    return jnp.where(allowed[None], scores, -1e30)


def attend(queries, keys_rot, values, segments, valid):
    length = queries.shape[0]
    block_rows = min(512, length)
    count = length // block_rows

    def one_block(index):
        start = index * block_rows
        q_block = lax.dynamic_slice_in_dim(queries, start, block_rows, 0)
        scores = block_scores(q_block, keys_rot, start, segments, valid)
        top = jnp.max(scores, axis=-1, keepdims=True)
        expo = jnp.exp(scores - top)
        total = jnp.sum(expo, axis=-1, keepdims=True)
        probs = (expo / total).astype(jnp.bfloat16)
        result = jnp.einsum("hqk,khd->qhd", probs, values, preferred_element_type=jnp.float32)
        return (result, top[..., 0] + jnp.log(total[..., 0]))

    blocks, log_sums = lax.map(one_block, jnp.arange(count))
    return (blocks.reshape(length, -1), log_sums)


def attend_back(queries, keys_rot, values, d_mixed, log_sums, segments, valid):
    length = queries.shape[0]
    block_rows = min(512, length)
    count = length // block_rows
    scale = HD ** (-0.5)

    def one_block(carry, index):
        d_keys, d_values = carry
        start = index * block_rows
        q_block = lax.dynamic_slice_in_dim(queries, start, block_rows, 0)
        d_block = lax.dynamic_slice_in_dim(d_mixed, start, block_rows, 0)
        scores = block_scores(q_block, keys_rot, start, segments, valid)
        probs = jnp.exp(scores - log_sums[index][..., None])
        d_values = d_values + jnp.einsum(
            "hqk,qhd->khd", probs.astype(jnp.bfloat16), d_block, preferred_element_type=jnp.float32
        )
        d_probs = jnp.einsum("qhd,khd->hqk", d_block, values, preferred_element_type=jnp.float32)
        delta = jnp.sum(d_probs * probs, axis=-1, keepdims=True)
        d_scores = (probs * (d_probs - delta)).astype(jnp.bfloat16)
        d_query = scale * jnp.einsum(
            "hqk,khd->qhd", d_scores, keys_rot, preferred_element_type=jnp.float32
        )
        d_keys = d_keys + scale * jnp.einsum(
            "hqk,qhd->khd", d_scores, q_block, preferred_element_type=jnp.float32
        )
        return ((d_keys, d_values), d_query)

    empty = jnp.zeros(keys_rot.shape, jnp.float32)
    (d_keys, d_values), d_queries = lax.scan(one_block, (empty, empty), jnp.arange(count))
    return (d_queries.reshape(queries.shape), d_keys, d_values)


def per_device(
    tokens, gain_attn, gain_mlp, w_qkv, w_out, w_gate_up, w_down, cotangent, segment_ids, valid_mask
):
    length = segment_ids.shape[0]
    heads_here = w_qkv.shape[2] // HD
    shape3 = (length, heads_here, HD)
    incoming = tokens.astype(jnp.float32)
    gain_one = gain_attn.astype(jnp.float32)
    gain_two = gain_mlp.astype(jnp.float32)
    cosine, sine = rope_tables(jnp.arange(length))
    inv_one = lax.rsqrt(jnp.mean(incoming * incoming, axis=-1, keepdims=True) + EPS)
    normed = (incoming * inv_one * gain_one).astype(jnp.bfloat16)
    normed_all = lax.all_gather(normed, "tensor", axis=0, tiled=True)
    project = jnp.einsum("td,cde->cte", normed_all, w_qkv, preferred_element_type=jnp.float32)
    queries = rotate(project[0].reshape(shape3), cosine, sine).astype(jnp.bfloat16)
    keys_rot = rotate(project[1].reshape(shape3), cosine, sine).astype(jnp.bfloat16)
    values = project[2].reshape(shape3).astype(jnp.bfloat16)
    mixed, log_sums = attend(queries, keys_rot, values, segment_ids, valid_mask)
    mixed = mixed.astype(jnp.bfloat16)
    middle = incoming + lax.psum_scatter(
        jnp.dot(mixed, w_out, preferred_element_type=jnp.float32).astype(jnp.bfloat16),
        "tensor",
        scatter_dimension=0,
        tiled=True,
    ).astype(jnp.float32)
    inv_two = lax.rsqrt(jnp.mean(middle * middle, axis=-1, keepdims=True) + EPS)
    normed_two = (middle * inv_two * gain_two).astype(jnp.bfloat16)
    normed_two_all = lax.all_gather(normed_two, "tensor", axis=0, tiled=True)
    gate = jnp.dot(normed_two_all, w_gate_up[0], preferred_element_type=jnp.float32)
    upper = jnp.dot(normed_two_all, w_gate_up[1], preferred_element_type=jnp.float32)
    sigma = jax.nn.sigmoid(gate)
    hidden = (gate * sigma * upper).astype(jnp.bfloat16)
    result = middle + lax.psum_scatter(
        jnp.dot(hidden, w_down, preferred_element_type=jnp.float32).astype(jnp.bfloat16),
        "tensor",
        scatter_dimension=0,
        tiled=True,
    ).astype(jnp.float32)
    output = result.astype(jnp.bfloat16)
    cot_all = lax.all_gather(cotangent, "tensor", axis=0, tiled=True)
    d_hidden = jnp.einsum("td,fd->tf", cot_all, w_down, preferred_element_type=jnp.float32)
    grad_down = jnp.einsum("tf,td->fd", hidden, cot_all, preferred_element_type=jnp.float32)
    d_upper = (d_hidden * gate * sigma).astype(jnp.bfloat16)
    d_gate = (d_hidden * upper * sigma * (1.0 + gate * (1.0 - sigma))).astype(jnp.bfloat16)
    grad_gate_up = jnp.stack(
        [
            jnp.einsum("td,tf->df", normed_two_all, d_gate, preferred_element_type=jnp.float32),
            jnp.einsum("td,tf->df", normed_two_all, d_upper, preferred_element_type=jnp.float32),
        ]
    )
    d_normed_two = lax.psum_scatter(
        (
            jnp.einsum("tf,df->td", d_gate, w_gate_up[0], preferred_element_type=jnp.float32)
            + jnp.einsum("tf,df->td", d_upper, w_gate_up[1], preferred_element_type=jnp.float32)
        ).astype(jnp.bfloat16),
        "tensor",
        scatter_dimension=0,
        tiled=True,
    ).astype(jnp.float32)
    scaled_two = gain_two * d_normed_two
    d_middle = (
        cotangent.astype(jnp.float32)
        + inv_two * scaled_two
        - middle * inv_two**3 * jnp.mean(scaled_two * middle, axis=-1, keepdims=True)
    )
    grad_gain_two = jnp.sum(d_normed_two * middle * inv_two, axis=0)
    d_middle_all = lax.all_gather(d_middle.astype(jnp.bfloat16), "tensor", axis=0, tiled=True)
    d_mixed = jnp.einsum(
        "td,ed->te", d_middle_all, w_out, preferred_element_type=jnp.float32
    ).astype(jnp.bfloat16)
    grad_out = jnp.einsum("te,td->ed", mixed, d_middle_all, preferred_element_type=jnp.float32)
    d_queries, d_keys, d_values = attend_back(
        queries, keys_rot, values, d_mixed.reshape(shape3), log_sums, segment_ids, valid_mask
    )
    d_project = jnp.stack(
        [
            rotate(d_queries, cosine, -sine).reshape(length, -1),
            rotate(d_keys, cosine, -sine).reshape(length, -1),
            d_values.reshape(length, -1),
        ]
    ).astype(jnp.bfloat16)
    grad_qkv = jnp.einsum("td,cte->cde", normed_all, d_project, preferred_element_type=jnp.float32)
    d_normed = lax.psum_scatter(
        jnp.einsum("cte,cde->td", d_project, w_qkv, preferred_element_type=jnp.float32).astype(
            jnp.bfloat16
        ),
        "tensor",
        scatter_dimension=0,
        tiled=True,
    ).astype(jnp.float32)
    scaled_one = gain_one * d_normed
    d_inputs = (
        d_middle
        + inv_one * scaled_one
        - incoming * inv_one**3 * jnp.mean(scaled_one * incoming, axis=-1, keepdims=True)
    )
    grad_gain_one = jnp.sum(d_normed * incoming * inv_one, axis=0)
    grad_gain_one, grad_gain_two = lax.psum((grad_gain_one, grad_gain_two), ("dp", "tensor"))
    grad_qkv, grad_out, grad_gate_up, grad_down = (
        lax.psum_scatter(
            grad_qkv.astype(jnp.bfloat16), "dp", scatter_dimension=1, tiled=True
        ).astype(jnp.float32),
        lax.psum_scatter(
            grad_out.astype(jnp.bfloat16), "dp", scatter_dimension=1, tiled=True
        ).astype(jnp.float32),
        lax.psum_scatter(
            grad_gate_up.astype(jnp.bfloat16), "dp", scatter_dimension=1, tiled=True
        ).astype(jnp.float32),
        lax.psum_scatter(
            grad_down.astype(jnp.bfloat16), "dp", scatter_dimension=1, tiled=True
        ).astype(jnp.float32),
    )
    return (
        output,
        d_inputs,
        grad_gain_one,
        grad_gain_two,
        grad_qkv,
        grad_out,
        grad_gate_up,
        grad_down,
    )


NT = (((1,), (1,)), ((), ()))
TN = (((0,), (0,)), ((), ()))
MEGA = 1024 * 1024


def chunks(total, step):
    return [(at, min(step, total - at)) for at in range(0, total, step)]


def dot(left, right, dims=None):
    if dims is None:
        return jnp.dot(left, right, preferred_element_type=jnp.float32)
    return lax.dot_general(left, right, dims, preferred_element_type=jnp.float32)


def in_vmem(count):
    return [pl.BlockSpec(memory_space=pltpu.VMEM)] * count


def in_smem():
    return [pl.BlockSpec(memory_space=pltpu.SMEM)]


def like(shape, kind=jnp.bfloat16):
    return jax.ShapeDtypeStruct(shape, kind)


def limit(megabytes):
    return pltpu.CompilerParams(vmem_limit_bytes=megabytes * MEGA)


def starts_of(blocks):
    at, starts = 0, []
    for block in blocks:
        starts.append((at, block.shape[0]))
        at += block.shape[0]
    return starts


def send_shapes(rows, width):
    half = rows // 2
    return [
        like((rows, width), jnp.float32),
        like((rows, width)),
        like((rows, width)),
        like((half, width)),
        like((half, width)),
    ]


def store_parts(part, targets, cols):
    for (start, rows), target in zip(starts_of(targets), targets):
        target[:, cols] = part[start : start + rows].astype(target.dtype)


def norm_kernel(tokens, gain, normed):
    wide = tokens[...].astype(jnp.float32)
    inverse = lax.rsqrt(jnp.mean(wide * wide, axis=-1, keepdims=True) + EPS)
    normed[...] = (wide * inverse * gain[...].astype(jnp.float32)).astype(jnp.bfloat16)


def norm(tokens, gain):
    return pl.pallas_call(
        norm_kernel,
        name="norm",
        out_shape=like(tokens.shape),
        in_specs=in_vmem(2),
        out_specs=in_vmem(1)[0],
        compiler_params=limit(4),
    )(tokens, gain)


def relay_kernel(to_x, to_y, via_x, via_y, next_x, next_y):
    half = via_x.shape[0]
    next_x[:half] = to_x[:half]
    next_x[half:] = (
        to_x[half:].astype(jnp.float32) + via_y[...].astype(jnp.float32)
    ).astype(jnp.bfloat16)
    next_y[:half] = (
        to_y[:half].astype(jnp.float32) + via_x[...].astype(jnp.float32)
    ).astype(jnp.bfloat16)
    next_y[half:] = to_y[half:]


def relay(to_x, to_y, via_x, via_y):
    return pl.pallas_call(
        relay_kernel,
        name="relay",
        out_shape=[like(to_x.shape), like(to_y.shape)],
        in_specs=in_vmem(4),
        out_specs=in_vmem(2),
        compiler_params=limit(4),
    )(to_x, to_y, via_x, via_y)


def middle_kernel(tokens, keep, got_x, got_y, gain, middle, normed):
    total = (
        tokens[...].astype(jnp.float32)
        + keep[...]
        + got_x[...].astype(jnp.float32)
        + got_y[...].astype(jnp.float32)
    )
    middle[...] = total
    inverse = lax.rsqrt(jnp.mean(total * total, axis=-1, keepdims=True) + EPS)
    normed[...] = (total * inverse * gain[...].astype(jnp.float32)).astype(jnp.bfloat16)


def make_middle(tokens, keep, got_x, got_y, gain):
    return pl.pallas_call(
        middle_kernel,
        name="make_middle",
        out_shape=[like(keep.shape, jnp.float32), like(keep.shape)],
        in_specs=in_vmem(5),
        out_specs=in_vmem(2),
        compiler_params=limit(6),
    )(tokens, keep, got_x, got_y, gain)


def norm_back_kernel(base, keep, got_x, got_y, source, gain, *outs):
    d_normed = keep[...] + got_x[...].astype(jnp.float32) + got_y[...].astype(jnp.float32)
    wide = source[...].astype(jnp.float32)
    inverse = lax.rsqrt(jnp.mean(wide * wide, axis=-1, keepdims=True) + EPS)
    scaled = gain[...].astype(jnp.float32) * d_normed
    slope = jnp.mean(scaled * wide, axis=-1, keepdims=True) * inverse * inverse * inverse
    total = base[...].astype(jnp.float32) + inverse * scaled - wide * slope
    outs[0][...] = total
    outs[1][...] = jnp.sum(d_normed * wide * inverse, axis=0, keepdims=True)
    if len(outs) == 3:
        outs[2][...] = total.astype(jnp.bfloat16)


def norm_back(base, keep, got_x, got_y, source, gain, low):
    return pl.pallas_call(
        norm_back_kernel,
        name="norm_back",
        out_shape=[like(keep.shape, jnp.float32), like((1, keep.shape[1]), jnp.float32)]
        + [like(keep.shape)] * low,
        in_specs=in_vmem(6),
        out_specs=in_vmem(2 + low),
        compiler_params=limit(8),
    )(base, keep, got_x, got_y, source, gain)


def project_kernel(
    rows_at, own, from_x, from_y, low, high, w_qkv, cosine, sine, normed, queries, keys, values
):
    for i, block in enumerate((own, from_x, from_y, low, high)):
        place = pl.multiple_of(rows_at[i], 64)
        normed[pl.ds(place, block.shape[0]), :] = block[...]
    for c, target in enumerate((queries, keys, values)):
        for at, size in chunks(target.shape[1], 2 * HD):
            part = dot(normed[...], w_qkv[c, :, at : at + size])
            for head in range(0, size, HD):
                piece = part[:, head : head + HD]
                if c < 2:
                    piece = piece * cosine[...] + pltpu.roll(piece, HD // 2, 1) * sine[...]
                target[:, at + head : at + head + HD] = piece.astype(jnp.bfloat16)


def project(rows_at, blocks, w_qkv, cosine, sine):
    rows, width = blocks[0].shape
    length = 4 * rows
    wide = w_qkv.shape[2]
    return pl.pallas_call(
        project_kernel,
        name="project",
        out_shape=[like((length, width))] + [like((length, wide))] * 3,
        in_specs=in_smem() + in_vmem(8),
        out_specs=in_vmem(4),
        compiler_params=limit(8),
    )(rows_at, *blocks, w_qkv, cosine, sine)


def attend_kernel(
    rows_at, queries, keys, values, w_out, seg_row, seg_col, valid_col,
    keep, to_x, to_y, far_low, far_high, probs, mixed, bias, joined,
):
    length, wide = queries.shape
    key_at = lax.broadcasted_iota(jnp.int32, (length, length), 0)
    query_at = lax.broadcasted_iota(jnp.int32, (length, length), 1)
    allowed = (
        (key_at <= query_at)
        & (seg_col[...] == seg_row[...])
        & ((valid_col[...] == 1) | (key_at == query_at))
    )
    bias[...] = jnp.where(allowed, 0.0, -1e30)
    for at in range(0, wide, HD):
        head = at // HD
        cols = slice(at, at + HD)
        for q_at, q_size in chunks(length, 256):
            seen = q_at + q_size
            scores = dot(keys[0:seen, cols], queries[q_at:seen, cols], NT)
            scores = scores * HD ** (-0.5) + bias[0:seen, q_at:seen]
            top = jnp.max(scores, axis=0, keepdims=True)
            expo = jnp.exp(scores - top)
            total = jnp.sum(expo, axis=0, keepdims=True)
            chance = (expo * (1.0 / total)).astype(jnp.bfloat16)
            probs[head, 0:seen, q_at:seen] = chance
            result = dot(values[0:seen, cols], chance, TN)
            joined[q_at:seen, cols] = result.T.astype(jnp.bfloat16)
    targets = [keep, to_x, to_y, far_low, far_high]
    for i, (start, size) in enumerate(starts_of(targets)):
        place = pl.multiple_of(rows_at[i], 64)
        mixed[start : start + size, :] = joined[pl.ds(place, size), :]
    for at, size in chunks(w_out.shape[1], 512):
        store_parts(dot(mixed[...], w_out[:, at : at + size]), targets, slice(at, at + size))


def attend_square(rows_at, queries, keys, values, w_out, seg_row, seg_col, valid_col):
    length, wide = queries.shape
    width = w_out.shape[1]
    heads = wide // HD
    return pl.pallas_call(
        attend_kernel,
        name="attend",
        out_shape=send_shapes(length // 4, width)
        + [like((heads, length, length)), like((length, wide))],
        in_specs=in_smem() + in_vmem(7),
        out_specs=in_vmem(7),
        scratch_shapes=[
            pltpu.VMEM((length, length), jnp.float32),
            pltpu.VMEM((length, wide), jnp.bfloat16),
        ],
        compiler_params=limit(8),
    )(rows_at, queries, keys, values, w_out, seg_row, seg_col, valid_col)


def d_hidden_kernel(own, from_x, from_y, low, high, w_down, d_hidden, cot_all):
    blocks = [own, from_x, from_y, low, high]
    for (start, size), block in zip(starts_of(blocks), blocks):
        cot_all[start : start + size, :] = block[...]
    for at, size in chunks(w_down.shape[0], 256):
        d_hidden[:, at : at + size] = dot(cot_all[...], w_down[at : at + size, :], NT)


def back_through_down(blocks, w_down):
    rows, width = blocks[0].shape
    length = 4 * rows
    units = w_down.shape[0]
    return pl.pallas_call(
        d_hidden_kernel,
        name="back_through_down",
        out_shape=[like((length, units), jnp.float32), like((length, width))],
        in_specs=in_vmem(6),
        out_specs=in_vmem(2),
        compiler_params=limit(6),
    )(*blocks, w_down)


def mlp_kernel(
    own, from_x, from_y, low, high, d_hidden, w_gate_up, normed, hidden, d_gate_up
):
    units = w_gate_up.shape[2]
    blocks = [own, from_x, from_y, low, high]
    for (start, size), block in zip(starts_of(blocks), blocks):
        normed[start : start + size, :] = block[...]
    for at, size in chunks(units, 256):
        here = slice(at, at + size)
        gate = dot(normed[...], w_gate_up[0, :, here])
        upper = dot(normed[...], w_gate_up[1, :, here])
        incoming = d_hidden[:, here]
        sigma = 1.0 / (1.0 + jnp.exp(-gate))
        silu = gate * sigma
        hidden[:, here] = (silu * upper).astype(jnp.bfloat16)
        d_gate_up[:, here] = (incoming * upper * sigma * (1.0 + gate * (1.0 - sigma))).astype(
            jnp.bfloat16
        )
        d_gate_up[:, units + at : units + at + size] = (incoming * silu).astype(jnp.bfloat16)


def mlp(blocks, d_hidden, w_gate_up):
    rows, width = blocks[0].shape
    length = 4 * rows
    units = w_gate_up.shape[2]
    return pl.pallas_call(
        mlp_kernel,
        name="mlp",
        out_shape=[like((length, width)), like((length, units)), like((length, 2 * units))],
        in_specs=in_vmem(7),
        out_specs=in_vmem(3),
        compiler_params=limit(8),
    )(*blocks, d_hidden, w_gate_up)


def mlp_back_kernel(d_gate_up, w_gate_up, *targets):
    units = w_gate_up.shape[2]
    for at, size in chunks(w_gate_up.shape[1], 256):
        part = dot(d_gate_up[:, 0:units], w_gate_up[0, at : at + size, :], NT) + dot(
            d_gate_up[:, units : 2 * units], w_gate_up[1, at : at + size, :], NT
        )
        store_parts(part, targets, slice(at, at + size))


def mlp_back(d_gate_up, w_gate_up):
    return pl.pallas_call(
        mlp_back_kernel,
        name="mlp_back",
        out_shape=send_shapes(d_gate_up.shape[0] // 4, w_gate_up.shape[1]),
        in_specs=in_vmem(2),
        out_specs=in_vmem(5),
        compiler_params=limit(6),
    )(d_gate_up, w_gate_up)


def down_kernel(hidden, w_down, *targets):
    for at, size in chunks(w_down.shape[1], 256):
        store_parts(dot(hidden[...], w_down[:, at : at + size]), targets, slice(at, at + size))


def through_down(hidden, w_down):
    return pl.pallas_call(
        down_kernel,
        name="through_down",
        out_shape=send_shapes(hidden.shape[0] // 4, w_down.shape[1]),
        in_specs=in_vmem(2),
        out_specs=in_vmem(5),
        compiler_params=limit(6),
    )(hidden, w_down)


def attend_back_kernel(
    rows_at, own, from_x, from_y, low, high, w_out, probs, queries, keys, values, cosine, sine,
    d_middle, d_project, d_mixed,
):
    length, wide = queries.shape
    blocks = [own, from_x, from_y, low, high]
    starts = starts_of(blocks)
    for (start, size), block in zip(starts, blocks):
        d_middle[start : start + size, :] = block[...]
    for at, size in chunks(wide, 256):
        part = dot(d_middle[...], w_out[at : at + size, :], NT).astype(jnp.bfloat16)
        for i, (start, rows) in enumerate(starts):
            place = pl.multiple_of(rows_at[i], 64)
            d_mixed[pl.ds(place, rows), at : at + size] = part[start : start + rows]
    scale = HD ** (-0.5)

    def back(turned, rows):
        return turned * cosine[rows, :] - pltpu.roll(turned, HD // 2, 1) * sine[rows, :]

    for at in range(0, wide, HD):
        head = at // HD
        cols = slice(at, at + HD)
        d_keys = d_values = None
        for q_at, q_size in reversed(chunks(length, 256)):
            seen = q_at + q_size
            rows = slice(q_at, seen)
            chance = probs[head, 0:seen, rows]
            d_out = d_mixed[rows, cols]
            d_chance = dot(values[0:seen, cols], d_out, NT)
            exact = chance.astype(jnp.float32)
            delta = jnp.sum(d_chance * exact, axis=0, keepdims=True)
            d_scores = (exact * (d_chance - delta)).astype(jnp.bfloat16)
            more_values = dot(chance, d_out)
            more_keys = dot(d_scores, queries[rows, cols])
            d_queries = dot(keys[0:seen, cols], d_scores, TN).T
            d_project[rows, cols] = back(d_queries * scale, rows).astype(jnp.bfloat16)
            if d_keys is None:
                d_keys, d_values = more_keys, more_values
            else:
                d_keys = jnp.concatenate([d_keys[:seen] + more_keys, d_keys[seen:]], axis=0)
                d_values = jnp.concatenate([d_values[:seen] + more_values, d_values[seen:]], axis=0)
        d_project[:, wide + at : wide + at + HD] = back(d_keys * scale, slice(0, length)).astype(
            jnp.bfloat16
        )
        d_project[:, 2 * wide + at : 2 * wide + at + HD] = d_values.astype(jnp.bfloat16)


def attend_back_square(rows_at, blocks, w_out, probs, queries, keys, values, cosine, sine):
    length, wide = queries.shape
    return pl.pallas_call(
        attend_back_kernel,
        name="attend_back",
        out_shape=[like((length, w_out.shape[1])), like((length, 3 * wide))],
        in_specs=in_smem() + in_vmem(12),
        out_specs=in_vmem(2),
        scratch_shapes=[pltpu.VMEM((length, wide), jnp.bfloat16)],
        compiler_params=limit(8),
    )(rows_at, *blocks, w_out, probs, queries, keys, values, cosine, sine)


def project_back_kernel(rows_at, d_project, w_qkv, *refs):
    targets, turned = refs[:5], refs[5]
    wide = w_qkv.shape[2]
    for i, (start, size) in enumerate(starts_of(targets)):
        place = pl.multiple_of(rows_at[i], 64)
        turned[start : start + size, :] = d_project[pl.ds(place, size), :]
    for at, size in chunks(w_qkv.shape[1], 256):
        part = sum(
            dot(turned[:, c * wide : (c + 1) * wide], w_qkv[c, at : at + size, :], NT)
            for c in range(3)
        )
        store_parts(part, targets, slice(at, at + size))


def project_back(rows_at, d_project, w_qkv):
    return pl.pallas_call(
        project_back_kernel,
        name="project_back",
        out_shape=send_shapes(d_project.shape[0] // 4, w_qkv.shape[1]),
        in_specs=in_smem() + in_vmem(2),
        out_specs=in_vmem(5),
        scratch_shapes=[pltpu.VMEM(d_project.shape, jnp.bfloat16)],
        compiler_params=limit(8),
    )(rows_at, d_project, w_qkv)


def weight_kernel(parts, base, which, *refs):
    splits, others = refs[:parts], refs[parts : 2 * parts]
    turned = refs[-1]
    out = refs[-2]
    more = refs[2 * parts] if len(refs) == 2 * parts + 3 else None
    count, piece, across = out.shape
    length = splits[0].shape[0]
    for i in range(count):
        place = pl.multiple_of(which[i] * piece, piece)
        for j, split in enumerate(splits):
            turned[:, j * length : (j + 1) * length] = split[:, pl.ds(place, piece)].T
        for at, size in chunks(across, 256):
            part = None
            for j, other in enumerate(others):
                term = dot(turned[:, j * length : (j + 1) * length], other[:, at : at + size])
                part = term if part is None else part + term
            if more is not None:
                part = part + more[base + i, :, at : at + size].astype(jnp.float32)
            out[i, :, at : at + size] = part.astype(out.dtype)


def weight_pieces(which, splits, others, more=None, base=0):
    count = which.shape[0]
    parts = len(splits)
    length = splits[0].shape[0]
    across = others[0].shape[1]
    piece = 256
    extra = [] if more is None else [more]
    return pl.pallas_call(
        functools.partial(weight_kernel, parts, base),
        name="weight_pieces",
        out_shape=like((count, piece, across)),
        in_specs=in_smem() + in_vmem(2 * parts + len(extra)),
        out_specs=in_vmem(1)[0],
        scratch_shapes=[pltpu.VMEM((piece, parts * length), jnp.bfloat16)],
        compiler_params=limit(6),
    )(which, *splits, *others, *extra)


def flips(size, bit):
    return [(i, i ^ bit) for i in range(size)]


def after(value, *earlier):
    return lax.optimization_barrier((value, *earlier))[0]


def over_tensor(values, bit):
    return lax.ppermute(values, "tensor", flips(4, bit))


def gather_near(own):
    return own, over_tensor(own, 1), over_tensor(own, 2)


def gather_far(own, from_x, from_y):
    half = own.shape[0] // 2
    low = over_tensor(from_y[:half], 1)
    high = over_tensor(from_x[half:], 2)
    return [own, from_x, from_y, low, high]


def scatter_far(keep, to_x, to_y, far_low, far_high):
    return keep, *relay(to_x, to_y, over_tensor(far_low, 1), over_tensor(far_high, 2))


def scatter_near(keep, to_x, to_y):
    return keep, over_tensor(to_x, 1), over_tensor(to_y, 2)


def over_cores(values):
    return lax.ppermute(values, "dp", flips(8, 1))


def to_inner(values):
    return lax.ppermute(values, "dp", [(0, 2), (1, 3), (6, 4), (7, 5)])


def to_outer(values):
    return lax.ppermute(values, "dp", [(2, 0), (3, 1), (4, 6), (5, 7)])


def over_middle(values):
    return lax.ppermute(values, "dp", [(2, 4), (3, 5), (4, 2), (5, 3)])


class Weight:
    def __init__(self, splits, others):
        self.splits, self.others = splits, others
        index = lax.axis_index("dp")
        place, self.core = index // 2, index % 2
        self.inner = (place == 1) | (place == 2)
        self.order = jnp.where(
            place < 2, jnp.array([3, 2, 0, 1]), jnp.array([0, 1, 3, 2])
        ).astype(jnp.int32)

    def sibling_part(self, *earlier):
        which = after(2 * self.order + 1 - self.core, *earlier)
        self.sibling_sum = weight_pieces(which, self.splits, self.others)
        self.theirs = over_cores(self.sibling_sum)

    def far_part(self, *earlier):
        which = after(2 * self.order[:2] + self.core, *earlier)
        self.far_sum = weight_pieces(which, self.splits, self.others, self.theirs, 0)
        self.far = over_middle(self.far_sum)

    def far_part_in_two(self, *earlier):
        which = after(2 * self.order[:2] + self.core, *earlier)
        first = weight_pieces(which[:1], self.splits, self.others, self.theirs, 0)
        self.far_sum = weight_pieces(
            after(which[1:], first), self.splits, self.others, self.theirs, 1
        )
        self.far_first = over_middle(first)
        self.far_second = over_middle(self.far_sum)
        self.far = jnp.concatenate([self.far_first, self.far_second], axis=0)

    def near_part(self, *earlier):
        which = after(2 * self.order[2:] + self.core, *earlier)
        self.near_sum = weight_pieces(which, self.splits, self.others, self.theirs, 2)

    def finish(self):
        total = self.near_sum.astype(jnp.float32) + self.far.astype(jnp.float32)
        given = to_outer(total[0].astype(jnp.bfloat16)).astype(jnp.float32)
        return jnp.where(self.inner, total[1], given)


def sum_everywhere(values):
    for axis, size, bit in (
        ("dp", 8, 1),
        ("tensor", 4, 1),
        ("tensor", 4, 2),
        ("dp", 8, 2),
        ("dp", 8, 4),
    ):
        values = values + lax.ppermute(values, axis, flips(size, bit))
    return values


def per_device_square(
    tokens, gain_attn, gain_mlp, w_qkv, w_out, w_gate_up, w_down, cotangent, segment_ids, valid_mask
):
    rows = tokens.shape[0]
    length = segment_ids.shape[0]
    low = jnp.bfloat16
    me = lax.axis_index("tensor")
    order = [me, me ^ 1, me ^ 2, me ^ 3]
    rows_at = jnp.stack([at * rows for at in order] + [order[3] * rows + rows // 2]).astype(jnp.int32)
    gain_one = gain_attn[None, :]
    gain_two = gain_mlp[None, :]

    normed = norm(tokens, gain_one)
    near = gather_near(normed)
    guest_cot_own = to_inner(cotangent)
    cosine, sine = rope_tables(after(jnp.arange(length), *near))
    cosine_full = jnp.concatenate([cosine, cosine], axis=1)
    sine_full = jnp.concatenate([-sine, sine], axis=1)
    blocks = gather_far(*near)
    cot_near = gather_near(after(cotangent, *blocks))
    normed_all, queries, keys, values = project(
        after(rows_at, guest_cot_own), blocks, w_qkv, cosine_full, sine_full
    )
    *sent, probs, mixed = attend_square(
        after(rows_at, normed_all, *cot_near),
        queries,
        keys,
        values,
        w_out,
        segment_ids[None, :],
        segment_ids[:, None],
        valid_mask[:, None],
    )
    guest_cot_near = [to_inner(part) for part in cot_near[1:]]
    keep, to_x, to_y = scatter_far(*sent)
    cot_blocks = gather_far(*(after(part, to_x) for part in cot_near))
    got = scatter_near(keep, to_x, to_y)
    d_hidden, cot_all = back_through_down(
        [after(cot_blocks[0], *guest_cot_near)] + cot_blocks[1:], w_down
    )
    middle, normed_two = make_middle(tokens, after(got[0], cot_all), *got[1:], gain_two)

    near = gather_near(normed_two)
    guest_cot_far = [to_inner(part) for part in cot_blocks[3:]]
    guest_own = to_inner(after(normed_two, *guest_cot_far))
    blocks = gather_far(*near)
    normed_two_all, hidden, d_gate_up = mlp(
        [after(blocks[0], *guest_cot_far)] + blocks[1:], d_hidden, w_gate_up
    )
    guest_near = [to_inner(part) for part in near[1:]]
    sent = mlp_back(d_gate_up, w_gate_up)
    guest_far = [to_inner(part) for part in blocks[3:]]
    keep, to_x, to_y = scatter_far(after(sent[0], guest_own), *sent[1:])
    to_x = after(to_x, *guest_near)
    guest_d_hidden, guest_cot_all = back_through_down(
        [after(guest_cot_own, to_x), *guest_cot_near, *guest_cot_far], w_down
    )
    got = scatter_near(keep, to_x, to_y)
    d_middle, gain_two_part, d_middle_low = norm_back(
        cotangent,
        after(got[0], guest_d_hidden, *guest_far),
        *got[1:],
        middle,
        gain_two,
        True,
    )
    near = gather_near(d_middle_low)
    guest_normed_two, guest_hidden, guest_d_gate_up = mlp(
        [guest_own, *guest_near, *guest_far], after(guest_d_hidden, d_middle_low), w_gate_up
    )
    blocks = gather_far(*near)
    down_weight = Weight([cot_all, guest_cot_all], [hidden, guest_hidden])
    gate_weight = Weight([normed_two_all, guest_normed_two], [d_gate_up, guest_d_gate_up])
    down_weight.sibling_part(*near)
    gate_weight.sibling_part(down_weight.sibling_sum)
    guest_normed = to_inner(after(normed_all, guest_hidden))
    down_weight.far_part(gate_weight.sibling_sum)

    d_middle_all, d_project = attend_back_square(
        after(rows_at, down_weight.far_sum),
        blocks,
        w_out,
        probs,
        queries,
        keys,
        values,
        cosine_full,
        sine_full,
    )
    guest_d_project = to_inner(d_project)
    gate_weight.far_part_in_two(d_project)
    sent = project_back(after(rows_at, gate_weight.far_sum), d_project, w_qkv)
    keep, to_x, to_y = scatter_far(*sent)
    out_sum = weight_pieces(
        after(jnp.arange(8, dtype=jnp.int32), to_x, to_y), [d_middle_all], [mixed]
    )
    grad_out = lax.psum_scatter(
        out_sum.reshape(length * 4, -1), "dp", scatter_dimension=0, tiled=True
    ).astype(jnp.float32)
    got = scatter_near(keep, to_x, to_y)
    down_sent = through_down(after(hidden, out_sum), w_down)
    d_inputs, gain_one_part = norm_back(
        d_middle, after(got[0], *down_sent, down_weight.far), *got[1:], tokens, gain_one, False
    )
    qkv_weight = Weight([normed_all, guest_normed], [d_project, guest_d_project])
    qkv_weight.sibling_part(d_inputs, gate_weight.far_first)
    keep, to_x, to_y = scatter_far(*(after(part, qkv_weight.sibling_sum) for part in down_sent))
    down_weight.near_part(to_x, to_y)
    gate_weight.near_part(down_weight.near_sum)
    gain_parts = jnp.concatenate([gain_one_part, gain_two_part], axis=0)
    grad_gains = sum_everywhere(after(gain_parts, gate_weight.near_sum))
    keep, got_x, got_y = scatter_near(keep, to_x, to_y)
    output = (middle + keep + got_x.astype(jnp.float32) + got_y.astype(jnp.float32)).astype(low)
    grad_down = down_weight.finish()
    qkv_weight.far_part(grad_gains, output, grad_down, gate_weight.far_second, grad_out)
    grad_gate_up = gate_weight.finish()
    qkv_weight.near_part(qkv_weight.far_sum)
    grad_qkv = qkv_weight.finish()
    wide = w_qkv.shape[2]
    units = w_down.shape[0]
    return (
        output,
        d_inputs,
        grad_gains[0],
        grad_gains[1],
        jnp.stack([grad_qkv[:, c * wide : (c + 1) * wide] for c in range(3)]),
        grad_out.T,
        jnp.stack([grad_gate_up[:, c * units : (c + 1) * units] for c in range(2)]),
        grad_down.T,
    )


def solution(mesh):
    placed = (
        P(("dp", "tensor"), None),
        P(),
        P(),
        P(None, None, "tensor"),
        P("tensor", None),
        P(None, None, "tensor"),
        P("tensor", None),
        P(("dp", "tensor"), None),
        P("dp"),
        P("dp"),
    )
    square = mesh.shape["tensor"] == 4 and mesh.shape["dp"] == 8
    return jax.shard_map(
        per_device_square if square else per_device,
        mesh=mesh,
        in_specs=placed,
        out_specs=(
            P(("dp", "tensor"), None),
            P(("dp", "tensor"), None),
            P(),
            P(),
            P(None, "dp", "tensor"),
            P("tensor", "dp"),
            P(None, "dp", "tensor"),
            P("tensor", "dp"),
        ),
        check_vma=False,
    )
```

```python
import functools
import math

import jax
import jax.numpy as jnp
from jax import lax
from jax.experimental import pallas as pl
from jax.experimental.pallas import tpu as pltpu
from jax.sharding import PartitionSpec as P

HD = 128


EPS = 1e-06
THETA = 10000.0


def rope_tables(places):
    positions = places.astype(jnp.float32)
    freqs = THETA ** (-(jnp.arange(HD // 2).astype(jnp.float32) * 2.0 / HD))
    angles = positions[:, None] * freqs[None, :]
    return (jnp.cos(angles), jnp.sin(angles))


def rotate(values, cosine, sine):
    half = values.shape[-1] // 2
    first = values[..., :half]
    second = values[..., half:]
    cosine = cosine[:, None, :]
    sine = sine[:, None, :]
    return jnp.concatenate(
        [first * cosine - second * sine, second * cosine + first * sine], axis=-1
    )


def block_scores(q_block, keys_rot, start, segments, valid):
    block_rows = q_block.shape[0]
    length = keys_rot.shape[0]
    key_pos = jnp.arange(length)
    row_pos = start + jnp.arange(block_rows)
    row_seg = lax.dynamic_slice_in_dim(segments, start, block_rows, 0)
    scores = jnp.einsum(
        "qhd,khd->hqk", q_block, keys_rot, preferred_element_type=jnp.float32
    ) * HD ** (-0.5)
    allowed = (
        (key_pos[None, :] <= row_pos[:, None])
        & (row_seg[:, None] == segments[None, :])
        & ((valid[None, :] == 1) | (key_pos[None, :] == row_pos[:, None]))
    )
    return jnp.where(allowed[None], scores, -1e30)


def attend(queries, keys_rot, values, segments, valid):
    length = queries.shape[0]
    block_rows = min(512, length)
    count = length // block_rows

    def one_block(index):
        start = index * block_rows
        q_block = lax.dynamic_slice_in_dim(queries, start, block_rows, 0)
        scores = block_scores(q_block, keys_rot, start, segments, valid)
        top = jnp.max(scores, axis=-1, keepdims=True)
        expo = jnp.exp(scores - top)
        total = jnp.sum(expo, axis=-1, keepdims=True)
        probs = (expo / total).astype(jnp.bfloat16)
        result = jnp.einsum("hqk,khd->qhd", probs, values, preferred_element_type=jnp.float32)
        return (result, top[..., 0] + jnp.log(total[..., 0]))

    blocks, log_sums = lax.map(one_block, jnp.arange(count))
    return (blocks.reshape(length, -1), log_sums)


def attend_back(queries, keys_rot, values, d_mixed, log_sums, segments, valid):
    length = queries.shape[0]
    block_rows = min(512, length)
    count = length // block_rows
    scale = HD ** (-0.5)

    def one_block(carry, index):
        d_keys, d_values = carry
        start = index * block_rows
        q_block = lax.dynamic_slice_in_dim(queries, start, block_rows, 0)
        d_block = lax.dynamic_slice_in_dim(d_mixed, start, block_rows, 0)
        scores = block_scores(q_block, keys_rot, start, segments, valid)
        probs = jnp.exp(scores - log_sums[index][..., None])
        d_values = d_values + jnp.einsum(
            "hqk,qhd->khd", probs.astype(jnp.bfloat16), d_block, preferred_element_type=jnp.float32
        )
        d_probs = jnp.einsum("qhd,khd->hqk", d_block, values, preferred_element_type=jnp.float32)
        delta = jnp.sum(d_probs * probs, axis=-1, keepdims=True)
        d_scores = (probs * (d_probs - delta)).astype(jnp.bfloat16)
        d_query = scale * jnp.einsum(
            "hqk,khd->qhd", d_scores, keys_rot, preferred_element_type=jnp.float32
        )
        d_keys = d_keys + scale * jnp.einsum(
            "hqk,qhd->khd", d_scores, q_block, preferred_element_type=jnp.float32
        )
        return ((d_keys, d_values), d_query)

    empty = jnp.zeros(keys_rot.shape, jnp.float32)
    (d_keys, d_values), d_queries = lax.scan(one_block, (empty, empty), jnp.arange(count))
    return (d_queries.reshape(queries.shape), d_keys, d_values)


def per_device(
    tokens, gain_attn, gain_mlp, w_qkv, w_out, w_gate_up, w_down, cotangent, segment_ids, valid_mask
):
    length = segment_ids.shape[0]
    heads_here = w_qkv.shape[2] // HD
    shape3 = (length, heads_here, HD)
    incoming = tokens.astype(jnp.float32)
    gain_one = gain_attn.astype(jnp.float32)
    gain_two = gain_mlp.astype(jnp.float32)
    cosine, sine = rope_tables(jnp.arange(length))
    inv_one = lax.rsqrt(jnp.mean(incoming * incoming, axis=-1, keepdims=True) + EPS)
    normed = (incoming * inv_one * gain_one).astype(jnp.bfloat16)
    normed_all = lax.all_gather(normed, "tensor", axis=0, tiled=True)
    project = jnp.einsum("td,cde->cte", normed_all, w_qkv, preferred_element_type=jnp.float32)
    queries = rotate(project[0].reshape(shape3), cosine, sine).astype(jnp.bfloat16)
    keys_rot = rotate(project[1].reshape(shape3), cosine, sine).astype(jnp.bfloat16)
    values = project[2].reshape(shape3).astype(jnp.bfloat16)
    mixed, log_sums = attend(queries, keys_rot, values, segment_ids, valid_mask)
    mixed = mixed.astype(jnp.bfloat16)
    middle = incoming + lax.psum_scatter(
        jnp.dot(mixed, w_out, preferred_element_type=jnp.float32).astype(jnp.bfloat16),
        "tensor",
        scatter_dimension=0,
        tiled=True,
    ).astype(jnp.float32)
    inv_two = lax.rsqrt(jnp.mean(middle * middle, axis=-1, keepdims=True) + EPS)
    normed_two = (middle * inv_two * gain_two).astype(jnp.bfloat16)
    normed_two_all = lax.all_gather(normed_two, "tensor", axis=0, tiled=True)
    gate = jnp.dot(normed_two_all, w_gate_up[0], preferred_element_type=jnp.float32)
    upper = jnp.dot(normed_two_all, w_gate_up[1], preferred_element_type=jnp.float32)
    sigma = jax.nn.sigmoid(gate)
    hidden = (gate * sigma * upper).astype(jnp.bfloat16)
    result = middle + lax.psum_scatter(
        jnp.dot(hidden, w_down, preferred_element_type=jnp.float32).astype(jnp.bfloat16),
        "tensor",
        scatter_dimension=0,
        tiled=True,
    ).astype(jnp.float32)
    output = result.astype(jnp.bfloat16)
    cot_all = lax.all_gather(cotangent, "tensor", axis=0, tiled=True)
    d_hidden = jnp.einsum("td,fd->tf", cot_all, w_down, preferred_element_type=jnp.float32)
    grad_down = jnp.einsum("tf,td->fd", hidden, cot_all, preferred_element_type=jnp.float32)
    d_upper = (d_hidden * gate * sigma).astype(jnp.bfloat16)
    d_gate = (d_hidden * upper * sigma * (1.0 + gate * (1.0 - sigma))).astype(jnp.bfloat16)
    grad_gate_up = jnp.stack(
        [
            jnp.einsum("td,tf->df", normed_two_all, d_gate, preferred_element_type=jnp.float32),
            jnp.einsum("td,tf->df", normed_two_all, d_upper, preferred_element_type=jnp.float32),
        ]
    )
    d_normed_two = lax.psum_scatter(
        (
            jnp.einsum("tf,df->td", d_gate, w_gate_up[0], preferred_element_type=jnp.float32)
            + jnp.einsum("tf,df->td", d_upper, w_gate_up[1], preferred_element_type=jnp.float32)
        ).astype(jnp.bfloat16),
        "tensor",
        scatter_dimension=0,
        tiled=True,
    ).astype(jnp.float32)
    scaled_two = gain_two * d_normed_two
    d_middle = (
        cotangent.astype(jnp.float32)
        + inv_two * scaled_two
        - middle * inv_two**3 * jnp.mean(scaled_two * middle, axis=-1, keepdims=True)
    )
    grad_gain_two = jnp.sum(d_normed_two * middle * inv_two, axis=0)
    d_middle_all = lax.all_gather(d_middle.astype(jnp.bfloat16), "tensor", axis=0, tiled=True)
    d_mixed = jnp.einsum(
        "td,ed->te", d_middle_all, w_out, preferred_element_type=jnp.float32
    ).astype(jnp.bfloat16)
    grad_out = jnp.einsum("te,td->ed", mixed, d_middle_all, preferred_element_type=jnp.float32)
    d_queries, d_keys, d_values = attend_back(
        queries, keys_rot, values, d_mixed.reshape(shape3), log_sums, segment_ids, valid_mask
    )
    d_project = jnp.stack(
        [
            rotate(d_queries, cosine, -sine).reshape(length, -1),
            rotate(d_keys, cosine, -sine).reshape(length, -1),
            d_values.reshape(length, -1),
        ]
    ).astype(jnp.bfloat16)
    grad_qkv = jnp.einsum("td,cte->cde", normed_all, d_project, preferred_element_type=jnp.float32)
    d_normed = lax.psum_scatter(
        jnp.einsum("cte,cde->td", d_project, w_qkv, preferred_element_type=jnp.float32).astype(
            jnp.bfloat16
        ),
        "tensor",
        scatter_dimension=0,
        tiled=True,
    ).astype(jnp.float32)
    scaled_one = gain_one * d_normed
    d_inputs = (
        d_middle
        + inv_one * scaled_one
        - incoming * inv_one**3 * jnp.mean(scaled_one * incoming, axis=-1, keepdims=True)
    )
    grad_gain_one = jnp.sum(d_normed * incoming * inv_one, axis=0)
    grad_gain_one, grad_gain_two = lax.psum((grad_gain_one, grad_gain_two), ("dp", "tensor"))
    grad_qkv, grad_out, grad_gate_up, grad_down = (
        lax.psum_scatter(
            grad_qkv.astype(jnp.bfloat16), "dp", scatter_dimension=1, tiled=True
        ).astype(jnp.float32),
        lax.psum_scatter(
            grad_out.astype(jnp.bfloat16), "dp", scatter_dimension=1, tiled=True
        ).astype(jnp.float32),
        lax.psum_scatter(
            grad_gate_up.astype(jnp.bfloat16), "dp", scatter_dimension=1, tiled=True
        ).astype(jnp.float32),
        lax.psum_scatter(
            grad_down.astype(jnp.bfloat16), "dp", scatter_dimension=1, tiled=True
        ).astype(jnp.float32),
    )
    return (
        output,
        d_inputs,
        grad_gain_one,
        grad_gain_two,
        grad_qkv,
        grad_out,
        grad_gate_up,
        grad_down,
    )


NT = (((1,), (1,)), ((), ()))
TN = (((0,), (0,)), ((), ()))
MEGA = 1024 * 1024


def chunks(total, step):
    return [(at, min(step, total - at)) for at in range(0, total, step)]


def dot(left, right, dims=None):
    if dims is None:
        return jnp.dot(left, right, preferred_element_type=jnp.float32)
    return lax.dot_general(left, right, dims, preferred_element_type=jnp.float32)


def in_vmem(count):
    return [pl.BlockSpec(memory_space=pltpu.VMEM)] * count


def in_smem():
    return [pl.BlockSpec(memory_space=pltpu.SMEM)]


def like(shape, kind=jnp.bfloat16):
    return jax.ShapeDtypeStruct(shape, kind)


def limit(megabytes):
    return pltpu.CompilerParams(vmem_limit_bytes=megabytes * MEGA)


def starts_of(blocks):
    at, starts = 0, []
    for block in blocks:
        starts.append((at, block.shape[0]))
        at += block.shape[0]
    return starts


def send_shapes(rows, width):
    half = rows // 2
    return [
        like((rows, width), jnp.float32),
        like((rows, width)),
        like((rows, width)),
        like((half, width)),
        like((half, width)),
    ]


def store_parts(part, targets, cols):
    for (start, rows), target in zip(starts_of(targets), targets):
        target[:, cols] = part[start : start + rows].astype(target.dtype)


def norm_kernel(tokens, gain, normed):
    wide = tokens[...].astype(jnp.float32)
    inverse = lax.rsqrt(jnp.mean(wide * wide, axis=-1, keepdims=True) + EPS)
    normed[...] = (wide * inverse * gain[...].astype(jnp.float32)).astype(jnp.bfloat16)


def norm(tokens, gain):
    return pl.pallas_call(
        norm_kernel,
        name="norm",
        out_shape=like(tokens.shape),
        in_specs=in_vmem(2),
        out_specs=in_vmem(1)[0],
        compiler_params=limit(4),
    )(tokens, gain)


def relay_kernel(to_x, to_y, via_x, via_y, next_x, next_y):
    half = via_x.shape[0]
    next_x[:half] = to_x[:half]
    next_x[half:] = (
        to_x[half:].astype(jnp.float32) + via_y[...].astype(jnp.float32)
    ).astype(jnp.bfloat16)
    next_y[:half] = (
        to_y[:half].astype(jnp.float32) + via_x[...].astype(jnp.float32)
    ).astype(jnp.bfloat16)
    next_y[half:] = to_y[half:]


def relay(to_x, to_y, via_x, via_y):
    return pl.pallas_call(
        relay_kernel,
        name="relay",
        out_shape=[like(to_x.shape), like(to_y.shape)],
        in_specs=in_vmem(4),
        out_specs=in_vmem(2),
        compiler_params=limit(4),
    )(to_x, to_y, via_x, via_y)


def middle_kernel(tokens, keep, got_x, got_y, gain, middle, normed):
    total = (
        tokens[...].astype(jnp.float32)
        + keep[...]
        + got_x[...].astype(jnp.float32)
        + got_y[...].astype(jnp.float32)
    )
    middle[...] = total
    inverse = lax.rsqrt(jnp.mean(total * total, axis=-1, keepdims=True) + EPS)
    normed[...] = (total * inverse * gain[...].astype(jnp.float32)).astype(jnp.bfloat16)


def make_middle(tokens, keep, got_x, got_y, gain):
    return pl.pallas_call(
        middle_kernel,
        name="make_middle",
        out_shape=[like(keep.shape, jnp.float32), like(keep.shape)],
        in_specs=in_vmem(5),
        out_specs=in_vmem(2),
        compiler_params=limit(6),
    )(tokens, keep, got_x, got_y, gain)


def norm_back_kernel(base, keep, got_x, got_y, source, gain, *outs):
    d_normed = keep[...] + got_x[...].astype(jnp.float32) + got_y[...].astype(jnp.float32)
    wide = source[...].astype(jnp.float32)
    inverse = lax.rsqrt(jnp.mean(wide * wide, axis=-1, keepdims=True) + EPS)
    scaled = gain[...].astype(jnp.float32) * d_normed
    slope = jnp.mean(scaled * wide, axis=-1, keepdims=True) * inverse * inverse * inverse
    total = base[...].astype(jnp.float32) + inverse * scaled - wide * slope
    outs[0][...] = total
    outs[1][...] = jnp.sum(d_normed * wide * inverse, axis=0, keepdims=True)
    if len(outs) == 3:
        outs[2][...] = total.astype(jnp.bfloat16)


def norm_back(base, keep, got_x, got_y, source, gain, low):
    return pl.pallas_call(
        norm_back_kernel,
        name="norm_back",
        out_shape=[like(keep.shape, jnp.float32), like((1, keep.shape[1]), jnp.float32)]
        + [like(keep.shape)] * low,
        in_specs=in_vmem(6),
        out_specs=in_vmem(2 + low),
        compiler_params=limit(8),
    )(base, keep, got_x, got_y, source, gain)


def prepare_kernel(w_qkv, w_out, segments, valid, cosine, sine, seg_col, valid_col):
    length = cosine.shape[0]
    half = HD // 2
    place = lax.broadcasted_iota(jnp.int32, (length, HD), 0).astype(jnp.float32)
    lane = lax.broadcasted_iota(jnp.int32, (length, HD), 1)
    step = jnp.where(lane < half, lane, lane - half).astype(jnp.float32)
    angle = place * jnp.exp(step * (-2.0 / HD * math.log(THETA)))
    cosine[...] = jnp.cos(angle)
    turn = jnp.sin(angle)
    sine[...] = jnp.where(lane < half, -turn, turn)
    seg_col[...] = jnp.broadcast_to(segments[...], (HD, length)).T
    valid_col[...] = jnp.broadcast_to(valid[...], (HD, length)).T


def prepare(w_qkv, w_out, segments, valid):
    length = segments.shape[1]
    return pl.pallas_call(
        prepare_kernel,
        name="prepare",
        out_shape=[like((length, HD), jnp.float32)] * 4,
        in_specs=in_vmem(4),
        out_specs=in_vmem(4),
        compiler_params=limit(6),
    )(w_qkv, w_out, segments, valid)


def project_kernel(
    rows_at, own, from_x, from_y, low, high, w_qkv, cosine, sine, normed, queries, keys, values
):
    for i, block in enumerate((own, from_x, from_y, low, high)):
        place = pl.multiple_of(rows_at[i], 64)
        normed[pl.ds(place, block.shape[0]), :] = block[...]
    for c, target in enumerate((queries, keys, values)):
        for at, size in chunks(target.shape[1], 2 * HD):
            part = dot(normed[...], w_qkv[c, :, at : at + size])
            for head in range(0, size, HD):
                piece = part[:, head : head + HD]
                if c < 2:
                    piece = piece * cosine[...] + pltpu.roll(piece, HD // 2, 1) * sine[...]
                target[:, at + head : at + head + HD] = piece.astype(jnp.bfloat16)


def project(rows_at, blocks, w_qkv, cosine, sine):
    rows, width = blocks[0].shape
    length = 4 * rows
    wide = w_qkv.shape[2]
    return pl.pallas_call(
        project_kernel,
        name="project",
        out_shape=[like((length, width))] + [like((length, wide))] * 3,
        in_specs=in_smem() + in_vmem(8),
        out_specs=in_vmem(4),
        compiler_params=limit(8),
    )(rows_at, *blocks, w_qkv, cosine, sine)


def attend_kernel(
    rows_at, queries, keys, values, w_out, seg_row, seg_col, valid_col,
    keep, to_x, to_y, far_low, far_high, probs, mixed, bias, joined,
):
    length, wide = queries.shape
    key_at = lax.broadcasted_iota(jnp.int32, (length, length), 0)
    query_at = lax.broadcasted_iota(jnp.int32, (length, length), 1)
    allowed = (
        (key_at <= query_at)
        & (seg_col[:, 0:1] == seg_row[...])
        & ((valid_col[:, 0:1] == 1.0) | (key_at == query_at))
    )
    bias[...] = jnp.where(allowed, 0.0, -1e30)
    for at in range(0, wide, HD):
        head = at // HD
        cols = slice(at, at + HD)
        for q_at, q_size in chunks(length, 256):
            seen = q_at + q_size
            scores = dot(keys[0:seen, cols], queries[q_at:seen, cols], NT)
            scores = scores * HD ** (-0.5) + bias[0:seen, q_at:seen]
            top = jnp.max(scores, axis=0, keepdims=True)
            expo = jnp.exp(scores - top)
            total = jnp.sum(expo, axis=0, keepdims=True)
            chance = (expo * (1.0 / total)).astype(jnp.bfloat16)
            probs[head, 0:seen, q_at:seen] = chance
            result = dot(values[0:seen, cols], chance, TN)
            joined[q_at:seen, cols] = result.T.astype(jnp.bfloat16)
    targets = [keep, to_x, to_y, far_low, far_high]
    for i, (start, size) in enumerate(starts_of(targets)):
        place = pl.multiple_of(rows_at[i], 64)
        mixed[start : start + size, :] = joined[pl.ds(place, size), :]
    for at, size in chunks(w_out.shape[1], 512):
        store_parts(dot(mixed[...], w_out[:, at : at + size]), targets, slice(at, at + size))


def attend_square(rows_at, queries, keys, values, w_out, seg_row, seg_col, valid_col):
    length, wide = queries.shape
    width = w_out.shape[1]
    heads = wide // HD
    return pl.pallas_call(
        attend_kernel,
        name="attend",
        out_shape=send_shapes(length // 4, width)
        + [like((heads, length, length)), like((length, wide))],
        in_specs=in_smem() + in_vmem(7),
        out_specs=in_vmem(7),
        scratch_shapes=[
            pltpu.VMEM((length, length), jnp.float32),
            pltpu.VMEM((length, wide), jnp.bfloat16),
        ],
        compiler_params=limit(8),
    )(rows_at, queries, keys, values, w_out, seg_row, seg_col, valid_col)


def d_hidden_kernel(own, from_x, from_y, low, high, w_down, d_hidden, cot_all):
    blocks = [own, from_x, from_y, low, high]
    for (start, size), block in zip(starts_of(blocks), blocks):
        cot_all[start : start + size, :] = block[...]
    for at, size in chunks(w_down.shape[0], 256):
        d_hidden[:, at : at + size] = dot(cot_all[...], w_down[at : at + size, :], NT)


def back_through_down(blocks, w_down):
    rows, width = blocks[0].shape
    length = 4 * rows
    units = w_down.shape[0]
    return pl.pallas_call(
        d_hidden_kernel,
        name="back_through_down",
        out_shape=[like((length, units), jnp.float32), like((length, width))],
        in_specs=in_vmem(6),
        out_specs=in_vmem(2),
        compiler_params=limit(6),
    )(*blocks, w_down)


def mlp_kernel(
    own, from_x, from_y, low, high, d_hidden, w_gate_up, normed, hidden, d_gate_up
):
    units = w_gate_up.shape[2]
    blocks = [own, from_x, from_y, low, high]
    for (start, size), block in zip(starts_of(blocks), blocks):
        normed[start : start + size, :] = block[...]
    for at, size in chunks(units, 256):
        here = slice(at, at + size)
        gate = dot(normed[...], w_gate_up[0, :, here])
        upper = dot(normed[...], w_gate_up[1, :, here])
        incoming = d_hidden[:, here]
        sigma = 1.0 / (1.0 + jnp.exp(-gate))
        silu = gate * sigma
        hidden[:, here] = (silu * upper).astype(jnp.bfloat16)
        d_gate_up[:, here] = (incoming * upper * sigma * (1.0 + gate * (1.0 - sigma))).astype(
            jnp.bfloat16
        )
        d_gate_up[:, units + at : units + at + size] = (incoming * silu).astype(jnp.bfloat16)


def mlp(blocks, d_hidden, w_gate_up):
    rows, width = blocks[0].shape
    length = 4 * rows
    units = w_gate_up.shape[2]
    return pl.pallas_call(
        mlp_kernel,
        name="mlp",
        out_shape=[like((length, width)), like((length, units)), like((length, 2 * units))],
        in_specs=in_vmem(7),
        out_specs=in_vmem(3),
        compiler_params=limit(8),
    )(*blocks, d_hidden, w_gate_up)


def mlp_back_kernel(d_gate_up, w_gate_up, *targets):
    units = w_gate_up.shape[2]
    for at, size in chunks(w_gate_up.shape[1], 256):
        part = dot(d_gate_up[:, 0:units], w_gate_up[0, at : at + size, :], NT) + dot(
            d_gate_up[:, units : 2 * units], w_gate_up[1, at : at + size, :], NT
        )
        store_parts(part, targets, slice(at, at + size))


def mlp_back(d_gate_up, w_gate_up):
    return pl.pallas_call(
        mlp_back_kernel,
        name="mlp_back",
        out_shape=send_shapes(d_gate_up.shape[0] // 4, w_gate_up.shape[1]),
        in_specs=in_vmem(2),
        out_specs=in_vmem(5),
        compiler_params=limit(6),
    )(d_gate_up, w_gate_up)


def down_kernel(hidden, w_down, *targets):
    for at, size in chunks(w_down.shape[1], 256):
        store_parts(dot(hidden[...], w_down[:, at : at + size]), targets, slice(at, at + size))


def through_down(hidden, w_down):
    return pl.pallas_call(
        down_kernel,
        name="through_down",
        out_shape=send_shapes(hidden.shape[0] // 4, w_down.shape[1]),
        in_specs=in_vmem(2),
        out_specs=in_vmem(5),
        compiler_params=limit(6),
    )(hidden, w_down)


def attend_back_kernel(
    rows_at, own, from_x, from_y, low, high, w_out, probs, queries, keys, values, cosine, sine,
    d_middle, d_project, d_mixed,
):
    length, wide = queries.shape
    blocks = [own, from_x, from_y, low, high]
    starts = starts_of(blocks)
    for (start, size), block in zip(starts, blocks):
        d_middle[start : start + size, :] = block[...]
    for at, size in chunks(wide, 256):
        part = dot(d_middle[...], w_out[at : at + size, :], NT).astype(jnp.bfloat16)
        for i, (start, rows) in enumerate(starts):
            place = pl.multiple_of(rows_at[i], 64)
            d_mixed[pl.ds(place, rows), at : at + size] = part[start : start + rows]
    scale = HD ** (-0.5)

    def back(turned, rows):
        return turned * cosine[rows, :] - pltpu.roll(turned, HD // 2, 1) * sine[rows, :]

    for at in range(0, wide, HD):
        head = at // HD
        cols = slice(at, at + HD)
        d_keys = d_values = None
        for q_at, q_size in reversed(chunks(length, 256)):
            seen = q_at + q_size
            rows = slice(q_at, seen)
            chance = probs[head, 0:seen, rows]
            d_out = d_mixed[rows, cols]
            d_chance = dot(values[0:seen, cols], d_out, NT)
            exact = chance.astype(jnp.float32)
            delta = jnp.sum(d_chance * exact, axis=0, keepdims=True)
            d_scores = (exact * (d_chance - delta)).astype(jnp.bfloat16)
            more_values = dot(chance, d_out)
            more_keys = dot(d_scores, queries[rows, cols])
            d_queries = dot(keys[0:seen, cols], d_scores, TN).T
            d_project[rows, cols] = back(d_queries * scale, rows).astype(jnp.bfloat16)
            if d_keys is None:
                d_keys, d_values = more_keys, more_values
            else:
                d_keys = jnp.concatenate([d_keys[:seen] + more_keys, d_keys[seen:]], axis=0)
                d_values = jnp.concatenate([d_values[:seen] + more_values, d_values[seen:]], axis=0)
        d_project[:, wide + at : wide + at + HD] = back(d_keys * scale, slice(0, length)).astype(
            jnp.bfloat16
        )
        d_project[:, 2 * wide + at : 2 * wide + at + HD] = d_values.astype(jnp.bfloat16)


def attend_back_square(rows_at, blocks, w_out, probs, queries, keys, values, cosine, sine):
    length, wide = queries.shape
    return pl.pallas_call(
        attend_back_kernel,
        name="attend_back",
        out_shape=[like((length, w_out.shape[1])), like((length, 3 * wide))],
        in_specs=in_smem() + in_vmem(12),
        out_specs=in_vmem(2),
        scratch_shapes=[pltpu.VMEM((length, wide), jnp.bfloat16)],
        compiler_params=limit(8),
    )(rows_at, *blocks, w_out, probs, queries, keys, values, cosine, sine)


def project_back_kernel(rows_at, d_project, w_qkv, *refs):
    targets, turned = refs[:5], refs[5]
    wide = w_qkv.shape[2]
    for i, (start, size) in enumerate(starts_of(targets)):
        place = pl.multiple_of(rows_at[i], 64)
        turned[start : start + size, :] = d_project[pl.ds(place, size), :]
    for at, size in chunks(w_qkv.shape[1], 256):
        part = sum(
            dot(turned[:, c * wide : (c + 1) * wide], w_qkv[c, at : at + size, :], NT)
            for c in range(3)
        )
        store_parts(part, targets, slice(at, at + size))


def project_back(rows_at, d_project, w_qkv):
    return pl.pallas_call(
        project_back_kernel,
        name="project_back",
        out_shape=send_shapes(d_project.shape[0] // 4, w_qkv.shape[1]),
        in_specs=in_smem() + in_vmem(2),
        out_specs=in_vmem(5),
        scratch_shapes=[pltpu.VMEM(d_project.shape, jnp.bfloat16)],
        compiler_params=limit(8),
    )(rows_at, d_project, w_qkv)


def finish_kernel(count, turn, inner, near, far, given, *outs):
    across = given.shape[1] // count
    for c in range(count):
        for at, size in chunks(across, 256):
            cols = slice(c * across + at, c * across + at + size)
            own = near[0, :, cols].astype(jnp.float32) + far[0, :, cols].astype(jnp.float32)
            total = jnp.where(inner[0] == 1, own, given[:, cols].astype(jnp.float32))
            if turn:
                outs[0][cols, :] = total.T
            else:
                outs[0][c, :, at : at + size] = total


def finish(inner, near, far, given, count, turn):
    piece, across = given.shape
    shape = (across, piece) if turn else (count, piece, across // count)
    return pl.pallas_call(
        functools.partial(finish_kernel, count, turn),
        name="finish",
        out_shape=like(shape, jnp.float32),
        in_specs=in_smem() + in_vmem(3),
        out_specs=in_vmem(1)[0],
        compiler_params=limit(10),
    )(inner, near, far, given)


def hand_kernel(near, far, out):
    for at, size in chunks(out.shape[1], 256):
        cols = slice(at, at + size)
        out[:, cols] = (
            near[0, :, cols].astype(jnp.float32) + far[0, :, cols].astype(jnp.float32)
        ).astype(jnp.bfloat16)


def hand(near, far):
    return pl.pallas_call(
        hand_kernel,
        name="hand",
        out_shape=like(near.shape[1:]),
        in_specs=in_vmem(2),
        out_specs=in_vmem(1)[0],
        compiler_params=limit(6),
    )(near, far)


def weight_kernel(parts, also, base, which, *refs):
    splits, others = refs[:parts], refs[parts : parts + also]
    turned = refs[-1]
    out = refs[-2]
    more = refs[parts + also] if len(refs) == parts + also + 3 else None
    count, piece, across = out.shape
    length = others[0].shape[0]
    for i in range(count):
        place = pl.multiple_of(which[i] * piece, piece)
        for (start, rows), split in zip(starts_of(splits), splits):
            turned[:, start : start + rows] = split[:, pl.ds(place, piece)].T
        for at, size in chunks(across, 256):
            part = None
            for j, other in enumerate(others):
                term = dot(turned[:, j * length : (j + 1) * length], other[:, at : at + size])
                part = term if part is None else part + term
            if more is not None:
                part = part + more[base + i, :, at : at + size].astype(jnp.float32)
            out[i, :, at : at + size] = part.astype(out.dtype)


def weight_pieces(which, splits, others, more=None, base=0):
    count = which.shape[0]
    parts, also = len(splits), len(others)
    length, across = others[0].shape
    piece = 256
    extra = [] if more is None else [more]
    return pl.pallas_call(
        functools.partial(weight_kernel, parts, also, base),
        name="weight_pieces",
        out_shape=like((count, piece, across)),
        in_specs=in_smem() + in_vmem(parts + also + len(extra)),
        out_specs=in_vmem(1)[0],
        scratch_shapes=[pltpu.VMEM((piece, also * length), jnp.bfloat16)],
        compiler_params=limit(12),
    )(which, *splits, *others, *extra)


def flips(size, bit):
    return [(i, i ^ bit) for i in range(size)]


def after(value, *earlier):
    return lax.optimization_barrier((value, *earlier))[0]


def over_tensor(values, bit):
    return lax.ppermute(values, "tensor", flips(4, bit))


def gather_near(own):
    return own, over_tensor(own, 1), over_tensor(own, 2)


def gather_far(own, from_x, from_y):
    half = own.shape[0] // 2
    low = over_tensor(from_y[:half], 1)
    high = over_tensor(from_x[half:], 2)
    return [own, from_x, from_y, low, high]


def scatter_far(keep, to_x, to_y, far_low, far_high):
    return keep, *relay(to_x, to_y, over_tensor(far_low, 1), over_tensor(far_high, 2))


def scatter_near(keep, to_x, to_y):
    return keep, over_tensor(to_x, 1), over_tensor(to_y, 2)


def over_cores(values):
    return lax.ppermute(values, "dp", flips(8, 1))


def to_inner(values):
    return lax.ppermute(values, "dp", [(0, 2), (1, 3), (6, 4), (7, 5)])


def to_outer(values):
    return lax.ppermute(values, "dp", [(2, 0), (3, 1), (4, 6), (5, 7)])


def over_middle(values):
    return lax.ppermute(values, "dp", [(2, 4), (3, 5), (4, 2), (5, 3)])


class Weight:
    def __init__(self, splits, others):
        self.splits, self.others = splits, others
        index = lax.axis_index("dp")
        place, self.core = index // 2, index % 2
        self.inner = (place == 1) | (place == 2)
        self.order = jnp.where(
            place < 2, jnp.array([3, 2, 0, 1]), jnp.array([0, 1, 3, 2])
        ).astype(jnp.int32)

    def sibling_part(self, *earlier):
        which = after(2 * self.order + 1 - self.core, *earlier)
        self.sibling_sum = weight_pieces(which, self.splits, self.others)
        self.theirs = over_cores(self.sibling_sum)

    def far_part(self, *earlier):
        which = after(2 * self.order[:2] + self.core, *earlier)
        far_outer = weight_pieces(which[:1], self.splits, self.others, self.theirs, 0)
        self.far_sum = weight_pieces(
            after(which[1:], far_outer), self.splits, self.others, self.theirs, 1
        )
        self.far_outer = over_middle(far_outer)
        self.far_own = over_middle(self.far_sum)

    def near_part(self, *earlier):
        which = after(2 * self.order[2:] + self.core, *earlier)
        self.near_outer = weight_pieces(which[:1], self.splits, self.others, self.theirs, 2)
        self.near_own = weight_pieces(
            after(which[1:], self.near_outer), self.splits, self.others, self.theirs, 3
        )

    def hand(self, *earlier):
        self.handed = hand(after(self.near_outer, *earlier), self.far_outer)
        self.given = to_outer(self.handed)

    def finish(self, count, turn):
        inner = self.inner.astype(jnp.int32).reshape(1)
        return finish(inner, self.near_own, self.far_own, self.given, count, turn)


def sum_flips(values, *steps):
    for axis, size, bit in steps:
        values = values + lax.ppermute(values, axis, flips(size, bit))
    return values


def per_device_square(
    tokens, gain_attn, gain_mlp, w_qkv, w_out, w_gate_up, w_down, cotangent, segment_ids, valid_mask
):
    rows = tokens.shape[0]
    length = segment_ids.shape[0]
    low = jnp.bfloat16
    me = lax.axis_index("tensor")
    order = [me, me ^ 1, me ^ 2, me ^ 3]
    rows_at = jnp.stack([at * rows for at in order] + [order[3] * rows + rows // 2]).astype(jnp.int32)
    gain_one = gain_attn[None, :]
    gain_two = gain_mlp[None, :]

    normed = norm(tokens, gain_one)
    near = gather_near(normed)
    guest_cot_own = to_inner(cotangent)
    cosine, sine, seg_col, valid_col = prepare(
        w_qkv,
        w_out,
        segment_ids.astype(jnp.float32)[None, :],
        valid_mask.astype(jnp.float32)[None, :],
    )
    near = (near[0], near[1], after(near[2], cosine))
    blocks = gather_far(*near)
    cot_near = gather_near(after(cotangent, *blocks))
    normed_all, queries, keys, values = project(
        after(rows_at, guest_cot_own), blocks, w_qkv, cosine, sine
    )
    *sent, probs, mixed = attend_square(
        after(rows_at, normed_all, *cot_near),
        queries,
        keys,
        values,
        w_out,
        segment_ids.astype(jnp.float32)[None, :],
        seg_col,
        valid_col,
    )
    guest_cot_near = [to_inner(part) for part in cot_near[1:]]
    keep, to_x, to_y = scatter_far(*sent)
    cot_blocks = gather_far(*(after(part, to_x) for part in cot_near))
    got = scatter_near(keep, to_x, to_y)
    d_hidden, cot_all = back_through_down(
        [after(cot_blocks[0], *guest_cot_near)] + cot_blocks[1:], w_down
    )
    middle, normed_two = make_middle(tokens, after(got[0], cot_all), *got[1:], gain_two)

    near = gather_near(normed_two)
    guest_cot_far = [to_inner(part) for part in cot_blocks[3:]]
    guest_own = to_inner(after(normed_two, *guest_cot_far))
    blocks = gather_far(*near)
    normed_two_all, hidden, d_gate_up = mlp(
        [after(blocks[0], *guest_cot_far)] + blocks[1:], d_hidden, w_gate_up
    )
    guest_near = [to_inner(part) for part in near[1:]]
    sent = mlp_back(after(d_gate_up, guest_near[0]), w_gate_up)
    guest_far = [to_inner(part) for part in blocks[3:]]
    keep, to_x, to_y = scatter_far(sent[0], after(sent[1], guest_own, guest_near[1]), *sent[2:])
    guest_d_hidden, guest_cot_all = back_through_down(
        [after(guest_cot_own, to_x), *guest_cot_near, *guest_cot_far], w_down
    )
    guest_normed = [to_inner(after(normed_all[: length // 2], to_x))]
    got = scatter_near(keep, to_x, to_y)
    guest_normed_two, guest_hidden, guest_d_gate_up = mlp(
        [guest_own, *guest_near, *guest_far], guest_d_hidden, w_gate_up
    )
    down_weight = Weight([cot_all, guest_cot_all], [hidden, guest_hidden])
    gate_weight = Weight([normed_two_all, guest_normed_two], [d_gate_up, guest_d_gate_up])
    down_weight.sibling_part()
    d_middle, gain_two_part, d_middle_low = norm_back(
        cotangent, after(got[0], down_weight.sibling_sum, *guest_normed), *got[1:], middle, gain_two, True
    )
    near = gather_near(d_middle_low)
    gate_weight.sibling_part(d_middle_low)
    down_weight.far_part(gate_weight.sibling_sum)
    blocks = gather_far(*near)
    guest_normed += [to_inner(after(normed_all[length // 2 :], guest_hidden))]

    d_middle_all, d_project = attend_back_square(
        after(rows_at, down_weight.far_sum),
        blocks,
        w_out,
        probs,
        queries,
        keys,
        values,
        cosine,
        sine,
    )
    guest_d_project = to_inner(d_project)
    gate_weight.far_part(d_project, down_weight.far_outer, *guest_normed)
    sent = project_back(after(rows_at, gate_weight.far_sum), d_project, w_qkv)
    keep, to_x, to_y = scatter_far(*sent)
    out_sum = weight_pieces(
        after(jnp.arange(8, dtype=jnp.int32), to_x, to_y, down_weight.far_own),
        [d_middle_all],
        [mixed],
    )
    grad_out = lax.psum_scatter(out_sum, "dp", scatter_dimension=0).astype(jnp.float32)
    got = scatter_near(keep, to_x, to_y)
    down_sent = through_down(after(hidden, out_sum), w_down)
    d_inputs, gain_one_part = norm_back(
        d_middle, after(got[0], *down_sent, guest_d_project), *got[1:], tokens, gain_one, False
    )
    down_weight.near_part(d_inputs)
    keep, to_x, to_y = scatter_far(*(after(part, d_inputs) for part in down_sent))
    gain_parts = sum_flips(
        jnp.concatenate([gain_one_part, gain_two_part], axis=0),
        ("dp", 8, 1),
        ("tensor", 4, 1),
        ("tensor", 4, 2),
    )
    down_weight.hand()
    qkv_weight = Weight([normed_all, *guest_normed], [d_project, guest_d_project])
    qkv_weight.sibling_part(gate_weight.far_outer, down_weight.handed, gain_parts, to_x, to_y)
    gate_weight.near_part(qkv_weight.sibling_sum)
    gate_weight.hand()
    qkv_weight.far_part(gate_weight.handed)
    keep, got_x, got_y = scatter_near(keep, to_x, to_y)
    qkv_weight.near_part(qkv_weight.far_sum)
    output = (
        middle
        + after(keep, qkv_weight.near_own)
        + got_x.astype(jnp.float32)
        + got_y.astype(jnp.float32)
    ).astype(low)
    grad_gains = sum_flips(after(gain_parts, output), ("dp", 8, 2), ("dp", 8, 4))
    grad_down = down_weight.finish(1, True)
    qkv_weight.hand(output, grad_down)
    grad_gate_up = gate_weight.finish(2, False)
    grad_qkv = qkv_weight.finish(3, False)
    return (
        output,
        d_inputs,
        grad_gains[0],
        grad_gains[1],
        grad_qkv,
        grad_out.T,
        grad_gate_up,
        grad_down,
    )


def solution(mesh):
    placed = (
        P(("dp", "tensor"), None),
        P(),
        P(),
        P(None, None, "tensor"),
        P("tensor", None),
        P(None, None, "tensor"),
        P("tensor", None),
        P(("dp", "tensor"), None),
        P("dp"),
        P("dp"),
    )
    square = mesh.shape["tensor"] == 4 and mesh.shape["dp"] == 8
    return jax.shard_map(
        per_device_square if square else per_device,
        mesh=mesh,
        in_specs=placed,
        out_specs=(
            P(("dp", "tensor"), None),
            P(("dp", "tensor"), None),
            P(),
            P(),
            P(None, "dp", "tensor"),
            P("tensor", "dp"),
            P(None, "dp", "tensor"),
            P("tensor", "dp"),
        ),
        check_vma=False,
    )
```

```python
import functools
import math

import jax
import jax.numpy as jnp
from jax import lax
from jax.experimental import pallas as pl
from jax.experimental.pallas import tpu as pltpu
from jax.sharding import PartitionSpec as P

HD = 128


EPS = 1e-06
THETA = 10000.0


def rope_tables(places):
    positions = places.astype(jnp.float32)
    freqs = THETA ** (-(jnp.arange(HD // 2).astype(jnp.float32) * 2.0 / HD))
    angles = positions[:, None] * freqs[None, :]
    return (jnp.cos(angles), jnp.sin(angles))


def rotate(values, cosine, sine):
    half = values.shape[-1] // 2
    first = values[..., :half]
    second = values[..., half:]
    cosine = cosine[:, None, :]
    sine = sine[:, None, :]
    return jnp.concatenate(
        [first * cosine - second * sine, second * cosine + first * sine], axis=-1
    )


def block_scores(q_block, keys_rot, start, segments, valid):
    block_rows = q_block.shape[0]
    length = keys_rot.shape[0]
    key_pos = jnp.arange(length)
    row_pos = start + jnp.arange(block_rows)
    row_seg = lax.dynamic_slice_in_dim(segments, start, block_rows, 0)
    scores = jnp.einsum(
        "qhd,khd->hqk", q_block, keys_rot, preferred_element_type=jnp.float32
    ) * HD ** (-0.5)
    allowed = (
        (key_pos[None, :] <= row_pos[:, None])
        & (row_seg[:, None] == segments[None, :])
        & ((valid[None, :] == 1) | (key_pos[None, :] == row_pos[:, None]))
    )
    return jnp.where(allowed[None], scores, -1e30)


def attend(queries, keys_rot, values, segments, valid):
    length = queries.shape[0]
    block_rows = min(512, length)
    count = length // block_rows

    def one_block(index):
        start = index * block_rows
        q_block = lax.dynamic_slice_in_dim(queries, start, block_rows, 0)
        scores = block_scores(q_block, keys_rot, start, segments, valid)
        top = jnp.max(scores, axis=-1, keepdims=True)
        expo = jnp.exp(scores - top)
        total = jnp.sum(expo, axis=-1, keepdims=True)
        probs = (expo / total).astype(jnp.bfloat16)
        result = jnp.einsum("hqk,khd->qhd", probs, values, preferred_element_type=jnp.float32)
        return (result, top[..., 0] + jnp.log(total[..., 0]))

    blocks, log_sums = lax.map(one_block, jnp.arange(count))
    return (blocks.reshape(length, -1), log_sums)


def attend_back(queries, keys_rot, values, d_mixed, log_sums, segments, valid):
    length = queries.shape[0]
    block_rows = min(512, length)
    count = length // block_rows
    scale = HD ** (-0.5)

    def one_block(carry, index):
        d_keys, d_values = carry
        start = index * block_rows
        q_block = lax.dynamic_slice_in_dim(queries, start, block_rows, 0)
        d_block = lax.dynamic_slice_in_dim(d_mixed, start, block_rows, 0)
        scores = block_scores(q_block, keys_rot, start, segments, valid)
        probs = jnp.exp(scores - log_sums[index][..., None])
        d_values = d_values + jnp.einsum(
            "hqk,qhd->khd", probs.astype(jnp.bfloat16), d_block, preferred_element_type=jnp.float32
        )
        d_probs = jnp.einsum("qhd,khd->hqk", d_block, values, preferred_element_type=jnp.float32)
        delta = jnp.sum(d_probs * probs, axis=-1, keepdims=True)
        d_scores = (probs * (d_probs - delta)).astype(jnp.bfloat16)
        d_query = scale * jnp.einsum(
            "hqk,khd->qhd", d_scores, keys_rot, preferred_element_type=jnp.float32
        )
        d_keys = d_keys + scale * jnp.einsum(
            "hqk,qhd->khd", d_scores, q_block, preferred_element_type=jnp.float32
        )
        return ((d_keys, d_values), d_query)

    empty = jnp.zeros(keys_rot.shape, jnp.float32)
    (d_keys, d_values), d_queries = lax.scan(one_block, (empty, empty), jnp.arange(count))
    return (d_queries.reshape(queries.shape), d_keys, d_values)


def per_device(
    tokens, gain_attn, gain_mlp, w_qkv, w_out, w_gate_up, w_down, cotangent, segment_ids, valid_mask
):
    length = segment_ids.shape[0]
    heads_here = w_qkv.shape[2] // HD
    shape3 = (length, heads_here, HD)
    incoming = tokens.astype(jnp.float32)
    gain_one = gain_attn.astype(jnp.float32)
    gain_two = gain_mlp.astype(jnp.float32)
    cosine, sine = rope_tables(jnp.arange(length))
    inv_one = lax.rsqrt(jnp.mean(incoming * incoming, axis=-1, keepdims=True) + EPS)
    normed = (incoming * inv_one * gain_one).astype(jnp.bfloat16)
    normed_all = lax.all_gather(normed, "tensor", axis=0, tiled=True)
    project = jnp.einsum("td,cde->cte", normed_all, w_qkv, preferred_element_type=jnp.float32)
    queries = rotate(project[0].reshape(shape3), cosine, sine).astype(jnp.bfloat16)
    keys_rot = rotate(project[1].reshape(shape3), cosine, sine).astype(jnp.bfloat16)
    values = project[2].reshape(shape3).astype(jnp.bfloat16)
    mixed, log_sums = attend(queries, keys_rot, values, segment_ids, valid_mask)
    mixed = mixed.astype(jnp.bfloat16)
    middle = incoming + lax.psum_scatter(
        jnp.dot(mixed, w_out, preferred_element_type=jnp.float32).astype(jnp.bfloat16),
        "tensor",
        scatter_dimension=0,
        tiled=True,
    ).astype(jnp.float32)
    inv_two = lax.rsqrt(jnp.mean(middle * middle, axis=-1, keepdims=True) + EPS)
    normed_two = (middle * inv_two * gain_two).astype(jnp.bfloat16)
    normed_two_all = lax.all_gather(normed_two, "tensor", axis=0, tiled=True)
    gate = jnp.dot(normed_two_all, w_gate_up[0], preferred_element_type=jnp.float32)
    upper = jnp.dot(normed_two_all, w_gate_up[1], preferred_element_type=jnp.float32)
    sigma = jax.nn.sigmoid(gate)
    hidden = (gate * sigma * upper).astype(jnp.bfloat16)
    result = middle + lax.psum_scatter(
        jnp.dot(hidden, w_down, preferred_element_type=jnp.float32).astype(jnp.bfloat16),
        "tensor",
        scatter_dimension=0,
        tiled=True,
    ).astype(jnp.float32)
    output = result.astype(jnp.bfloat16)
    cot_all = lax.all_gather(cotangent, "tensor", axis=0, tiled=True)
    d_hidden = jnp.einsum("td,fd->tf", cot_all, w_down, preferred_element_type=jnp.float32)
    grad_down = jnp.einsum("tf,td->fd", hidden, cot_all, preferred_element_type=jnp.float32)
    d_upper = (d_hidden * gate * sigma).astype(jnp.bfloat16)
    d_gate = (d_hidden * upper * sigma * (1.0 + gate * (1.0 - sigma))).astype(jnp.bfloat16)
    grad_gate_up = jnp.stack(
        [
            jnp.einsum("td,tf->df", normed_two_all, d_gate, preferred_element_type=jnp.float32),
            jnp.einsum("td,tf->df", normed_two_all, d_upper, preferred_element_type=jnp.float32),
        ]
    )
    d_normed_two = lax.psum_scatter(
        (
            jnp.einsum("tf,df->td", d_gate, w_gate_up[0], preferred_element_type=jnp.float32)
            + jnp.einsum("tf,df->td", d_upper, w_gate_up[1], preferred_element_type=jnp.float32)
        ).astype(jnp.bfloat16),
        "tensor",
        scatter_dimension=0,
        tiled=True,
    ).astype(jnp.float32)
    scaled_two = gain_two * d_normed_two
    d_middle = (
        cotangent.astype(jnp.float32)
        + inv_two * scaled_two
        - middle * inv_two**3 * jnp.mean(scaled_two * middle, axis=-1, keepdims=True)
    )
    grad_gain_two = jnp.sum(d_normed_two * middle * inv_two, axis=0)
    d_middle_all = lax.all_gather(d_middle.astype(jnp.bfloat16), "tensor", axis=0, tiled=True)
    d_mixed = jnp.einsum(
        "td,ed->te", d_middle_all, w_out, preferred_element_type=jnp.float32
    ).astype(jnp.bfloat16)
    grad_out = jnp.einsum("te,td->ed", mixed, d_middle_all, preferred_element_type=jnp.float32)
    d_queries, d_keys, d_values = attend_back(
        queries, keys_rot, values, d_mixed.reshape(shape3), log_sums, segment_ids, valid_mask
    )
    d_project = jnp.stack(
        [
            rotate(d_queries, cosine, -sine).reshape(length, -1),
            rotate(d_keys, cosine, -sine).reshape(length, -1),
            d_values.reshape(length, -1),
        ]
    ).astype(jnp.bfloat16)
    grad_qkv = jnp.einsum("td,cte->cde", normed_all, d_project, preferred_element_type=jnp.float32)
    d_normed = lax.psum_scatter(
        jnp.einsum("cte,cde->td", d_project, w_qkv, preferred_element_type=jnp.float32).astype(
            jnp.bfloat16
        ),
        "tensor",
        scatter_dimension=0,
        tiled=True,
    ).astype(jnp.float32)
    scaled_one = gain_one * d_normed
    d_inputs = (
        d_middle
        + inv_one * scaled_one
        - incoming * inv_one**3 * jnp.mean(scaled_one * incoming, axis=-1, keepdims=True)
    )
    grad_gain_one = jnp.sum(d_normed * incoming * inv_one, axis=0)
    grad_gain_one, grad_gain_two = lax.psum((grad_gain_one, grad_gain_two), ("dp", "tensor"))
    grad_qkv, grad_out, grad_gate_up, grad_down = (
        lax.psum_scatter(
            grad_qkv.astype(jnp.bfloat16), "dp", scatter_dimension=1, tiled=True
        ).astype(jnp.float32),
        lax.psum_scatter(
            grad_out.astype(jnp.bfloat16), "dp", scatter_dimension=1, tiled=True
        ).astype(jnp.float32),
        lax.psum_scatter(
            grad_gate_up.astype(jnp.bfloat16), "dp", scatter_dimension=1, tiled=True
        ).astype(jnp.float32),
        lax.psum_scatter(
            grad_down.astype(jnp.bfloat16), "dp", scatter_dimension=1, tiled=True
        ).astype(jnp.float32),
    )
    return (
        output,
        d_inputs,
        grad_gain_one,
        grad_gain_two,
        grad_qkv,
        grad_out,
        grad_gate_up,
        grad_down,
    )


NT = (((1,), (1,)), ((), ()))
TN = (((0,), (0,)), ((), ()))
MEGA = 1024 * 1024


def chunks(total, step):
    return [(at, min(step, total - at)) for at in range(0, total, step)]


def dot(left, right, dims=None):
    if dims is None:
        return jnp.dot(left, right, preferred_element_type=jnp.float32)
    return lax.dot_general(left, right, dims, preferred_element_type=jnp.float32)


def in_vmem(count):
    return [pl.BlockSpec(memory_space=pltpu.VMEM)] * count


def in_smem():
    return [pl.BlockSpec(memory_space=pltpu.SMEM)]


def like(shape, kind=jnp.bfloat16):
    return jax.ShapeDtypeStruct(shape, kind)


def limit(megabytes):
    return pltpu.CompilerParams(vmem_limit_bytes=megabytes * MEGA)


def starts_of(blocks):
    at, starts = 0, []
    for block in blocks:
        starts.append((at, block.shape[0]))
        at += block.shape[0]
    return starts


def send_shapes(rows, width):
    half = rows // 2
    return [
        like((rows, width), jnp.float32),
        like((rows, width)),
        like((rows, width)),
        like((half, width)),
        like((half, width)),
    ]


def store_parts(part, targets, cols):
    for (start, rows), target in zip(starts_of(targets), targets):
        target[:, cols] = part[start : start + rows].astype(target.dtype)


def norm_kernel(tokens, gain, normed):
    wide = tokens[...].astype(jnp.float32)
    inverse = lax.rsqrt(jnp.mean(wide * wide, axis=-1, keepdims=True) + EPS)
    normed[...] = (wide * inverse * gain[...].astype(jnp.float32)).astype(jnp.bfloat16)


def norm(tokens, gain):
    return pl.pallas_call(
        norm_kernel,
        name="norm",
        out_shape=like(tokens.shape),
        in_specs=in_vmem(2),
        out_specs=in_vmem(1)[0],
        compiler_params=limit(4),
    )(tokens, gain)


def relay_kernel(to_x, to_y, via_x, via_y, next_x, next_y):
    half = via_x.shape[0]
    next_x[:half] = to_x[:half]
    next_x[half:] = (
        to_x[half:].astype(jnp.float32) + via_y[...].astype(jnp.float32)
    ).astype(jnp.bfloat16)
    next_y[:half] = (
        to_y[:half].astype(jnp.float32) + via_x[...].astype(jnp.float32)
    ).astype(jnp.bfloat16)
    next_y[half:] = to_y[half:]


def relay(to_x, to_y, via_x, via_y):
    return pl.pallas_call(
        relay_kernel,
        name="relay",
        out_shape=[like(to_x.shape), like(to_y.shape)],
        in_specs=in_vmem(4),
        out_specs=in_vmem(2),
        compiler_params=limit(4),
    )(to_x, to_y, via_x, via_y)


def middle_kernel(tokens, keep, got_x, got_y, gain, middle, normed):
    total = (
        tokens[...].astype(jnp.float32)
        + keep[...]
        + got_x[...].astype(jnp.float32)
        + got_y[...].astype(jnp.float32)
    )
    middle[...] = total
    inverse = lax.rsqrt(jnp.mean(total * total, axis=-1, keepdims=True) + EPS)
    normed[...] = (total * inverse * gain[...].astype(jnp.float32)).astype(jnp.bfloat16)


def make_middle(tokens, keep, got_x, got_y, gain):
    return pl.pallas_call(
        middle_kernel,
        name="make_middle",
        out_shape=[like(keep.shape, jnp.float32), like(keep.shape)],
        in_specs=in_vmem(5),
        out_specs=in_vmem(2),
        compiler_params=limit(6),
    )(tokens, keep, got_x, got_y, gain)


def norm_back_kernel(base, keep, got_x, got_y, source, gain, *outs):
    d_normed = keep[...] + got_x[...].astype(jnp.float32) + got_y[...].astype(jnp.float32)
    wide = source[...].astype(jnp.float32)
    inverse = lax.rsqrt(jnp.mean(wide * wide, axis=-1, keepdims=True) + EPS)
    scaled = gain[...].astype(jnp.float32) * d_normed
    slope = jnp.mean(scaled * wide, axis=-1, keepdims=True) * inverse * inverse * inverse
    total = base[...].astype(jnp.float32) + inverse * scaled - wide * slope
    outs[0][...] = total
    outs[1][...] = jnp.sum(d_normed * wide * inverse, axis=0, keepdims=True)
    if len(outs) == 3:
        outs[2][...] = total.astype(jnp.bfloat16)


def norm_back(base, keep, got_x, got_y, source, gain, low):
    return pl.pallas_call(
        norm_back_kernel,
        name="norm_back",
        out_shape=[like(keep.shape, jnp.float32), like((1, keep.shape[1]), jnp.float32)]
        + [like(keep.shape)] * low,
        in_specs=in_vmem(6),
        out_specs=in_vmem(2 + low),
        compiler_params=limit(8),
    )(base, keep, got_x, got_y, source, gain)


def prepare_kernel(segments, valid, cosine, sine, seg_col, valid_col):
    length = cosine.shape[0]
    half = HD // 2
    place = lax.broadcasted_iota(jnp.int32, (length, HD), 0).astype(jnp.float32)
    lane = lax.broadcasted_iota(jnp.int32, (length, HD), 1)
    step = jnp.where(lane < half, lane, lane - half).astype(jnp.float32)
    angle = place * jnp.exp(step * (-2.0 / HD * math.log(THETA)))
    cosine[...] = jnp.cos(angle)
    turn = jnp.sin(angle)
    sine[...] = jnp.where(lane < half, -turn, turn)
    seg_col[...] = jnp.broadcast_to(segments[...], (HD, length)).T
    valid_col[...] = jnp.broadcast_to(valid[...], (HD, length)).T


def prepare(segments, valid):
    length = segments.shape[1]
    return pl.pallas_call(
        prepare_kernel,
        name="prepare",
        out_shape=[like((length, HD), jnp.float32)] * 4,
        in_specs=in_vmem(2),
        out_specs=in_vmem(4),
        compiler_params=limit(6),
    )(segments, valid)


def project_kernel(
    rows_at, own, from_x, from_y, low, high, w_qkv, cosine, sine, normed, queries, keys, values
):
    for i, block in enumerate((own, from_x, from_y, low, high)):
        place = pl.multiple_of(rows_at[i], 64)
        normed[pl.ds(place, block.shape[0]), :] = block[...]
    for c, target in enumerate((queries, keys, values)):
        for at, size in chunks(target.shape[1], 2 * HD):
            part = dot(normed[...], w_qkv[c, :, at : at + size])
            for head in range(0, size, HD):
                piece = part[:, head : head + HD]
                if c < 2:
                    piece = piece * cosine[...] + pltpu.roll(piece, HD // 2, 1) * sine[...]
                target[:, at + head : at + head + HD] = piece.astype(jnp.bfloat16)


def project(rows_at, blocks, w_qkv, cosine, sine):
    rows, width = blocks[0].shape
    length = 4 * rows
    wide = w_qkv.shape[2]
    return pl.pallas_call(
        project_kernel,
        name="project",
        out_shape=[like((length, width))] + [like((length, wide))] * 3,
        in_specs=in_smem() + in_vmem(8),
        out_specs=in_vmem(4),
        compiler_params=limit(8),
    )(rows_at, *blocks, w_qkv, cosine, sine)


def attend_kernel(
    rows_at, queries, keys, values, w_out, seg_row, seg_col, valid_col,
    keep, to_x, to_y, far_low, far_high, probs, mixed, bias, joined,
):
    length, wide = queries.shape
    key_at = lax.broadcasted_iota(jnp.int32, (length, length), 0)
    query_at = lax.broadcasted_iota(jnp.int32, (length, length), 1)
    allowed = (
        (key_at <= query_at)
        & (seg_col[:, 0:1] == seg_row[...])
        & ((valid_col[:, 0:1] == 1.0) | (key_at == query_at))
    )
    bias[...] = jnp.where(allowed, 0.0, -1e30)
    for at in range(0, wide, HD):
        head = at // HD
        cols = slice(at, at + HD)
        for q_at, q_size in chunks(length, 256):
            seen = q_at + q_size
            scores = dot(keys[0:seen, cols], queries[q_at:seen, cols], NT)
            scores = scores * HD ** (-0.5) + bias[0:seen, q_at:seen]
            top = jnp.max(scores, axis=0, keepdims=True)
            expo = jnp.exp(scores - top)
            total = jnp.sum(expo, axis=0, keepdims=True)
            chance = (expo * (1.0 / total)).astype(jnp.bfloat16)
            probs[head, 0:seen, q_at:seen] = chance
            result = dot(values[0:seen, cols], chance, TN)
            joined[q_at:seen, cols] = result.T.astype(jnp.bfloat16)
    targets = [keep, to_x, to_y, far_low, far_high]
    for i, (start, size) in enumerate(starts_of(targets)):
        place = pl.multiple_of(rows_at[i], 64)
        mixed[start : start + size, :] = joined[pl.ds(place, size), :]
    for at, size in chunks(w_out.shape[1], 512):
        store_parts(dot(mixed[...], w_out[:, at : at + size]), targets, slice(at, at + size))


def attend_square(rows_at, queries, keys, values, w_out, seg_row, seg_col, valid_col):
    length, wide = queries.shape
    width = w_out.shape[1]
    heads = wide // HD
    return pl.pallas_call(
        attend_kernel,
        name="attend",
        out_shape=send_shapes(length // 4, width)
        + [like((heads, length, length)), like((length, wide))],
        in_specs=in_smem() + in_vmem(7),
        out_specs=in_vmem(7),
        scratch_shapes=[
            pltpu.VMEM((length, length), jnp.float32),
            pltpu.VMEM((length, wide), jnp.bfloat16),
        ],
        compiler_params=limit(8),
    )(rows_at, queries, keys, values, w_out, seg_row, seg_col, valid_col)


def d_hidden_kernel(own, from_x, from_y, low, high, w_down, d_hidden, cot_all):
    blocks = [own, from_x, from_y, low, high]
    for (start, size), block in zip(starts_of(blocks), blocks):
        cot_all[start : start + size, :] = block[...]
    for at, size in chunks(w_down.shape[0], 256):
        d_hidden[:, at : at + size] = dot(cot_all[...], w_down[at : at + size, :], NT)


def back_through_down(blocks, w_down):
    rows, width = blocks[0].shape
    length = 4 * rows
    units = w_down.shape[0]
    return pl.pallas_call(
        d_hidden_kernel,
        name="back_through_down",
        out_shape=[like((length, units), jnp.float32), like((length, width))],
        in_specs=in_vmem(6),
        out_specs=in_vmem(2),
        compiler_params=limit(6),
    )(*blocks, w_down)


def mlp_kernel(
    own, from_x, from_y, low, high, d_hidden, w_gate_up, normed, hidden, d_gate_up
):
    units = w_gate_up.shape[2]
    blocks = [own, from_x, from_y, low, high]
    for (start, size), block in zip(starts_of(blocks), blocks):
        normed[start : start + size, :] = block[...]
    for at, size in chunks(units, 256):
        here = slice(at, at + size)
        gate = dot(normed[...], w_gate_up[0, :, here])
        upper = dot(normed[...], w_gate_up[1, :, here])
        incoming = d_hidden[:, here]
        sigma = 1.0 / (1.0 + jnp.exp(-gate))
        silu = gate * sigma
        hidden[:, here] = (silu * upper).astype(jnp.bfloat16)
        d_gate_up[:, here] = (incoming * upper * sigma * (1.0 + gate * (1.0 - sigma))).astype(
            jnp.bfloat16
        )
        d_gate_up[:, units + at : units + at + size] = (incoming * silu).astype(jnp.bfloat16)


def mlp(blocks, d_hidden, w_gate_up):
    rows, width = blocks[0].shape
    length = 4 * rows
    units = w_gate_up.shape[2]
    return pl.pallas_call(
        mlp_kernel,
        name="mlp",
        out_shape=[like((length, width)), like((length, units)), like((length, 2 * units))],
        in_specs=in_vmem(7),
        out_specs=in_vmem(3),
        compiler_params=limit(8),
    )(*blocks, d_hidden, w_gate_up)


def mlp_back_kernel(d_gate_up, w_gate_up, *targets):
    units = w_gate_up.shape[2]
    for at, size in chunks(w_gate_up.shape[1], 256):
        part = dot(d_gate_up[:, 0:units], w_gate_up[0, at : at + size, :], NT) + dot(
            d_gate_up[:, units : 2 * units], w_gate_up[1, at : at + size, :], NT
        )
        store_parts(part, targets, slice(at, at + size))


def mlp_back(d_gate_up, w_gate_up):
    return pl.pallas_call(
        mlp_back_kernel,
        name="mlp_back",
        out_shape=send_shapes(d_gate_up.shape[0] // 4, w_gate_up.shape[1]),
        in_specs=in_vmem(2),
        out_specs=in_vmem(5),
        compiler_params=limit(6),
    )(d_gate_up, w_gate_up)


def down_kernel(hidden, w_down, *targets):
    for at, size in chunks(w_down.shape[1], 256):
        store_parts(dot(hidden[...], w_down[:, at : at + size]), targets, slice(at, at + size))


def through_down(hidden, w_down):
    return pl.pallas_call(
        down_kernel,
        name="through_down",
        out_shape=send_shapes(hidden.shape[0] // 4, w_down.shape[1]),
        in_specs=in_vmem(2),
        out_specs=in_vmem(5),
        compiler_params=limit(6),
    )(hidden, w_down)


def attend_back_kernel(
    rows_at, own, from_x, from_y, low, high, w_out, probs, queries, keys, values, cosine, sine,
    d_middle, d_project, d_mixed,
):
    length, wide = queries.shape
    blocks = [own, from_x, from_y, low, high]
    starts = starts_of(blocks)
    for (start, size), block in zip(starts, blocks):
        d_middle[start : start + size, :] = block[...]
    for at, size in chunks(wide, 256):
        part = dot(d_middle[...], w_out[at : at + size, :], NT).astype(jnp.bfloat16)
        for i, (start, rows) in enumerate(starts):
            place = pl.multiple_of(rows_at[i], 64)
            d_mixed[pl.ds(place, rows), at : at + size] = part[start : start + rows]
    scale = HD ** (-0.5)

    def back(turned, rows):
        return turned * cosine[rows, :] - pltpu.roll(turned, HD // 2, 1) * sine[rows, :]

    for at in range(0, wide, HD):
        head = at // HD
        cols = slice(at, at + HD)
        d_keys = d_values = None
        for q_at, q_size in reversed(chunks(length, 256)):
            seen = q_at + q_size
            rows = slice(q_at, seen)
            chance = probs[head, 0:seen, rows]
            d_out = d_mixed[rows, cols]
            d_chance = dot(values[0:seen, cols], d_out, NT)
            exact = chance.astype(jnp.float32)
            delta = jnp.sum(d_chance * exact, axis=0, keepdims=True)
            d_scores = (exact * (d_chance - delta)).astype(jnp.bfloat16)
            more_values = dot(chance, d_out)
            more_keys = dot(d_scores, queries[rows, cols])
            d_queries = dot(keys[0:seen, cols], d_scores, TN).T
            d_project[rows, cols] = back(d_queries * scale, rows).astype(jnp.bfloat16)
            if d_keys is None:
                d_keys, d_values = more_keys, more_values
            else:
                d_keys = jnp.concatenate([d_keys[:seen] + more_keys, d_keys[seen:]], axis=0)
                d_values = jnp.concatenate([d_values[:seen] + more_values, d_values[seen:]], axis=0)
        d_project[:, wide + at : wide + at + HD] = back(d_keys * scale, slice(0, length)).astype(
            jnp.bfloat16
        )
        d_project[:, 2 * wide + at : 2 * wide + at + HD] = d_values.astype(jnp.bfloat16)


def attend_back_square(rows_at, blocks, w_out, probs, queries, keys, values, cosine, sine):
    length, wide = queries.shape
    return pl.pallas_call(
        attend_back_kernel,
        name="attend_back",
        out_shape=[like((length, w_out.shape[1])), like((length, 3 * wide))],
        in_specs=in_smem() + in_vmem(12),
        out_specs=in_vmem(2),
        scratch_shapes=[pltpu.VMEM((length, wide), jnp.bfloat16)],
        compiler_params=limit(8),
    )(rows_at, *blocks, w_out, probs, queries, keys, values, cosine, sine)


def project_back_kernel(rows_at, d_project, w_qkv, *refs):
    targets, turned = refs[:5], refs[5]
    wide = w_qkv.shape[2]
    for i, (start, size) in enumerate(starts_of(targets)):
        place = pl.multiple_of(rows_at[i], 64)
        turned[start : start + size, :] = d_project[pl.ds(place, size), :]
    for at, size in chunks(w_qkv.shape[1], 256):
        part = sum(
            dot(turned[:, c * wide : (c + 1) * wide], w_qkv[c, at : at + size, :], NT)
            for c in range(3)
        )
        store_parts(part, targets, slice(at, at + size))


def project_back(rows_at, d_project, w_qkv):
    return pl.pallas_call(
        project_back_kernel,
        name="project_back",
        out_shape=send_shapes(d_project.shape[0] // 4, w_qkv.shape[1]),
        in_specs=in_smem() + in_vmem(2),
        out_specs=in_vmem(5),
        scratch_shapes=[pltpu.VMEM(d_project.shape, jnp.bfloat16)],
        compiler_params=limit(8),
    )(rows_at, d_project, w_qkv)


def weight_kernel(layout, base, spot, which, *refs):
    turned, out = refs[-1], refs[-2]
    more = refs[-3] if spot is not None else None
    count, piece, _ = out.shape
    for i in range(count):
        place = pl.multiple_of(which[base + i] * piece, piece)
        at_ref = column = 0
        for pairs in layout:
            splits = refs[at_ref : at_ref + pairs]
            others = refs[at_ref + pairs : at_ref + 2 * pairs]
            at_ref += 2 * pairs
            length, across = others[0].shape
            for j, split in enumerate(splits):
                turned[:, j * length : (j + 1) * length] = split[:, pl.ds(place, piece)].T
            for at, size in chunks(across, 256):
                part = None
                for j, other in enumerate(others):
                    term = dot(turned[:, j * length : (j + 1) * length], other[:, at : at + size])
                    part = term if part is None else part + term
                cols = slice(column + at, column + at + size)
                if more is not None:
                    part = part + more[spot + i, :, cols].astype(jnp.float32)
                out[i, :, cols] = part.astype(out.dtype)
            column += across


def weight_pieces(which, base, count, groups, more=None, spot=None):
    layout = [len(splits) for splits, _ in groups]
    refs = [ref for splits, others in groups for ref in (*splits, *others)]
    extra = [] if more is None else [more]
    length = groups[0][1][0].shape[0]
    across = sum(others[0].shape[1] for _, others in groups)
    piece = groups[0][0][0].shape[1] // 8
    return pl.pallas_call(
        functools.partial(weight_kernel, layout, base, spot),
        name="weight_pieces",
        out_shape=like((count, piece, across)),
        in_specs=in_smem() + in_vmem(len(refs) + len(extra)),
        out_specs=in_vmem(1)[0],
        scratch_shapes=[pltpu.VMEM((piece, max(layout) * length), jnp.bfloat16)],
        compiler_params=limit(10),
    )(which, *refs, *extra)


def join_kernel(here_outer, here_own, there_outer, there_own, outer, own):
    for here, there, out in ((here_outer, there_outer, outer), (here_own, there_own, own)):
        for at, size in chunks(out.shape[2], 256):
            cols = slice(at, at + size)
            out[0, :, cols] = (
                here[0, :, cols].astype(jnp.float32) + there[0, :, cols].astype(jnp.float32)
            ).astype(jnp.bfloat16)


def join(here, there):
    shape = here[0].shape
    return pl.pallas_call(
        join_kernel,
        name="join",
        out_shape=[like(shape), like(shape)],
        in_specs=in_vmem(4),
        out_specs=in_vmem(2),
        compiler_params=limit(6),
    )(*here, *there)


def hand_kernel(near, far, out):
    for at, size in chunks(out.shape[1], 256):
        cols = slice(at, at + size)
        out[:, cols] = (
            near[0, :, cols].astype(jnp.float32) + far[0, :, cols].astype(jnp.float32)
        ).astype(jnp.bfloat16)


def hand(near, far):
    return pl.pallas_call(
        hand_kernel,
        name="hand",
        out_shape=like(near.shape[1:]),
        in_specs=in_vmem(2),
        out_specs=in_vmem(1)[0],
        compiler_params=limit(6),
    )(near, far)


def finish_kernel(parts, count_inner, inner, *refs):
    count = len(refs) - len(parts)
    here = [ref for ref in refs[:count_inner]]
    outer = [ref for ref in refs[count_inner:count]]

    def total(sources, cols):
        found = None
        for source in sources:
            term = source[0, :, cols] if len(source.shape) == 3 else source[:, cols]
            term = term.astype(jnp.float32)
            found = term if found is None else found + term
        return found

    column = 0
    for (planes, across, turn), out in zip(parts, refs[count:]):
        for c in range(planes):
            for at, size in chunks(across, 256):
                cols = slice(column + at, column + at + size)
                value = jnp.where(inner[0] == 1, total(here, cols), total(outer, cols))
                if turn:
                    out[at : at + size, :] = value.T
                else:
                    out[c, :, at : at + size] = value
            column += across


def finish(inner, here, outer, parts):
    piece = here[0].shape[-2]
    return pl.pallas_call(
        functools.partial(finish_kernel, parts, len(here)),
        name="finish",
        out_shape=[
            like((across, piece) if turn else (planes, piece, across), jnp.float32)
            for planes, across, turn in parts
        ],
        in_specs=in_smem() + in_vmem(len(here) + len(outer)),
        out_specs=in_vmem(len(parts)),
        compiler_params=limit(8),
    )(inner, *here, *outer)


def flips(size, bit):
    return [(i, i ^ bit) for i in range(size)]


def after(value, *earlier):
    return lax.optimization_barrier((value, *earlier))[0]


def over_tensor(values, bit):
    return lax.ppermute(values, "tensor", flips(4, bit))


def gather_near(own):
    return own, over_tensor(own, 1), over_tensor(own, 2)


def gather_far(own, from_x, from_y):
    half = own.shape[0] // 2
    low = over_tensor(from_y[:half], 1)
    high = over_tensor(from_x[half:], 2)
    return [own, from_x, from_y, low, high]


def scatter_far(keep, to_x, to_y, far_low, far_high):
    return keep, *relay(to_x, to_y, over_tensor(far_low, 1), over_tensor(far_high, 2))


def scatter_near(keep, to_x, to_y):
    return keep, over_tensor(to_x, 1), over_tensor(to_y, 2)


def over_cores(values):
    return lax.ppermute(values, "dp", flips(8, 1))


def to_inner(values):
    return lax.ppermute(values, "dp", [(0, 2), (1, 3), (6, 4), (7, 5)])


def to_outer(values):
    return lax.ppermute(values, "dp", [(2, 0), (3, 1), (4, 6), (5, 7)])


def over_middle(values):
    return lax.ppermute(values, "dp", [(2, 4), (3, 5), (4, 2), (5, 3)])


class Weight:
    def __init__(self, places, groups):
        self.which_theirs, self.which_mine, self.inner = places
        self.groups = groups

    def sibling_part(self):
        self.sibling_sum = weight_pieces(self.which_theirs, 0, 4, self.groups)
        self.theirs = over_cores(self.sibling_sum)

    def own_part(self, base, count, *earlier):
        more = after(self.theirs, *earlier) if earlier else self.theirs
        return weight_pieces(self.which_mine, base, count, self.groups, more, base)


def sum_flips(values, *steps):
    for axis, size, bit in steps:
        values = values + lax.ppermute(values, axis, flips(size, bit))
    return values


def per_device_square(
    tokens, gain_attn, gain_mlp, w_qkv, w_out, w_gate_up, w_down, cotangent, segment_ids, valid_mask
):
    rows = tokens.shape[0]
    length = segment_ids.shape[0]
    low = jnp.bfloat16
    me = lax.axis_index("tensor")
    order = [me, me ^ 1, me ^ 2, me ^ 3]
    rows_at = jnp.stack([at * rows for at in order] + [order[3] * rows + rows // 2]).astype(jnp.int32)
    index = lax.axis_index("dp")
    place, core = index // 2, index % 2
    line_order = jnp.where(place < 2, jnp.array([3, 2, 0, 1]), jnp.array([0, 1, 3, 2]))
    places = (
        (2 * line_order + 1 - core).astype(jnp.int32),
        (2 * line_order + core).astype(jnp.int32),
        ((place == 1) | (place == 2)).astype(jnp.int32).reshape(1),
    )
    gain_one = gain_attn[None, :]
    gain_two = gain_mlp[None, :]

    tokens = after(tokens, rows_at, *places)
    normed = norm(tokens, gain_one)
    near = gather_near(normed)
    cosine, sine, seg_col, valid_col = prepare(
        segment_ids.astype(jnp.float32)[None, :],
        valid_mask.astype(jnp.float32)[None, :],
    )
    near = (near[0], near[1], after(near[2], cosine))
    guest_cot_own = to_inner(cotangent)
    blocks = gather_far(*near)
    cot_near = gather_near(after(cotangent, *blocks))
    normed_all, queries, keys, values = project(rows_at, blocks, w_qkv, cosine, sine)
    *sent, probs, mixed = attend_square(
        rows_at,
        after(queries, *cot_near, guest_cot_own),
        keys,
        values,
        w_out,
        segment_ids.astype(jnp.float32)[None, :],
        seg_col,
        valid_col,
    )
    guest_cot_near = [to_inner(part) for part in cot_near[1:]]
    keep, to_x, to_y = scatter_far(*sent)
    cot_blocks = gather_far(*(after(part, to_x) for part in cot_near))
    got = scatter_near(keep, to_x, to_y)
    d_hidden, cot_all = back_through_down(
        [after(cot_blocks[0], *guest_cot_near)] + cot_blocks[1:], w_down
    )
    middle, normed_two = make_middle(
        tokens, after(got[0], cot_all), *got[1:], gain_two
    )

    near = gather_near(normed_two)
    guest_cot_far = [to_inner(part) for part in cot_blocks[3:]]
    guest_own = to_inner(normed_two)
    blocks = gather_far(*near)
    normed_two_all, hidden, d_gate_up = mlp(
        [after(blocks[0], *guest_cot_far)] + blocks[1:], d_hidden, w_gate_up
    )
    guest_near = [to_inner(part) for part in near[1:]]
    guest_far = [to_inner(part) for part in blocks[3:]]
    sent = mlp_back(after(d_gate_up, guest_own), w_gate_up)
    down = Weight(places, [([after(cot_all, *sent)], [hidden])])
    down.sibling_part()
    keep, to_x, to_y = scatter_far(
        sent[0], after(sent[1], down.sibling_sum, *guest_near), *sent[2:]
    )
    got = scatter_near(keep, to_x, to_y)
    down_far = [down.own_part(0, 1, to_x, to_y)]
    down_far += [down.own_part(1, 1, down_far[0])]
    down_arrived = [to_inner(part) for part in down_far]
    guest_d_hidden, guest_cot_all = back_through_down(
        [after(guest_cot_own, down_far[1]), *guest_cot_near, *guest_cot_far], w_down
    )
    d_middle, gain_two_part, d_middle_low = norm_back(
        cotangent,
        after(got[0], guest_d_hidden, down_arrived[0]),
        *got[1:],
        middle,
        gain_two,
        True,
    )
    near = gather_near(d_middle_low)
    guest_normed_two, _, guest_d_gate_up = mlp(
        [after(guest_own, d_middle_low), *guest_near, *guest_far], guest_d_hidden, w_gate_up
    )
    gate = Weight(
        places, [([normed_two_all, after(guest_normed_two, down_arrived[1])], [d_gate_up, guest_d_gate_up])]
    )
    gate.sibling_part()
    down_far[0] = after(down_far[0], gate.sibling_sum)
    down_outer, down_own = join(down_far, down_arrived)
    down_joined = down_own
    down_outer, down_own = over_middle(down_outer), over_middle(down_own)
    blocks = gather_far(near[0], *(after(part, gate.sibling_sum) for part in near[1:]))

    d_middle_all, d_project = attend_back_square(
        rows_at, blocks, w_out, after(probs, down_joined), queries, keys, values, cosine, sine
    )
    late = Weight(places, [([normed_all], [d_project]), ([d_middle_all], [mixed])])
    late.sibling_part()
    gate_outer = gate.own_part(0, 1, late.sibling_sum)
    gate_own = gate.own_part(1, 1, gate_outer)
    late_far = [late.own_part(0, 1, gate_own)]
    late_far += [late.own_part(1, 1, late_far[0])]
    late_arrived = [to_inner(part) for part in late_far]
    gate_outer, gate_own = over_middle(gate_outer), over_middle(gate_own)
    sent = project_back(rows_at, after(d_project, *late_far, down_outer), w_qkv)
    keep, to_x, to_y = scatter_far(sent[0], after(sent[1], down_own), *sent[2:])
    got = scatter_near(keep, to_x, to_y)
    late_near = late.own_part(2, 1, to_x, to_y), late.own_part(3, 1, to_x, to_y)
    late_near_arrived = to_inner(late_near[1])
    down_near = down.own_part(2, 1, *late_near), down.own_part(3, 1, *late_near)
    down_near_arrived = to_inner(down_near[1])
    d_inputs, gain_one_part = norm_back(
        d_middle, after(got[0], *down_near), *got[1:], tokens, gain_one, False
    )
    gate_near = gate.own_part(2, 1, d_inputs, gate_outer), gate.own_part(3, 1, d_inputs, gate_outer)
    down_given = to_outer(hand(after(down_near[0], *gate_near), down_outer))
    gain_parts = sum_flips(
        after(jnp.concatenate([gain_one_part, gain_two_part], axis=0), *gate_near),
        ("dp", 8, 1),
        ("tensor", 4, 1),
        ("tensor", 4, 2),
    )
    late_far[0] = after(late_far[0], gain_parts, late_near_arrived)
    late_outer, late_own = join(late_far, late_arrived)
    late_outer, late_own = over_middle(late_outer), over_middle(late_own)
    gate_given = to_outer(hand(gate_near[0], gate_outer))
    sent = through_down(after(hidden, *late_arrived, gate_own, *gate_near), w_down)
    keep, got_x, got_y = scatter_near(*scatter_far(*sent))
    output = (middle + keep + got_x.astype(jnp.float32) + got_y.astype(jnp.float32)).astype(low)
    grad_gains = sum_flips(after(gain_parts, output), ("dp", 8, 2), ("dp", 8, 4))
    inner = places[2]
    units, wide = w_down.shape[0], w_qkv.shape[2]
    (grad_down,) = finish(
        inner,
        [down_near[1], down_near_arrived, down_own],
        [down_near[0], down_given],
        [(1, units, True)],
    )
    (grad_gate_up,) = finish(inner, [gate_near[1], gate_own], [gate_given], [(2, units, False)])
    late_given = to_outer(hand(late_near[0], late_outer))
    grad_qkv, grad_out = finish(
        inner,
        [late_near[1], late_near_arrived, late_own],
        [late_near[0], late_given],
        [(3, wide, False), (1, wide, True)],
    )
    return (
        output,
        d_inputs,
        grad_gains[0],
        grad_gains[1],
        grad_qkv,
        grad_out,
        grad_gate_up,
        grad_down,
    )


def solution(mesh):
    placed = (
        P(("dp", "tensor"), None),
        P(),
        P(),
        P(None, None, "tensor"),
        P("tensor", None),
        P(None, None, "tensor"),
        P("tensor", None),
        P(("dp", "tensor"), None),
        P("dp"),
        P("dp"),
    )
    square = mesh.shape["tensor"] == 4 and mesh.shape["dp"] == 8
    return jax.shard_map(
        per_device_square if square else per_device,
        mesh=mesh,
        in_specs=placed,
        out_specs=(
            P(("dp", "tensor"), None),
            P(("dp", "tensor"), None),
            P(),
            P(),
            P(None, "dp", "tensor"),
            P("tensor", "dp"),
            P(None, "dp", "tensor"),
            P("tensor", "dp"),
        ),
        check_vma=False,
    )
```

```python
import functools
import math

import jax
import jax.numpy as jnp
from jax import lax
from jax.experimental import pallas as pl
from jax.experimental.pallas import tpu as pltpu
from jax.sharding import PartitionSpec as P

HD = 128


EPS = 1e-06
THETA = 10000.0


def rope_tables(places):
    positions = places.astype(jnp.float32)
    freqs = THETA ** (-(jnp.arange(HD // 2).astype(jnp.float32) * 2.0 / HD))
    angles = positions[:, None] * freqs[None, :]
    return (jnp.cos(angles), jnp.sin(angles))


def rotate(values, cosine, sine):
    half = values.shape[-1] // 2
    first = values[..., :half]
    second = values[..., half:]
    cosine = cosine[:, None, :]
    sine = sine[:, None, :]
    return jnp.concatenate(
        [first * cosine - second * sine, second * cosine + first * sine], axis=-1
    )


def block_scores(q_block, keys_rot, start, segments, valid):
    block_rows = q_block.shape[0]
    length = keys_rot.shape[0]
    key_pos = jnp.arange(length)
    row_pos = start + jnp.arange(block_rows)
    row_seg = lax.dynamic_slice_in_dim(segments, start, block_rows, 0)
    scores = jnp.einsum(
        "qhd,khd->hqk", q_block, keys_rot, preferred_element_type=jnp.float32
    ) * HD ** (-0.5)
    allowed = (
        (key_pos[None, :] <= row_pos[:, None])
        & (row_seg[:, None] == segments[None, :])
        & ((valid[None, :] == 1) | (key_pos[None, :] == row_pos[:, None]))
    )
    return jnp.where(allowed[None], scores, -1e30)


def attend(queries, keys_rot, values, segments, valid):
    length = queries.shape[0]
    block_rows = min(512, length)
    count = length // block_rows

    def one_block(index):
        start = index * block_rows
        q_block = lax.dynamic_slice_in_dim(queries, start, block_rows, 0)
        scores = block_scores(q_block, keys_rot, start, segments, valid)
        top = jnp.max(scores, axis=-1, keepdims=True)
        expo = jnp.exp(scores - top)
        total = jnp.sum(expo, axis=-1, keepdims=True)
        probs = (expo / total).astype(jnp.bfloat16)
        result = jnp.einsum("hqk,khd->qhd", probs, values, preferred_element_type=jnp.float32)
        return (result, top[..., 0] + jnp.log(total[..., 0]))

    blocks, log_sums = lax.map(one_block, jnp.arange(count))
    return (blocks.reshape(length, -1), log_sums)


def attend_back(queries, keys_rot, values, d_mixed, log_sums, segments, valid):
    length = queries.shape[0]
    block_rows = min(512, length)
    count = length // block_rows
    scale = HD ** (-0.5)

    def one_block(carry, index):
        d_keys, d_values = carry
        start = index * block_rows
        q_block = lax.dynamic_slice_in_dim(queries, start, block_rows, 0)
        d_block = lax.dynamic_slice_in_dim(d_mixed, start, block_rows, 0)
        scores = block_scores(q_block, keys_rot, start, segments, valid)
        probs = jnp.exp(scores - log_sums[index][..., None])
        d_values = d_values + jnp.einsum(
            "hqk,qhd->khd", probs.astype(jnp.bfloat16), d_block, preferred_element_type=jnp.float32
        )
        d_probs = jnp.einsum("qhd,khd->hqk", d_block, values, preferred_element_type=jnp.float32)
        delta = jnp.sum(d_probs * probs, axis=-1, keepdims=True)
        d_scores = (probs * (d_probs - delta)).astype(jnp.bfloat16)
        d_query = scale * jnp.einsum(
            "hqk,khd->qhd", d_scores, keys_rot, preferred_element_type=jnp.float32
        )
        d_keys = d_keys + scale * jnp.einsum(
            "hqk,qhd->khd", d_scores, q_block, preferred_element_type=jnp.float32
        )
        return ((d_keys, d_values), d_query)

    empty = jnp.zeros(keys_rot.shape, jnp.float32)
    (d_keys, d_values), d_queries = lax.scan(one_block, (empty, empty), jnp.arange(count))
    return (d_queries.reshape(queries.shape), d_keys, d_values)


def per_device(
    tokens, gain_attn, gain_mlp, w_qkv, w_out, w_gate_up, w_down, cotangent, segment_ids, valid_mask
):
    length = segment_ids.shape[0]
    heads_here = w_qkv.shape[2] // HD
    shape3 = (length, heads_here, HD)
    incoming = tokens.astype(jnp.float32)
    gain_one = gain_attn.astype(jnp.float32)
    gain_two = gain_mlp.astype(jnp.float32)
    cosine, sine = rope_tables(jnp.arange(length))
    inv_one = lax.rsqrt(jnp.mean(incoming * incoming, axis=-1, keepdims=True) + EPS)
    normed = (incoming * inv_one * gain_one).astype(jnp.bfloat16)
    normed_all = lax.all_gather(normed, "tensor", axis=0, tiled=True)
    project = jnp.einsum("td,cde->cte", normed_all, w_qkv, preferred_element_type=jnp.float32)
    queries = rotate(project[0].reshape(shape3), cosine, sine).astype(jnp.bfloat16)
    keys_rot = rotate(project[1].reshape(shape3), cosine, sine).astype(jnp.bfloat16)
    values = project[2].reshape(shape3).astype(jnp.bfloat16)
    mixed, log_sums = attend(queries, keys_rot, values, segment_ids, valid_mask)
    mixed = mixed.astype(jnp.bfloat16)
    middle = incoming + lax.psum_scatter(
        jnp.dot(mixed, w_out, preferred_element_type=jnp.float32).astype(jnp.bfloat16),
        "tensor",
        scatter_dimension=0,
        tiled=True,
    ).astype(jnp.float32)
    inv_two = lax.rsqrt(jnp.mean(middle * middle, axis=-1, keepdims=True) + EPS)
    normed_two = (middle * inv_two * gain_two).astype(jnp.bfloat16)
    normed_two_all = lax.all_gather(normed_two, "tensor", axis=0, tiled=True)
    gate = jnp.dot(normed_two_all, w_gate_up[0], preferred_element_type=jnp.float32)
    upper = jnp.dot(normed_two_all, w_gate_up[1], preferred_element_type=jnp.float32)
    sigma = jax.nn.sigmoid(gate)
    hidden = (gate * sigma * upper).astype(jnp.bfloat16)
    result = middle + lax.psum_scatter(
        jnp.dot(hidden, w_down, preferred_element_type=jnp.float32).astype(jnp.bfloat16),
        "tensor",
        scatter_dimension=0,
        tiled=True,
    ).astype(jnp.float32)
    output = result.astype(jnp.bfloat16)
    cot_all = lax.all_gather(cotangent, "tensor", axis=0, tiled=True)
    d_hidden = jnp.einsum("td,fd->tf", cot_all, w_down, preferred_element_type=jnp.float32)
    grad_down = jnp.einsum("tf,td->fd", hidden, cot_all, preferred_element_type=jnp.float32)
    d_upper = (d_hidden * gate * sigma).astype(jnp.bfloat16)
    d_gate = (d_hidden * upper * sigma * (1.0 + gate * (1.0 - sigma))).astype(jnp.bfloat16)
    grad_gate_up = jnp.stack(
        [
            jnp.einsum("td,tf->df", normed_two_all, d_gate, preferred_element_type=jnp.float32),
            jnp.einsum("td,tf->df", normed_two_all, d_upper, preferred_element_type=jnp.float32),
        ]
    )
    d_normed_two = lax.psum_scatter(
        (
            jnp.einsum("tf,df->td", d_gate, w_gate_up[0], preferred_element_type=jnp.float32)
            + jnp.einsum("tf,df->td", d_upper, w_gate_up[1], preferred_element_type=jnp.float32)
        ).astype(jnp.bfloat16),
        "tensor",
        scatter_dimension=0,
        tiled=True,
    ).astype(jnp.float32)
    scaled_two = gain_two * d_normed_two
    d_middle = (
        cotangent.astype(jnp.float32)
        + inv_two * scaled_two
        - middle * inv_two**3 * jnp.mean(scaled_two * middle, axis=-1, keepdims=True)
    )
    grad_gain_two = jnp.sum(d_normed_two * middle * inv_two, axis=0)
    d_middle_all = lax.all_gather(d_middle.astype(jnp.bfloat16), "tensor", axis=0, tiled=True)
    d_mixed = jnp.einsum(
        "td,ed->te", d_middle_all, w_out, preferred_element_type=jnp.float32
    ).astype(jnp.bfloat16)
    grad_out = jnp.einsum("te,td->ed", mixed, d_middle_all, preferred_element_type=jnp.float32)
    d_queries, d_keys, d_values = attend_back(
        queries, keys_rot, values, d_mixed.reshape(shape3), log_sums, segment_ids, valid_mask
    )
    d_project = jnp.stack(
        [
            rotate(d_queries, cosine, -sine).reshape(length, -1),
            rotate(d_keys, cosine, -sine).reshape(length, -1),
            d_values.reshape(length, -1),
        ]
    ).astype(jnp.bfloat16)
    grad_qkv = jnp.einsum("td,cte->cde", normed_all, d_project, preferred_element_type=jnp.float32)
    d_normed = lax.psum_scatter(
        jnp.einsum("cte,cde->td", d_project, w_qkv, preferred_element_type=jnp.float32).astype(
            jnp.bfloat16
        ),
        "tensor",
        scatter_dimension=0,
        tiled=True,
    ).astype(jnp.float32)
    scaled_one = gain_one * d_normed
    d_inputs = (
        d_middle
        + inv_one * scaled_one
        - incoming * inv_one**3 * jnp.mean(scaled_one * incoming, axis=-1, keepdims=True)
    )
    grad_gain_one = jnp.sum(d_normed * incoming * inv_one, axis=0)
    grad_gain_one, grad_gain_two = lax.psum((grad_gain_one, grad_gain_two), ("dp", "tensor"))
    grad_qkv, grad_out, grad_gate_up, grad_down = (
        lax.psum_scatter(
            grad_qkv.astype(jnp.bfloat16), "dp", scatter_dimension=1, tiled=True
        ).astype(jnp.float32),
        lax.psum_scatter(
            grad_out.astype(jnp.bfloat16), "dp", scatter_dimension=1, tiled=True
        ).astype(jnp.float32),
        lax.psum_scatter(
            grad_gate_up.astype(jnp.bfloat16), "dp", scatter_dimension=1, tiled=True
        ).astype(jnp.float32),
        lax.psum_scatter(
            grad_down.astype(jnp.bfloat16), "dp", scatter_dimension=1, tiled=True
        ).astype(jnp.float32),
    )
    return (
        output,
        d_inputs,
        grad_gain_one,
        grad_gain_two,
        grad_qkv,
        grad_out,
        grad_gate_up,
        grad_down,
    )


NT = (((1,), (1,)), ((), ()))
TN = (((0,), (0,)), ((), ()))
MEGA = 1024 * 1024


def chunks(total, step):
    return [(at, min(step, total - at)) for at in range(0, total, step)]


def dot(left, right, dims=None):
    if dims is None:
        return jnp.dot(left, right, preferred_element_type=jnp.float32)
    return lax.dot_general(left, right, dims, preferred_element_type=jnp.float32)


def in_vmem(count):
    return [pl.BlockSpec(memory_space=pltpu.VMEM)] * count


def in_smem():
    return [pl.BlockSpec(memory_space=pltpu.SMEM)]


def like(shape, kind=jnp.bfloat16):
    return jax.ShapeDtypeStruct(shape, kind)


def limit(megabytes):
    return pltpu.CompilerParams(vmem_limit_bytes=megabytes * MEGA)


def starts_of(blocks):
    at, starts = 0, []
    for block in blocks:
        starts.append((at, block.shape[0]))
        at += block.shape[0]
    return starts


def send_shapes(rows, width):
    half = rows // 2
    return [
        like((rows, width), jnp.float32),
        like((rows, width)),
        like((rows, width)),
        like((half, width)),
        like((half, width)),
    ]


def store_parts(part, targets, cols):
    for (start, rows), target in zip(starts_of(targets), targets):
        target[:, cols] = part[start : start + rows].astype(target.dtype)


def norm_kernel(tokens, gain, normed):
    wide = tokens[...].astype(jnp.float32)
    inverse = lax.rsqrt(jnp.mean(wide * wide, axis=-1, keepdims=True) + EPS)
    normed[...] = (wide * inverse * gain[...].astype(jnp.float32)).astype(jnp.bfloat16)


def norm(tokens, gain):
    return pl.pallas_call(
        norm_kernel,
        name="norm",
        out_shape=like(tokens.shape),
        in_specs=in_vmem(2),
        out_specs=in_vmem(1)[0],
        compiler_params=limit(4),
    )(tokens, gain)


def relay_kernel(to_x, to_y, via_x, via_y, next_x, next_y):
    half = via_x.shape[0]
    next_x[:half] = to_x[:half]
    next_x[half:] = (
        to_x[half:].astype(jnp.float32) + via_y[...].astype(jnp.float32)
    ).astype(jnp.bfloat16)
    next_y[:half] = (
        to_y[:half].astype(jnp.float32) + via_x[...].astype(jnp.float32)
    ).astype(jnp.bfloat16)
    next_y[half:] = to_y[half:]


def relay(to_x, to_y, via_x, via_y):
    return pl.pallas_call(
        relay_kernel,
        name="relay",
        out_shape=[like(to_x.shape), like(to_y.shape)],
        in_specs=in_vmem(4),
        out_specs=in_vmem(2),
        compiler_params=limit(4),
    )(to_x, to_y, via_x, via_y)


def middle_kernel(tokens, keep, got_x, got_y, gain, middle, normed):
    total = (
        tokens[...].astype(jnp.float32)
        + keep[...]
        + got_x[...].astype(jnp.float32)
        + got_y[...].astype(jnp.float32)
    )
    middle[...] = total
    inverse = lax.rsqrt(jnp.mean(total * total, axis=-1, keepdims=True) + EPS)
    normed[...] = (total * inverse * gain[...].astype(jnp.float32)).astype(jnp.bfloat16)


def make_middle(tokens, keep, got_x, got_y, gain):
    return pl.pallas_call(
        middle_kernel,
        name="make_middle",
        out_shape=[like(keep.shape, jnp.float32), like(keep.shape)],
        in_specs=in_vmem(5),
        out_specs=in_vmem(2),
        compiler_params=limit(6),
    )(tokens, keep, got_x, got_y, gain)


def norm_back_kernel(base, keep, got_x, got_y, source, gain, *outs):
    d_normed = keep[...] + got_x[...].astype(jnp.float32) + got_y[...].astype(jnp.float32)
    wide = source[...].astype(jnp.float32)
    inverse = lax.rsqrt(jnp.mean(wide * wide, axis=-1, keepdims=True) + EPS)
    scaled = gain[...].astype(jnp.float32) * d_normed
    slope = jnp.mean(scaled * wide, axis=-1, keepdims=True) * inverse * inverse * inverse
    total = base[...].astype(jnp.float32) + inverse * scaled - wide * slope
    outs[0][...] = total
    outs[1][...] = jnp.sum(d_normed * wide * inverse, axis=0, keepdims=True)
    if len(outs) == 3:
        outs[2][...] = total.astype(jnp.bfloat16)


def norm_back(base, keep, got_x, got_y, source, gain, low):
    return pl.pallas_call(
        norm_back_kernel,
        name="norm_back",
        out_shape=[like(keep.shape, jnp.float32), like((1, keep.shape[1]), jnp.float32)]
        + [like(keep.shape)] * low,
        in_specs=in_vmem(6),
        out_specs=in_vmem(2 + low),
        compiler_params=limit(8),
    )(base, keep, got_x, got_y, source, gain)


def prepare_kernel(segments, valid, cosine, sine, seg_col, valid_col):
    length = cosine.shape[0]
    half = HD // 2
    place = lax.broadcasted_iota(jnp.int32, (length, HD), 0).astype(jnp.float32)
    lane = lax.broadcasted_iota(jnp.int32, (length, HD), 1)
    step = jnp.where(lane < half, lane, lane - half).astype(jnp.float32)
    angle = place * jnp.exp(step * (-2.0 / HD * math.log(THETA)))
    cosine[...] = jnp.cos(angle)
    turn = jnp.sin(angle)
    sine[...] = jnp.where(lane < half, -turn, turn)
    seg_col[...] = jnp.broadcast_to(segments[...], (HD, length)).T
    valid_col[...] = jnp.broadcast_to(valid[...], (HD, length)).T


def prepare(segments, valid):
    length = segments.shape[1]
    return pl.pallas_call(
        prepare_kernel,
        name="prepare",
        out_shape=[like((length, HD), jnp.float32)] * 4,
        in_specs=in_vmem(2),
        out_specs=in_vmem(4),
        compiler_params=limit(6),
    )(segments, valid)


def project_kernel(
    rows_at, own, from_x, from_y, low, high, w_qkv, cosine, sine, normed, queries, keys, values
):
    for i, block in enumerate((own, from_x, from_y, low, high)):
        place = pl.multiple_of(rows_at[i], 64)
        normed[pl.ds(place, block.shape[0]), :] = block[...]
    for c, target in enumerate((queries, keys, values)):
        for at, size in chunks(target.shape[1], 2 * HD):
            part = dot(normed[...], w_qkv[c, :, at : at + size])
            for head in range(0, size, HD):
                piece = part[:, head : head + HD]
                if c < 2:
                    piece = piece * cosine[...] + pltpu.roll(piece, HD // 2, 1) * sine[...]
                target[:, at + head : at + head + HD] = piece.astype(jnp.bfloat16)


def project(rows_at, blocks, w_qkv, cosine, sine):
    rows, width = blocks[0].shape
    length = 4 * rows
    wide = w_qkv.shape[2]
    return pl.pallas_call(
        project_kernel,
        name="project",
        out_shape=[like((length, width))] + [like((length, wide))] * 3,
        in_specs=in_smem() + in_vmem(8),
        out_specs=in_vmem(4),
        compiler_params=limit(8),
    )(rows_at, *blocks, w_qkv, cosine, sine)


def attend_kernel(
    rows_at, queries, keys, values, w_out, seg_row, seg_col, valid_col,
    keep, to_x, to_y, far_low, far_high, probs, mixed, bias, joined,
):
    length, wide = queries.shape
    key_at = lax.broadcasted_iota(jnp.int32, (length, length), 0)
    query_at = lax.broadcasted_iota(jnp.int32, (length, length), 1)
    allowed = (
        (key_at <= query_at)
        & (seg_col[:, 0:1] == seg_row[...])
        & ((valid_col[:, 0:1] == 1.0) | (key_at == query_at))
    )
    bias[...] = jnp.where(allowed, 0.0, -1e30)
    for at in range(0, wide, HD):
        head = at // HD
        cols = slice(at, at + HD)
        for q_at, q_size in chunks(length, 256):
            seen = q_at + q_size
            scores = dot(keys[0:seen, cols], queries[q_at:seen, cols], NT)
            scores = scores * HD ** (-0.5) + bias[0:seen, q_at:seen]
            top = jnp.max(scores, axis=0, keepdims=True)
            expo = jnp.exp(scores - top)
            total = jnp.sum(expo, axis=0, keepdims=True)
            chance = (expo * (1.0 / total)).astype(jnp.bfloat16)
            probs[head, 0:seen, q_at:seen] = chance
            result = dot(values[0:seen, cols], chance, TN)
            joined[q_at:seen, cols] = result.T.astype(jnp.bfloat16)
    targets = [keep, to_x, to_y, far_low, far_high]
    for i, (start, size) in enumerate(starts_of(targets)):
        place = pl.multiple_of(rows_at[i], 64)
        mixed[start : start + size, :] = joined[pl.ds(place, size), :]
    for at, size in chunks(w_out.shape[1], 512):
        store_parts(dot(mixed[...], w_out[:, at : at + size]), targets, slice(at, at + size))


def attend_square(rows_at, queries, keys, values, w_out, seg_row, seg_col, valid_col):
    length, wide = queries.shape
    width = w_out.shape[1]
    heads = wide // HD
    return pl.pallas_call(
        attend_kernel,
        name="attend",
        out_shape=send_shapes(length // 4, width)
        + [like((heads, length, length)), like((length, wide))],
        in_specs=in_smem() + in_vmem(7),
        out_specs=in_vmem(7),
        scratch_shapes=[
            pltpu.VMEM((length, length), jnp.float32),
            pltpu.VMEM((length, wide), jnp.bfloat16),
        ],
        compiler_params=limit(8),
    )(rows_at, queries, keys, values, w_out, seg_row, seg_col, valid_col)


def d_hidden_kernel(own, from_x, from_y, low, high, w_down, d_hidden, cot_all):
    blocks = [own, from_x, from_y, low, high]
    for (start, size), block in zip(starts_of(blocks), blocks):
        cot_all[start : start + size, :] = block[...]
    for at, size in chunks(w_down.shape[0], 256):
        d_hidden[:, at : at + size] = dot(cot_all[...], w_down[at : at + size, :], NT)


def back_through_down(blocks, w_down):
    rows, width = blocks[0].shape
    length = 4 * rows
    units = w_down.shape[0]
    return pl.pallas_call(
        d_hidden_kernel,
        name="back_through_down",
        out_shape=[like((length, units), jnp.float32), like((length, width))],
        in_specs=in_vmem(6),
        out_specs=in_vmem(2),
        compiler_params=limit(6),
    )(*blocks, w_down)


def mlp_kernel(
    own, from_x, from_y, low, high, d_hidden, w_gate_up, normed, hidden, d_gate_up
):
    units = w_gate_up.shape[2]
    blocks = [own, from_x, from_y, low, high]
    for (start, size), block in zip(starts_of(blocks), blocks):
        normed[start : start + size, :] = block[...]
    for at, size in chunks(units, 256):
        here = slice(at, at + size)
        gate = dot(normed[...], w_gate_up[0, :, here])
        upper = dot(normed[...], w_gate_up[1, :, here])
        incoming = d_hidden[:, here]
        sigma = 1.0 / (1.0 + jnp.exp(-gate))
        silu = gate * sigma
        hidden[:, here] = (silu * upper).astype(jnp.bfloat16)
        d_gate_up[:, here] = (incoming * upper * sigma * (1.0 + gate * (1.0 - sigma))).astype(
            jnp.bfloat16
        )
        d_gate_up[:, units + at : units + at + size] = (incoming * silu).astype(jnp.bfloat16)


def mlp(blocks, d_hidden, w_gate_up):
    rows, width = blocks[0].shape
    length = 4 * rows
    units = w_gate_up.shape[2]
    return pl.pallas_call(
        mlp_kernel,
        name="mlp",
        out_shape=[like((length, width)), like((length, units)), like((length, 2 * units))],
        in_specs=in_vmem(7),
        out_specs=in_vmem(3),
        compiler_params=limit(8),
    )(*blocks, d_hidden, w_gate_up)


def mlp_back_kernel(d_gate_up, w_gate_up, *targets):
    units = w_gate_up.shape[2]
    for at, size in chunks(w_gate_up.shape[1], 256):
        part = dot(d_gate_up[:, 0:units], w_gate_up[0, at : at + size, :], NT) + dot(
            d_gate_up[:, units : 2 * units], w_gate_up[1, at : at + size, :], NT
        )
        store_parts(part, targets, slice(at, at + size))


def mlp_back(d_gate_up, w_gate_up):
    return pl.pallas_call(
        mlp_back_kernel,
        name="mlp_back",
        out_shape=send_shapes(d_gate_up.shape[0] // 4, w_gate_up.shape[1]),
        in_specs=in_vmem(2),
        out_specs=in_vmem(5),
        compiler_params=limit(6),
    )(d_gate_up, w_gate_up)


def down_kernel(hidden, w_down, *targets):
    for at, size in chunks(w_down.shape[1], 256):
        store_parts(dot(hidden[...], w_down[:, at : at + size]), targets, slice(at, at + size))


def through_down(hidden, w_down):
    return pl.pallas_call(
        down_kernel,
        name="through_down",
        out_shape=send_shapes(hidden.shape[0] // 4, w_down.shape[1]),
        in_specs=in_vmem(2),
        out_specs=in_vmem(5),
        compiler_params=limit(6),
    )(hidden, w_down)


def attend_back_kernel(
    rows_at, own, from_x, from_y, low, high, w_out, probs, queries, keys, values, cosine, sine,
    d_middle, d_project, d_mixed,
):
    length, wide = queries.shape
    blocks = [own, from_x, from_y, low, high]
    starts = starts_of(blocks)
    for (start, size), block in zip(starts, blocks):
        d_middle[start : start + size, :] = block[...]
    for at, size in chunks(wide, 256):
        part = dot(d_middle[...], w_out[at : at + size, :], NT).astype(jnp.bfloat16)
        for i, (start, rows) in enumerate(starts):
            place = pl.multiple_of(rows_at[i], 64)
            d_mixed[pl.ds(place, rows), at : at + size] = part[start : start + rows]
    scale = HD ** (-0.5)

    def back(turned, rows):
        return turned * cosine[rows, :] - pltpu.roll(turned, HD // 2, 1) * sine[rows, :]

    for at in range(0, wide, HD):
        head = at // HD
        cols = slice(at, at + HD)
        d_keys = d_values = None
        for q_at, q_size in reversed(chunks(length, 256)):
            seen = q_at + q_size
            rows = slice(q_at, seen)
            chance = probs[head, 0:seen, rows]
            d_out = d_mixed[rows, cols]
            d_chance = dot(values[0:seen, cols], d_out, NT)
            exact = chance.astype(jnp.float32)
            delta = jnp.sum(d_chance * exact, axis=0, keepdims=True)
            d_scores = (exact * (d_chance - delta)).astype(jnp.bfloat16)
            more_values = dot(chance, d_out)
            more_keys = dot(d_scores, queries[rows, cols])
            d_queries = dot(keys[0:seen, cols], d_scores, TN).T
            d_project[rows, cols] = back(d_queries * scale, rows).astype(jnp.bfloat16)
            if d_keys is None:
                d_keys, d_values = more_keys, more_values
            else:
                d_keys = jnp.concatenate([d_keys[:seen] + more_keys, d_keys[seen:]], axis=0)
                d_values = jnp.concatenate([d_values[:seen] + more_values, d_values[seen:]], axis=0)
        d_project[:, wide + at : wide + at + HD] = back(d_keys * scale, slice(0, length)).astype(
            jnp.bfloat16
        )
        d_project[:, 2 * wide + at : 2 * wide + at + HD] = d_values.astype(jnp.bfloat16)


def attend_back_square(rows_at, blocks, w_out, probs, queries, keys, values, cosine, sine):
    length, wide = queries.shape
    return pl.pallas_call(
        attend_back_kernel,
        name="attend_back",
        out_shape=[like((length, w_out.shape[1])), like((length, 3 * wide))],
        in_specs=in_smem() + in_vmem(12),
        out_specs=in_vmem(2),
        scratch_shapes=[pltpu.VMEM((length, wide), jnp.bfloat16)],
        compiler_params=limit(8),
    )(rows_at, *blocks, w_out, probs, queries, keys, values, cosine, sine)


def project_back_kernel(rows_at, d_project, w_qkv, *refs):
    targets, turned = refs[:5], refs[5]
    wide = w_qkv.shape[2]
    for i, (start, size) in enumerate(starts_of(targets)):
        place = pl.multiple_of(rows_at[i], 64)
        turned[start : start + size, :] = d_project[pl.ds(place, size), :]
    for at, size in chunks(w_qkv.shape[1], 256):
        part = sum(
            dot(turned[:, c * wide : (c + 1) * wide], w_qkv[c, at : at + size, :], NT)
            for c in range(3)
        )
        store_parts(part, targets, slice(at, at + size))


def project_back(rows_at, d_project, w_qkv):
    return pl.pallas_call(
        project_back_kernel,
        name="project_back",
        out_shape=send_shapes(d_project.shape[0] // 4, w_qkv.shape[1]),
        in_specs=in_smem() + in_vmem(2),
        out_specs=in_vmem(5),
        scratch_shapes=[pltpu.VMEM(d_project.shape, jnp.bfloat16)],
        compiler_params=limit(8),
    )(rows_at, d_project, w_qkv)


def weight_kernel(layout, base, spot, which, *refs):
    turned, out = refs[-1], refs[-2]
    more = refs[-3] if spot is not None else None
    count, piece, _ = out.shape
    for i in range(count):
        place = pl.multiple_of(which[base + i] * piece, piece)
        at_ref = column = 0
        for pairs in layout:
            splits = refs[at_ref : at_ref + pairs]
            others = refs[at_ref + pairs : at_ref + 2 * pairs]
            at_ref += 2 * pairs
            length, across = others[0].shape
            for j, split in enumerate(splits):
                turned[:, j * length : (j + 1) * length] = split[:, pl.ds(place, piece)].T
            for at, size in chunks(across, 256):
                part = None
                for j, other in enumerate(others):
                    term = dot(turned[:, j * length : (j + 1) * length], other[:, at : at + size])
                    part = term if part is None else part + term
                cols = slice(column + at, column + at + size)
                if more is not None:
                    part = part + more[spot + i, :, cols].astype(jnp.float32)
                out[i, :, cols] = part.astype(out.dtype)
            column += across


def weight_pieces(which, base, count, groups, more=None, spot=None):
    layout = [len(splits) for splits, _ in groups]
    refs = [ref for splits, others in groups for ref in (*splits, *others)]
    extra = [] if more is None else [more]
    length = groups[0][1][0].shape[0]
    across = sum(others[0].shape[1] for _, others in groups)
    piece = groups[0][0][0].shape[1] // 8
    return pl.pallas_call(
        functools.partial(weight_kernel, layout, base, spot),
        name="weight_pieces",
        out_shape=like((count, piece, across)),
        in_specs=in_smem() + in_vmem(len(refs) + len(extra)),
        out_specs=in_vmem(1)[0],
        scratch_shapes=[pltpu.VMEM((piece, max(layout) * length), jnp.bfloat16)],
        compiler_params=limit(16),
    )(which, *refs, *extra)


def join_kernel(here_outer, here_own, there_outer, there_own, outer, own):
    for here, there, out in ((here_outer, there_outer, outer), (here_own, there_own, own)):
        for at, size in chunks(out.shape[2], 256):
            cols = slice(at, at + size)
            out[0, :, cols] = (
                here[0, :, cols].astype(jnp.float32) + there[0, :, cols].astype(jnp.float32)
            ).astype(jnp.bfloat16)


def join(here, there):
    shape = here[0].shape
    return pl.pallas_call(
        join_kernel,
        name="join",
        out_shape=[like(shape), like(shape)],
        in_specs=in_vmem(4),
        out_specs=in_vmem(2),
        compiler_params=limit(6),
    )(*here, *there)


def hand_kernel(near, far, out):
    for at, size in chunks(out.shape[1], 256):
        cols = slice(at, at + size)
        out[:, cols] = (
            near[0, :, cols].astype(jnp.float32) + far[0, :, cols].astype(jnp.float32)
        ).astype(jnp.bfloat16)


def hand(near, far):
    return pl.pallas_call(
        hand_kernel,
        name="hand",
        out_shape=like(near.shape[1:]),
        in_specs=in_vmem(2),
        out_specs=in_vmem(1)[0],
        compiler_params=limit(6),
    )(near, far)


def finish_kernel(parts, count_inner, inner, *refs):
    count = len(refs) - len(parts)
    here = [ref for ref in refs[:count_inner]]
    outer = [ref for ref in refs[count_inner:count]]

    def total(sources, cols):
        found = None
        for source in sources:
            term = source[0, :, cols] if len(source.shape) == 3 else source[:, cols]
            term = term.astype(jnp.float32)
            found = term if found is None else found + term
        return found

    column = 0
    for (planes, across, turn), out in zip(parts, refs[count:]):
        for c in range(planes):
            for at, size in chunks(across, 256):
                cols = slice(column + at, column + at + size)
                value = jnp.where(inner[0] == 1, total(here, cols), total(outer, cols))
                if turn:
                    out[at : at + size, :] = value.T
                else:
                    out[c, :, at : at + size] = value
            column += across


def spread_kernel(parts, total, *outs):
    column = 0
    for (planes, across, turn), out in zip(parts, outs):
        for c in range(planes):
            for at, size in chunks(across, 256):
                value = total[:, column + at : column + at + size].astype(jnp.float32)
                if turn:
                    out[at : at + size, :] = value.T
                else:
                    out[c, :, at : at + size] = value
            column += across


def spread(total, parts):
    piece = total.shape[0]
    return pl.pallas_call(
        functools.partial(spread_kernel, parts),
        name="spread",
        out_shape=[
            like((across, piece) if turn else (planes, piece, across), jnp.float32)
            for planes, across, turn in parts
        ],
        in_specs=in_vmem(1),
        out_specs=in_vmem(len(parts)),
        compiler_params=limit(6),
    )(total)


def finish(inner, here, outer, parts):
    piece = here[0].shape[-2]
    return pl.pallas_call(
        functools.partial(finish_kernel, parts, len(here)),
        name="finish",
        out_shape=[
            like((across, piece) if turn else (planes, piece, across), jnp.float32)
            for planes, across, turn in parts
        ],
        in_specs=in_smem() + in_vmem(len(here) + len(outer)),
        out_specs=in_vmem(len(parts)),
        compiler_params=limit(8),
    )(inner, *here, *outer)


def flips(size, bit):
    return [(i, i ^ bit) for i in range(size)]


def after(value, *earlier):
    return lax.optimization_barrier((value, *earlier))[0]


def over_tensor(values, bit):
    return lax.ppermute(values, "tensor", flips(4, bit))


def gather_near(own):
    return own, over_tensor(own, 1), over_tensor(own, 2)


def gather_far(own, from_x, from_y):
    half = own.shape[0] // 2
    low = over_tensor(from_y[:half], 1)
    high = over_tensor(from_x[half:], 2)
    return [own, from_x, from_y, low, high]


def scatter_far(keep, to_x, to_y, far_low, far_high):
    return keep, *relay(to_x, to_y, over_tensor(far_low, 1), over_tensor(far_high, 2))


def scatter_near(keep, to_x, to_y):
    return keep, over_tensor(to_x, 1), over_tensor(to_y, 2)


def over_cores(values):
    return lax.ppermute(values, "dp", flips(8, 1))


def to_inner(values):
    return lax.ppermute(values, "dp", [(0, 2), (1, 3), (6, 4), (7, 5)])


def to_outer(values):
    return lax.ppermute(values, "dp", [(2, 0), (3, 1), (4, 6), (5, 7)])


def over_middle(values):
    return lax.ppermute(values, "dp", [(2, 4), (3, 5), (4, 2), (5, 3)])


class Weight:
    def __init__(self, places, groups):
        self.which_theirs, self.which_mine = places[:2]
        self.groups = groups

    def sibling_part(self):
        self.sibling_sum = weight_pieces(self.which_theirs, 0, 4, self.groups)
        self.theirs = over_cores(self.sibling_sum)

    def scatter(self, *earlier):
        self.chip_sum = self.own_part(0, 4, *earlier)
        return lax.psum_scatter(
            self.chip_sum,
            "dp",
            scatter_dimension=0,
            axis_index_groups=[[0, 2, 4, 6], [1, 3, 5, 7]],
        )

    def own_part(self, base, count, *earlier):
        more = after(self.theirs, *earlier) if earlier else self.theirs
        return weight_pieces(self.which_mine, base, count, self.groups, more, base)


def sum_flips(values, *steps):
    for axis, size, bit in steps:
        values = values + lax.ppermute(values, axis, flips(size, bit))
    return values


def per_device_square(
    tokens, gain_attn, gain_mlp, w_qkv, w_out, w_gate_up, w_down, cotangent, segment_ids, valid_mask
):
    rows = tokens.shape[0]
    length = segment_ids.shape[0]
    low = jnp.bfloat16
    me = lax.axis_index("tensor")
    order = [me, me ^ 1, me ^ 2, me ^ 3]
    rows_at = jnp.stack([at * rows for at in order] + [order[3] * rows + rows // 2]).astype(jnp.int32)
    index = lax.axis_index("dp")
    place, core = index // 2, index % 2
    line_order = jnp.where(place < 2, jnp.array([3, 2, 0, 1]), jnp.array([0, 1, 3, 2]))
    places = (
        (2 * line_order + 1 - core).astype(jnp.int32),
        (2 * line_order + core).astype(jnp.int32),
        ((place == 1) | (place == 2)).astype(jnp.int32).reshape(1),
    )
    in_order = (
        (2 * jnp.arange(4) + 1 - core).astype(jnp.int32),
        (2 * jnp.arange(4) + core).astype(jnp.int32),
    )
    gain_one = gain_attn[None, :]
    gain_two = gain_mlp[None, :]

    tokens = after(tokens, rows_at, *places, *in_order)
    normed = norm(tokens, gain_one)
    near = gather_near(normed)
    cosine, sine, seg_col, valid_col = prepare(
        segment_ids.astype(jnp.float32)[None, :],
        valid_mask.astype(jnp.float32)[None, :],
    )
    near = (near[0], near[1], after(near[2], cosine))
    blocks = gather_far(*near)
    cot_near = gather_near(after(cotangent, *blocks))
    normed_all, queries, keys, values = project(rows_at, blocks, w_qkv, cosine, sine)
    *sent, probs, mixed = attend_square(
        rows_at,
        after(queries, *cot_near),
        keys,
        values,
        w_out,
        segment_ids.astype(jnp.float32)[None, :],
        seg_col,
        valid_col,
    )
    keep, to_x, to_y = scatter_far(*sent)
    cot_blocks = gather_far(*(after(part, to_x) for part in cot_near))
    got = scatter_near(keep, to_x, to_y)
    d_hidden, cot_all = back_through_down(cot_blocks, w_down)
    middle, normed_two = make_middle(tokens, after(got[0], cot_all), *got[1:], gain_two)

    blocks = gather_far(*gather_near(normed_two))
    normed_two_all, hidden, d_gate_up = mlp(blocks, d_hidden, w_gate_up)
    down = Weight(in_order, [([cot_all], [hidden])])
    gate = Weight(in_order, [([normed_two_all], [d_gate_up])])
    down.sibling_part()
    gate.groups = [([after(normed_two_all, down.sibling_sum)], [d_gate_up])]
    gate.sibling_part()
    down_total = down.scatter(gate.sibling_sum)
    gate_total = gate.scatter(down.chip_sum)
    sent = mlp_back(after(d_gate_up, gate.chip_sum), w_gate_up)
    got = scatter_near(*scatter_far(*sent))
    d_middle, gain_two_part, d_middle_low = norm_back(
        cotangent, *got, middle, gain_two, True
    )
    blocks = gather_far(*gather_near(d_middle_low))

    d_middle_all, d_project = attend_back_square(
        rows_at, blocks, w_out, probs, queries, keys, values, cosine, sine
    )
    late = Weight(places, [([normed_all], [d_project]), ([d_middle_all], [mixed])])
    late.sibling_part()
    sent = project_back(rows_at, after(d_project, late.sibling_sum), w_qkv)
    keep, to_x, to_y = scatter_far(*sent)
    late_far = [late.own_part(0, 1, *sent)]
    late_far += [late.own_part(1, 1, late_far[0])]
    late_arrived = [to_inner(part) for part in late_far]
    late_near = [late.own_part(2, 1, late_far[1])]
    late_near += [late.own_part(3, 1, late_near[0])]
    late_near_arrived = to_inner(late_near[1])
    got = scatter_near(keep, after(to_x, late_near[1]), to_y)
    sent = through_down(after(hidden, late_near[1]), w_down)
    d_inputs, gain_one_part = norm_back(
        d_middle, after(got[0], *sent), *got[1:], tokens, gain_one, False
    )
    keep, to_x, to_y = scatter_far(*(after(part, d_inputs) for part in sent))
    gain_parts = sum_flips(
        jnp.concatenate([gain_one_part, gain_two_part], axis=0),
        ("dp", 8, 1),
        ("tensor", 4, 1),
        ("tensor", 4, 2),
    )
    keep, got_x, got_y = scatter_near(keep, to_x, to_y)
    output = (middle + keep + got_x.astype(jnp.float32) + got_y.astype(jnp.float32)).astype(low)
    late_far[0] = after(late_far[0], output, gain_parts)
    late_outer, late_own = join(late_far, late_arrived)
    late_outer, late_own = over_middle(late_outer), over_middle(late_own)
    grad_gains = sum_flips(after(gain_parts, output), ("dp", 8, 2), ("dp", 8, 4))
    units, wide = w_down.shape[0], w_qkv.shape[2]
    late_given = to_outer(hand(after(late_near[0], gate_total, down_total), late_outer))
    grad_qkv, grad_out = finish(
        places[2],
        [late_near[1], late_near_arrived, late_own],
        [late_near[0], late_given],
        [(3, wide, False), (1, wide, True)],
    )
    (grad_down,) = spread(down_total, [(1, units, True)])
    (grad_gate_up,) = spread(gate_total, [(2, units, False)])
    return (
        output,
        d_inputs,
        grad_gains[0],
        grad_gains[1],
        grad_qkv,
        grad_out,
        grad_gate_up,
        grad_down,
    )


def solution(mesh):
    placed = (
        P(("dp", "tensor"), None),
        P(),
        P(),
        P(None, None, "tensor"),
        P("tensor", None),
        P(None, None, "tensor"),
        P("tensor", None),
        P(("dp", "tensor"), None),
        P("dp"),
        P("dp"),
    )
    square = mesh.shape["tensor"] == 4 and mesh.shape["dp"] == 8
    return jax.shard_map(
        per_device_square if square else per_device,
        mesh=mesh,
        in_specs=placed,
        out_specs=(
            P(("dp", "tensor"), None),
            P(("dp", "tensor"), None),
            P(),
            P(),
            P(None, "dp", "tensor"),
            P("tensor", "dp"),
            P(None, "dp", "tensor"),
            P("tensor", "dp"),
        ),
        check_vma=False,
    )
```

```python
import functools
import math

import jax
import jax.numpy as jnp
from jax import lax
from jax.experimental import pallas as pl
from jax.experimental.pallas import tpu as pltpu
from jax.sharding import PartitionSpec as P

HD = 128


EPS = 1e-06
THETA = 10000.0


def rope_tables(places):
    positions = places.astype(jnp.float32)
    freqs = THETA ** (-(jnp.arange(HD // 2).astype(jnp.float32) * 2.0 / HD))
    angles = positions[:, None] * freqs[None, :]
    return (jnp.cos(angles), jnp.sin(angles))


def rotate(values, cosine, sine):
    half = values.shape[-1] // 2
    first = values[..., :half]
    second = values[..., half:]
    cosine = cosine[:, None, :]
    sine = sine[:, None, :]
    return jnp.concatenate(
        [first * cosine - second * sine, second * cosine + first * sine], axis=-1
    )


def block_scores(q_block, keys_rot, start, segments, valid):
    block_rows = q_block.shape[0]
    length = keys_rot.shape[0]
    key_pos = jnp.arange(length)
    row_pos = start + jnp.arange(block_rows)
    row_seg = lax.dynamic_slice_in_dim(segments, start, block_rows, 0)
    scores = jnp.einsum(
        "qhd,khd->hqk", q_block, keys_rot, preferred_element_type=jnp.float32
    ) * HD ** (-0.5)
    allowed = (
        (key_pos[None, :] <= row_pos[:, None])
        & (row_seg[:, None] == segments[None, :])
        & ((valid[None, :] == 1) | (key_pos[None, :] == row_pos[:, None]))
    )
    return jnp.where(allowed[None], scores, -1e30)


def attend(queries, keys_rot, values, segments, valid):
    length = queries.shape[0]
    block_rows = min(512, length)
    count = length // block_rows

    def one_block(index):
        start = index * block_rows
        q_block = lax.dynamic_slice_in_dim(queries, start, block_rows, 0)
        scores = block_scores(q_block, keys_rot, start, segments, valid)
        top = jnp.max(scores, axis=-1, keepdims=True)
        expo = jnp.exp(scores - top)
        total = jnp.sum(expo, axis=-1, keepdims=True)
        probs = (expo / total).astype(jnp.bfloat16)
        result = jnp.einsum("hqk,khd->qhd", probs, values, preferred_element_type=jnp.float32)
        return (result, top[..., 0] + jnp.log(total[..., 0]))

    blocks, log_sums = lax.map(one_block, jnp.arange(count))
    return (blocks.reshape(length, -1), log_sums)


def attend_back(queries, keys_rot, values, d_mixed, log_sums, segments, valid):
    length = queries.shape[0]
    block_rows = min(512, length)
    count = length // block_rows
    scale = HD ** (-0.5)

    def one_block(carry, index):
        d_keys, d_values = carry
        start = index * block_rows
        q_block = lax.dynamic_slice_in_dim(queries, start, block_rows, 0)
        d_block = lax.dynamic_slice_in_dim(d_mixed, start, block_rows, 0)
        scores = block_scores(q_block, keys_rot, start, segments, valid)
        probs = jnp.exp(scores - log_sums[index][..., None])
        d_values = d_values + jnp.einsum(
            "hqk,qhd->khd", probs.astype(jnp.bfloat16), d_block, preferred_element_type=jnp.float32
        )
        d_probs = jnp.einsum("qhd,khd->hqk", d_block, values, preferred_element_type=jnp.float32)
        delta = jnp.sum(d_probs * probs, axis=-1, keepdims=True)
        d_scores = (probs * (d_probs - delta)).astype(jnp.bfloat16)
        d_query = scale * jnp.einsum(
            "hqk,khd->qhd", d_scores, keys_rot, preferred_element_type=jnp.float32
        )
        d_keys = d_keys + scale * jnp.einsum(
            "hqk,qhd->khd", d_scores, q_block, preferred_element_type=jnp.float32
        )
        return ((d_keys, d_values), d_query)

    empty = jnp.zeros(keys_rot.shape, jnp.float32)
    (d_keys, d_values), d_queries = lax.scan(one_block, (empty, empty), jnp.arange(count))
    return (d_queries.reshape(queries.shape), d_keys, d_values)


def per_device(
    tokens, gain_attn, gain_mlp, w_qkv, w_out, w_gate_up, w_down, cotangent, segment_ids, valid_mask
):
    length = segment_ids.shape[0]
    heads_here = w_qkv.shape[2] // HD
    shape3 = (length, heads_here, HD)
    incoming = tokens.astype(jnp.float32)
    gain_one = gain_attn.astype(jnp.float32)
    gain_two = gain_mlp.astype(jnp.float32)
    cosine, sine = rope_tables(jnp.arange(length))
    inv_one = lax.rsqrt(jnp.mean(incoming * incoming, axis=-1, keepdims=True) + EPS)
    normed = (incoming * inv_one * gain_one).astype(jnp.bfloat16)
    normed_all = lax.all_gather(normed, "tensor", axis=0, tiled=True)
    project = jnp.einsum("td,cde->cte", normed_all, w_qkv, preferred_element_type=jnp.float32)
    queries = rotate(project[0].reshape(shape3), cosine, sine).astype(jnp.bfloat16)
    keys_rot = rotate(project[1].reshape(shape3), cosine, sine).astype(jnp.bfloat16)
    values = project[2].reshape(shape3).astype(jnp.bfloat16)
    mixed, log_sums = attend(queries, keys_rot, values, segment_ids, valid_mask)
    mixed = mixed.astype(jnp.bfloat16)
    middle = incoming + lax.psum_scatter(
        jnp.dot(mixed, w_out, preferred_element_type=jnp.float32).astype(jnp.bfloat16),
        "tensor",
        scatter_dimension=0,
        tiled=True,
    ).astype(jnp.float32)
    inv_two = lax.rsqrt(jnp.mean(middle * middle, axis=-1, keepdims=True) + EPS)
    normed_two = (middle * inv_two * gain_two).astype(jnp.bfloat16)
    normed_two_all = lax.all_gather(normed_two, "tensor", axis=0, tiled=True)
    gate = jnp.dot(normed_two_all, w_gate_up[0], preferred_element_type=jnp.float32)
    upper = jnp.dot(normed_two_all, w_gate_up[1], preferred_element_type=jnp.float32)
    sigma = jax.nn.sigmoid(gate)
    hidden = (gate * sigma * upper).astype(jnp.bfloat16)
    result = middle + lax.psum_scatter(
        jnp.dot(hidden, w_down, preferred_element_type=jnp.float32).astype(jnp.bfloat16),
        "tensor",
        scatter_dimension=0,
        tiled=True,
    ).astype(jnp.float32)
    output = result.astype(jnp.bfloat16)
    cot_all = lax.all_gather(cotangent, "tensor", axis=0, tiled=True)
    d_hidden = jnp.einsum("td,fd->tf", cot_all, w_down, preferred_element_type=jnp.float32)
    grad_down = jnp.einsum("tf,td->fd", hidden, cot_all, preferred_element_type=jnp.float32)
    d_upper = (d_hidden * gate * sigma).astype(jnp.bfloat16)
    d_gate = (d_hidden * upper * sigma * (1.0 + gate * (1.0 - sigma))).astype(jnp.bfloat16)
    grad_gate_up = jnp.stack(
        [
            jnp.einsum("td,tf->df", normed_two_all, d_gate, preferred_element_type=jnp.float32),
            jnp.einsum("td,tf->df", normed_two_all, d_upper, preferred_element_type=jnp.float32),
        ]
    )
    d_normed_two = lax.psum_scatter(
        (
            jnp.einsum("tf,df->td", d_gate, w_gate_up[0], preferred_element_type=jnp.float32)
            + jnp.einsum("tf,df->td", d_upper, w_gate_up[1], preferred_element_type=jnp.float32)
        ).astype(jnp.bfloat16),
        "tensor",
        scatter_dimension=0,
        tiled=True,
    ).astype(jnp.float32)
    scaled_two = gain_two * d_normed_two
    d_middle = (
        cotangent.astype(jnp.float32)
        + inv_two * scaled_two
        - middle * inv_two**3 * jnp.mean(scaled_two * middle, axis=-1, keepdims=True)
    )
    grad_gain_two = jnp.sum(d_normed_two * middle * inv_two, axis=0)
    d_middle_all = lax.all_gather(d_middle.astype(jnp.bfloat16), "tensor", axis=0, tiled=True)
    d_mixed = jnp.einsum(
        "td,ed->te", d_middle_all, w_out, preferred_element_type=jnp.float32
    ).astype(jnp.bfloat16)
    grad_out = jnp.einsum("te,td->ed", mixed, d_middle_all, preferred_element_type=jnp.float32)
    d_queries, d_keys, d_values = attend_back(
        queries, keys_rot, values, d_mixed.reshape(shape3), log_sums, segment_ids, valid_mask
    )
    d_project = jnp.stack(
        [
            rotate(d_queries, cosine, -sine).reshape(length, -1),
            rotate(d_keys, cosine, -sine).reshape(length, -1),
            d_values.reshape(length, -1),
        ]
    ).astype(jnp.bfloat16)
    grad_qkv = jnp.einsum("td,cte->cde", normed_all, d_project, preferred_element_type=jnp.float32)
    d_normed = lax.psum_scatter(
        jnp.einsum("cte,cde->td", d_project, w_qkv, preferred_element_type=jnp.float32).astype(
            jnp.bfloat16
        ),
        "tensor",
        scatter_dimension=0,
        tiled=True,
    ).astype(jnp.float32)
    scaled_one = gain_one * d_normed
    d_inputs = (
        d_middle
        + inv_one * scaled_one
        - incoming * inv_one**3 * jnp.mean(scaled_one * incoming, axis=-1, keepdims=True)
    )
    grad_gain_one = jnp.sum(d_normed * incoming * inv_one, axis=0)
    grad_gain_one, grad_gain_two = lax.psum((grad_gain_one, grad_gain_two), ("dp", "tensor"))
    grad_qkv, grad_out, grad_gate_up, grad_down = (
        lax.psum_scatter(
            grad_qkv.astype(jnp.bfloat16), "dp", scatter_dimension=1, tiled=True
        ).astype(jnp.float32),
        lax.psum_scatter(
            grad_out.astype(jnp.bfloat16), "dp", scatter_dimension=1, tiled=True
        ).astype(jnp.float32),
        lax.psum_scatter(
            grad_gate_up.astype(jnp.bfloat16), "dp", scatter_dimension=1, tiled=True
        ).astype(jnp.float32),
        lax.psum_scatter(
            grad_down.astype(jnp.bfloat16), "dp", scatter_dimension=1, tiled=True
        ).astype(jnp.float32),
    )
    return (
        output,
        d_inputs,
        grad_gain_one,
        grad_gain_two,
        grad_qkv,
        grad_out,
        grad_gate_up,
        grad_down,
    )


NT = (((1,), (1,)), ((), ()))
TN = (((0,), (0,)), ((), ()))
MEGA = 1024 * 1024


def chunks(total, step):
    return [(at, min(step, total - at)) for at in range(0, total, step)]


def dot(left, right, dims=None):
    if dims is None:
        return jnp.dot(left, right, preferred_element_type=jnp.float32)
    return lax.dot_general(left, right, dims, preferred_element_type=jnp.float32)


def in_vmem(count):
    return [pl.BlockSpec(memory_space=pltpu.VMEM)] * count


def in_smem():
    return [pl.BlockSpec(memory_space=pltpu.SMEM)]


def like(shape, kind=jnp.bfloat16):
    return jax.ShapeDtypeStruct(shape, kind)


def limit(megabytes):
    return pltpu.CompilerParams(vmem_limit_bytes=megabytes * MEGA)


def starts_of(blocks):
    at, starts = 0, []
    for block in blocks:
        starts.append((at, block.shape[0]))
        at += block.shape[0]
    return starts


def send_shapes(rows, width):
    half = rows // 2
    return [
        like((rows, width), jnp.float32),
        like((rows, width)),
        like((rows, width)),
        like((half, width)),
        like((half, width)),
    ]


def store_parts(part, targets, cols):
    for (start, rows), target in zip(starts_of(targets), targets):
        target[:, cols] = part[start : start + rows].astype(target.dtype)


def norm_kernel(tokens, gain, normed):
    wide = tokens[...].astype(jnp.float32)
    inverse = lax.rsqrt(jnp.mean(wide * wide, axis=-1, keepdims=True) + EPS)
    normed[...] = (wide * inverse * gain[...].astype(jnp.float32)).astype(jnp.bfloat16)


def norm(tokens, gain):
    return pl.pallas_call(
        norm_kernel,
        name="norm",
        out_shape=like(tokens.shape),
        in_specs=in_vmem(2),
        out_specs=in_vmem(1)[0],
        compiler_params=limit(4),
    )(tokens, gain)


def relay_kernel(to_x, to_y, via_x, via_y, next_x, next_y):
    half = via_x.shape[0]
    next_x[:half] = to_x[:half]
    next_x[half:] = (
        to_x[half:].astype(jnp.float32) + via_y[...].astype(jnp.float32)
    ).astype(jnp.bfloat16)
    next_y[:half] = (
        to_y[:half].astype(jnp.float32) + via_x[...].astype(jnp.float32)
    ).astype(jnp.bfloat16)
    next_y[half:] = to_y[half:]


def relay(to_x, to_y, via_x, via_y):
    return pl.pallas_call(
        relay_kernel,
        name="relay",
        out_shape=[like(to_x.shape), like(to_y.shape)],
        in_specs=in_vmem(4),
        out_specs=in_vmem(2),
        compiler_params=limit(4),
    )(to_x, to_y, via_x, via_y)


def middle_kernel(tokens, keep, got_x, got_y, gain, middle, normed):
    total = (
        tokens[...].astype(jnp.float32)
        + keep[...]
        + got_x[...].astype(jnp.float32)
        + got_y[...].astype(jnp.float32)
    )
    middle[...] = total
    inverse = lax.rsqrt(jnp.mean(total * total, axis=-1, keepdims=True) + EPS)
    normed[...] = (total * inverse * gain[...].astype(jnp.float32)).astype(jnp.bfloat16)


def make_middle(tokens, keep, got_x, got_y, gain):
    return pl.pallas_call(
        middle_kernel,
        name="make_middle",
        out_shape=[like(keep.shape, jnp.float32), like(keep.shape)],
        in_specs=in_vmem(5),
        out_specs=in_vmem(2),
        compiler_params=limit(6),
    )(tokens, keep, got_x, got_y, gain)


def norm_back_kernel(base, keep, got_x, got_y, source, gain, *outs):
    d_normed = keep[...] + got_x[...].astype(jnp.float32) + got_y[...].astype(jnp.float32)
    wide = source[...].astype(jnp.float32)
    inverse = lax.rsqrt(jnp.mean(wide * wide, axis=-1, keepdims=True) + EPS)
    scaled = gain[...].astype(jnp.float32) * d_normed
    slope = jnp.mean(scaled * wide, axis=-1, keepdims=True) * inverse * inverse * inverse
    total = base[...].astype(jnp.float32) + inverse * scaled - wide * slope
    outs[0][...] = total
    outs[1][...] = jnp.sum(d_normed * wide * inverse, axis=0, keepdims=True)
    if len(outs) == 3:
        outs[2][...] = total.astype(jnp.bfloat16)


def norm_back(base, keep, got_x, got_y, source, gain, low):
    return pl.pallas_call(
        norm_back_kernel,
        name="norm_back",
        out_shape=[like(keep.shape, jnp.float32), like((1, keep.shape[1]), jnp.float32)]
        + [like(keep.shape)] * low,
        in_specs=in_vmem(6),
        out_specs=in_vmem(2 + low),
        compiler_params=limit(8),
    )(base, keep, got_x, got_y, source, gain)


def prepare_kernel(segments, valid, cosine, sine, seg_col, valid_col):
    length = cosine.shape[0]
    half = HD // 2
    place = lax.broadcasted_iota(jnp.int32, (length, HD), 0).astype(jnp.float32)
    lane = lax.broadcasted_iota(jnp.int32, (length, HD), 1)
    step = jnp.where(lane < half, lane, lane - half).astype(jnp.float32)
    angle = place * jnp.exp(step * (-2.0 / HD * math.log(THETA)))
    cosine[...] = jnp.cos(angle)
    turn = jnp.sin(angle)
    sine[...] = jnp.where(lane < half, -turn, turn)
    seg_col[...] = jnp.broadcast_to(segments[...], (HD, length)).T
    valid_col[...] = jnp.broadcast_to(valid[...], (HD, length)).T


def prepare(segments, valid):
    length = segments.shape[1]
    return pl.pallas_call(
        prepare_kernel,
        name="prepare",
        out_shape=[like((length, HD), jnp.float32)] * 4,
        in_specs=in_vmem(2),
        out_specs=in_vmem(4),
        compiler_params=limit(6),
    )(segments, valid)


def project_kernel(
    rows_at, own, from_x, from_y, low, high, w_qkv, cosine, sine, normed, queries, keys, values
):
    for i, block in enumerate((own, from_x, from_y, low, high)):
        place = pl.multiple_of(rows_at[i], 64)
        normed[pl.ds(place, block.shape[0]), :] = block[...]
    for c, target in enumerate((queries, keys, values)):
        for at, size in chunks(target.shape[1], 2 * HD):
            part = dot(normed[...], w_qkv[c, :, at : at + size])
            for head in range(0, size, HD):
                piece = part[:, head : head + HD]
                if c < 2:
                    piece = piece * cosine[...] + pltpu.roll(piece, HD // 2, 1) * sine[...]
                target[:, at + head : at + head + HD] = piece.astype(jnp.bfloat16)


def project(rows_at, blocks, w_qkv, cosine, sine):
    rows, width = blocks[0].shape
    length = 4 * rows
    wide = w_qkv.shape[2]
    return pl.pallas_call(
        project_kernel,
        name="project",
        out_shape=[like((length, width))] + [like((length, wide))] * 3,
        in_specs=in_smem() + in_vmem(8),
        out_specs=in_vmem(4),
        compiler_params=limit(8),
    )(rows_at, *blocks, w_qkv, cosine, sine)


def attend_kernel(
    rows_at, queries, keys, values, w_out, seg_row, seg_col, valid_col,
    keep, to_x, to_y, far_low, far_high, probs, mixed, bias, joined,
):
    length, wide = queries.shape
    key_at = lax.broadcasted_iota(jnp.int32, (length, length), 0)
    query_at = lax.broadcasted_iota(jnp.int32, (length, length), 1)
    allowed = (
        (key_at <= query_at)
        & (seg_col[:, 0:1] == seg_row[...])
        & ((valid_col[:, 0:1] == 1.0) | (key_at == query_at))
    )
    bias[...] = jnp.where(allowed, 0.0, -1e30)
    for at in range(0, wide, HD):
        head = at // HD
        cols = slice(at, at + HD)
        for q_at, q_size in chunks(length, 256):
            seen = q_at + q_size
            scores = dot(keys[0:seen, cols], queries[q_at:seen, cols], NT)
            scores = scores * HD ** (-0.5) + bias[0:seen, q_at:seen]
            top = jnp.max(scores, axis=0, keepdims=True)
            expo = jnp.exp(scores - top)
            total = jnp.sum(expo, axis=0, keepdims=True)
            chance = (expo * (1.0 / total)).astype(jnp.bfloat16)
            probs[head, 0:seen, q_at:seen] = chance
            result = dot(values[0:seen, cols], chance, TN)
            joined[q_at:seen, cols] = result.T.astype(jnp.bfloat16)
    targets = [keep, to_x, to_y, far_low, far_high]
    for i, (start, size) in enumerate(starts_of(targets)):
        place = pl.multiple_of(rows_at[i], 64)
        mixed[start : start + size, :] = joined[pl.ds(place, size), :]
    for at, size in chunks(w_out.shape[1], 512):
        store_parts(dot(mixed[...], w_out[:, at : at + size]), targets, slice(at, at + size))


def attend_square(rows_at, queries, keys, values, w_out, seg_row, seg_col, valid_col):
    length, wide = queries.shape
    width = w_out.shape[1]
    heads = wide // HD
    return pl.pallas_call(
        attend_kernel,
        name="attend",
        out_shape=send_shapes(length // 4, width)
        + [like((heads, length, length)), like((length, wide))],
        in_specs=in_smem() + in_vmem(7),
        out_specs=in_vmem(7),
        scratch_shapes=[
            pltpu.VMEM((length, length), jnp.float32),
            pltpu.VMEM((length, wide), jnp.bfloat16),
        ],
        compiler_params=limit(8),
    )(rows_at, queries, keys, values, w_out, seg_row, seg_col, valid_col)


def d_hidden_kernel(own, from_x, from_y, low, high, w_down, d_hidden, cot_all):
    blocks = [own, from_x, from_y, low, high]
    for (start, size), block in zip(starts_of(blocks), blocks):
        cot_all[start : start + size, :] = block[...]
    for at, size in chunks(w_down.shape[0], 256):
        d_hidden[:, at : at + size] = dot(cot_all[...], w_down[at : at + size, :], NT)


def back_through_down(blocks, w_down):
    rows, width = blocks[0].shape
    length = 4 * rows
    units = w_down.shape[0]
    return pl.pallas_call(
        d_hidden_kernel,
        name="back_through_down",
        out_shape=[like((length, units), jnp.float32), like((length, width))],
        in_specs=in_vmem(6),
        out_specs=in_vmem(2),
        compiler_params=limit(6),
    )(*blocks, w_down)


def mlp_kernel(
    own, from_x, from_y, low, high, d_hidden, w_gate_up, normed, hidden, d_gate_up
):
    units = w_gate_up.shape[2]
    blocks = [own, from_x, from_y, low, high]
    for (start, size), block in zip(starts_of(blocks), blocks):
        normed[start : start + size, :] = block[...]
    for at, size in chunks(units, 256):
        here = slice(at, at + size)
        gate = dot(normed[...], w_gate_up[0, :, here])
        upper = dot(normed[...], w_gate_up[1, :, here])
        incoming = d_hidden[:, here]
        sigma = 1.0 / (1.0 + jnp.exp(-gate))
        silu = gate * sigma
        hidden[:, here] = (silu * upper).astype(jnp.bfloat16)
        d_gate_up[:, here] = (incoming * upper * sigma * (1.0 + gate * (1.0 - sigma))).astype(
            jnp.bfloat16
        )
        d_gate_up[:, units + at : units + at + size] = (incoming * silu).astype(jnp.bfloat16)


def mlp(blocks, d_hidden, w_gate_up):
    rows, width = blocks[0].shape
    length = 4 * rows
    units = w_gate_up.shape[2]
    return pl.pallas_call(
        mlp_kernel,
        name="mlp",
        out_shape=[like((length, width)), like((length, units)), like((length, 2 * units))],
        in_specs=in_vmem(7),
        out_specs=in_vmem(3),
        compiler_params=limit(8),
    )(*blocks, d_hidden, w_gate_up)


def mlp_back_kernel(d_gate_up, w_gate_up, *targets):
    units = w_gate_up.shape[2]
    for at, size in chunks(w_gate_up.shape[1], 256):
        part = dot(d_gate_up[:, 0:units], w_gate_up[0, at : at + size, :], NT) + dot(
            d_gate_up[:, units : 2 * units], w_gate_up[1, at : at + size, :], NT
        )
        store_parts(part, targets, slice(at, at + size))


def mlp_back(d_gate_up, w_gate_up):
    return pl.pallas_call(
        mlp_back_kernel,
        name="mlp_back",
        out_shape=send_shapes(d_gate_up.shape[0] // 4, w_gate_up.shape[1]),
        in_specs=in_vmem(2),
        out_specs=in_vmem(5),
        compiler_params=limit(6),
    )(d_gate_up, w_gate_up)


def down_kernel(hidden, w_down, *targets):
    for at, size in chunks(w_down.shape[1], 256):
        store_parts(dot(hidden[...], w_down[:, at : at + size]), targets, slice(at, at + size))


def through_down(hidden, w_down):
    return pl.pallas_call(
        down_kernel,
        name="through_down",
        out_shape=send_shapes(hidden.shape[0] // 4, w_down.shape[1]),
        in_specs=in_vmem(2),
        out_specs=in_vmem(5),
        compiler_params=limit(6),
    )(hidden, w_down)


def attend_back_kernel(
    rows_at, own, from_x, from_y, low, high, w_out, probs, queries, keys, values, cosine, sine,
    d_middle, d_project, d_mixed,
):
    length, wide = queries.shape
    blocks = [own, from_x, from_y, low, high]
    starts = starts_of(blocks)
    for (start, size), block in zip(starts, blocks):
        d_middle[start : start + size, :] = block[...]
    for at, size in chunks(wide, 256):
        part = dot(d_middle[...], w_out[at : at + size, :], NT).astype(jnp.bfloat16)
        for i, (start, rows) in enumerate(starts):
            place = pl.multiple_of(rows_at[i], 64)
            d_mixed[pl.ds(place, rows), at : at + size] = part[start : start + rows]
    scale = HD ** (-0.5)

    def back(turned, rows):
        return turned * cosine[rows, :] - pltpu.roll(turned, HD // 2, 1) * sine[rows, :]

    for at in range(0, wide, HD):
        head = at // HD
        cols = slice(at, at + HD)
        d_keys = d_values = None
        for q_at, q_size in reversed(chunks(length, 256)):
            seen = q_at + q_size
            rows = slice(q_at, seen)
            chance = probs[head, 0:seen, rows]
            d_out = d_mixed[rows, cols]
            d_chance = dot(values[0:seen, cols], d_out, NT)
            exact = chance.astype(jnp.float32)
            delta = jnp.sum(d_chance * exact, axis=0, keepdims=True)
            d_scores = (exact * (d_chance - delta)).astype(jnp.bfloat16)
            more_values = dot(chance, d_out)
            more_keys = dot(d_scores, queries[rows, cols])
            d_queries = dot(keys[0:seen, cols], d_scores, TN).T
            d_project[rows, cols] = back(d_queries * scale, rows).astype(jnp.bfloat16)
            if d_keys is None:
                d_keys, d_values = more_keys, more_values
            else:
                d_keys = jnp.concatenate([d_keys[:seen] + more_keys, d_keys[seen:]], axis=0)
                d_values = jnp.concatenate([d_values[:seen] + more_values, d_values[seen:]], axis=0)
        d_project[:, wide + at : wide + at + HD] = back(d_keys * scale, slice(0, length)).astype(
            jnp.bfloat16
        )
        d_project[:, 2 * wide + at : 2 * wide + at + HD] = d_values.astype(jnp.bfloat16)


def attend_back_square(rows_at, blocks, w_out, probs, queries, keys, values, cosine, sine):
    length, wide = queries.shape
    return pl.pallas_call(
        attend_back_kernel,
        name="attend_back",
        out_shape=[like((length, w_out.shape[1])), like((length, 3 * wide))],
        in_specs=in_smem() + in_vmem(12),
        out_specs=in_vmem(2),
        scratch_shapes=[pltpu.VMEM((length, wide), jnp.bfloat16)],
        compiler_params=limit(8),
    )(rows_at, *blocks, w_out, probs, queries, keys, values, cosine, sine)


def project_back_kernel(rows_at, d_project, w_qkv, *refs):
    targets, turned = refs[:5], refs[5]
    wide = w_qkv.shape[2]
    for i, (start, size) in enumerate(starts_of(targets)):
        place = pl.multiple_of(rows_at[i], 64)
        turned[start : start + size, :] = d_project[pl.ds(place, size), :]
    for at, size in chunks(w_qkv.shape[1], 256):
        part = sum(
            dot(turned[:, c * wide : (c + 1) * wide], w_qkv[c, at : at + size, :], NT)
            for c in range(3)
        )
        store_parts(part, targets, slice(at, at + size))


def project_back(rows_at, d_project, w_qkv):
    return pl.pallas_call(
        project_back_kernel,
        name="project_back",
        out_shape=send_shapes(d_project.shape[0] // 4, w_qkv.shape[1]),
        in_specs=in_smem() + in_vmem(2),
        out_specs=in_vmem(5),
        scratch_shapes=[pltpu.VMEM(d_project.shape, jnp.bfloat16)],
        compiler_params=limit(8),
    )(rows_at, d_project, w_qkv)


def weight_kernel(layout, base, spot, which, *refs):
    turned, out = refs[-1], refs[-2]
    more = refs[-3] if spot is not None else None
    count, piece, _ = out.shape
    for i in range(count):
        place = pl.multiple_of(which[base + i] * piece, piece)
        at_ref = column = 0
        for pairs in layout:
            splits = refs[at_ref : at_ref + pairs]
            others = refs[at_ref + pairs : at_ref + 2 * pairs]
            at_ref += 2 * pairs
            length, across = others[0].shape
            for j, split in enumerate(splits):
                turned[:, j * length : (j + 1) * length] = split[:, pl.ds(place, piece)].T
            for at, size in chunks(across, 256):
                part = None
                for j, other in enumerate(others):
                    term = dot(turned[:, j * length : (j + 1) * length], other[:, at : at + size])
                    part = term if part is None else part + term
                cols = slice(column + at, column + at + size)
                if more is not None:
                    part = part + more[spot + i, :, cols].astype(jnp.float32)
                out[i, :, cols] = part.astype(out.dtype)
            column += across


def weight_pieces(which, base, count, groups, more=None, spot=None):
    layout = [len(splits) for splits, _ in groups]
    refs = [ref for splits, others in groups for ref in (*splits, *others)]
    extra = [] if more is None else [more]
    length = groups[0][1][0].shape[0]
    across = sum(others[0].shape[1] for _, others in groups)
    piece = groups[0][0][0].shape[1] // 8
    return pl.pallas_call(
        functools.partial(weight_kernel, layout, base, spot),
        name="weight_pieces",
        out_shape=like((count, piece, across)),
        in_specs=in_smem() + in_vmem(len(refs) + len(extra)),
        out_specs=in_vmem(1)[0],
        scratch_shapes=[pltpu.VMEM((piece, max(layout) * length), jnp.bfloat16)],
        compiler_params=limit(16),
    )(which, *refs, *extra)


def add_kernel(here, there, out):
    for at, size in chunks(out.shape[2], 256):
        cols = slice(at, at + size)
        out[0, :, cols] = (
            here[0, :, cols].astype(jnp.float32) + there[0, :, cols].astype(jnp.float32)
        ).astype(jnp.bfloat16)


def add_pieces(here, there):
    return pl.pallas_call(
        add_kernel,
        name="add_pieces",
        out_shape=like(here.shape),
        in_specs=in_vmem(2),
        out_specs=in_vmem(1)[0],
        compiler_params=limit(6),
    )(here, there)


def spread_kernel(parts, count, *refs):
    sources, outs = refs[:count], refs[count:]
    column = 0
    for (planes, across, turn), out in zip(parts, outs):
        for c in range(planes):
            for at, size in chunks(across, 256):
                cols = slice(column + at, column + at + size)
                value = sum(source[0, :, cols].astype(jnp.float32) for source in sources)
                if turn:
                    out[at : at + size, :] = value.T
                else:
                    out[c, :, at : at + size] = value
            column += across


def spread(sources, parts):
    piece = sources[0].shape[1]
    return pl.pallas_call(
        functools.partial(spread_kernel, parts, len(sources)),
        name="spread",
        out_shape=[
            like((across, piece) if turn else (planes, piece, across), jnp.float32)
            for planes, across, turn in parts
        ],
        in_specs=in_vmem(len(sources)),
        out_specs=in_vmem(len(parts)),
        compiler_params=limit(8),
    )(*sources)


def gains_kernel(chip, *refs):
    sources, out, kept = refs[:4], refs[4], refs[5]
    for back, source in enumerate(sources):
        kept[lax.rem(chip[0] + 4 - back, 4)] = source[...]
    out[...] = (kept[0] + kept[1]) + (kept[2] + kept[3])


def sum_gains(chip, sources):
    return pl.pallas_call(
        gains_kernel,
        name="sum_gains",
        out_shape=like(sources[0].shape, jnp.float32),
        in_specs=in_smem() + in_vmem(4),
        out_specs=in_vmem(1)[0],
        scratch_shapes=[pltpu.VMEM((4, *sources[0].shape), jnp.float32)],
        compiler_params=limit(4),
    )(chip, *sources)


def flips(size, bit):
    return [(i, i ^ bit) for i in range(size)]


def after(value, *earlier):
    return lax.optimization_barrier((value, *earlier))[0]


def over_tensor(values, bit):
    return lax.ppermute(values, "tensor", flips(4, bit))


def gather_near(own):
    return own, over_tensor(own, 1), over_tensor(own, 2)


def gather_far(own, from_x, from_y):
    half = own.shape[0] // 2
    low = over_tensor(from_y[:half], 1)
    high = over_tensor(from_x[half:], 2)
    return [own, from_x, from_y, low, high]


def scatter_far(keep, to_x, to_y, far_low, far_high):
    return keep, *relay(to_x, to_y, over_tensor(far_low, 1), over_tensor(far_high, 2))


def scatter_near(keep, to_x, to_y):
    return keep, over_tensor(to_x, 1), over_tensor(to_y, 2)


def over_cores(values):
    return lax.ppermute(values, "dp", flips(8, 1))


def up_the_line(values):
    return lax.ppermute(values, "dp", [(i, (i + 2) % 8) for i in range(8)])


class Weight:
    def __init__(self, places, groups):
        self.which_theirs, self.which_mine = places[:2]
        self.groups = groups

    def sibling_part(self):
        self.sibling_sum = weight_pieces(self.which_theirs, 0, 4, self.groups)
        self.theirs = over_cores(self.sibling_sum)

    def scatter(self, *earlier):
        self.chip_sum = self.own_part(0, 4, *earlier)
        return lax.psum_scatter(
            self.chip_sum,
            "dp",
            scatter_dimension=0,
            axis_index_groups=[[0, 2, 4, 6], [1, 3, 5, 7]],
        )

    def own_part(self, base, count, *earlier):
        more = after(self.theirs, *earlier) if earlier else self.theirs
        return weight_pieces(self.which_mine, base, count, self.groups, more, base)


def sum_flips(values, *steps):
    for axis, size, bit in steps:
        values = values + lax.ppermute(values, axis, flips(size, bit))
    return values


def per_device_square(
    tokens, gain_attn, gain_mlp, w_qkv, w_out, w_gate_up, w_down, cotangent, segment_ids, valid_mask
):
    rows = tokens.shape[0]
    length = segment_ids.shape[0]
    low = jnp.bfloat16
    me = lax.axis_index("tensor")
    order = [me, me ^ 1, me ^ 2, me ^ 3]
    rows_at = jnp.stack([at * rows for at in order] + [order[3] * rows + rows // 2]).astype(jnp.int32)
    index = lax.axis_index("dp")
    place, core = index // 2, index % 2
    ring = (place + jnp.array([3, 2, 1, 0])) % 4
    in_turn = ((2 * ring + 1 - core).astype(jnp.int32), (2 * ring + core).astype(jnp.int32))
    in_order = (
        (2 * jnp.arange(4) + 1 - core).astype(jnp.int32),
        (2 * jnp.arange(4) + core).astype(jnp.int32),
    )
    chip = place.astype(jnp.int32).reshape(1)
    gain_one = gain_attn[None, :]
    gain_two = gain_mlp[None, :]

    tokens = after(tokens, rows_at, chip, *in_turn, *in_order)
    normed = norm(tokens, gain_one)
    near = gather_near(normed)
    cosine, sine, seg_col, valid_col = prepare(
        segment_ids.astype(jnp.float32)[None, :],
        valid_mask.astype(jnp.float32)[None, :],
    )
    near = (near[0], near[1], after(near[2], cosine))
    blocks = gather_far(*near)
    cot_near = gather_near(after(cotangent, *blocks))
    normed_all, queries, keys, values = project(rows_at, blocks, w_qkv, cosine, sine)
    *sent, probs, mixed = attend_square(
        rows_at,
        after(queries, *cot_near),
        keys,
        values,
        w_out,
        segment_ids.astype(jnp.float32)[None, :],
        seg_col,
        valid_col,
    )
    keep, to_x, to_y = scatter_far(*sent)
    cot_blocks = gather_far(*(after(part, to_x) for part in cot_near))
    got = scatter_near(keep, to_x, to_y)
    d_hidden, cot_all = back_through_down(cot_blocks, w_down)
    middle, normed_two = make_middle(tokens, after(got[0], cot_all), *got[1:], gain_two)

    blocks = gather_far(*gather_near(normed_two))
    normed_two_all, hidden, d_gate_up = mlp(blocks, d_hidden, w_gate_up)
    down = Weight(in_order, [([cot_all], [hidden])])
    gate = Weight(in_order, [([normed_two_all], [d_gate_up])])
    down.sibling_part()
    gate.groups = [([after(normed_two_all, down.sibling_sum)], [d_gate_up])]
    gate.sibling_part()
    down_total = down.scatter(gate.sibling_sum)
    gate_total = gate.scatter(down.chip_sum)
    sent = mlp_back(after(d_gate_up, gate.chip_sum), w_gate_up)
    got = scatter_near(*scatter_far(*sent))
    d_middle, gain_two_part, d_middle_low = norm_back(
        cotangent, *got, middle, gain_two, True
    )
    blocks = gather_far(*gather_near(d_middle_low))

    d_middle_all, d_project = attend_back_square(
        rows_at, blocks, w_out, probs, queries, keys, values, cosine, sine
    )
    late = Weight(in_turn, [([normed_all], [d_project]), ([d_middle_all], [mixed])])
    late.sibling_part()
    sent = project_back(rows_at, after(d_project, late.sibling_sum), w_qkv)
    keep, to_x, to_y = scatter_far(*sent)
    parts = [late.own_part(0, 1, *sent)]
    turn_one = up_the_line(parts[0])
    for turn in range(1, 4):
        parts.append(late.own_part(turn, 1, parts[-1]))
    got = scatter_near(keep, after(to_x, parts[3]), to_y)
    sent = through_down(after(hidden, parts[3]), w_down)
    d_inputs, gain_one_part = norm_back(
        d_middle, after(got[0], *sent), *got[1:], tokens, gain_one, False
    )
    keep, to_x, to_y = scatter_far(*(after(part, d_inputs) for part in sent))
    so_far = add_pieces(after(parts[1], to_x, to_y), turn_one)
    turn_two = up_the_line(so_far)
    gains = [
        sum_flips(
            after(jnp.concatenate([gain_one_part, gain_two_part], axis=0), so_far),
            ("dp", 8, 1),
            ("tensor", 4, 1),
            ("tensor", 4, 2),
        )
    ]
    gains.append(up_the_line(gains[-1]))
    keep, got_x, got_y = scatter_near(keep, to_x, to_y)
    output = (middle + keep + got_x.astype(jnp.float32) + got_y.astype(jnp.float32)).astype(low)
    so_far = add_pieces(after(parts[2], output, gains[-1]), turn_two)
    turn_three = up_the_line(so_far)
    for _ in range(2):
        gains.append(up_the_line(after(gains[-1], so_far)))
    units, wide = w_down.shape[0], w_qkv.shape[2]
    (grad_down,) = spread([after(down_total, so_far)[None]], [(1, units, True)])
    (grad_gate_up,) = spread([after(gate_total, grad_down)[None]], [(2, units, False)])
    grad_gains = sum_gains(chip, [gains[0], *(after(part, grad_gate_up) for part in gains[1:])])
    grad_qkv, grad_out = spread(
        [after(parts[3], grad_gate_up), turn_three], [(3, wide, False), (1, wide, True)]
    )
    return (
        output,
        d_inputs,
        grad_gains[0],
        grad_gains[1],
        grad_qkv,
        grad_out,
        grad_gate_up,
        grad_down,
    )


def solution(mesh):
    placed = (
        P(("dp", "tensor"), None),
        P(),
        P(),
        P(None, None, "tensor"),
        P("tensor", None),
        P(None, None, "tensor"),
        P("tensor", None),
        P(("dp", "tensor"), None),
        P("dp"),
        P("dp"),
    )
    square = mesh.shape["tensor"] == 4 and mesh.shape["dp"] == 8
    return jax.shard_map(
        per_device_square if square else per_device,
        mesh=mesh,
        in_specs=placed,
        out_specs=(
            P(("dp", "tensor"), None),
            P(("dp", "tensor"), None),
            P(),
            P(),
            P(None, "dp", "tensor"),
            P("tensor", "dp"),
            P(None, "dp", "tensor"),
            P("tensor", "dp"),
        ),
        check_vma=False,
    )
```

```python
import functools
import math

import jax
import jax.numpy as jnp
from jax import lax
from jax.experimental import pallas as pl
from jax.experimental.pallas import tpu as pltpu
from jax.sharding import PartitionSpec as P

HD = 128


EPS = 1e-06
THETA = 10000.0


def rope_tables(places):
    positions = places.astype(jnp.float32)
    freqs = THETA ** (-(jnp.arange(HD // 2).astype(jnp.float32) * 2.0 / HD))
    angles = positions[:, None] * freqs[None, :]
    return (jnp.cos(angles), jnp.sin(angles))


def rotate(values, cosine, sine):
    half = values.shape[-1] // 2
    first = values[..., :half]
    second = values[..., half:]
    cosine = cosine[:, None, :]
    sine = sine[:, None, :]
    return jnp.concatenate(
        [first * cosine - second * sine, second * cosine + first * sine], axis=-1
    )


def block_scores(q_block, keys_rot, start, segments, valid):
    block_rows = q_block.shape[0]
    length = keys_rot.shape[0]
    key_pos = jnp.arange(length)
    row_pos = start + jnp.arange(block_rows)
    row_seg = lax.dynamic_slice_in_dim(segments, start, block_rows, 0)
    scores = jnp.einsum(
        "qhd,khd->hqk", q_block, keys_rot, preferred_element_type=jnp.float32
    ) * HD ** (-0.5)
    allowed = (
        (key_pos[None, :] <= row_pos[:, None])
        & (row_seg[:, None] == segments[None, :])
        & ((valid[None, :] == 1) | (key_pos[None, :] == row_pos[:, None]))
    )
    return jnp.where(allowed[None], scores, -1e30)


def attend(queries, keys_rot, values, segments, valid):
    length = queries.shape[0]
    block_rows = min(512, length)
    count = length // block_rows

    def one_block(index):
        start = index * block_rows
        q_block = lax.dynamic_slice_in_dim(queries, start, block_rows, 0)
        scores = block_scores(q_block, keys_rot, start, segments, valid)
        top = jnp.max(scores, axis=-1, keepdims=True)
        expo = jnp.exp(scores - top)
        total = jnp.sum(expo, axis=-1, keepdims=True)
        probs = (expo / total).astype(jnp.bfloat16)
        result = jnp.einsum("hqk,khd->qhd", probs, values, preferred_element_type=jnp.float32)
        return (result, top[..., 0] + jnp.log(total[..., 0]))

    blocks, log_sums = lax.map(one_block, jnp.arange(count))
    return (blocks.reshape(length, -1), log_sums)


def attend_back(queries, keys_rot, values, d_mixed, log_sums, segments, valid):
    length = queries.shape[0]
    block_rows = min(512, length)
    count = length // block_rows
    scale = HD ** (-0.5)

    def one_block(carry, index):
        d_keys, d_values = carry
        start = index * block_rows
        q_block = lax.dynamic_slice_in_dim(queries, start, block_rows, 0)
        d_block = lax.dynamic_slice_in_dim(d_mixed, start, block_rows, 0)
        scores = block_scores(q_block, keys_rot, start, segments, valid)
        probs = jnp.exp(scores - log_sums[index][..., None])
        d_values = d_values + jnp.einsum(
            "hqk,qhd->khd", probs.astype(jnp.bfloat16), d_block, preferred_element_type=jnp.float32
        )
        d_probs = jnp.einsum("qhd,khd->hqk", d_block, values, preferred_element_type=jnp.float32)
        delta = jnp.sum(d_probs * probs, axis=-1, keepdims=True)
        d_scores = (probs * (d_probs - delta)).astype(jnp.bfloat16)
        d_query = scale * jnp.einsum(
            "hqk,khd->qhd", d_scores, keys_rot, preferred_element_type=jnp.float32
        )
        d_keys = d_keys + scale * jnp.einsum(
            "hqk,qhd->khd", d_scores, q_block, preferred_element_type=jnp.float32
        )
        return ((d_keys, d_values), d_query)

    empty = jnp.zeros(keys_rot.shape, jnp.float32)
    (d_keys, d_values), d_queries = lax.scan(one_block, (empty, empty), jnp.arange(count))
    return (d_queries.reshape(queries.shape), d_keys, d_values)


def per_device(
    tokens, gain_attn, gain_mlp, w_qkv, w_out, w_gate_up, w_down, cotangent, segment_ids, valid_mask
):
    length = segment_ids.shape[0]
    heads_here = w_qkv.shape[2] // HD
    shape3 = (length, heads_here, HD)
    incoming = tokens.astype(jnp.float32)
    gain_one = gain_attn.astype(jnp.float32)
    gain_two = gain_mlp.astype(jnp.float32)
    cosine, sine = rope_tables(jnp.arange(length))
    inv_one = lax.rsqrt(jnp.mean(incoming * incoming, axis=-1, keepdims=True) + EPS)
    normed = (incoming * inv_one * gain_one).astype(jnp.bfloat16)
    normed_all = lax.all_gather(normed, "tensor", axis=0, tiled=True)
    project = jnp.einsum("td,cde->cte", normed_all, w_qkv, preferred_element_type=jnp.float32)
    queries = rotate(project[0].reshape(shape3), cosine, sine).astype(jnp.bfloat16)
    keys_rot = rotate(project[1].reshape(shape3), cosine, sine).astype(jnp.bfloat16)
    values = project[2].reshape(shape3).astype(jnp.bfloat16)
    mixed, log_sums = attend(queries, keys_rot, values, segment_ids, valid_mask)
    mixed = mixed.astype(jnp.bfloat16)
    middle = incoming + lax.psum_scatter(
        jnp.dot(mixed, w_out, preferred_element_type=jnp.float32).astype(jnp.bfloat16),
        "tensor",
        scatter_dimension=0,
        tiled=True,
    ).astype(jnp.float32)
    inv_two = lax.rsqrt(jnp.mean(middle * middle, axis=-1, keepdims=True) + EPS)
    normed_two = (middle * inv_two * gain_two).astype(jnp.bfloat16)
    normed_two_all = lax.all_gather(normed_two, "tensor", axis=0, tiled=True)
    gate = jnp.dot(normed_two_all, w_gate_up[0], preferred_element_type=jnp.float32)
    upper = jnp.dot(normed_two_all, w_gate_up[1], preferred_element_type=jnp.float32)
    sigma = jax.nn.sigmoid(gate)
    hidden = (gate * sigma * upper).astype(jnp.bfloat16)
    result = middle + lax.psum_scatter(
        jnp.dot(hidden, w_down, preferred_element_type=jnp.float32).astype(jnp.bfloat16),
        "tensor",
        scatter_dimension=0,
        tiled=True,
    ).astype(jnp.float32)
    output = result.astype(jnp.bfloat16)
    cot_all = lax.all_gather(cotangent, "tensor", axis=0, tiled=True)
    d_hidden = jnp.einsum("td,fd->tf", cot_all, w_down, preferred_element_type=jnp.float32)
    grad_down = jnp.einsum("tf,td->fd", hidden, cot_all, preferred_element_type=jnp.float32)
    d_upper = (d_hidden * gate * sigma).astype(jnp.bfloat16)
    d_gate = (d_hidden * upper * sigma * (1.0 + gate * (1.0 - sigma))).astype(jnp.bfloat16)
    grad_gate_up = jnp.stack(
        [
            jnp.einsum("td,tf->df", normed_two_all, d_gate, preferred_element_type=jnp.float32),
            jnp.einsum("td,tf->df", normed_two_all, d_upper, preferred_element_type=jnp.float32),
        ]
    )
    d_normed_two = lax.psum_scatter(
        (
            jnp.einsum("tf,df->td", d_gate, w_gate_up[0], preferred_element_type=jnp.float32)
            + jnp.einsum("tf,df->td", d_upper, w_gate_up[1], preferred_element_type=jnp.float32)
        ).astype(jnp.bfloat16),
        "tensor",
        scatter_dimension=0,
        tiled=True,
    ).astype(jnp.float32)
    scaled_two = gain_two * d_normed_two
    d_middle = (
        cotangent.astype(jnp.float32)
        + inv_two * scaled_two
        - middle * inv_two**3 * jnp.mean(scaled_two * middle, axis=-1, keepdims=True)
    )
    grad_gain_two = jnp.sum(d_normed_two * middle * inv_two, axis=0)
    d_middle_all = lax.all_gather(d_middle.astype(jnp.bfloat16), "tensor", axis=0, tiled=True)
    d_mixed = jnp.einsum(
        "td,ed->te", d_middle_all, w_out, preferred_element_type=jnp.float32
    ).astype(jnp.bfloat16)
    grad_out = jnp.einsum("te,td->ed", mixed, d_middle_all, preferred_element_type=jnp.float32)
    d_queries, d_keys, d_values = attend_back(
        queries, keys_rot, values, d_mixed.reshape(shape3), log_sums, segment_ids, valid_mask
    )
    d_project = jnp.stack(
        [
            rotate(d_queries, cosine, -sine).reshape(length, -1),
            rotate(d_keys, cosine, -sine).reshape(length, -1),
            d_values.reshape(length, -1),
        ]
    ).astype(jnp.bfloat16)
    grad_qkv = jnp.einsum("td,cte->cde", normed_all, d_project, preferred_element_type=jnp.float32)
    d_normed = lax.psum_scatter(
        jnp.einsum("cte,cde->td", d_project, w_qkv, preferred_element_type=jnp.float32).astype(
            jnp.bfloat16
        ),
        "tensor",
        scatter_dimension=0,
        tiled=True,
    ).astype(jnp.float32)
    scaled_one = gain_one * d_normed
    d_inputs = (
        d_middle
        + inv_one * scaled_one
        - incoming * inv_one**3 * jnp.mean(scaled_one * incoming, axis=-1, keepdims=True)
    )
    grad_gain_one = jnp.sum(d_normed * incoming * inv_one, axis=0)
    grad_gain_one, grad_gain_two = lax.psum((grad_gain_one, grad_gain_two), ("dp", "tensor"))
    grad_qkv, grad_out, grad_gate_up, grad_down = (
        lax.psum_scatter(
            grad_qkv.astype(jnp.bfloat16), "dp", scatter_dimension=1, tiled=True
        ).astype(jnp.float32),
        lax.psum_scatter(
            grad_out.astype(jnp.bfloat16), "dp", scatter_dimension=1, tiled=True
        ).astype(jnp.float32),
        lax.psum_scatter(
            grad_gate_up.astype(jnp.bfloat16), "dp", scatter_dimension=1, tiled=True
        ).astype(jnp.float32),
        lax.psum_scatter(
            grad_down.astype(jnp.bfloat16), "dp", scatter_dimension=1, tiled=True
        ).astype(jnp.float32),
    )
    return (
        output,
        d_inputs,
        grad_gain_one,
        grad_gain_two,
        grad_qkv,
        grad_out,
        grad_gate_up,
        grad_down,
    )


NT = (((1,), (1,)), ((), ()))
TN = (((0,), (0,)), ((), ()))
MEGA = 1024 * 1024


def chunks(total, step):
    return [(at, min(step, total - at)) for at in range(0, total, step)]


def dot(left, right, dims=None):
    if dims is None:
        return jnp.dot(left, right, preferred_element_type=jnp.float32)
    return lax.dot_general(left, right, dims, preferred_element_type=jnp.float32)


def in_vmem(count):
    return [pl.BlockSpec(memory_space=pltpu.VMEM)] * count


def in_smem():
    return [pl.BlockSpec(memory_space=pltpu.SMEM)]


def like(shape, kind=jnp.bfloat16):
    return jax.ShapeDtypeStruct(shape, kind)


def limit(megabytes):
    return pltpu.CompilerParams(vmem_limit_bytes=megabytes * MEGA)


def starts_of(blocks):
    at, starts = 0, []
    for block in blocks:
        starts.append((at, block.shape[0]))
        at += block.shape[0]
    return starts


def send_shapes(rows, width):
    half = rows // 2
    return [
        like((rows, width), jnp.float32),
        like((rows, width)),
        like((rows, width)),
        like((half, width)),
        like((half, width)),
    ]


def store_parts(part, targets, cols):
    for (start, rows), target in zip(starts_of(targets), targets):
        target[:, cols] = part[start : start + rows].astype(target.dtype)


def norm_kernel(tokens, gain, normed):
    wide = tokens[...].astype(jnp.float32)
    inverse = lax.rsqrt(jnp.mean(wide * wide, axis=-1, keepdims=True) + EPS)
    normed[...] = (wide * inverse * gain[...].astype(jnp.float32)).astype(jnp.bfloat16)


def norm(tokens, gain):
    return pl.pallas_call(
        norm_kernel,
        name="norm",
        out_shape=like(tokens.shape),
        in_specs=in_vmem(2),
        out_specs=in_vmem(1)[0],
        compiler_params=limit(4),
    )(tokens, gain)


def relay_kernel(to_x, to_y, via_x, via_y, next_x, next_y):
    half = via_x.shape[0]
    next_x[:half] = to_x[:half]
    next_x[half:] = (
        to_x[half:].astype(jnp.float32) + via_y[...].astype(jnp.float32)
    ).astype(jnp.bfloat16)
    next_y[:half] = (
        to_y[:half].astype(jnp.float32) + via_x[...].astype(jnp.float32)
    ).astype(jnp.bfloat16)
    next_y[half:] = to_y[half:]


def relay(to_x, to_y, via_x, via_y):
    return pl.pallas_call(
        relay_kernel,
        name="relay",
        out_shape=[like(to_x.shape), like(to_y.shape)],
        in_specs=in_vmem(4),
        out_specs=in_vmem(2),
        compiler_params=limit(4),
    )(to_x, to_y, via_x, via_y)


def middle_kernel(tokens, keep, got_x, got_y, gain, middle, normed):
    total = (
        tokens[...].astype(jnp.float32)
        + keep[...]
        + got_x[...].astype(jnp.float32)
        + got_y[...].astype(jnp.float32)
    )
    middle[...] = total
    inverse = lax.rsqrt(jnp.mean(total * total, axis=-1, keepdims=True) + EPS)
    normed[...] = (total * inverse * gain[...].astype(jnp.float32)).astype(jnp.bfloat16)


def make_middle(tokens, keep, got_x, got_y, gain):
    return pl.pallas_call(
        middle_kernel,
        name="make_middle",
        out_shape=[like(keep.shape, jnp.float32), like(keep.shape)],
        in_specs=in_vmem(5),
        out_specs=in_vmem(2),
        compiler_params=limit(6),
    )(tokens, keep, got_x, got_y, gain)


def norm_back_kernel(base, keep, got_x, got_y, source, gain, *outs):
    d_normed = keep[...] + got_x[...].astype(jnp.float32) + got_y[...].astype(jnp.float32)
    wide = source[...].astype(jnp.float32)
    inverse = lax.rsqrt(jnp.mean(wide * wide, axis=-1, keepdims=True) + EPS)
    scaled = gain[...].astype(jnp.float32) * d_normed
    slope = jnp.mean(scaled * wide, axis=-1, keepdims=True) * inverse * inverse * inverse
    total = base[...].astype(jnp.float32) + inverse * scaled - wide * slope
    outs[0][...] = total
    outs[1][...] = jnp.sum(d_normed * wide * inverse, axis=0, keepdims=True)
    if len(outs) == 3:
        outs[2][...] = total.astype(jnp.bfloat16)


def norm_back(base, keep, got_x, got_y, source, gain, low):
    return pl.pallas_call(
        norm_back_kernel,
        name="norm_back",
        out_shape=[like(keep.shape, jnp.float32), like((1, keep.shape[1]), jnp.float32)]
        + [like(keep.shape)] * low,
        in_specs=in_vmem(6),
        out_specs=in_vmem(2 + low),
        compiler_params=limit(8),
    )(base, keep, got_x, got_y, source, gain)


def prepare_kernel(segments, valid, cosine, sine, seg_col, valid_col):
    length = cosine.shape[0]
    half = HD // 2
    place = lax.broadcasted_iota(jnp.int32, (length, HD), 0).astype(jnp.float32)
    lane = lax.broadcasted_iota(jnp.int32, (length, HD), 1)
    step = jnp.where(lane < half, lane, lane - half).astype(jnp.float32)
    angle = place * jnp.exp(step * (-2.0 / HD * math.log(THETA)))
    cosine[...] = jnp.cos(angle)
    turn = jnp.sin(angle)
    sine[...] = jnp.where(lane < half, -turn, turn)
    seg_col[...] = jnp.broadcast_to(segments[...], (HD, length)).T
    valid_col[...] = jnp.broadcast_to(valid[...], (HD, length)).T


def prepare(segments, valid):
    length = segments.shape[1]
    return pl.pallas_call(
        prepare_kernel,
        name="prepare",
        out_shape=[like((length, HD), jnp.float32)] * 4,
        in_specs=in_vmem(2),
        out_specs=in_vmem(4),
        compiler_params=limit(6),
    )(segments, valid)


def project_kernel(
    rows_at, own, from_x, from_y, low, high, w_qkv, cosine, sine, normed, queries, keys, values
):
    for i, block in enumerate((own, from_x, from_y, low, high)):
        place = pl.multiple_of(rows_at[i], 64)
        normed[pl.ds(place, block.shape[0]), :] = block[...]
    for c, target in enumerate((queries, keys, values)):
        for at, size in chunks(target.shape[1], 2 * HD):
            part = dot(normed[...], w_qkv[c, :, at : at + size])
            for head in range(0, size, HD):
                piece = part[:, head : head + HD]
                if c < 2:
                    piece = piece * cosine[...] + pltpu.roll(piece, HD // 2, 1) * sine[...]
                target[:, at + head : at + head + HD] = piece.astype(jnp.bfloat16)


def project(rows_at, blocks, w_qkv, cosine, sine):
    rows, width = blocks[0].shape
    length = 4 * rows
    wide = w_qkv.shape[2]
    return pl.pallas_call(
        project_kernel,
        name="project",
        out_shape=[like((length, width))] + [like((length, wide))] * 3,
        in_specs=in_smem() + in_vmem(8),
        out_specs=in_vmem(4),
        compiler_params=limit(8),
    )(rows_at, *blocks, w_qkv, cosine, sine)


def attend_kernel(
    rows_at, queries, keys, values, w_out, seg_row, seg_col, valid_col,
    keep, to_x, to_y, far_low, far_high, probs, mixed, bias, joined,
):
    length, wide = queries.shape
    key_at = lax.broadcasted_iota(jnp.int32, (length, length), 0)
    query_at = lax.broadcasted_iota(jnp.int32, (length, length), 1)
    allowed = (
        (key_at <= query_at)
        & (seg_col[:, 0:1] == seg_row[...])
        & ((valid_col[:, 0:1] == 1.0) | (key_at == query_at))
    )
    bias[...] = jnp.where(allowed, 0.0, -1e30)
    for at in range(0, wide, HD):
        head = at // HD
        cols = slice(at, at + HD)
        for q_at, q_size in chunks(length, 256):
            seen = q_at + q_size
            scores = dot(keys[0:seen, cols], queries[q_at:seen, cols], NT)
            scores = scores * HD ** (-0.5) + bias[0:seen, q_at:seen]
            top = jnp.max(scores, axis=0, keepdims=True)
            expo = jnp.exp(scores - top)
            total = jnp.sum(expo, axis=0, keepdims=True)
            chance = (expo * (1.0 / total)).astype(jnp.bfloat16)
            probs[head, 0:seen, q_at:seen] = chance
            result = dot(values[0:seen, cols], chance, TN)
            joined[q_at:seen, cols] = result.T.astype(jnp.bfloat16)
    targets = [keep, to_x, to_y, far_low, far_high]
    for i, (start, size) in enumerate(starts_of(targets)):
        place = pl.multiple_of(rows_at[i], 64)
        mixed[start : start + size, :] = joined[pl.ds(place, size), :]
    for at, size in chunks(w_out.shape[1], 512):
        store_parts(dot(mixed[...], w_out[:, at : at + size]), targets, slice(at, at + size))


def attend_square(rows_at, queries, keys, values, w_out, seg_row, seg_col, valid_col):
    length, wide = queries.shape
    width = w_out.shape[1]
    heads = wide // HD
    return pl.pallas_call(
        attend_kernel,
        name="attend",
        out_shape=send_shapes(length // 4, width)
        + [like((heads, length, length)), like((length, wide))],
        in_specs=in_smem() + in_vmem(7),
        out_specs=in_vmem(7),
        scratch_shapes=[
            pltpu.VMEM((length, length), jnp.float32),
            pltpu.VMEM((length, wide), jnp.bfloat16),
        ],
        compiler_params=limit(8),
    )(rows_at, queries, keys, values, w_out, seg_row, seg_col, valid_col)


def d_hidden_kernel(own, from_x, from_y, low, high, w_down, d_hidden, cot_all):
    blocks = [own, from_x, from_y, low, high]
    for (start, size), block in zip(starts_of(blocks), blocks):
        cot_all[start : start + size, :] = block[...]
    for at, size in chunks(w_down.shape[0], 256):
        d_hidden[:, at : at + size] = dot(cot_all[...], w_down[at : at + size, :], NT)


def back_through_down(blocks, w_down):
    rows, width = blocks[0].shape
    length = 4 * rows
    units = w_down.shape[0]
    return pl.pallas_call(
        d_hidden_kernel,
        name="back_through_down",
        out_shape=[like((length, units), jnp.float32), like((length, width))],
        in_specs=in_vmem(6),
        out_specs=in_vmem(2),
        compiler_params=limit(6),
    )(*blocks, w_down)


def mlp_kernel(
    own, from_x, from_y, low, high, d_hidden, w_gate_up, normed, hidden, d_gate_up
):
    units = w_gate_up.shape[2]
    blocks = [own, from_x, from_y, low, high]
    for (start, size), block in zip(starts_of(blocks), blocks):
        normed[start : start + size, :] = block[...]
    for at, size in chunks(units, 256):
        here = slice(at, at + size)
        gate = dot(normed[...], w_gate_up[0, :, here])
        upper = dot(normed[...], w_gate_up[1, :, here])
        incoming = d_hidden[:, here]
        sigma = 1.0 / (1.0 + jnp.exp(-gate))
        silu = gate * sigma
        hidden[:, here] = (silu * upper).astype(jnp.bfloat16)
        d_gate_up[:, here] = (incoming * upper * sigma * (1.0 + gate * (1.0 - sigma))).astype(
            jnp.bfloat16
        )
        d_gate_up[:, units + at : units + at + size] = (incoming * silu).astype(jnp.bfloat16)


def mlp(blocks, d_hidden, w_gate_up):
    rows, width = blocks[0].shape
    length = 4 * rows
    units = w_gate_up.shape[2]
    return pl.pallas_call(
        mlp_kernel,
        name="mlp",
        out_shape=[like((length, width)), like((length, units)), like((length, 2 * units))],
        in_specs=in_vmem(7),
        out_specs=in_vmem(3),
        compiler_params=limit(8),
    )(*blocks, d_hidden, w_gate_up)


def mlp_back_kernel(d_gate_up, w_gate_up, *targets):
    units = w_gate_up.shape[2]
    for at, size in chunks(w_gate_up.shape[1], 256):
        part = dot(d_gate_up[:, 0:units], w_gate_up[0, at : at + size, :], NT) + dot(
            d_gate_up[:, units : 2 * units], w_gate_up[1, at : at + size, :], NT
        )
        store_parts(part, targets, slice(at, at + size))


def mlp_back(d_gate_up, w_gate_up):
    return pl.pallas_call(
        mlp_back_kernel,
        name="mlp_back",
        out_shape=send_shapes(d_gate_up.shape[0] // 4, w_gate_up.shape[1]),
        in_specs=in_vmem(2),
        out_specs=in_vmem(5),
        compiler_params=limit(6),
    )(d_gate_up, w_gate_up)


def down_kernel(hidden, w_down, *targets):
    for at, size in chunks(w_down.shape[1], 256):
        store_parts(dot(hidden[...], w_down[:, at : at + size]), targets, slice(at, at + size))


def through_down(hidden, w_down):
    return pl.pallas_call(
        down_kernel,
        name="through_down",
        out_shape=send_shapes(hidden.shape[0] // 4, w_down.shape[1]),
        in_specs=in_vmem(2),
        out_specs=in_vmem(5),
        compiler_params=limit(6),
    )(hidden, w_down)


def attend_back_kernel(
    rows_at, own, from_x, from_y, low, high, w_out, probs, queries, keys, values, cosine, sine,
    d_middle, d_project, d_mixed,
):
    length, wide = queries.shape
    blocks = [own, from_x, from_y, low, high]
    starts = starts_of(blocks)
    for (start, size), block in zip(starts, blocks):
        d_middle[start : start + size, :] = block[...]
    for at, size in chunks(wide, 256):
        part = dot(d_middle[...], w_out[at : at + size, :], NT).astype(jnp.bfloat16)
        for i, (start, rows) in enumerate(starts):
            place = pl.multiple_of(rows_at[i], 64)
            d_mixed[pl.ds(place, rows), at : at + size] = part[start : start + rows]
    scale = HD ** (-0.5)

    def back(turned, rows):
        return turned * cosine[rows, :] - pltpu.roll(turned, HD // 2, 1) * sine[rows, :]

    for at in range(0, wide, HD):
        head = at // HD
        cols = slice(at, at + HD)
        d_keys = d_values = None
        for q_at, q_size in reversed(chunks(length, 256)):
            seen = q_at + q_size
            rows = slice(q_at, seen)
            chance = probs[head, 0:seen, rows]
            d_out = d_mixed[rows, cols]
            d_chance = dot(values[0:seen, cols], d_out, NT)
            exact = chance.astype(jnp.float32)
            delta = jnp.sum(d_chance * exact, axis=0, keepdims=True)
            d_scores = (exact * (d_chance - delta)).astype(jnp.bfloat16)
            more_values = dot(chance, d_out)
            more_keys = dot(d_scores, queries[rows, cols])
            d_queries = dot(keys[0:seen, cols], d_scores, TN).T
            d_project[rows, cols] = back(d_queries * scale, rows).astype(jnp.bfloat16)
            if d_keys is None:
                d_keys, d_values = more_keys, more_values
            else:
                d_keys = jnp.concatenate([d_keys[:seen] + more_keys, d_keys[seen:]], axis=0)
                d_values = jnp.concatenate([d_values[:seen] + more_values, d_values[seen:]], axis=0)
        d_project[:, wide + at : wide + at + HD] = back(d_keys * scale, slice(0, length)).astype(
            jnp.bfloat16
        )
        d_project[:, 2 * wide + at : 2 * wide + at + HD] = d_values.astype(jnp.bfloat16)


def attend_back_square(rows_at, blocks, w_out, probs, queries, keys, values, cosine, sine):
    length, wide = queries.shape
    return pl.pallas_call(
        attend_back_kernel,
        name="attend_back",
        out_shape=[like((length, w_out.shape[1])), like((length, 3 * wide))],
        in_specs=in_smem() + in_vmem(12),
        out_specs=in_vmem(2),
        scratch_shapes=[pltpu.VMEM((length, wide), jnp.bfloat16)],
        compiler_params=limit(8),
    )(rows_at, *blocks, w_out, probs, queries, keys, values, cosine, sine)


def project_back_kernel(rows_at, d_project, w_qkv, *refs):
    targets, turned = refs[:5], refs[5]
    wide = w_qkv.shape[2]
    for i, (start, size) in enumerate(starts_of(targets)):
        place = pl.multiple_of(rows_at[i], 64)
        turned[start : start + size, :] = d_project[pl.ds(place, size), :]
    for at, size in chunks(w_qkv.shape[1], 256):
        part = sum(
            dot(turned[:, c * wide : (c + 1) * wide], w_qkv[c, at : at + size, :], NT)
            for c in range(3)
        )
        store_parts(part, targets, slice(at, at + size))


def project_back(rows_at, d_project, w_qkv):
    return pl.pallas_call(
        project_back_kernel,
        name="project_back",
        out_shape=send_shapes(d_project.shape[0] // 4, w_qkv.shape[1]),
        in_specs=in_smem() + in_vmem(2),
        out_specs=in_vmem(5),
        scratch_shapes=[pltpu.VMEM(d_project.shape, jnp.bfloat16)],
        compiler_params=limit(8),
    )(rows_at, d_project, w_qkv)


def weight_kernel(layout, base, spot, which, *refs):
    turned, out = refs[-1], refs[-2]
    more = refs[-3] if spot is not None else None
    count, piece, _ = out.shape
    for i in range(count):
        place = pl.multiple_of(which[base + i] * piece, piece)
        at_ref = column = 0
        for pairs in layout:
            splits = refs[at_ref : at_ref + pairs]
            others = refs[at_ref + pairs : at_ref + 2 * pairs]
            at_ref += 2 * pairs
            length, across = others[0].shape
            for j, split in enumerate(splits):
                turned[:, j * length : (j + 1) * length] = split[:, pl.ds(place, piece)].T
            for at, size in chunks(across, 256):
                part = None
                for j, other in enumerate(others):
                    term = dot(turned[:, j * length : (j + 1) * length], other[:, at : at + size])
                    part = term if part is None else part + term
                cols = slice(column + at, column + at + size)
                if more is not None:
                    part = part + more[spot + i, :, cols].astype(jnp.float32)
                out[i, :, cols] = part.astype(out.dtype)
            column += across


def weight_pieces(which, base, count, groups, more=None, spot=None):
    layout = [len(splits) for splits, _ in groups]
    refs = [ref for splits, others in groups for ref in (*splits, *others)]
    extra = [] if more is None else [more]
    length = groups[0][1][0].shape[0]
    across = sum(others[0].shape[1] for _, others in groups)
    piece = groups[0][0][0].shape[1] // 8
    return pl.pallas_call(
        functools.partial(weight_kernel, layout, base, spot),
        name="weight_pieces",
        out_shape=like((count, piece, across)),
        in_specs=in_smem() + in_vmem(len(refs) + len(extra)),
        out_specs=in_vmem(1)[0],
        scratch_shapes=[pltpu.VMEM((piece, max(layout) * length), jnp.bfloat16)],
        compiler_params=limit(16),
    )(which, *refs, *extra)


def add_kernel(here, there, out):
    for at, size in chunks(out.shape[2], 256):
        cols = slice(at, at + size)
        out[0, :, cols] = (
            here[0, :, cols].astype(jnp.float32) + there[0, :, cols].astype(jnp.float32)
        ).astype(jnp.bfloat16)


def add_pieces(here, there):
    return pl.pallas_call(
        add_kernel,
        name="add_pieces",
        out_shape=like(here.shape),
        in_specs=in_vmem(2),
        out_specs=in_vmem(1)[0],
        compiler_params=limit(6),
    )(here, there)


def spread_kernel(parts, count, *refs):
    sources, outs = refs[:count], refs[count:]
    column = 0
    for (planes, across, turn), out in zip(parts, outs):
        for c in range(planes):
            for at, size in chunks(across, 256):
                cols = slice(column + at, column + at + size)
                value = sum(source[0, :, cols].astype(jnp.float32) for source in sources)
                if turn:
                    out[at : at + size, :] = value.T
                else:
                    out[c, :, at : at + size] = value
            column += across


def spread(sources, parts):
    piece = sources[0].shape[1]
    return pl.pallas_call(
        functools.partial(spread_kernel, parts, len(sources)),
        name="spread",
        out_shape=[
            like((across, piece) if turn else (planes, piece, across), jnp.float32)
            for planes, across, turn in parts
        ],
        in_specs=in_vmem(len(sources)),
        out_specs=in_vmem(len(parts)),
        compiler_params=limit(8),
    )(*sources)


def gains_kernel(chip, *refs):
    sources, out, kept = refs[:4], refs[4], refs[5]
    for back, source in enumerate(sources):
        kept[lax.rem(chip[0] + 4 - back, 4)] = source[...]
    out[...] = (kept[0] + kept[1]) + (kept[2] + kept[3])


def sum_gains(chip, sources):
    return pl.pallas_call(
        gains_kernel,
        name="sum_gains",
        out_shape=like(sources[0].shape, jnp.float32),
        in_specs=in_smem() + in_vmem(4),
        out_specs=in_vmem(1)[0],
        scratch_shapes=[pltpu.VMEM((4, *sources[0].shape), jnp.float32)],
        compiler_params=limit(4),
    )(chip, *sources)


def flips(size, bit):
    return [(i, i ^ bit) for i in range(size)]


def after(value, *earlier):
    return lax.optimization_barrier((value, *earlier))[0]


def over_tensor(values, bit):
    return lax.ppermute(values, "tensor", flips(4, bit))


def gather_near(own):
    return own, over_tensor(own, 1), over_tensor(own, 2)


def gather_far(own, from_x, from_y):
    half = own.shape[0] // 2
    low = over_tensor(from_y[:half], 1)
    high = over_tensor(from_x[half:], 2)
    return [own, from_x, from_y, low, high]


def scatter_far(keep, to_x, to_y, far_low, far_high):
    return keep, *relay(to_x, to_y, over_tensor(far_low, 1), over_tensor(far_high, 2))


def scatter_near(keep, to_x, to_y):
    return keep, over_tensor(to_x, 1), over_tensor(to_y, 2)


def over_cores(values):
    return lax.ppermute(values, "dp", flips(8, 1))


def up_the_line(values, chips=1):
    return lax.ppermute(values, "dp", [(i, (i + 2 * chips) % 8) for i in range(8)])


class Weight:
    def __init__(self, places, groups):
        self.which_theirs, self.which_mine = places[:2]
        self.groups = groups

    def sibling_part(self):
        self.sibling_sum = weight_pieces(self.which_theirs, 0, 4, self.groups)
        self.theirs = over_cores(self.sibling_sum)

    def scatter(self, *earlier):
        self.chip_sum = self.own_part(0, 4, *earlier)
        return lax.psum_scatter(
            self.chip_sum,
            "dp",
            scatter_dimension=0,
            axis_index_groups=[[0, 2, 4, 6], [1, 3, 5, 7]],
        )

    def own_part(self, base, count, *earlier):
        more = after(self.theirs, *earlier) if earlier else self.theirs
        return weight_pieces(self.which_mine, base, count, self.groups, more, base)


def sum_flips(values, *steps):
    for axis, size, bit in steps:
        values = values + lax.ppermute(values, axis, flips(size, bit))
    return values


def per_device_square(
    tokens, gain_attn, gain_mlp, w_qkv, w_out, w_gate_up, w_down, cotangent, segment_ids, valid_mask
):
    rows = tokens.shape[0]
    length = segment_ids.shape[0]
    low = jnp.bfloat16
    me = lax.axis_index("tensor")
    order = [me, me ^ 1, me ^ 2, me ^ 3]
    rows_at = jnp.stack([at * rows for at in order] + [order[3] * rows + rows // 2]).astype(jnp.int32)
    index = lax.axis_index("dp")
    place, core = index // 2, index % 2
    ring = (place + jnp.array([3, 2, 1, 0])) % 4
    in_turn = ((2 * ring + 1 - core).astype(jnp.int32), (2 * ring + core).astype(jnp.int32))
    in_order = (
        (2 * jnp.arange(4) + 1 - core).astype(jnp.int32),
        (2 * jnp.arange(4) + core).astype(jnp.int32),
    )
    chip = place.astype(jnp.int32).reshape(1)
    gain_one = gain_attn[None, :]
    gain_two = gain_mlp[None, :]

    tokens = after(tokens, rows_at, chip, *in_turn, *in_order)
    normed = norm(tokens, gain_one)
    near = gather_near(normed)
    cosine, sine, seg_col, valid_col = prepare(
        segment_ids.astype(jnp.float32)[None, :],
        valid_mask.astype(jnp.float32)[None, :],
    )
    near = (near[0], near[1], after(near[2], cosine))
    blocks = gather_far(*near)
    cot_near = gather_near(after(cotangent, *blocks))
    normed_all, queries, keys, values = project(rows_at, blocks, w_qkv, cosine, sine)
    *sent, probs, mixed = attend_square(
        rows_at,
        after(queries, *cot_near),
        keys,
        values,
        w_out,
        segment_ids.astype(jnp.float32)[None, :],
        seg_col,
        valid_col,
    )
    keep, to_x, to_y = scatter_far(*sent)
    cot_blocks = gather_far(*(after(part, to_x) for part in cot_near))
    got = scatter_near(keep, to_x, to_y)
    middle, normed_two = make_middle(tokens, *got, gain_two)

    near = gather_near(normed_two)
    d_hidden, cot_all = back_through_down(
        [after(cot_blocks[0], normed_two)] + cot_blocks[1:], w_down
    )
    blocks = gather_far(near[0], after(near[1], d_hidden), near[2])
    normed_two_all, hidden, d_gate_up = mlp(blocks, d_hidden, w_gate_up)
    down = Weight(in_order, [([cot_all], [hidden])])
    down.sibling_part()
    gate = Weight(in_turn, [([after(normed_two_all, down.sibling_sum)], [d_gate_up])])
    gate.sibling_part()
    down_total = down.scatter(gate.sibling_sum)
    parts = [gate.own_part(0, 1, down.chip_sum)]
    turn = up_the_line(parts[0])
    sent = mlp_back(after(d_gate_up, parts[0]), w_gate_up)
    keep, to_x, to_y = scatter_far(*sent)
    for place in range(1, 4):
        parts.append(gate.own_part(place, 1, parts[-1], to_x, to_y))
    got = scatter_near(keep, to_x, to_y)
    d_middle, gain_two_part, d_middle_low = norm_back(
        cotangent, after(got[0], parts[3]), *got[1:], middle, gain_two, True
    )
    near = gather_near(d_middle_low)
    so_far = add_pieces(after(parts[1], *near), turn)
    turn = up_the_line(so_far)
    blocks = gather_far(near[0], after(near[1], so_far), near[2])

    d_middle_all, d_project = attend_back_square(
        rows_at,
        [after(blocks[0], down_total)] + blocks[1:],
        w_out,
        probs,
        queries,
        keys,
        values,
        cosine,
        sine,
    )
    late = Weight(in_order, [([normed_all], [d_project]), ([d_middle_all], [mixed])])
    late.sibling_part()
    so_far = add_pieces(after(parts[2], late.sibling_sum), turn)
    turn = up_the_line(so_far)
    sent = project_back(rows_at, after(d_project, so_far), w_qkv)
    keep, to_x, to_y = scatter_far(*sent)
    late_total = late.scatter(*sent)
    got = scatter_near(keep, after(to_x, late.chip_sum), to_y)
    sent = through_down(after(hidden, late.chip_sum), w_down)
    d_inputs, gain_one_part = norm_back(
        d_middle, after(got[0], *sent), *got[1:], tokens, gain_one, False
    )
    keep, to_x, to_y = scatter_far(*(after(part, d_inputs, turn) for part in sent))
    gains = sum_flips(
        after(jnp.concatenate([gain_one_part, gain_two_part], axis=0), to_x, to_y),
        ("dp", 8, 1),
        ("tensor", 4, 1),
        ("tensor", 4, 2),
    )
    gains = [gains] + [up_the_line(gains, chips) for chips in (1, 2, 3)]
    keep, got_x, got_y = scatter_near(keep, to_x, to_y)
    output = (middle + keep + got_x.astype(jnp.float32) + got_y.astype(jnp.float32)).astype(low)
    grad_gains = sum_gains(chip, [after(gains[0], output), *gains[1:]])
    units, wide = w_down.shape[0], w_qkv.shape[2]
    (grad_down,) = spread([after(down_total, grad_gains)[None]], [(1, units, True)])
    (grad_gate_up,) = spread([after(parts[3], grad_down), turn], [(2, units, False)])
    grad_qkv, grad_out = spread(
        [after(late_total, grad_gate_up)[None]], [(3, wide, False), (1, wide, True)]
    )
    return (
        output,
        d_inputs,
        grad_gains[0],
        grad_gains[1],
        grad_qkv,
        grad_out,
        grad_gate_up,
        grad_down,
    )


def solution(mesh):
    placed = (
        P(("dp", "tensor"), None),
        P(),
        P(),
        P(None, None, "tensor"),
        P("tensor", None),
        P(None, None, "tensor"),
        P("tensor", None),
        P(("dp", "tensor"), None),
        P("dp"),
        P("dp"),
    )
    square = mesh.shape["tensor"] == 4 and mesh.shape["dp"] == 8
    return jax.shard_map(
        per_device_square if square else per_device,
        mesh=mesh,
        in_specs=placed,
        out_specs=(
            P(("dp", "tensor"), None),
            P(("dp", "tensor"), None),
            P(),
            P(),
            P(None, "dp", "tensor"),
            P("tensor", "dp"),
            P(None, "dp", "tensor"),
            P("tensor", "dp"),
        ),
        check_vma=False,
    )
```

```python
import functools
import math

import jax
import jax.numpy as jnp
from jax import lax
from jax.experimental import pallas as pl
from jax.experimental.pallas import tpu as pltpu
from jax.sharding import PartitionSpec as P

HD = 128


EPS = 1e-06
THETA = 10000.0


def rope_tables(places):
    positions = places.astype(jnp.float32)
    freqs = THETA ** (-(jnp.arange(HD // 2).astype(jnp.float32) * 2.0 / HD))
    angles = positions[:, None] * freqs[None, :]
    return (jnp.cos(angles), jnp.sin(angles))


def rotate(values, cosine, sine):
    half = values.shape[-1] // 2
    first = values[..., :half]
    second = values[..., half:]
    cosine = cosine[:, None, :]
    sine = sine[:, None, :]
    return jnp.concatenate(
        [first * cosine - second * sine, second * cosine + first * sine], axis=-1
    )


def block_scores(q_block, keys_rot, start, segments, valid):
    block_rows = q_block.shape[0]
    length = keys_rot.shape[0]
    key_pos = jnp.arange(length)
    row_pos = start + jnp.arange(block_rows)
    row_seg = lax.dynamic_slice_in_dim(segments, start, block_rows, 0)
    scores = jnp.einsum(
        "qhd,khd->hqk", q_block, keys_rot, preferred_element_type=jnp.float32
    ) * HD ** (-0.5)
    allowed = (
        (key_pos[None, :] <= row_pos[:, None])
        & (row_seg[:, None] == segments[None, :])
        & ((valid[None, :] == 1) | (key_pos[None, :] == row_pos[:, None]))
    )
    return jnp.where(allowed[None], scores, -1e30)


def attend(queries, keys_rot, values, segments, valid):
    length = queries.shape[0]
    block_rows = min(512, length)
    count = length // block_rows

    def one_block(index):
        start = index * block_rows
        q_block = lax.dynamic_slice_in_dim(queries, start, block_rows, 0)
        scores = block_scores(q_block, keys_rot, start, segments, valid)
        top = jnp.max(scores, axis=-1, keepdims=True)
        expo = jnp.exp(scores - top)
        total = jnp.sum(expo, axis=-1, keepdims=True)
        probs = (expo / total).astype(jnp.bfloat16)
        result = jnp.einsum("hqk,khd->qhd", probs, values, preferred_element_type=jnp.float32)
        return (result, top[..., 0] + jnp.log(total[..., 0]))

    blocks, log_sums = lax.map(one_block, jnp.arange(count))
    return (blocks.reshape(length, -1), log_sums)


def attend_back(queries, keys_rot, values, d_mixed, log_sums, segments, valid):
    length = queries.shape[0]
    block_rows = min(512, length)
    count = length // block_rows
    scale = HD ** (-0.5)

    def one_block(carry, index):
        d_keys, d_values = carry
        start = index * block_rows
        q_block = lax.dynamic_slice_in_dim(queries, start, block_rows, 0)
        d_block = lax.dynamic_slice_in_dim(d_mixed, start, block_rows, 0)
        scores = block_scores(q_block, keys_rot, start, segments, valid)
        probs = jnp.exp(scores - log_sums[index][..., None])
        d_values = d_values + jnp.einsum(
            "hqk,qhd->khd", probs.astype(jnp.bfloat16), d_block, preferred_element_type=jnp.float32
        )
        d_probs = jnp.einsum("qhd,khd->hqk", d_block, values, preferred_element_type=jnp.float32)
        delta = jnp.sum(d_probs * probs, axis=-1, keepdims=True)
        d_scores = (probs * (d_probs - delta)).astype(jnp.bfloat16)
        d_query = scale * jnp.einsum(
            "hqk,khd->qhd", d_scores, keys_rot, preferred_element_type=jnp.float32
        )
        d_keys = d_keys + scale * jnp.einsum(
            "hqk,qhd->khd", d_scores, q_block, preferred_element_type=jnp.float32
        )
        return ((d_keys, d_values), d_query)

    empty = jnp.zeros(keys_rot.shape, jnp.float32)
    (d_keys, d_values), d_queries = lax.scan(one_block, (empty, empty), jnp.arange(count))
    return (d_queries.reshape(queries.shape), d_keys, d_values)


def per_device(
    tokens, gain_attn, gain_mlp, w_qkv, w_out, w_gate_up, w_down, cotangent, segment_ids, valid_mask
):
    length = segment_ids.shape[0]
    heads_here = w_qkv.shape[2] // HD
    shape3 = (length, heads_here, HD)
    incoming = tokens.astype(jnp.float32)
    gain_one = gain_attn.astype(jnp.float32)
    gain_two = gain_mlp.astype(jnp.float32)
    cosine, sine = rope_tables(jnp.arange(length))
    inv_one = lax.rsqrt(jnp.mean(incoming * incoming, axis=-1, keepdims=True) + EPS)
    normed = (incoming * inv_one * gain_one).astype(jnp.bfloat16)
    normed_all = lax.all_gather(normed, "tensor", axis=0, tiled=True)
    project = jnp.einsum("td,cde->cte", normed_all, w_qkv, preferred_element_type=jnp.float32)
    queries = rotate(project[0].reshape(shape3), cosine, sine).astype(jnp.bfloat16)
    keys_rot = rotate(project[1].reshape(shape3), cosine, sine).astype(jnp.bfloat16)
    values = project[2].reshape(shape3).astype(jnp.bfloat16)
    mixed, log_sums = attend(queries, keys_rot, values, segment_ids, valid_mask)
    mixed = mixed.astype(jnp.bfloat16)
    middle = incoming + lax.psum_scatter(
        jnp.dot(mixed, w_out, preferred_element_type=jnp.float32).astype(jnp.bfloat16),
        "tensor",
        scatter_dimension=0,
        tiled=True,
    ).astype(jnp.float32)
    inv_two = lax.rsqrt(jnp.mean(middle * middle, axis=-1, keepdims=True) + EPS)
    normed_two = (middle * inv_two * gain_two).astype(jnp.bfloat16)
    normed_two_all = lax.all_gather(normed_two, "tensor", axis=0, tiled=True)
    gate = jnp.dot(normed_two_all, w_gate_up[0], preferred_element_type=jnp.float32)
    upper = jnp.dot(normed_two_all, w_gate_up[1], preferred_element_type=jnp.float32)
    sigma = jax.nn.sigmoid(gate)
    hidden = (gate * sigma * upper).astype(jnp.bfloat16)
    result = middle + lax.psum_scatter(
        jnp.dot(hidden, w_down, preferred_element_type=jnp.float32).astype(jnp.bfloat16),
        "tensor",
        scatter_dimension=0,
        tiled=True,
    ).astype(jnp.float32)
    output = result.astype(jnp.bfloat16)
    cot_all = lax.all_gather(cotangent, "tensor", axis=0, tiled=True)
    d_hidden = jnp.einsum("td,fd->tf", cot_all, w_down, preferred_element_type=jnp.float32)
    grad_down = jnp.einsum("tf,td->fd", hidden, cot_all, preferred_element_type=jnp.float32)
    d_upper = (d_hidden * gate * sigma).astype(jnp.bfloat16)
    d_gate = (d_hidden * upper * sigma * (1.0 + gate * (1.0 - sigma))).astype(jnp.bfloat16)
    grad_gate_up = jnp.stack(
        [
            jnp.einsum("td,tf->df", normed_two_all, d_gate, preferred_element_type=jnp.float32),
            jnp.einsum("td,tf->df", normed_two_all, d_upper, preferred_element_type=jnp.float32),
        ]
    )
    d_normed_two = lax.psum_scatter(
        (
            jnp.einsum("tf,df->td", d_gate, w_gate_up[0], preferred_element_type=jnp.float32)
            + jnp.einsum("tf,df->td", d_upper, w_gate_up[1], preferred_element_type=jnp.float32)
        ).astype(jnp.bfloat16),
        "tensor",
        scatter_dimension=0,
        tiled=True,
    ).astype(jnp.float32)
    scaled_two = gain_two * d_normed_two
    d_middle = (
        cotangent.astype(jnp.float32)
        + inv_two * scaled_two
        - middle * inv_two**3 * jnp.mean(scaled_two * middle, axis=-1, keepdims=True)
    )
    grad_gain_two = jnp.sum(d_normed_two * middle * inv_two, axis=0)
    d_middle_all = lax.all_gather(d_middle.astype(jnp.bfloat16), "tensor", axis=0, tiled=True)
    d_mixed = jnp.einsum(
        "td,ed->te", d_middle_all, w_out, preferred_element_type=jnp.float32
    ).astype(jnp.bfloat16)
    grad_out = jnp.einsum("te,td->ed", mixed, d_middle_all, preferred_element_type=jnp.float32)
    d_queries, d_keys, d_values = attend_back(
        queries, keys_rot, values, d_mixed.reshape(shape3), log_sums, segment_ids, valid_mask
    )
    d_project = jnp.stack(
        [
            rotate(d_queries, cosine, -sine).reshape(length, -1),
            rotate(d_keys, cosine, -sine).reshape(length, -1),
            d_values.reshape(length, -1),
        ]
    ).astype(jnp.bfloat16)
    grad_qkv = jnp.einsum("td,cte->cde", normed_all, d_project, preferred_element_type=jnp.float32)
    d_normed = lax.psum_scatter(
        jnp.einsum("cte,cde->td", d_project, w_qkv, preferred_element_type=jnp.float32).astype(
            jnp.bfloat16
        ),
        "tensor",
        scatter_dimension=0,
        tiled=True,
    ).astype(jnp.float32)
    scaled_one = gain_one * d_normed
    d_inputs = (
        d_middle
        + inv_one * scaled_one
        - incoming * inv_one**3 * jnp.mean(scaled_one * incoming, axis=-1, keepdims=True)
    )
    grad_gain_one = jnp.sum(d_normed * incoming * inv_one, axis=0)
    grad_gain_one, grad_gain_two = lax.psum((grad_gain_one, grad_gain_two), ("dp", "tensor"))
    grad_qkv, grad_out, grad_gate_up, grad_down = (
        lax.psum_scatter(
            grad_qkv.astype(jnp.bfloat16), "dp", scatter_dimension=1, tiled=True
        ).astype(jnp.float32),
        lax.psum_scatter(
            grad_out.astype(jnp.bfloat16), "dp", scatter_dimension=1, tiled=True
        ).astype(jnp.float32),
        lax.psum_scatter(
            grad_gate_up.astype(jnp.bfloat16), "dp", scatter_dimension=1, tiled=True
        ).astype(jnp.float32),
        lax.psum_scatter(
            grad_down.astype(jnp.bfloat16), "dp", scatter_dimension=1, tiled=True
        ).astype(jnp.float32),
    )
    return (
        output,
        d_inputs,
        grad_gain_one,
        grad_gain_two,
        grad_qkv,
        grad_out,
        grad_gate_up,
        grad_down,
    )


NT = (((1,), (1,)), ((), ()))
TN = (((0,), (0,)), ((), ()))
MEGA = 1024 * 1024


def chunks(total, step):
    return [(at, min(step, total - at)) for at in range(0, total, step)]


def dot(left, right, dims=None):
    if dims is None:
        return jnp.dot(left, right, preferred_element_type=jnp.float32)
    return lax.dot_general(left, right, dims, preferred_element_type=jnp.float32)


def in_vmem(count):
    return [pl.BlockSpec(memory_space=pltpu.VMEM)] * count


def in_smem():
    return [pl.BlockSpec(memory_space=pltpu.SMEM)]


def like(shape, kind=jnp.bfloat16):
    return jax.ShapeDtypeStruct(shape, kind)


def limit(megabytes):
    return pltpu.CompilerParams(vmem_limit_bytes=megabytes * MEGA)


def starts_of(blocks):
    at, starts = 0, []
    for block in blocks:
        starts.append((at, block.shape[0]))
        at += block.shape[0]
    return starts


def send_shapes(rows, width):
    half = rows // 2
    return [
        like((rows, width), jnp.float32),
        like((rows, width)),
        like((rows, width)),
        like((half, width)),
        like((half, width)),
    ]


def store_parts(part, targets, cols):
    for (start, rows), target in zip(starts_of(targets), targets):
        target[:, cols] = part[start : start + rows].astype(target.dtype)


def norm_kernel(tokens, gain, normed):
    wide = tokens[...].astype(jnp.float32)
    inverse = lax.rsqrt(jnp.mean(wide * wide, axis=-1, keepdims=True) + EPS)
    normed[...] = (wide * inverse * gain[...].astype(jnp.float32)).astype(jnp.bfloat16)


def norm(tokens, gain):
    return pl.pallas_call(
        norm_kernel,
        name="norm",
        out_shape=like(tokens.shape),
        in_specs=in_vmem(2),
        out_specs=in_vmem(1)[0],
        compiler_params=limit(4),
    )(tokens, gain)


def relay_kernel(to_x, to_y, via_x, via_y, next_x, next_y):
    half = via_x.shape[0]
    next_x[:half] = to_x[:half]
    next_x[half:] = (
        to_x[half:].astype(jnp.float32) + via_y[...].astype(jnp.float32)
    ).astype(jnp.bfloat16)
    next_y[:half] = (
        to_y[:half].astype(jnp.float32) + via_x[...].astype(jnp.float32)
    ).astype(jnp.bfloat16)
    next_y[half:] = to_y[half:]


def relay(to_x, to_y, via_x, via_y):
    return pl.pallas_call(
        relay_kernel,
        name="relay",
        out_shape=[like(to_x.shape), like(to_y.shape)],
        in_specs=in_vmem(4),
        out_specs=in_vmem(2),
        compiler_params=limit(4),
    )(to_x, to_y, via_x, via_y)


def middle_kernel(tokens, keep, got_x, got_y, gain, middle, normed):
    total = (
        tokens[...].astype(jnp.float32)
        + keep[...]
        + got_x[...].astype(jnp.float32)
        + got_y[...].astype(jnp.float32)
    )
    middle[...] = total
    inverse = lax.rsqrt(jnp.mean(total * total, axis=-1, keepdims=True) + EPS)
    normed[...] = (total * inverse * gain[...].astype(jnp.float32)).astype(jnp.bfloat16)


def make_middle(tokens, keep, got_x, got_y, gain):
    return pl.pallas_call(
        middle_kernel,
        name="make_middle",
        out_shape=[like(keep.shape, jnp.float32), like(keep.shape)],
        in_specs=in_vmem(5),
        out_specs=in_vmem(2),
        compiler_params=limit(6),
    )(tokens, keep, got_x, got_y, gain)


def norm_back_kernel(base, keep, got_x, got_y, source, gain, *outs):
    d_normed = keep[...] + got_x[...].astype(jnp.float32) + got_y[...].astype(jnp.float32)
    wide = source[...].astype(jnp.float32)
    inverse = lax.rsqrt(jnp.mean(wide * wide, axis=-1, keepdims=True) + EPS)
    scaled = gain[...].astype(jnp.float32) * d_normed
    slope = jnp.mean(scaled * wide, axis=-1, keepdims=True) * inverse * inverse * inverse
    total = base[...].astype(jnp.float32) + inverse * scaled - wide * slope
    outs[0][...] = total
    outs[1][...] = jnp.sum(d_normed * wide * inverse, axis=0, keepdims=True)
    if len(outs) == 3:
        outs[2][...] = total.astype(jnp.bfloat16)


def norm_back(base, keep, got_x, got_y, source, gain, low):
    return pl.pallas_call(
        norm_back_kernel,
        name="norm_back",
        out_shape=[like(keep.shape, jnp.float32), like((1, keep.shape[1]), jnp.float32)]
        + [like(keep.shape)] * low,
        in_specs=in_vmem(6),
        out_specs=in_vmem(2 + low),
        compiler_params=limit(8),
    )(base, keep, got_x, got_y, source, gain)


def prepare_kernel(segments, valid, cosine, sine, seg_col, valid_col):
    length = cosine.shape[0]
    half = HD // 2
    place = lax.broadcasted_iota(jnp.int32, (length, HD), 0).astype(jnp.float32)
    lane = lax.broadcasted_iota(jnp.int32, (length, HD), 1)
    step = jnp.where(lane < half, lane, lane - half).astype(jnp.float32)
    angle = place * jnp.exp(step * (-2.0 / HD * math.log(THETA)))
    cosine[...] = jnp.cos(angle)
    turn = jnp.sin(angle)
    sine[...] = jnp.where(lane < half, -turn, turn)
    seg_col[...] = jnp.broadcast_to(segments[...], (HD, length)).T
    valid_col[...] = jnp.broadcast_to(valid[...], (HD, length)).T


def prepare(segments, valid):
    length = segments.shape[1]
    return pl.pallas_call(
        prepare_kernel,
        name="prepare",
        out_shape=[like((length, HD), jnp.float32)] * 4,
        in_specs=in_vmem(2),
        out_specs=in_vmem(4),
        compiler_params=limit(6),
    )(segments, valid)


def project_kernel(
    rows_at, own, from_x, from_y, low, high, w_qkv, cosine, sine, normed, queries, keys, values
):
    for i, block in enumerate((own, from_x, from_y, low, high)):
        place = pl.multiple_of(rows_at[i], 64)
        normed[pl.ds(place, block.shape[0]), :] = block[...]
    for c, target in enumerate((queries, keys, values)):
        for at, size in chunks(target.shape[1], 2 * HD):
            part = dot(normed[...], w_qkv[c, :, at : at + size])
            for head in range(0, size, HD):
                piece = part[:, head : head + HD]
                if c < 2:
                    piece = piece * cosine[...] + pltpu.roll(piece, HD // 2, 1) * sine[...]
                target[:, at + head : at + head + HD] = piece.astype(jnp.bfloat16)


def project(rows_at, blocks, w_qkv, cosine, sine):
    rows, width = blocks[0].shape
    length = 4 * rows
    wide = w_qkv.shape[2]
    return pl.pallas_call(
        project_kernel,
        name="project",
        out_shape=[like((length, width))] + [like((length, wide))] * 3,
        in_specs=in_smem() + in_vmem(8),
        out_specs=in_vmem(4),
        compiler_params=limit(8),
    )(rows_at, *blocks, w_qkv, cosine, sine)


def attend_kernel(
    rows_at, queries, keys, values, w_out, seg_row, seg_col, valid_col,
    keep, to_x, to_y, far_low, far_high, probs, mixed, bias, joined,
):
    length, wide = queries.shape
    key_at = lax.broadcasted_iota(jnp.int32, (length, length), 0)
    query_at = lax.broadcasted_iota(jnp.int32, (length, length), 1)
    allowed = (
        (key_at <= query_at)
        & (seg_col[:, 0:1] == seg_row[...])
        & ((valid_col[:, 0:1] == 1.0) | (key_at == query_at))
    )
    bias[...] = jnp.where(allowed, 0.0, -1e30)
    for at in range(0, wide, HD):
        head = at // HD
        cols = slice(at, at + HD)
        for q_at, q_size in chunks(length, 256):
            seen = q_at + q_size
            scores = dot(keys[0:seen, cols], queries[q_at:seen, cols], NT)
            scores = scores * HD ** (-0.5) + bias[0:seen, q_at:seen]
            top = jnp.max(scores, axis=0, keepdims=True)
            expo = jnp.exp(scores - top)
            total = jnp.sum(expo, axis=0, keepdims=True)
            chance = (expo * (1.0 / total)).astype(jnp.bfloat16)
            probs[head, 0:seen, q_at:seen] = chance
            result = dot(values[0:seen, cols], chance, TN)
            joined[q_at:seen, cols] = result.T.astype(jnp.bfloat16)
    targets = [keep, to_x, to_y, far_low, far_high]
    for i, (start, size) in enumerate(starts_of(targets)):
        place = pl.multiple_of(rows_at[i], 64)
        mixed[start : start + size, :] = joined[pl.ds(place, size), :]
    for at, size in chunks(w_out.shape[1], 512):
        store_parts(dot(mixed[...], w_out[:, at : at + size]), targets, slice(at, at + size))


def attend_square(rows_at, queries, keys, values, w_out, seg_row, seg_col, valid_col):
    length, wide = queries.shape
    width = w_out.shape[1]
    heads = wide // HD
    return pl.pallas_call(
        attend_kernel,
        name="attend",
        out_shape=send_shapes(length // 4, width)
        + [like((heads, length, length)), like((length, wide))],
        in_specs=in_smem() + in_vmem(7),
        out_specs=in_vmem(7),
        scratch_shapes=[
            pltpu.VMEM((length, length), jnp.float32),
            pltpu.VMEM((length, wide), jnp.bfloat16),
        ],
        compiler_params=limit(8),
    )(rows_at, queries, keys, values, w_out, seg_row, seg_col, valid_col)


def d_hidden_kernel(own, from_x, from_y, low, high, w_down, d_hidden, cot_all):
    blocks = [own, from_x, from_y, low, high]
    for (start, size), block in zip(starts_of(blocks), blocks):
        cot_all[start : start + size, :] = block[...]
    for at, size in chunks(w_down.shape[0], 256):
        d_hidden[:, at : at + size] = dot(cot_all[...], w_down[at : at + size, :], NT)


def back_through_down(blocks, w_down):
    rows, width = blocks[0].shape
    length = 4 * rows
    units = w_down.shape[0]
    return pl.pallas_call(
        d_hidden_kernel,
        name="back_through_down",
        out_shape=[like((length, units), jnp.float32), like((length, width))],
        in_specs=in_vmem(6),
        out_specs=in_vmem(2),
        compiler_params=limit(6),
    )(*blocks, w_down)


def mlp_kernel(
    own, from_x, from_y, low, high, d_hidden, w_gate_up, normed, hidden, d_gate_up
):
    units = w_gate_up.shape[2]
    blocks = [own, from_x, from_y, low, high]
    for (start, size), block in zip(starts_of(blocks), blocks):
        normed[start : start + size, :] = block[...]
    for at, size in chunks(units, 256):
        here = slice(at, at + size)
        gate = dot(normed[...], w_gate_up[0, :, here])
        upper = dot(normed[...], w_gate_up[1, :, here])
        incoming = d_hidden[:, here]
        sigma = 1.0 / (1.0 + jnp.exp(-gate))
        silu = gate * sigma
        hidden[:, here] = (silu * upper).astype(jnp.bfloat16)
        d_gate_up[:, here] = (incoming * upper * sigma * (1.0 + gate * (1.0 - sigma))).astype(
            jnp.bfloat16
        )
        d_gate_up[:, units + at : units + at + size] = (incoming * silu).astype(jnp.bfloat16)


def mlp(blocks, d_hidden, w_gate_up):
    rows, width = blocks[0].shape
    length = 4 * rows
    units = w_gate_up.shape[2]
    return pl.pallas_call(
        mlp_kernel,
        name="mlp",
        out_shape=[like((length, width)), like((length, units)), like((length, 2 * units))],
        in_specs=in_vmem(7),
        out_specs=in_vmem(3),
        compiler_params=limit(8),
    )(*blocks, d_hidden, w_gate_up)


def mlp_back_kernel(d_gate_up, w_gate_up, *targets):
    units = w_gate_up.shape[2]
    for at, size in chunks(w_gate_up.shape[1], 256):
        part = dot(d_gate_up[:, 0:units], w_gate_up[0, at : at + size, :], NT) + dot(
            d_gate_up[:, units : 2 * units], w_gate_up[1, at : at + size, :], NT
        )
        store_parts(part, targets, slice(at, at + size))


def mlp_back(d_gate_up, w_gate_up):
    return pl.pallas_call(
        mlp_back_kernel,
        name="mlp_back",
        out_shape=send_shapes(d_gate_up.shape[0] // 4, w_gate_up.shape[1]),
        in_specs=in_vmem(2),
        out_specs=in_vmem(5),
        compiler_params=limit(6),
    )(d_gate_up, w_gate_up)


def down_kernel(hidden, w_down, *targets):
    for at, size in chunks(w_down.shape[1], 256):
        store_parts(dot(hidden[...], w_down[:, at : at + size]), targets, slice(at, at + size))


def through_down(hidden, w_down):
    return pl.pallas_call(
        down_kernel,
        name="through_down",
        out_shape=send_shapes(hidden.shape[0] // 4, w_down.shape[1]),
        in_specs=in_vmem(2),
        out_specs=in_vmem(5),
        compiler_params=limit(6),
    )(hidden, w_down)


def attend_back_kernel(
    rows_at, own, from_x, from_y, low, high, w_out, probs, queries, keys, values, cosine, sine,
    d_middle, d_project, d_mixed,
):
    length, wide = queries.shape
    blocks = [own, from_x, from_y, low, high]
    starts = starts_of(blocks)
    for (start, size), block in zip(starts, blocks):
        d_middle[start : start + size, :] = block[...]
    for at, size in chunks(wide, 256):
        part = dot(d_middle[...], w_out[at : at + size, :], NT).astype(jnp.bfloat16)
        for i, (start, rows) in enumerate(starts):
            place = pl.multiple_of(rows_at[i], 64)
            d_mixed[pl.ds(place, rows), at : at + size] = part[start : start + rows]
    scale = HD ** (-0.5)

    def back(turned, rows):
        return turned * cosine[rows, :] - pltpu.roll(turned, HD // 2, 1) * sine[rows, :]

    for at in range(0, wide, HD):
        head = at // HD
        cols = slice(at, at + HD)
        d_keys = d_values = None
        for q_at, q_size in reversed(chunks(length, 256)):
            seen = q_at + q_size
            rows = slice(q_at, seen)
            chance = probs[head, 0:seen, rows]
            d_out = d_mixed[rows, cols]
            d_chance = dot(values[0:seen, cols], d_out, NT)
            exact = chance.astype(jnp.float32)
            delta = jnp.sum(d_chance * exact, axis=0, keepdims=True)
            d_scores = (exact * (d_chance - delta)).astype(jnp.bfloat16)
            more_values = dot(chance, d_out)
            more_keys = dot(d_scores, queries[rows, cols])
            d_queries = dot(keys[0:seen, cols], d_scores, TN).T
            d_project[rows, cols] = back(d_queries * scale, rows).astype(jnp.bfloat16)
            if d_keys is None:
                d_keys, d_values = more_keys, more_values
            else:
                d_keys = jnp.concatenate([d_keys[:seen] + more_keys, d_keys[seen:]], axis=0)
                d_values = jnp.concatenate([d_values[:seen] + more_values, d_values[seen:]], axis=0)
        d_project[:, wide + at : wide + at + HD] = back(d_keys * scale, slice(0, length)).astype(
            jnp.bfloat16
        )
        d_project[:, 2 * wide + at : 2 * wide + at + HD] = d_values.astype(jnp.bfloat16)


def attend_back_square(rows_at, blocks, w_out, probs, queries, keys, values, cosine, sine):
    length, wide = queries.shape
    return pl.pallas_call(
        attend_back_kernel,
        name="attend_back",
        out_shape=[like((length, w_out.shape[1])), like((length, 3 * wide))],
        in_specs=in_smem() + in_vmem(12),
        out_specs=in_vmem(2),
        scratch_shapes=[pltpu.VMEM((length, wide), jnp.bfloat16)],
        compiler_params=limit(8),
    )(rows_at, *blocks, w_out, probs, queries, keys, values, cosine, sine)


def project_back_kernel(rows_at, d_project, w_qkv, *refs):
    targets, turned = refs[:5], refs[5]
    wide = w_qkv.shape[2]
    for i, (start, size) in enumerate(starts_of(targets)):
        place = pl.multiple_of(rows_at[i], 64)
        turned[start : start + size, :] = d_project[pl.ds(place, size), :]
    for at, size in chunks(w_qkv.shape[1], 256):
        part = sum(
            dot(turned[:, c * wide : (c + 1) * wide], w_qkv[c, at : at + size, :], NT)
            for c in range(3)
        )
        store_parts(part, targets, slice(at, at + size))


def project_back(rows_at, d_project, w_qkv):
    return pl.pallas_call(
        project_back_kernel,
        name="project_back",
        out_shape=send_shapes(d_project.shape[0] // 4, w_qkv.shape[1]),
        in_specs=in_smem() + in_vmem(2),
        out_specs=in_vmem(5),
        scratch_shapes=[pltpu.VMEM(d_project.shape, jnp.bfloat16)],
        compiler_params=limit(8),
    )(rows_at, d_project, w_qkv)


def weight_kernel(layout, base, spot, which, *refs):
    turned, out = refs[-1], refs[-2]
    more = refs[-3] if spot is not None else None
    count, piece, _ = out.shape
    for i in range(count):
        place = pl.multiple_of(which[base + i] * piece, piece)
        at_ref = column = 0
        for pairs in layout:
            splits = refs[at_ref : at_ref + pairs]
            others = refs[at_ref + pairs : at_ref + 2 * pairs]
            at_ref += 2 * pairs
            length, across = others[0].shape
            for j, split in enumerate(splits):
                turned[:, j * length : (j + 1) * length] = split[:, pl.ds(place, piece)].T
            for at, size in chunks(across, 256):
                part = None
                for j, other in enumerate(others):
                    term = dot(turned[:, j * length : (j + 1) * length], other[:, at : at + size])
                    part = term if part is None else part + term
                cols = slice(column + at, column + at + size)
                if more is not None:
                    part = part + more[spot + i, :, cols].astype(jnp.float32)
                out[i, :, cols] = part.astype(out.dtype)
            column += across


def weight_pieces(which, base, count, groups, more=None, spot=None):
    layout = [len(splits) for splits, _ in groups]
    refs = [ref for splits, others in groups for ref in (*splits, *others)]
    extra = [] if more is None else [more]
    length = groups[0][1][0].shape[0]
    across = sum(others[0].shape[1] for _, others in groups)
    piece = groups[0][0][0].shape[1] // 8
    return pl.pallas_call(
        functools.partial(weight_kernel, layout, base, spot),
        name="weight_pieces",
        out_shape=like((count, piece, across)),
        in_specs=in_smem() + in_vmem(len(refs) + len(extra)),
        out_specs=in_vmem(1)[0],
        scratch_shapes=[pltpu.VMEM((piece, max(layout) * length), jnp.bfloat16)],
        compiler_params=limit(16),
    )(which, *refs, *extra)


def join_kernel(here_outer, here_own, there_outer, there_own, outer, own):
    for here, there, out in ((here_outer, there_outer, outer), (here_own, there_own, own)):
        for at, size in chunks(out.shape[2], 256):
            cols = slice(at, at + size)
            out[0, :, cols] = (
                here[0, :, cols].astype(jnp.float32) + there[0, :, cols].astype(jnp.float32)
            ).astype(jnp.bfloat16)


def join(here, there):
    shape = here[0].shape
    return pl.pallas_call(
        join_kernel,
        name="join",
        out_shape=[like(shape), like(shape)],
        in_specs=in_vmem(4),
        out_specs=in_vmem(2),
        compiler_params=limit(6),
    )(*here, *there)


def hand_kernel(near, far, out):
    for at, size in chunks(out.shape[1], 256):
        cols = slice(at, at + size)
        out[:, cols] = (
            near[0, :, cols].astype(jnp.float32) + far[0, :, cols].astype(jnp.float32)
        ).astype(jnp.bfloat16)


def hand(near, far):
    return pl.pallas_call(
        hand_kernel,
        name="hand",
        out_shape=like(near.shape[1:]),
        in_specs=in_vmem(2),
        out_specs=in_vmem(1)[0],
        compiler_params=limit(6),
    )(near, far)


def finish_kernel(parts, count_inner, inner, *refs):
    count = len(refs) - len(parts)
    here = [ref for ref in refs[:count_inner]]
    outer = [ref for ref in refs[count_inner:count]]

    def total(sources, cols):
        found = None
        for source in sources:
            term = source[0, :, cols] if len(source.shape) == 3 else source[:, cols]
            term = term.astype(jnp.float32)
            found = term if found is None else found + term
        return found

    column = 0
    for (planes, across, turn), out in zip(parts, refs[count:]):
        for c in range(planes):
            for at, size in chunks(across, 256):
                cols = slice(column + at, column + at + size)
                value = jnp.where(inner[0] == 1, total(here, cols), total(outer, cols))
                if turn:
                    out[at : at + size, :] = value.T
                else:
                    out[c, :, at : at + size] = value
            column += across


def finish(inner, here, outer, parts):
    piece = here[0].shape[-2]
    return pl.pallas_call(
        functools.partial(finish_kernel, parts, len(here)),
        name="finish",
        out_shape=[
            like((across, piece) if turn else (planes, piece, across), jnp.float32)
            for planes, across, turn in parts
        ],
        in_specs=in_smem() + in_vmem(len(here) + len(outer)),
        out_specs=in_vmem(len(parts)),
        compiler_params=limit(8),
    )(inner, *here, *outer)


def gains_kernel(chip, *refs):
    sources, out, kept = refs[:4], refs[4], refs[5]
    for back, source in enumerate(sources):
        kept[lax.rem(chip[0] + 4 - back, 4)] = source[...]
    out[...] = (kept[0] + kept[1]) + (kept[2] + kept[3])


def sum_gains(chip, sources):
    return pl.pallas_call(
        gains_kernel,
        name="sum_gains",
        out_shape=like(sources[0].shape, jnp.float32),
        in_specs=in_smem() + in_vmem(4),
        out_specs=in_vmem(1)[0],
        scratch_shapes=[pltpu.VMEM((4, *sources[0].shape), jnp.float32)],
        compiler_params=limit(4),
    )(chip, *sources)


def flips(size, bit):
    return [(i, i ^ bit) for i in range(size)]


def after(value, *earlier):
    return lax.optimization_barrier((value, *earlier))[0]


def over_tensor(values, bit):
    return lax.ppermute(values, "tensor", flips(4, bit))


def gather_near(own):
    return own, over_tensor(own, 1), over_tensor(own, 2)


def gather_far(own, from_x, from_y):
    half = own.shape[0] // 2
    low = over_tensor(from_y[:half], 1)
    high = over_tensor(from_x[half:], 2)
    return [own, from_x, from_y, low, high]


def scatter_far(keep, to_x, to_y, far_low, far_high):
    return keep, *relay(to_x, to_y, over_tensor(far_low, 1), over_tensor(far_high, 2))


def scatter_near(keep, to_x, to_y):
    return keep, over_tensor(to_x, 1), over_tensor(to_y, 2)


def over_cores(values):
    return lax.ppermute(values, "dp", flips(8, 1))


def up_the_line(values, chips):
    return lax.ppermute(values, "dp", [(i, (i + 2 * chips) % 8) for i in range(8)])


def to_inner(values):
    return lax.ppermute(values, "dp", [(0, 2), (1, 3), (6, 4), (7, 5)])


def to_outer(values):
    return lax.ppermute(values, "dp", [(2, 0), (3, 1), (4, 6), (5, 7)])


def over_middle(values):
    return lax.ppermute(values, "dp", [(2, 4), (3, 5), (4, 2), (5, 3)])


class Weight:
    def __init__(self, places, groups):
        self.which_theirs, self.which_mine, self.inner = places
        self.groups = groups

    def sibling_part(self):
        self.sibling_sum = weight_pieces(self.which_theirs, 0, 4, self.groups)
        self.theirs = over_cores(self.sibling_sum)

    def own_part(self, base, count, *earlier):
        more = after(self.theirs, *earlier) if earlier else self.theirs
        return weight_pieces(self.which_mine, base, count, self.groups, more, base)


def sum_flips(values, *steps):
    for axis, size, bit in steps:
        values = values + lax.ppermute(values, axis, flips(size, bit))
    return values


def per_device_square(
    tokens, gain_attn, gain_mlp, w_qkv, w_out, w_gate_up, w_down, cotangent, segment_ids, valid_mask
):
    rows = tokens.shape[0]
    length = segment_ids.shape[0]
    low = jnp.bfloat16
    me = lax.axis_index("tensor")
    order = [me, me ^ 1, me ^ 2, me ^ 3]
    rows_at = jnp.stack([at * rows for at in order] + [order[3] * rows + rows // 2]).astype(jnp.int32)
    index = lax.axis_index("dp")
    place, core = index // 2, index % 2
    line_order = jnp.where(place < 2, jnp.array([3, 2, 0, 1]), jnp.array([0, 1, 3, 2]))
    places = (
        (2 * line_order + 1 - core).astype(jnp.int32),
        (2 * line_order + core).astype(jnp.int32),
        ((place == 1) | (place == 2)).astype(jnp.int32).reshape(1),
    )
    chip = place.astype(jnp.int32).reshape(1)
    gain_one = gain_attn[None, :]
    gain_two = gain_mlp[None, :]

    tokens = after(tokens, rows_at, chip, *places)
    normed = norm(tokens, gain_one)
    near = gather_near(normed)
    cosine, sine, seg_col, valid_col = prepare(
        segment_ids.astype(jnp.float32)[None, :],
        valid_mask.astype(jnp.float32)[None, :],
    )
    near = (near[0], near[1], after(near[2], cosine))
    guest_cot_own = to_inner(cotangent)
    blocks = gather_far(*near)
    cot_near = gather_near(after(cotangent, *blocks))
    normed_all, queries, keys, values = project(
        rows_at, [after(blocks[0], guest_cot_own)] + blocks[1:], w_qkv, cosine, sine
    )
    *sent, probs, mixed = attend_square(
        rows_at,
        after(queries, *cot_near),
        keys,
        values,
        w_out,
        segment_ids.astype(jnp.float32)[None, :],
        seg_col,
        valid_col,
    )
    guest_cot_near = [to_inner(part) for part in cot_near[1:]]
    keep, to_x, to_y = scatter_far(*sent)
    cot_blocks = gather_far(*(after(part, to_x) for part in cot_near))
    got = scatter_near(keep, to_x, to_y)
    d_hidden, cot_all = back_through_down(
        [after(cot_blocks[0], *guest_cot_near)] + cot_blocks[1:], w_down
    )
    middle, normed_two = make_middle(tokens, after(got[0], cot_all), *got[1:], gain_two)

    near = gather_near(normed_two)
    guest_cot_far = [to_inner(part) for part in cot_blocks[3:]]
    guest_own = to_inner(after(normed_two, *guest_cot_far))
    blocks = gather_far(*near)
    normed_two_all, hidden, d_gate_up = mlp(
        [after(blocks[0], *guest_cot_far)] + blocks[1:], d_hidden, w_gate_up
    )
    guest_near = [to_inner(part) for part in near[1:]]
    guest_far = [to_inner(part) for part in blocks[3:]]
    sent = mlp_back(d_gate_up, w_gate_up)
    keep, to_x, to_y = scatter_far(*sent)
    to_x = after(to_x, guest_own, *guest_near)
    guest_d_hidden, guest_cot_all = back_through_down(
        [after(guest_cot_own, to_x), *guest_cot_near, *guest_cot_far], w_down
    )
    got = scatter_near(keep, to_x, to_y)
    d_middle, gain_two_part, d_middle_low = norm_back(
        cotangent, after(got[0], guest_d_hidden), *got[1:], middle, gain_two, True
    )
    near = gather_near(d_middle_low)
    guest_normed_two, guest_hidden, guest_d_gate_up = mlp(
        [after(guest_own, d_middle_low), *guest_near, *guest_far], guest_d_hidden, w_gate_up
    )
    down = Weight(places, [([cot_all, guest_cot_all], [hidden, guest_hidden])])
    down.sibling_part()
    gate = Weight(
        places,
        [
            (
                [normed_two_all, after(guest_normed_two, down.sibling_sum)],
                [d_gate_up, guest_d_gate_up],
            )
        ],
    )
    gate.sibling_part()
    blocks = gather_far(*near)
    down_outer = down.own_part(0, 1, gate.sibling_sum)
    down_own = down.own_part(1, 1, down_outer)
    gate_outer = gate.own_part(0, 1, down_own)
    gate_own = gate.own_part(1, 1, gate_outer)

    down_crossed = over_middle(down_outer)
    d_middle_all, d_project = attend_back_square(
        rows_at,
        blocks,
        w_out,
        after(probs, gate_own, down_crossed),
        queries,
        keys,
        values,
        cosine,
        sine,
    )
    down_outer, down_own = down_crossed, over_middle(down_own)
    gate_outer, gate_own = over_middle(gate_outer), over_middle(gate_own)
    late = Weight(places, [([normed_all], [d_project]), ([d_middle_all], [mixed])])
    late.sibling_part()
    sent = project_back(rows_at, after(d_project, late.sibling_sum), w_qkv)
    late_far = [late.own_part(0, 1, *sent)]
    late_far += [late.own_part(1, 1, late_far[0])]
    late_arrived = [to_inner(part) for part in late_far]
    keep, to_x, to_y = scatter_far(sent[0], after(sent[1], late_far[1], gate_outer), *sent[2:])
    late_near = [late.own_part(2, 1, to_x, to_y)]
    late_near += [late.own_part(3, 1, late_near[0])]
    late_near_arrived = to_inner(late_near[1])
    got = scatter_near(keep, to_x, to_y)
    down_near = [down.own_part(2, 1, late_near[1])]
    down_near += [down.own_part(3, 1, down_near[0])]
    down_given = to_outer(hand(after(down_near[0], down_near[1]), down_outer))
    d_inputs, gain_one_part = norm_back(
        d_middle,
        after(got[0], *down_near, late_arrived[0], down_own),
        *got[1:],
        tokens,
        gain_one,
        False,
    )
    sent = through_down(after(hidden, d_inputs), w_down)
    keep, to_x, to_y = scatter_far(*sent)
    gate_near = [gate.own_part(2, 1, to_x, to_y)]
    gate_near += [gate.own_part(3, 1, gate_near[0])]
    inner = places[2]
    units, wide = w_down.shape[0], w_qkv.shape[2]
    (grad_down,) = finish(
        inner,
        [after(down_near[1], gate_near[1], late_arrived[1]), down_own],
        [down_given],
        [(1, units, True)],
    )
    gate_given = to_outer(hand(after(gate_near[0], grad_down), gate_outer))
    gains = sum_flips(
        after(jnp.concatenate([gain_one_part, gain_two_part], axis=0), gate_near[1]),
        ("dp", 8, 1),
        ("tensor", 4, 1),
        ("tensor", 4, 2),
    )
    gains = [gains] + [up_the_line(gains, chips) for chips in (1, 2, 3)]
    keep, got_x, got_y = scatter_near(keep, to_x, to_y)
    output = (middle + keep + got_x.astype(jnp.float32) + got_y.astype(jnp.float32)).astype(low)
    late_far[0] = after(late_far[0], output, grad_down, gate_own)
    late_outer, late_own = join(late_far, late_arrived)
    late_outer, late_own = over_middle(late_outer), over_middle(late_own)
    grad_gains = sum_gains(chip, [after(gains[0], output), *gains[1:]])
    (grad_gate_up,) = finish(
        inner,
        [after(gate_near[1], grad_gains, late_near_arrived), gate_own],
        [gate_given],
        [(2, units, False)],
    )
    late_given = to_outer(hand(after(late_near[0], grad_gate_up), late_outer))
    grad_qkv, grad_out = finish(
        inner,
        [late_near[1], late_near_arrived, late_own],
        [late_near[0], late_given],
        [(3, wide, False), (1, wide, True)],
    )
    return (
        output,
        d_inputs,
        grad_gains[0],
        grad_gains[1],
        grad_qkv,
        grad_out,
        grad_gate_up,
        grad_down,
    )


def solution(mesh):
    placed = (
        P(("dp", "tensor"), None),
        P(),
        P(),
        P(None, None, "tensor"),
        P("tensor", None),
        P(None, None, "tensor"),
        P("tensor", None),
        P(("dp", "tensor"), None),
        P("dp"),
        P("dp"),
    )
    square = mesh.shape["tensor"] == 4 and mesh.shape["dp"] == 8
    return jax.shard_map(
        per_device_square if square else per_device,
        mesh=mesh,
        in_specs=placed,
        out_specs=(
            P(("dp", "tensor"), None),
            P(("dp", "tensor"), None),
            P(),
            P(),
            P(None, "dp", "tensor"),
            P("tensor", "dp"),
            P(None, "dp", "tensor"),
            P("tensor", "dp"),
        ),
        check_vma=False,
    )
```

```python
import functools
import math

import jax
import jax.numpy as jnp
from jax import lax
from jax.experimental import pallas as pl
from jax.experimental.pallas import tpu as pltpu
from jax.sharding import PartitionSpec as P

HD = 128


EPS = 1e-06
THETA = 10000.0


def rope_tables(places):
    positions = places.astype(jnp.float32)
    freqs = THETA ** (-(jnp.arange(HD // 2).astype(jnp.float32) * 2.0 / HD))
    angles = positions[:, None] * freqs[None, :]
    return (jnp.cos(angles), jnp.sin(angles))


def rotate(values, cosine, sine):
    half = values.shape[-1] // 2
    first = values[..., :half]
    second = values[..., half:]
    cosine = cosine[:, None, :]
    sine = sine[:, None, :]
    return jnp.concatenate(
        [first * cosine - second * sine, second * cosine + first * sine], axis=-1
    )


def block_scores(q_block, keys_rot, start, segments, valid):
    block_rows = q_block.shape[0]
    length = keys_rot.shape[0]
    key_pos = jnp.arange(length)
    row_pos = start + jnp.arange(block_rows)
    row_seg = lax.dynamic_slice_in_dim(segments, start, block_rows, 0)
    scores = jnp.einsum(
        "qhd,khd->hqk", q_block, keys_rot, preferred_element_type=jnp.float32
    ) * HD ** (-0.5)
    allowed = (
        (key_pos[None, :] <= row_pos[:, None])
        & (row_seg[:, None] == segments[None, :])
        & ((valid[None, :] == 1) | (key_pos[None, :] == row_pos[:, None]))
    )
    return jnp.where(allowed[None], scores, -1e30)


def attend(queries, keys_rot, values, segments, valid):
    length = queries.shape[0]
    block_rows = min(512, length)
    count = length // block_rows

    def one_block(index):
        start = index * block_rows
        q_block = lax.dynamic_slice_in_dim(queries, start, block_rows, 0)
        scores = block_scores(q_block, keys_rot, start, segments, valid)
        top = jnp.max(scores, axis=-1, keepdims=True)
        expo = jnp.exp(scores - top)
        total = jnp.sum(expo, axis=-1, keepdims=True)
        probs = (expo / total).astype(jnp.bfloat16)
        result = jnp.einsum("hqk,khd->qhd", probs, values, preferred_element_type=jnp.float32)
        return (result, top[..., 0] + jnp.log(total[..., 0]))

    blocks, log_sums = lax.map(one_block, jnp.arange(count))
    return (blocks.reshape(length, -1), log_sums)


def attend_back(queries, keys_rot, values, d_mixed, log_sums, segments, valid):
    length = queries.shape[0]
    block_rows = min(512, length)
    count = length // block_rows
    scale = HD ** (-0.5)

    def one_block(carry, index):
        d_keys, d_values = carry
        start = index * block_rows
        q_block = lax.dynamic_slice_in_dim(queries, start, block_rows, 0)
        d_block = lax.dynamic_slice_in_dim(d_mixed, start, block_rows, 0)
        scores = block_scores(q_block, keys_rot, start, segments, valid)
        probs = jnp.exp(scores - log_sums[index][..., None])
        d_values = d_values + jnp.einsum(
            "hqk,qhd->khd", probs.astype(jnp.bfloat16), d_block, preferred_element_type=jnp.float32
        )
        d_probs = jnp.einsum("qhd,khd->hqk", d_block, values, preferred_element_type=jnp.float32)
        delta = jnp.sum(d_probs * probs, axis=-1, keepdims=True)
        d_scores = (probs * (d_probs - delta)).astype(jnp.bfloat16)
        d_query = scale * jnp.einsum(
            "hqk,khd->qhd", d_scores, keys_rot, preferred_element_type=jnp.float32
        )
        d_keys = d_keys + scale * jnp.einsum(
            "hqk,qhd->khd", d_scores, q_block, preferred_element_type=jnp.float32
        )
        return ((d_keys, d_values), d_query)

    empty = jnp.zeros(keys_rot.shape, jnp.float32)
    (d_keys, d_values), d_queries = lax.scan(one_block, (empty, empty), jnp.arange(count))
    return (d_queries.reshape(queries.shape), d_keys, d_values)


def per_device(
    tokens, gain_attn, gain_mlp, w_qkv, w_out, w_gate_up, w_down, cotangent, segment_ids, valid_mask
):
    length = segment_ids.shape[0]
    heads_here = w_qkv.shape[2] // HD
    shape3 = (length, heads_here, HD)
    incoming = tokens.astype(jnp.float32)
    gain_one = gain_attn.astype(jnp.float32)
    gain_two = gain_mlp.astype(jnp.float32)
    cosine, sine = rope_tables(jnp.arange(length))
    inv_one = lax.rsqrt(jnp.mean(incoming * incoming, axis=-1, keepdims=True) + EPS)
    normed = (incoming * inv_one * gain_one).astype(jnp.bfloat16)
    normed_all = lax.all_gather(normed, "tensor", axis=0, tiled=True)
    project = jnp.einsum("td,cde->cte", normed_all, w_qkv, preferred_element_type=jnp.float32)
    queries = rotate(project[0].reshape(shape3), cosine, sine).astype(jnp.bfloat16)
    keys_rot = rotate(project[1].reshape(shape3), cosine, sine).astype(jnp.bfloat16)
    values = project[2].reshape(shape3).astype(jnp.bfloat16)
    mixed, log_sums = attend(queries, keys_rot, values, segment_ids, valid_mask)
    mixed = mixed.astype(jnp.bfloat16)
    middle = incoming + lax.psum_scatter(
        jnp.dot(mixed, w_out, preferred_element_type=jnp.float32).astype(jnp.bfloat16),
        "tensor",
        scatter_dimension=0,
        tiled=True,
    ).astype(jnp.float32)
    inv_two = lax.rsqrt(jnp.mean(middle * middle, axis=-1, keepdims=True) + EPS)
    normed_two = (middle * inv_two * gain_two).astype(jnp.bfloat16)
    normed_two_all = lax.all_gather(normed_two, "tensor", axis=0, tiled=True)
    gate = jnp.dot(normed_two_all, w_gate_up[0], preferred_element_type=jnp.float32)
    upper = jnp.dot(normed_two_all, w_gate_up[1], preferred_element_type=jnp.float32)
    sigma = jax.nn.sigmoid(gate)
    hidden = (gate * sigma * upper).astype(jnp.bfloat16)
    result = middle + lax.psum_scatter(
        jnp.dot(hidden, w_down, preferred_element_type=jnp.float32).astype(jnp.bfloat16),
        "tensor",
        scatter_dimension=0,
        tiled=True,
    ).astype(jnp.float32)
    output = result.astype(jnp.bfloat16)
    cot_all = lax.all_gather(cotangent, "tensor", axis=0, tiled=True)
    d_hidden = jnp.einsum("td,fd->tf", cot_all, w_down, preferred_element_type=jnp.float32)
    grad_down = jnp.einsum("tf,td->fd", hidden, cot_all, preferred_element_type=jnp.float32)
    d_upper = (d_hidden * gate * sigma).astype(jnp.bfloat16)
    d_gate = (d_hidden * upper * sigma * (1.0 + gate * (1.0 - sigma))).astype(jnp.bfloat16)
    grad_gate_up = jnp.stack(
        [
            jnp.einsum("td,tf->df", normed_two_all, d_gate, preferred_element_type=jnp.float32),
            jnp.einsum("td,tf->df", normed_two_all, d_upper, preferred_element_type=jnp.float32),
        ]
    )
    d_normed_two = lax.psum_scatter(
        (
            jnp.einsum("tf,df->td", d_gate, w_gate_up[0], preferred_element_type=jnp.float32)
            + jnp.einsum("tf,df->td", d_upper, w_gate_up[1], preferred_element_type=jnp.float32)
        ).astype(jnp.bfloat16),
        "tensor",
        scatter_dimension=0,
        tiled=True,
    ).astype(jnp.float32)
    scaled_two = gain_two * d_normed_two
    d_middle = (
        cotangent.astype(jnp.float32)
        + inv_two * scaled_two
        - middle * inv_two**3 * jnp.mean(scaled_two * middle, axis=-1, keepdims=True)
    )
    grad_gain_two = jnp.sum(d_normed_two * middle * inv_two, axis=0)
    d_middle_all = lax.all_gather(d_middle.astype(jnp.bfloat16), "tensor", axis=0, tiled=True)
    d_mixed = jnp.einsum(
        "td,ed->te", d_middle_all, w_out, preferred_element_type=jnp.float32
    ).astype(jnp.bfloat16)
    grad_out = jnp.einsum("te,td->ed", mixed, d_middle_all, preferred_element_type=jnp.float32)
    d_queries, d_keys, d_values = attend_back(
        queries, keys_rot, values, d_mixed.reshape(shape3), log_sums, segment_ids, valid_mask
    )
    d_project = jnp.stack(
        [
            rotate(d_queries, cosine, -sine).reshape(length, -1),
            rotate(d_keys, cosine, -sine).reshape(length, -1),
            d_values.reshape(length, -1),
        ]
    ).astype(jnp.bfloat16)
    grad_qkv = jnp.einsum("td,cte->cde", normed_all, d_project, preferred_element_type=jnp.float32)
    d_normed = lax.psum_scatter(
        jnp.einsum("cte,cde->td", d_project, w_qkv, preferred_element_type=jnp.float32).astype(
            jnp.bfloat16
        ),
        "tensor",
        scatter_dimension=0,
        tiled=True,
    ).astype(jnp.float32)
    scaled_one = gain_one * d_normed
    d_inputs = (
        d_middle
        + inv_one * scaled_one
        - incoming * inv_one**3 * jnp.mean(scaled_one * incoming, axis=-1, keepdims=True)
    )
    grad_gain_one = jnp.sum(d_normed * incoming * inv_one, axis=0)
    grad_gain_one, grad_gain_two = lax.psum((grad_gain_one, grad_gain_two), ("dp", "tensor"))
    grad_qkv, grad_out, grad_gate_up, grad_down = (
        lax.psum_scatter(
            grad_qkv.astype(jnp.bfloat16), "dp", scatter_dimension=1, tiled=True
        ).astype(jnp.float32),
        lax.psum_scatter(
            grad_out.astype(jnp.bfloat16), "dp", scatter_dimension=1, tiled=True
        ).astype(jnp.float32),
        lax.psum_scatter(
            grad_gate_up.astype(jnp.bfloat16), "dp", scatter_dimension=1, tiled=True
        ).astype(jnp.float32),
        lax.psum_scatter(
            grad_down.astype(jnp.bfloat16), "dp", scatter_dimension=1, tiled=True
        ).astype(jnp.float32),
    )
    return (
        output,
        d_inputs,
        grad_gain_one,
        grad_gain_two,
        grad_qkv,
        grad_out,
        grad_gate_up,
        grad_down,
    )


NT = (((1,), (1,)), ((), ()))
TN = (((0,), (0,)), ((), ()))
MEGA = 1024 * 1024


def chunks(total, step):
    return [(at, min(step, total - at)) for at in range(0, total, step)]


def dot(left, right, dims=None):
    if dims is None:
        return jnp.dot(left, right, preferred_element_type=jnp.float32)
    return lax.dot_general(left, right, dims, preferred_element_type=jnp.float32)


def in_vmem(count):
    return [pl.BlockSpec(memory_space=pltpu.VMEM)] * count


def in_smem():
    return [pl.BlockSpec(memory_space=pltpu.SMEM)]


def like(shape, kind=jnp.bfloat16):
    return jax.ShapeDtypeStruct(shape, kind)


def limit(megabytes):
    return pltpu.CompilerParams(vmem_limit_bytes=megabytes * MEGA)


def starts_of(blocks):
    at, starts = 0, []
    for block in blocks:
        starts.append((at, block.shape[0]))
        at += block.shape[0]
    return starts


def send_shapes(rows, width):
    half = rows // 2
    return [
        like((rows, width), jnp.float32),
        like((rows, width)),
        like((rows, width)),
        like((half, width)),
        like((half, width)),
    ]


def store_parts(part, targets, cols):
    for (start, rows), target in zip(starts_of(targets), targets):
        target[:, cols] = part[start : start + rows].astype(target.dtype)


def norm_kernel(tokens, gain, normed):
    wide = tokens[...].astype(jnp.float32)
    inverse = lax.rsqrt(jnp.mean(wide * wide, axis=-1, keepdims=True) + EPS)
    normed[...] = (wide * inverse * gain[...].astype(jnp.float32)).astype(jnp.bfloat16)


def norm(tokens, gain):
    return pl.pallas_call(
        norm_kernel,
        name="norm",
        out_shape=like(tokens.shape),
        in_specs=in_vmem(2),
        out_specs=in_vmem(1)[0],
        compiler_params=limit(4),
    )(tokens, gain)


def relay_kernel(to_x, to_y, via_x, via_y, next_x, next_y):
    half = via_x.shape[0]
    next_x[:half] = to_x[:half]
    next_x[half:] = (
        to_x[half:].astype(jnp.float32) + via_y[...].astype(jnp.float32)
    ).astype(jnp.bfloat16)
    next_y[:half] = (
        to_y[:half].astype(jnp.float32) + via_x[...].astype(jnp.float32)
    ).astype(jnp.bfloat16)
    next_y[half:] = to_y[half:]


def relay(to_x, to_y, via_x, via_y):
    return pl.pallas_call(
        relay_kernel,
        name="relay",
        out_shape=[like(to_x.shape), like(to_y.shape)],
        in_specs=in_vmem(4),
        out_specs=in_vmem(2),
        compiler_params=limit(4),
    )(to_x, to_y, via_x, via_y)


def middle_kernel(tokens, keep, got_x, got_y, gain, middle, normed):
    total = (
        tokens[...].astype(jnp.float32)
        + keep[...]
        + got_x[...].astype(jnp.float32)
        + got_y[...].astype(jnp.float32)
    )
    middle[...] = total
    inverse = lax.rsqrt(jnp.mean(total * total, axis=-1, keepdims=True) + EPS)
    normed[...] = (total * inverse * gain[...].astype(jnp.float32)).astype(jnp.bfloat16)


def make_middle(tokens, keep, got_x, got_y, gain):
    return pl.pallas_call(
        middle_kernel,
        name="make_middle",
        out_shape=[like(keep.shape, jnp.float32), like(keep.shape)],
        in_specs=in_vmem(5),
        out_specs=in_vmem(2),
        compiler_params=limit(6),
    )(tokens, keep, got_x, got_y, gain)


def norm_back_kernel(base, keep, got_x, got_y, source, gain, *outs):
    d_normed = keep[...] + got_x[...].astype(jnp.float32) + got_y[...].astype(jnp.float32)
    wide = source[...].astype(jnp.float32)
    inverse = lax.rsqrt(jnp.mean(wide * wide, axis=-1, keepdims=True) + EPS)
    scaled = gain[...].astype(jnp.float32) * d_normed
    slope = jnp.mean(scaled * wide, axis=-1, keepdims=True) * inverse * inverse * inverse
    total = base[...].astype(jnp.float32) + inverse * scaled - wide * slope
    outs[0][...] = total
    outs[1][...] = jnp.sum(d_normed * wide * inverse, axis=0, keepdims=True)
    if len(outs) == 3:
        outs[2][...] = total.astype(jnp.bfloat16)


def norm_back(base, keep, got_x, got_y, source, gain, low):
    return pl.pallas_call(
        norm_back_kernel,
        name="norm_back",
        out_shape=[like(keep.shape, jnp.float32), like((1, keep.shape[1]), jnp.float32)]
        + [like(keep.shape)] * low,
        in_specs=in_vmem(6),
        out_specs=in_vmem(2 + low),
        compiler_params=limit(8),
    )(base, keep, got_x, got_y, source, gain)


def prepare_kernel(segments, valid, cosine, sine, seg_col, valid_col):
    length = cosine.shape[0]
    half = HD // 2
    place = lax.broadcasted_iota(jnp.int32, (length, HD), 0).astype(jnp.float32)
    lane = lax.broadcasted_iota(jnp.int32, (length, HD), 1)
    step = jnp.where(lane < half, lane, lane - half).astype(jnp.float32)
    angle = place * jnp.exp(step * (-2.0 / HD * math.log(THETA)))
    cosine[...] = jnp.cos(angle)
    turn = jnp.sin(angle)
    sine[...] = jnp.where(lane < half, -turn, turn)
    seg_col[...] = jnp.broadcast_to(segments[...], (HD, length)).T
    valid_col[...] = jnp.broadcast_to(valid[...], (HD, length)).T


def prepare(segments, valid):
    length = segments.shape[1]
    return pl.pallas_call(
        prepare_kernel,
        name="prepare",
        out_shape=[like((length, HD), jnp.float32)] * 4,
        in_specs=in_vmem(2),
        out_specs=in_vmem(4),
        compiler_params=limit(6),
    )(segments, valid)


def project_kernel(
    rows_at, own, from_x, from_y, low, high, w_qkv, cosine, sine, normed, queries, keys, values
):
    for i, block in enumerate((own, from_x, from_y, low, high)):
        place = pl.multiple_of(rows_at[i], 64)
        normed[pl.ds(place, block.shape[0]), :] = block[...]
    for c, target in enumerate((queries, keys, values)):
        for at, size in chunks(target.shape[1], 2 * HD):
            part = dot(normed[...], w_qkv[c, :, at : at + size])
            for head in range(0, size, HD):
                piece = part[:, head : head + HD]
                if c < 2:
                    piece = piece * cosine[...] + pltpu.roll(piece, HD // 2, 1) * sine[...]
                target[:, at + head : at + head + HD] = piece.astype(jnp.bfloat16)


def project(rows_at, blocks, w_qkv, cosine, sine):
    rows, width = blocks[0].shape
    length = 4 * rows
    wide = w_qkv.shape[2]
    return pl.pallas_call(
        project_kernel,
        name="project",
        out_shape=[like((length, width))] + [like((length, wide))] * 3,
        in_specs=in_smem() + in_vmem(8),
        out_specs=in_vmem(4),
        compiler_params=limit(8),
    )(rows_at, *blocks, w_qkv, cosine, sine)


def attend_kernel(
    rows_at, queries, keys, values, w_out, seg_row, seg_col, valid_col,
    keep, to_x, to_y, far_low, far_high, probs, mixed, bias, joined,
):
    length, wide = queries.shape
    key_at = lax.broadcasted_iota(jnp.int32, (length, length), 0)
    query_at = lax.broadcasted_iota(jnp.int32, (length, length), 1)
    allowed = (
        (key_at <= query_at)
        & (seg_col[:, 0:1] == seg_row[...])
        & ((valid_col[:, 0:1] == 1.0) | (key_at == query_at))
    )
    bias[...] = jnp.where(allowed, 0.0, -1e30)
    for at in range(0, wide, HD):
        head = at // HD
        cols = slice(at, at + HD)
        for q_at, q_size in chunks(length, 256):
            seen = q_at + q_size
            scores = dot(keys[0:seen, cols], queries[q_at:seen, cols], NT)
            scores = scores * HD ** (-0.5) + bias[0:seen, q_at:seen]
            top = jnp.max(scores, axis=0, keepdims=True)
            expo = jnp.exp(scores - top)
            total = jnp.sum(expo, axis=0, keepdims=True)
            chance = (expo * (1.0 / total)).astype(jnp.bfloat16)
            probs[head, 0:seen, q_at:seen] = chance
            result = dot(values[0:seen, cols], chance, TN)
            joined[q_at:seen, cols] = result.T.astype(jnp.bfloat16)
    targets = [keep, to_x, to_y, far_low, far_high]
    for i, (start, size) in enumerate(starts_of(targets)):
        place = pl.multiple_of(rows_at[i], 64)
        mixed[start : start + size, :] = joined[pl.ds(place, size), :]
    for at, size in chunks(w_out.shape[1], 512):
        store_parts(dot(mixed[...], w_out[:, at : at + size]), targets, slice(at, at + size))


def attend_square(rows_at, queries, keys, values, w_out, seg_row, seg_col, valid_col):
    length, wide = queries.shape
    width = w_out.shape[1]
    heads = wide // HD
    return pl.pallas_call(
        attend_kernel,
        name="attend",
        out_shape=send_shapes(length // 4, width)
        + [like((heads, length, length)), like((length, wide))],
        in_specs=in_smem() + in_vmem(7),
        out_specs=in_vmem(7),
        scratch_shapes=[
            pltpu.VMEM((length, length), jnp.float32),
            pltpu.VMEM((length, wide), jnp.bfloat16),
        ],
        compiler_params=limit(8),
    )(rows_at, queries, keys, values, w_out, seg_row, seg_col, valid_col)


def d_hidden_kernel(own, from_x, from_y, low, high, w_down, d_hidden, cot_all):
    blocks = [own, from_x, from_y, low, high]
    for (start, size), block in zip(starts_of(blocks), blocks):
        cot_all[start : start + size, :] = block[...]
    for at, size in chunks(w_down.shape[0], 256):
        d_hidden[:, at : at + size] = dot(cot_all[...], w_down[at : at + size, :], NT)


def back_through_down(blocks, w_down):
    rows, width = blocks[0].shape
    length = 4 * rows
    units = w_down.shape[0]
    return pl.pallas_call(
        d_hidden_kernel,
        name="back_through_down",
        out_shape=[like((length, units), jnp.float32), like((length, width))],
        in_specs=in_vmem(6),
        out_specs=in_vmem(2),
        compiler_params=limit(6),
    )(*blocks, w_down)


def mlp_kernel(
    own, from_x, from_y, low, high, d_hidden, w_gate_up, normed, hidden, d_gate_up
):
    units = w_gate_up.shape[2]
    blocks = [own, from_x, from_y, low, high]
    for (start, size), block in zip(starts_of(blocks), blocks):
        normed[start : start + size, :] = block[...]
    for at, size in chunks(units, 256):
        here = slice(at, at + size)
        gate = dot(normed[...], w_gate_up[0, :, here])
        upper = dot(normed[...], w_gate_up[1, :, here])
        incoming = d_hidden[:, here]
        sigma = 1.0 / (1.0 + jnp.exp(-gate))
        silu = gate * sigma
        hidden[:, here] = (silu * upper).astype(jnp.bfloat16)
        d_gate_up[:, here] = (incoming * upper * sigma * (1.0 + gate * (1.0 - sigma))).astype(
            jnp.bfloat16
        )
        d_gate_up[:, units + at : units + at + size] = (incoming * silu).astype(jnp.bfloat16)


def mlp(blocks, d_hidden, w_gate_up):
    rows, width = blocks[0].shape
    length = 4 * rows
    units = w_gate_up.shape[2]
    return pl.pallas_call(
        mlp_kernel,
        name="mlp",
        out_shape=[like((length, width)), like((length, units)), like((length, 2 * units))],
        in_specs=in_vmem(7),
        out_specs=in_vmem(3),
        compiler_params=limit(8),
    )(*blocks, d_hidden, w_gate_up)


def mlp_back_kernel(d_gate_up, w_gate_up, *targets):
    units = w_gate_up.shape[2]
    for at, size in chunks(w_gate_up.shape[1], 256):
        part = dot(d_gate_up[:, 0:units], w_gate_up[0, at : at + size, :], NT) + dot(
            d_gate_up[:, units : 2 * units], w_gate_up[1, at : at + size, :], NT
        )
        store_parts(part, targets, slice(at, at + size))


def mlp_back(d_gate_up, w_gate_up):
    return pl.pallas_call(
        mlp_back_kernel,
        name="mlp_back",
        out_shape=send_shapes(d_gate_up.shape[0] // 4, w_gate_up.shape[1]),
        in_specs=in_vmem(2),
        out_specs=in_vmem(5),
        compiler_params=limit(6),
    )(d_gate_up, w_gate_up)


def down_kernel(hidden, w_down, *targets):
    for at, size in chunks(w_down.shape[1], 256):
        store_parts(dot(hidden[...], w_down[:, at : at + size]), targets, slice(at, at + size))


def through_down(hidden, w_down):
    return pl.pallas_call(
        down_kernel,
        name="through_down",
        out_shape=send_shapes(hidden.shape[0] // 4, w_down.shape[1]),
        in_specs=in_vmem(2),
        out_specs=in_vmem(5),
        compiler_params=limit(6),
    )(hidden, w_down)


def attend_back_kernel(
    rows_at, own, from_x, from_y, low, high, w_out, probs, queries, keys, values, cosine, sine,
    d_middle, d_project, d_mixed,
):
    length, wide = queries.shape
    blocks = [own, from_x, from_y, low, high]
    starts = starts_of(blocks)
    for (start, size), block in zip(starts, blocks):
        d_middle[start : start + size, :] = block[...]
    for at, size in chunks(wide, 256):
        part = dot(d_middle[...], w_out[at : at + size, :], NT).astype(jnp.bfloat16)
        for i, (start, rows) in enumerate(starts):
            place = pl.multiple_of(rows_at[i], 64)
            d_mixed[pl.ds(place, rows), at : at + size] = part[start : start + rows]
    scale = HD ** (-0.5)

    def back(turned, rows):
        return turned * cosine[rows, :] - pltpu.roll(turned, HD // 2, 1) * sine[rows, :]

    for at in range(0, wide, HD):
        head = at // HD
        cols = slice(at, at + HD)
        d_keys = d_values = None
        for q_at, q_size in reversed(chunks(length, 256)):
            seen = q_at + q_size
            rows = slice(q_at, seen)
            chance = probs[head, 0:seen, rows]
            d_out = d_mixed[rows, cols]
            d_chance = dot(values[0:seen, cols], d_out, NT)
            exact = chance.astype(jnp.float32)
            delta = jnp.sum(d_chance * exact, axis=0, keepdims=True)
            d_scores = (exact * (d_chance - delta)).astype(jnp.bfloat16)
            more_values = dot(chance, d_out)
            more_keys = dot(d_scores, queries[rows, cols])
            d_queries = dot(keys[0:seen, cols], d_scores, TN).T
            d_project[rows, cols] = back(d_queries * scale, rows).astype(jnp.bfloat16)
            if d_keys is None:
                d_keys, d_values = more_keys, more_values
            else:
                d_keys = jnp.concatenate([d_keys[:seen] + more_keys, d_keys[seen:]], axis=0)
                d_values = jnp.concatenate([d_values[:seen] + more_values, d_values[seen:]], axis=0)
        d_project[:, wide + at : wide + at + HD] = back(d_keys * scale, slice(0, length)).astype(
            jnp.bfloat16
        )
        d_project[:, 2 * wide + at : 2 * wide + at + HD] = d_values.astype(jnp.bfloat16)


def attend_back_square(rows_at, blocks, w_out, probs, queries, keys, values, cosine, sine):
    length, wide = queries.shape
    return pl.pallas_call(
        attend_back_kernel,
        name="attend_back",
        out_shape=[like((length, w_out.shape[1])), like((length, 3 * wide))],
        in_specs=in_smem() + in_vmem(12),
        out_specs=in_vmem(2),
        scratch_shapes=[pltpu.VMEM((length, wide), jnp.bfloat16)],
        compiler_params=limit(8),
    )(rows_at, *blocks, w_out, probs, queries, keys, values, cosine, sine)


def project_back_kernel(rows_at, d_project, w_qkv, *refs):
    targets, turned = refs[:5], refs[5]
    wide = w_qkv.shape[2]
    for i, (start, size) in enumerate(starts_of(targets)):
        place = pl.multiple_of(rows_at[i], 64)
        turned[start : start + size, :] = d_project[pl.ds(place, size), :]
    for at, size in chunks(w_qkv.shape[1], 256):
        part = sum(
            dot(turned[:, c * wide : (c + 1) * wide], w_qkv[c, at : at + size, :], NT)
            for c in range(3)
        )
        store_parts(part, targets, slice(at, at + size))


def project_back(rows_at, d_project, w_qkv):
    return pl.pallas_call(
        project_back_kernel,
        name="project_back",
        out_shape=send_shapes(d_project.shape[0] // 4, w_qkv.shape[1]),
        in_specs=in_smem() + in_vmem(2),
        out_specs=in_vmem(5),
        scratch_shapes=[pltpu.VMEM(d_project.shape, jnp.bfloat16)],
        compiler_params=limit(8),
    )(rows_at, d_project, w_qkv)


def weight_kernel(layout, base, spot, which, *refs):
    turned, out = refs[-1], refs[-2]
    more = refs[-3] if spot is not None else None
    count, piece, _ = out.shape
    for i in range(count):
        place = pl.multiple_of(which[base + i] * piece, piece)
        at_ref = column = 0
        for pairs in layout:
            splits = refs[at_ref : at_ref + pairs]
            others = refs[at_ref + pairs : at_ref + 2 * pairs]
            at_ref += 2 * pairs
            length, across = others[0].shape
            for j, split in enumerate(splits):
                turned[:, j * length : (j + 1) * length] = split[:, pl.ds(place, piece)].T
            for at, size in chunks(across, 256):
                part = None
                for j, other in enumerate(others):
                    term = dot(turned[:, j * length : (j + 1) * length], other[:, at : at + size])
                    part = term if part is None else part + term
                cols = slice(column + at, column + at + size)
                if more is not None:
                    part = part + more[spot + i, :, cols].astype(jnp.float32)
                out[i, :, cols] = part.astype(out.dtype)
            column += across


def weight_pieces(which, base, count, groups, more=None, spot=None):
    layout = [len(splits) for splits, _ in groups]
    refs = [ref for splits, others in groups for ref in (*splits, *others)]
    extra = [] if more is None else [more]
    length = groups[0][1][0].shape[0]
    across = sum(others[0].shape[1] for _, others in groups)
    piece = groups[0][0][0].shape[1] // 8
    return pl.pallas_call(
        functools.partial(weight_kernel, layout, base, spot),
        name="weight_pieces",
        out_shape=like((count, piece, across)),
        in_specs=in_smem() + in_vmem(len(refs) + len(extra)),
        out_specs=in_vmem(1)[0],
        scratch_shapes=[pltpu.VMEM((piece, max(layout) * length), jnp.bfloat16)],
        compiler_params=limit(16),
    )(which, *refs, *extra)


def join_kernel(here_outer, here_own, there_outer, there_own, outer, own):
    for here, there, out in ((here_outer, there_outer, outer), (here_own, there_own, own)):
        for at, size in chunks(out.shape[2], 256):
            cols = slice(at, at + size)
            out[0, :, cols] = (
                here[0, :, cols].astype(jnp.float32) + there[0, :, cols].astype(jnp.float32)
            ).astype(jnp.bfloat16)


def join(here, there):
    shape = here[0].shape
    return pl.pallas_call(
        join_kernel,
        name="join",
        out_shape=[like(shape), like(shape)],
        in_specs=in_vmem(4),
        out_specs=in_vmem(2),
        compiler_params=limit(6),
    )(*here, *there)


def hand_kernel(near, far, out):
    for at, size in chunks(out.shape[1], 256):
        cols = slice(at, at + size)
        out[:, cols] = (
            near[0, :, cols].astype(jnp.float32) + far[0, :, cols].astype(jnp.float32)
        ).astype(jnp.bfloat16)


def hand(near, far):
    return pl.pallas_call(
        hand_kernel,
        name="hand",
        out_shape=like(near.shape[1:]),
        in_specs=in_vmem(2),
        out_specs=in_vmem(1)[0],
        compiler_params=limit(6),
    )(near, far)


def finish_kernel(parts, count_inner, inner, *refs):
    count = len(refs) - len(parts)
    here = [ref for ref in refs[:count_inner]]
    outer = [ref for ref in refs[count_inner:count]]

    def total(sources, cols):
        found = None
        for source in sources:
            term = source[0, :, cols] if len(source.shape) == 3 else source[:, cols]
            term = term.astype(jnp.float32)
            found = term if found is None else found + term
        return found

    column = 0
    for (planes, across, turn), out in zip(parts, refs[count:]):
        for c in range(planes):
            for at, size in chunks(across, 256):
                cols = slice(column + at, column + at + size)
                value = jnp.where(inner[0] == 1, total(here, cols), total(outer, cols))
                if turn:
                    out[at : at + size, :] = value.T
                else:
                    out[c, :, at : at + size] = value
            column += across


def finish(inner, here, outer, parts):
    piece = here[0].shape[-2]
    return pl.pallas_call(
        functools.partial(finish_kernel, parts, len(here)),
        name="finish",
        out_shape=[
            like((across, piece) if turn else (planes, piece, across), jnp.float32)
            for planes, across, turn in parts
        ],
        in_specs=in_smem() + in_vmem(len(here) + len(outer)),
        out_specs=in_vmem(len(parts)),
        compiler_params=limit(8),
    )(inner, *here, *outer)


def gains_kernel(chip, *refs):
    sources, out, kept = refs[:4], refs[4], refs[5]
    for back, source in enumerate(sources):
        kept[lax.rem(chip[0] + 4 - back, 4)] = source[...]
    out[...] = (kept[0] + kept[1]) + (kept[2] + kept[3])


def sum_gains(chip, sources):
    return pl.pallas_call(
        gains_kernel,
        name="sum_gains",
        out_shape=like(sources[0].shape, jnp.float32),
        in_specs=in_smem() + in_vmem(4),
        out_specs=in_vmem(1)[0],
        scratch_shapes=[pltpu.VMEM((4, *sources[0].shape), jnp.float32)],
        compiler_params=limit(4),
    )(chip, *sources)


def flips(size, bit):
    return [(i, i ^ bit) for i in range(size)]


def after(value, *earlier):
    return lax.optimization_barrier((value, *earlier))[0]


def over_tensor(values, bit):
    return lax.ppermute(values, "tensor", flips(4, bit))


def gather_near(own):
    return own, over_tensor(own, 1), over_tensor(own, 2)


def gather_far(own, from_x, from_y):
    half = own.shape[0] // 2
    low = over_tensor(from_y[:half], 1)
    high = over_tensor(from_x[half:], 2)
    return [own, from_x, from_y, low, high]


def scatter_far(keep, to_x, to_y, far_low, far_high):
    return keep, *relay(to_x, to_y, over_tensor(far_low, 1), over_tensor(far_high, 2))


def scatter_near(keep, to_x, to_y):
    return keep, over_tensor(to_x, 1), over_tensor(to_y, 2)


def over_cores(values):
    return lax.ppermute(values, "dp", flips(8, 1))


def up_the_line(values, chips):
    return lax.ppermute(values, "dp", [(i, (i + 2 * chips) % 8) for i in range(8)])


def to_inner(values):
    return lax.ppermute(values, "dp", [(0, 2), (1, 3), (6, 4), (7, 5)])


def to_outer(values):
    return lax.ppermute(values, "dp", [(2, 0), (3, 1), (4, 6), (5, 7)])


def over_middle(values):
    return lax.ppermute(values, "dp", [(2, 4), (3, 5), (4, 2), (5, 3)])


class Weight:
    def __init__(self, places, groups):
        self.which_theirs, self.which_mine, self.inner = places
        self.groups = groups

    def sibling_part(self):
        self.sibling_sum = weight_pieces(self.which_theirs, 0, 4, self.groups)
        self.theirs = over_cores(self.sibling_sum)

    def own_part(self, base, count, *earlier):
        more = after(self.theirs, *earlier) if earlier else self.theirs
        return weight_pieces(self.which_mine, base, count, self.groups, more, base)


def sum_flips(values, *steps):
    for axis, size, bit in steps:
        values = values + lax.ppermute(values, axis, flips(size, bit))
    return values


def per_device_square(
    tokens, gain_attn, gain_mlp, w_qkv, w_out, w_gate_up, w_down, cotangent, segment_ids, valid_mask
):
    rows = tokens.shape[0]
    length = segment_ids.shape[0]
    low = jnp.bfloat16
    me = lax.axis_index("tensor")
    order = [me, me ^ 1, me ^ 2, me ^ 3]
    rows_at = jnp.stack([at * rows for at in order] + [order[3] * rows + rows // 2]).astype(jnp.int32)
    index = lax.axis_index("dp")
    place, core = index // 2, index % 2
    line_order = jnp.where(place < 2, jnp.array([3, 2, 0, 1]), jnp.array([0, 1, 3, 2]))
    places = (
        (2 * line_order + 1 - core).astype(jnp.int32),
        (2 * line_order + core).astype(jnp.int32),
        ((place == 1) | (place == 2)).astype(jnp.int32).reshape(1),
    )
    chip = place.astype(jnp.int32).reshape(1)
    gain_one = gain_attn[None, :]
    gain_two = gain_mlp[None, :]

    tokens = after(tokens, rows_at, chip, *places)
    normed = norm(tokens, gain_one)
    near = gather_near(normed)
    cosine, sine, seg_col, valid_col = prepare(
        segment_ids.astype(jnp.float32)[None, :],
        valid_mask.astype(jnp.float32)[None, :],
    )
    near = (near[0], near[1], after(near[2], cosine))
    guest_cot_own = to_inner(cotangent)
    blocks = gather_far(*near)
    cot_near = gather_near(after(cotangent, *blocks))
    normed_all, queries, keys, values = project(
        rows_at, blocks, w_qkv, cosine, sine
    )
    *sent, probs, mixed = attend_square(
        rows_at,
        after(queries, *cot_near, guest_cot_own),
        keys,
        values,
        w_out,
        segment_ids.astype(jnp.float32)[None, :],
        seg_col,
        valid_col,
    )
    guest_cot_near = [to_inner(part) for part in cot_near[1:]]
    keep, to_x, to_y = scatter_far(*sent)
    cot_blocks = gather_far(*(after(part, to_x) for part in cot_near))
    got = scatter_near(keep, to_x, to_y)
    d_hidden, cot_all = back_through_down(
        [after(cot_blocks[0], *guest_cot_near)] + cot_blocks[1:], w_down
    )
    middle, normed_two = make_middle(tokens, after(got[0], cot_all), *got[1:], gain_two)

    near = gather_near(normed_two)
    guest_cot_far = [to_inner(part) for part in cot_blocks[3:]]
    guest_own = to_inner(after(normed_two, *guest_cot_far))
    blocks = gather_far(*near)
    normed_two_all, hidden, d_gate_up = mlp(
        [after(blocks[0], *guest_cot_far)] + blocks[1:], d_hidden, w_gate_up
    )
    guest_near = [to_inner(part) for part in near[1:]]
    guest_far = [to_inner(part) for part in blocks[3:]]
    sent = mlp_back(d_gate_up, w_gate_up)
    keep, to_x, to_y = scatter_far(*sent)
    to_x = after(to_x, guest_own, *guest_near)
    guest_d_hidden, guest_cot_all = back_through_down(
        [after(guest_cot_own, to_x), *guest_cot_near, *guest_cot_far], w_down
    )
    got = scatter_near(keep, to_x, to_y)
    d_middle, gain_two_part, d_middle_low = norm_back(
        cotangent, after(got[0], guest_d_hidden), *got[1:], middle, gain_two, True
    )
    near = gather_near(d_middle_low)
    guest_normed_two, guest_hidden, guest_d_gate_up = mlp(
        [after(guest_own, d_middle_low), *guest_near, *guest_far], guest_d_hidden, w_gate_up
    )
    down = Weight(places, [([cot_all, guest_cot_all], [hidden, guest_hidden])])
    down.sibling_part()
    gate = Weight(
        places,
        [
            (
                [normed_two_all, after(guest_normed_two, down.sibling_sum)],
                [d_gate_up, guest_d_gate_up],
            )
        ],
    )
    gate.sibling_part()
    blocks = gather_far(*near)
    down_outer = down.own_part(0, 1, gate.sibling_sum)
    down_own = down.own_part(1, 1, down_outer)
    gate_outer = gate.own_part(0, 1, down_own)
    gate_own = gate.own_part(1, 1, gate_outer)
    down_outer = over_middle(down_outer)

    d_middle_all, d_project = attend_back_square(
        rows_at,
        blocks,
        w_out,
        after(probs, gate_own, down_outer),
        queries,
        keys,
        values,
        cosine,
        sine,
    )
    down_own = over_middle(down_own)
    gate_outer, gate_own = over_middle(gate_outer), over_middle(gate_own)
    late = Weight(places, [([normed_all], [d_project]), ([d_middle_all], [mixed])])
    late.sibling_part()
    late_far = [late.own_part(0, 1, late.sibling_sum)]
    late_far += [late.own_part(1, 1, late_far[0])]
    late_arrived = [to_inner(part) for part in late_far]
    sent = project_back(rows_at, after(d_project, late_far[1]), w_qkv)
    keep, to_x, to_y = scatter_far(sent[0], after(sent[1], gate_outer), *sent[2:])
    late_near = [late.own_part(2, 1, to_x, to_y)]
    late_near += [late.own_part(3, 1, late_near[0])]
    late_near_arrived = to_inner(late_near[1])
    got = scatter_near(keep, to_x, to_y)
    down_near = [down.own_part(2, 1, late_near[1])]
    down_near += [down.own_part(3, 1, down_near[0])]
    down_given = to_outer(hand(after(down_near[0], down_near[1]), down_outer))
    d_inputs, gain_one_part = norm_back(
        d_middle,
        after(got[0], *down_near, late_arrived[0], down_own),
        *got[1:],
        tokens,
        gain_one,
        False,
    )
    sent = through_down(after(hidden, d_inputs, late_arrived[1]), w_down)
    keep, to_x, to_y = scatter_far(*sent)
    gains = sum_flips(
        after(jnp.concatenate([gain_one_part, gain_two_part], axis=0), to_x, to_y),
        ("dp", 8, 1),
        ("tensor", 4, 1),
        ("tensor", 4, 2),
    )
    late_far[0] = after(late_far[0], gains, gate_own)
    late_outer, late_own = join(late_far, late_arrived)
    gate_near = [gate.own_part(2, 1, late_own)]
    gate_near += [gate.own_part(3, 1, gate_near[0])]
    late_outer, late_own = over_middle(late_outer), over_middle(late_own)
    inner = places[2]
    units, wide = w_down.shape[0], w_qkv.shape[2]
    (grad_down,) = finish(
        inner,
        [after(down_near[1], gate_near[1], late_near_arrived), down_own],
        [down_given],
        [(1, units, True)],
    )
    gains = [gains] + [up_the_line(gains, chips) for chips in (1, 2, 3)]
    keep, got_x, got_y = scatter_near(keep, to_x, to_y)
    output = (
        middle + after(keep, grad_down) + got_x.astype(jnp.float32) + got_y.astype(jnp.float32)
    ).astype(low)
    gate_given = to_outer(hand(after(gate_near[0], output), gate_outer))
    grad_gains = sum_gains(chip, [after(gains[0], output), *gains[1:]])
    late_given = to_outer(hand(after(late_near[0], grad_gains), late_outer))
    (grad_gate_up,) = finish(
        inner,
        [after(gate_near[1], grad_gains, late_own), gate_own],
        [gate_given],
        [(2, units, False)],
    )
    grad_qkv, grad_out = finish(
        inner,
        [late_near[1], late_near_arrived, late_own],
        [late_near[0], late_given],
        [(3, wide, False), (1, wide, True)],
    )
    return (
        output,
        d_inputs,
        grad_gains[0],
        grad_gains[1],
        grad_qkv,
        grad_out,
        grad_gate_up,
        grad_down,
    )


def solution(mesh):
    placed = (
        P(("dp", "tensor"), None),
        P(),
        P(),
        P(None, None, "tensor"),
        P("tensor", None),
        P(None, None, "tensor"),
        P("tensor", None),
        P(("dp", "tensor"), None),
        P("dp"),
        P("dp"),
    )
    square = mesh.shape["tensor"] == 4 and mesh.shape["dp"] == 8
    return jax.shard_map(
        per_device_square if square else per_device,
        mesh=mesh,
        in_specs=placed,
        out_specs=(
            P(("dp", "tensor"), None),
            P(("dp", "tensor"), None),
            P(),
            P(),
            P(None, "dp", "tensor"),
            P("tensor", "dp"),
            P(None, "dp", "tensor"),
            P("tensor", "dp"),
        ),
        check_vma=False,
    )
```

```python
import functools
import math

import jax
import jax.numpy as jnp
from jax import lax
from jax.experimental import pallas as pl
from jax.experimental.pallas import tpu as pltpu
from jax.sharding import PartitionSpec as P

HD = 128


EPS = 1e-06
THETA = 10000.0


def rope_tables(places):
    positions = places.astype(jnp.float32)
    freqs = THETA ** (-(jnp.arange(HD // 2).astype(jnp.float32) * 2.0 / HD))
    angles = positions[:, None] * freqs[None, :]
    return (jnp.cos(angles), jnp.sin(angles))


def rotate(values, cosine, sine):
    half = values.shape[-1] // 2
    first = values[..., :half]
    second = values[..., half:]
    cosine = cosine[:, None, :]
    sine = sine[:, None, :]
    return jnp.concatenate(
        [first * cosine - second * sine, second * cosine + first * sine], axis=-1
    )


def block_scores(q_block, keys_rot, start, segments, valid):
    block_rows = q_block.shape[0]
    length = keys_rot.shape[0]
    key_pos = jnp.arange(length)
    row_pos = start + jnp.arange(block_rows)
    row_seg = lax.dynamic_slice_in_dim(segments, start, block_rows, 0)
    scores = jnp.einsum(
        "qhd,khd->hqk", q_block, keys_rot, preferred_element_type=jnp.float32
    ) * HD ** (-0.5)
    allowed = (
        (key_pos[None, :] <= row_pos[:, None])
        & (row_seg[:, None] == segments[None, :])
        & ((valid[None, :] == 1) | (key_pos[None, :] == row_pos[:, None]))
    )
    return jnp.where(allowed[None], scores, -1e30)


def attend(queries, keys_rot, values, segments, valid):
    length = queries.shape[0]
    block_rows = min(512, length)
    count = length // block_rows

    def one_block(index):
        start = index * block_rows
        q_block = lax.dynamic_slice_in_dim(queries, start, block_rows, 0)
        scores = block_scores(q_block, keys_rot, start, segments, valid)
        top = jnp.max(scores, axis=-1, keepdims=True)
        expo = jnp.exp(scores - top)
        total = jnp.sum(expo, axis=-1, keepdims=True)
        probs = (expo / total).astype(jnp.bfloat16)
        result = jnp.einsum("hqk,khd->qhd", probs, values, preferred_element_type=jnp.float32)
        return (result, top[..., 0] + jnp.log(total[..., 0]))

    blocks, log_sums = lax.map(one_block, jnp.arange(count))
    return (blocks.reshape(length, -1), log_sums)


def attend_back(queries, keys_rot, values, d_mixed, log_sums, segments, valid):
    length = queries.shape[0]
    block_rows = min(512, length)
    count = length // block_rows
    scale = HD ** (-0.5)

    def one_block(carry, index):
        d_keys, d_values = carry
        start = index * block_rows
        q_block = lax.dynamic_slice_in_dim(queries, start, block_rows, 0)
        d_block = lax.dynamic_slice_in_dim(d_mixed, start, block_rows, 0)
        scores = block_scores(q_block, keys_rot, start, segments, valid)
        probs = jnp.exp(scores - log_sums[index][..., None])
        d_values = d_values + jnp.einsum(
            "hqk,qhd->khd", probs.astype(jnp.bfloat16), d_block, preferred_element_type=jnp.float32
        )
        d_probs = jnp.einsum("qhd,khd->hqk", d_block, values, preferred_element_type=jnp.float32)
        delta = jnp.sum(d_probs * probs, axis=-1, keepdims=True)
        d_scores = (probs * (d_probs - delta)).astype(jnp.bfloat16)
        d_query = scale * jnp.einsum(
            "hqk,khd->qhd", d_scores, keys_rot, preferred_element_type=jnp.float32
        )
        d_keys = d_keys + scale * jnp.einsum(
            "hqk,qhd->khd", d_scores, q_block, preferred_element_type=jnp.float32
        )
        return ((d_keys, d_values), d_query)

    empty = jnp.zeros(keys_rot.shape, jnp.float32)
    (d_keys, d_values), d_queries = lax.scan(one_block, (empty, empty), jnp.arange(count))
    return (d_queries.reshape(queries.shape), d_keys, d_values)


def per_device(
    tokens, gain_attn, gain_mlp, w_qkv, w_out, w_gate_up, w_down, cotangent, segment_ids, valid_mask
):
    length = segment_ids.shape[0]
    heads_here = w_qkv.shape[2] // HD
    shape3 = (length, heads_here, HD)
    incoming = tokens.astype(jnp.float32)
    gain_one = gain_attn.astype(jnp.float32)
    gain_two = gain_mlp.astype(jnp.float32)
    cosine, sine = rope_tables(jnp.arange(length))
    inv_one = lax.rsqrt(jnp.mean(incoming * incoming, axis=-1, keepdims=True) + EPS)
    normed = (incoming * inv_one * gain_one).astype(jnp.bfloat16)
    normed_all = lax.all_gather(normed, "tensor", axis=0, tiled=True)
    project = jnp.einsum("td,cde->cte", normed_all, w_qkv, preferred_element_type=jnp.float32)
    queries = rotate(project[0].reshape(shape3), cosine, sine).astype(jnp.bfloat16)
    keys_rot = rotate(project[1].reshape(shape3), cosine, sine).astype(jnp.bfloat16)
    values = project[2].reshape(shape3).astype(jnp.bfloat16)
    mixed, log_sums = attend(queries, keys_rot, values, segment_ids, valid_mask)
    mixed = mixed.astype(jnp.bfloat16)
    middle = incoming + lax.psum_scatter(
        jnp.dot(mixed, w_out, preferred_element_type=jnp.float32).astype(jnp.bfloat16),
        "tensor",
        scatter_dimension=0,
        tiled=True,
    ).astype(jnp.float32)
    inv_two = lax.rsqrt(jnp.mean(middle * middle, axis=-1, keepdims=True) + EPS)
    normed_two = (middle * inv_two * gain_two).astype(jnp.bfloat16)
    normed_two_all = lax.all_gather(normed_two, "tensor", axis=0, tiled=True)
    gate = jnp.dot(normed_two_all, w_gate_up[0], preferred_element_type=jnp.float32)
    upper = jnp.dot(normed_two_all, w_gate_up[1], preferred_element_type=jnp.float32)
    sigma = jax.nn.sigmoid(gate)
    hidden = (gate * sigma * upper).astype(jnp.bfloat16)
    result = middle + lax.psum_scatter(
        jnp.dot(hidden, w_down, preferred_element_type=jnp.float32).astype(jnp.bfloat16),
        "tensor",
        scatter_dimension=0,
        tiled=True,
    ).astype(jnp.float32)
    output = result.astype(jnp.bfloat16)
    cot_all = lax.all_gather(cotangent, "tensor", axis=0, tiled=True)
    d_hidden = jnp.einsum("td,fd->tf", cot_all, w_down, preferred_element_type=jnp.float32)
    grad_down = jnp.einsum("tf,td->fd", hidden, cot_all, preferred_element_type=jnp.float32)
    d_upper = (d_hidden * gate * sigma).astype(jnp.bfloat16)
    d_gate = (d_hidden * upper * sigma * (1.0 + gate * (1.0 - sigma))).astype(jnp.bfloat16)
    grad_gate_up = jnp.stack(
        [
            jnp.einsum("td,tf->df", normed_two_all, d_gate, preferred_element_type=jnp.float32),
            jnp.einsum("td,tf->df", normed_two_all, d_upper, preferred_element_type=jnp.float32),
        ]
    )
    d_normed_two = lax.psum_scatter(
        (
            jnp.einsum("tf,df->td", d_gate, w_gate_up[0], preferred_element_type=jnp.float32)
            + jnp.einsum("tf,df->td", d_upper, w_gate_up[1], preferred_element_type=jnp.float32)
        ).astype(jnp.bfloat16),
        "tensor",
        scatter_dimension=0,
        tiled=True,
    ).astype(jnp.float32)
    scaled_two = gain_two * d_normed_two
    d_middle = (
        cotangent.astype(jnp.float32)
        + inv_two * scaled_two
        - middle * inv_two**3 * jnp.mean(scaled_two * middle, axis=-1, keepdims=True)
    )
    grad_gain_two = jnp.sum(d_normed_two * middle * inv_two, axis=0)
    d_middle_all = lax.all_gather(d_middle.astype(jnp.bfloat16), "tensor", axis=0, tiled=True)
    d_mixed = jnp.einsum(
        "td,ed->te", d_middle_all, w_out, preferred_element_type=jnp.float32
    ).astype(jnp.bfloat16)
    grad_out = jnp.einsum("te,td->ed", mixed, d_middle_all, preferred_element_type=jnp.float32)
    d_queries, d_keys, d_values = attend_back(
        queries, keys_rot, values, d_mixed.reshape(shape3), log_sums, segment_ids, valid_mask
    )
    d_project = jnp.stack(
        [
            rotate(d_queries, cosine, -sine).reshape(length, -1),
            rotate(d_keys, cosine, -sine).reshape(length, -1),
            d_values.reshape(length, -1),
        ]
    ).astype(jnp.bfloat16)
    grad_qkv = jnp.einsum("td,cte->cde", normed_all, d_project, preferred_element_type=jnp.float32)
    d_normed = lax.psum_scatter(
        jnp.einsum("cte,cde->td", d_project, w_qkv, preferred_element_type=jnp.float32).astype(
            jnp.bfloat16
        ),
        "tensor",
        scatter_dimension=0,
        tiled=True,
    ).astype(jnp.float32)
    scaled_one = gain_one * d_normed
    d_inputs = (
        d_middle
        + inv_one * scaled_one
        - incoming * inv_one**3 * jnp.mean(scaled_one * incoming, axis=-1, keepdims=True)
    )
    grad_gain_one = jnp.sum(d_normed * incoming * inv_one, axis=0)
    grad_gain_one, grad_gain_two = lax.psum((grad_gain_one, grad_gain_two), ("dp", "tensor"))
    grad_qkv, grad_out, grad_gate_up, grad_down = (
        lax.psum_scatter(
            grad_qkv.astype(jnp.bfloat16), "dp", scatter_dimension=1, tiled=True
        ).astype(jnp.float32),
        lax.psum_scatter(
            grad_out.astype(jnp.bfloat16), "dp", scatter_dimension=1, tiled=True
        ).astype(jnp.float32),
        lax.psum_scatter(
            grad_gate_up.astype(jnp.bfloat16), "dp", scatter_dimension=1, tiled=True
        ).astype(jnp.float32),
        lax.psum_scatter(
            grad_down.astype(jnp.bfloat16), "dp", scatter_dimension=1, tiled=True
        ).astype(jnp.float32),
    )
    return (
        output,
        d_inputs,
        grad_gain_one,
        grad_gain_two,
        grad_qkv,
        grad_out,
        grad_gate_up,
        grad_down,
    )


NT = (((1,), (1,)), ((), ()))
TN = (((0,), (0,)), ((), ()))
MEGA = 1024 * 1024


def chunks(total, step):
    return [(at, min(step, total - at)) for at in range(0, total, step)]


def dot(left, right, dims=None):
    if dims is None:
        return jnp.dot(left, right, preferred_element_type=jnp.float32)
    return lax.dot_general(left, right, dims, preferred_element_type=jnp.float32)


def in_vmem(count):
    return [pl.BlockSpec(memory_space=pltpu.VMEM)] * count


def in_smem():
    return [pl.BlockSpec(memory_space=pltpu.SMEM)]


def like(shape, kind=jnp.bfloat16):
    return jax.ShapeDtypeStruct(shape, kind)


def limit(megabytes):
    return pltpu.CompilerParams(vmem_limit_bytes=megabytes * MEGA)


def starts_of(blocks):
    at, starts = 0, []
    for block in blocks:
        starts.append((at, block.shape[0]))
        at += block.shape[0]
    return starts


def send_shapes(rows, width):
    half = rows // 2
    return [
        like((rows, width), jnp.float32),
        like((rows, width)),
        like((rows, width)),
        like((half, width)),
        like((half, width)),
    ]


def store_parts(part, targets, cols):
    for (start, rows), target in zip(starts_of(targets), targets):
        target[:, cols] = part[start : start + rows].astype(target.dtype)


def norm_kernel(tokens, gain, normed):
    wide = tokens[...].astype(jnp.float32)
    inverse = lax.rsqrt(jnp.mean(wide * wide, axis=-1, keepdims=True) + EPS)
    normed[...] = (wide * inverse * gain[...].astype(jnp.float32)).astype(jnp.bfloat16)


def norm(tokens, gain):
    return pl.pallas_call(
        norm_kernel,
        name="norm",
        out_shape=like(tokens.shape),
        in_specs=in_vmem(2),
        out_specs=in_vmem(1)[0],
        compiler_params=limit(4),
    )(tokens, gain)


def relay_kernel(to_x, to_y, via_x, via_y, next_x, next_y):
    half = via_x.shape[0]
    next_x[:half] = to_x[:half]
    next_x[half:] = (
        to_x[half:].astype(jnp.float32) + via_y[...].astype(jnp.float32)
    ).astype(jnp.bfloat16)
    next_y[:half] = (
        to_y[:half].astype(jnp.float32) + via_x[...].astype(jnp.float32)
    ).astype(jnp.bfloat16)
    next_y[half:] = to_y[half:]


def relay(to_x, to_y, via_x, via_y):
    return pl.pallas_call(
        relay_kernel,
        name="relay",
        out_shape=[like(to_x.shape), like(to_y.shape)],
        in_specs=in_vmem(4),
        out_specs=in_vmem(2),
        compiler_params=limit(4),
    )(to_x, to_y, via_x, via_y)


def middle_kernel(tokens, keep, got_x, got_y, gain, middle, normed):
    total = (
        tokens[...].astype(jnp.float32)
        + keep[...]
        + got_x[...].astype(jnp.float32)
        + got_y[...].astype(jnp.float32)
    )
    middle[...] = total
    inverse = lax.rsqrt(jnp.mean(total * total, axis=-1, keepdims=True) + EPS)
    normed[...] = (total * inverse * gain[...].astype(jnp.float32)).astype(jnp.bfloat16)


def make_middle(tokens, keep, got_x, got_y, gain):
    return pl.pallas_call(
        middle_kernel,
        name="make_middle",
        out_shape=[like(keep.shape, jnp.float32), like(keep.shape)],
        in_specs=in_vmem(5),
        out_specs=in_vmem(2),
        compiler_params=limit(6),
    )(tokens, keep, got_x, got_y, gain)


def norm_back_kernel(base, keep, got_x, got_y, source, gain, *outs):
    d_normed = keep[...] + got_x[...].astype(jnp.float32) + got_y[...].astype(jnp.float32)
    wide = source[...].astype(jnp.float32)
    inverse = lax.rsqrt(jnp.mean(wide * wide, axis=-1, keepdims=True) + EPS)
    scaled = gain[...].astype(jnp.float32) * d_normed
    slope = jnp.mean(scaled * wide, axis=-1, keepdims=True) * inverse * inverse * inverse
    total = base[...].astype(jnp.float32) + inverse * scaled - wide * slope
    outs[0][...] = total
    outs[1][...] = jnp.sum(d_normed * wide * inverse, axis=0, keepdims=True)
    if len(outs) == 3:
        outs[2][...] = total.astype(jnp.bfloat16)


def norm_back(base, keep, got_x, got_y, source, gain, low):
    return pl.pallas_call(
        norm_back_kernel,
        name="norm_back",
        out_shape=[like(keep.shape, jnp.float32), like((1, keep.shape[1]), jnp.float32)]
        + [like(keep.shape)] * low,
        in_specs=in_vmem(6),
        out_specs=in_vmem(2 + low),
        compiler_params=limit(8),
    )(base, keep, got_x, got_y, source, gain)


def prepare_kernel(segments, valid, cosine, sine, seg_col, valid_col):
    length = cosine.shape[0]
    half = HD // 2
    place = lax.broadcasted_iota(jnp.int32, (length, HD), 0).astype(jnp.float32)
    lane = lax.broadcasted_iota(jnp.int32, (length, HD), 1)
    step = jnp.where(lane < half, lane, lane - half).astype(jnp.float32)
    angle = place * jnp.exp(step * (-2.0 / HD * math.log(THETA)))
    cosine[...] = jnp.cos(angle)
    turn = jnp.sin(angle)
    sine[...] = jnp.where(lane < half, -turn, turn)
    seg_col[...] = jnp.broadcast_to(segments[...], (HD, length)).T
    valid_col[...] = jnp.broadcast_to(valid[...], (HD, length)).T


def prepare(segments, valid):
    length = segments.shape[1]
    return pl.pallas_call(
        prepare_kernel,
        name="prepare",
        out_shape=[like((length, HD), jnp.float32)] * 4,
        in_specs=in_vmem(2),
        out_specs=in_vmem(4),
        compiler_params=limit(6),
    )(segments, valid)


def project_kernel(
    rows_at, own, from_x, from_y, low, high, w_qkv, cosine, sine, normed, queries, keys, values
):
    for i, block in enumerate((own, from_x, from_y, low, high)):
        place = pl.multiple_of(rows_at[i], 64)
        normed[pl.ds(place, block.shape[0]), :] = block[...]
    for c, target in enumerate((queries, keys, values)):
        for at, size in chunks(target.shape[1], 2 * HD):
            part = dot(normed[...], w_qkv[c, :, at : at + size])
            for head in range(0, size, HD):
                piece = part[:, head : head + HD]
                if c < 2:
                    piece = piece * cosine[...] + pltpu.roll(piece, HD // 2, 1) * sine[...]
                target[:, at + head : at + head + HD] = piece.astype(jnp.bfloat16)


def project(rows_at, blocks, w_qkv, cosine, sine):
    rows, width = blocks[0].shape
    length = 4 * rows
    wide = w_qkv.shape[2]
    return pl.pallas_call(
        project_kernel,
        name="project",
        out_shape=[like((length, width))] + [like((length, wide))] * 3,
        in_specs=in_smem() + in_vmem(8),
        out_specs=in_vmem(4),
        compiler_params=limit(8),
    )(rows_at, *blocks, w_qkv, cosine, sine)


def attend_kernel(
    rows_at, queries, keys, values, w_out, seg_row, seg_col, valid_col,
    keep, to_x, to_y, far_low, far_high, probs, mixed, bias, joined,
):
    length, wide = queries.shape
    key_at = lax.broadcasted_iota(jnp.int32, (length, length), 0)
    query_at = lax.broadcasted_iota(jnp.int32, (length, length), 1)
    allowed = (
        (key_at <= query_at)
        & (seg_col[:, 0:1] == seg_row[...])
        & ((valid_col[:, 0:1] == 1.0) | (key_at == query_at))
    )
    bias[...] = jnp.where(allowed, 0.0, -1e30)
    for at in range(0, wide, HD):
        head = at // HD
        cols = slice(at, at + HD)
        for q_at, q_size in chunks(length, 256):
            seen = q_at + q_size
            scores = dot(keys[0:seen, cols], queries[q_at:seen, cols], NT)
            scores = scores * HD ** (-0.5) + bias[0:seen, q_at:seen]
            top = jnp.max(scores, axis=0, keepdims=True)
            expo = jnp.exp(scores - top)
            total = jnp.sum(expo, axis=0, keepdims=True)
            chance = (expo * (1.0 / total)).astype(jnp.bfloat16)
            probs[head, 0:seen, q_at:seen] = chance
            result = dot(values[0:seen, cols], chance, TN)
            joined[q_at:seen, cols] = result.T.astype(jnp.bfloat16)
    targets = [keep, to_x, to_y, far_low, far_high]
    for i, (start, size) in enumerate(starts_of(targets)):
        place = pl.multiple_of(rows_at[i], 64)
        mixed[start : start + size, :] = joined[pl.ds(place, size), :]
    for at, size in chunks(w_out.shape[1], 512):
        store_parts(dot(mixed[...], w_out[:, at : at + size]), targets, slice(at, at + size))


def attend_square(rows_at, queries, keys, values, w_out, seg_row, seg_col, valid_col):
    length, wide = queries.shape
    width = w_out.shape[1]
    heads = wide // HD
    return pl.pallas_call(
        attend_kernel,
        name="attend",
        out_shape=send_shapes(length // 4, width)
        + [like((heads, length, length)), like((length, wide))],
        in_specs=in_smem() + in_vmem(7),
        out_specs=in_vmem(7),
        scratch_shapes=[
            pltpu.VMEM((length, length), jnp.float32),
            pltpu.VMEM((length, wide), jnp.bfloat16),
        ],
        compiler_params=limit(8),
    )(rows_at, queries, keys, values, w_out, seg_row, seg_col, valid_col)


def d_hidden_kernel(own, from_x, from_y, low, high, w_down, d_hidden, cot_all):
    blocks = [own, from_x, from_y, low, high]
    for (start, size), block in zip(starts_of(blocks), blocks):
        cot_all[start : start + size, :] = block[...]
    for at, size in chunks(w_down.shape[0], 256):
        d_hidden[:, at : at + size] = dot(cot_all[...], w_down[at : at + size, :], NT)


def back_through_down(blocks, w_down):
    rows, width = blocks[0].shape
    length = 4 * rows
    units = w_down.shape[0]
    return pl.pallas_call(
        d_hidden_kernel,
        name="back_through_down",
        out_shape=[like((length, units), jnp.float32), like((length, width))],
        in_specs=in_vmem(6),
        out_specs=in_vmem(2),
        compiler_params=limit(6),
    )(*blocks, w_down)


def mlp_kernel(
    own, from_x, from_y, low, high, d_hidden, w_gate_up, normed, hidden, d_gate_up
):
    units = w_gate_up.shape[2]
    blocks = [own, from_x, from_y, low, high]
    for (start, size), block in zip(starts_of(blocks), blocks):
        normed[start : start + size, :] = block[...]
    for at, size in chunks(units, 256):
        here = slice(at, at + size)
        gate = dot(normed[...], w_gate_up[0, :, here])
        upper = dot(normed[...], w_gate_up[1, :, here])
        incoming = d_hidden[:, here]
        sigma = 1.0 / (1.0 + jnp.exp(-gate))
        silu = gate * sigma
        hidden[:, here] = (silu * upper).astype(jnp.bfloat16)
        d_gate_up[:, here] = (incoming * upper * sigma * (1.0 + gate * (1.0 - sigma))).astype(
            jnp.bfloat16
        )
        d_gate_up[:, units + at : units + at + size] = (incoming * silu).astype(jnp.bfloat16)


def mlp(blocks, d_hidden, w_gate_up):
    rows, width = blocks[0].shape
    length = 4 * rows
    units = w_gate_up.shape[2]
    return pl.pallas_call(
        mlp_kernel,
        name="mlp",
        out_shape=[like((length, width)), like((length, units)), like((length, 2 * units))],
        in_specs=in_vmem(7),
        out_specs=in_vmem(3),
        compiler_params=limit(8),
    )(*blocks, d_hidden, w_gate_up)


def mlp_back_kernel(d_gate_up, w_gate_up, *targets):
    units = w_gate_up.shape[2]
    for at, size in chunks(w_gate_up.shape[1], 256):
        part = dot(d_gate_up[:, 0:units], w_gate_up[0, at : at + size, :], NT) + dot(
            d_gate_up[:, units : 2 * units], w_gate_up[1, at : at + size, :], NT
        )
        store_parts(part, targets, slice(at, at + size))


def mlp_back(d_gate_up, w_gate_up):
    return pl.pallas_call(
        mlp_back_kernel,
        name="mlp_back",
        out_shape=send_shapes(d_gate_up.shape[0] // 4, w_gate_up.shape[1]),
        in_specs=in_vmem(2),
        out_specs=in_vmem(5),
        compiler_params=limit(6),
    )(d_gate_up, w_gate_up)


def down_kernel(hidden, w_down, *targets):
    for at, size in chunks(w_down.shape[1], 256):
        store_parts(dot(hidden[...], w_down[:, at : at + size]), targets, slice(at, at + size))


def through_down(hidden, w_down):
    return pl.pallas_call(
        down_kernel,
        name="through_down",
        out_shape=send_shapes(hidden.shape[0] // 4, w_down.shape[1]),
        in_specs=in_vmem(2),
        out_specs=in_vmem(5),
        compiler_params=limit(6),
    )(hidden, w_down)


def attend_back_kernel(
    rows_at, own, from_x, from_y, low, high, w_out, probs, queries, keys, values, cosine, sine,
    d_middle, d_project, d_mixed,
):
    length, wide = queries.shape
    blocks = [own, from_x, from_y, low, high]
    starts = starts_of(blocks)
    for (start, size), block in zip(starts, blocks):
        d_middle[start : start + size, :] = block[...]
    for at, size in chunks(wide, 256):
        part = dot(d_middle[...], w_out[at : at + size, :], NT).astype(jnp.bfloat16)
        for i, (start, rows) in enumerate(starts):
            place = pl.multiple_of(rows_at[i], 64)
            d_mixed[pl.ds(place, rows), at : at + size] = part[start : start + rows]
    scale = HD ** (-0.5)

    def back(turned, rows):
        return turned * cosine[rows, :] - pltpu.roll(turned, HD // 2, 1) * sine[rows, :]

    for at in range(0, wide, HD):
        head = at // HD
        cols = slice(at, at + HD)
        d_keys = d_values = None
        for q_at, q_size in reversed(chunks(length, 256)):
            seen = q_at + q_size
            rows = slice(q_at, seen)
            chance = probs[head, 0:seen, rows]
            d_out = d_mixed[rows, cols]
            d_chance = dot(values[0:seen, cols], d_out, NT)
            exact = chance.astype(jnp.float32)
            delta = jnp.sum(d_chance * exact, axis=0, keepdims=True)
            d_scores = (exact * (d_chance - delta)).astype(jnp.bfloat16)
            more_values = dot(chance, d_out)
            more_keys = dot(d_scores, queries[rows, cols])
            d_queries = dot(keys[0:seen, cols], d_scores, TN).T
            d_project[rows, cols] = back(d_queries * scale, rows).astype(jnp.bfloat16)
            if d_keys is None:
                d_keys, d_values = more_keys, more_values
            else:
                d_keys = jnp.concatenate([d_keys[:seen] + more_keys, d_keys[seen:]], axis=0)
                d_values = jnp.concatenate([d_values[:seen] + more_values, d_values[seen:]], axis=0)
        d_project[:, wide + at : wide + at + HD] = back(d_keys * scale, slice(0, length)).astype(
            jnp.bfloat16
        )
        d_project[:, 2 * wide + at : 2 * wide + at + HD] = d_values.astype(jnp.bfloat16)


def attend_back_square(rows_at, blocks, w_out, probs, queries, keys, values, cosine, sine):
    length, wide = queries.shape
    return pl.pallas_call(
        attend_back_kernel,
        name="attend_back",
        out_shape=[like((length, w_out.shape[1])), like((length, 3 * wide))],
        in_specs=in_smem() + in_vmem(12),
        out_specs=in_vmem(2),
        scratch_shapes=[pltpu.VMEM((length, wide), jnp.bfloat16)],
        compiler_params=limit(8),
    )(rows_at, *blocks, w_out, probs, queries, keys, values, cosine, sine)


def project_back_kernel(rows_at, d_project, w_qkv, *refs):
    targets, turned = refs[:5], refs[5]
    wide = w_qkv.shape[2]
    for i, (start, size) in enumerate(starts_of(targets)):
        place = pl.multiple_of(rows_at[i], 64)
        turned[start : start + size, :] = d_project[pl.ds(place, size), :]
    for at, size in chunks(w_qkv.shape[1], 256):
        part = sum(
            dot(turned[:, c * wide : (c + 1) * wide], w_qkv[c, at : at + size, :], NT)
            for c in range(3)
        )
        store_parts(part, targets, slice(at, at + size))


def project_back(rows_at, d_project, w_qkv):
    return pl.pallas_call(
        project_back_kernel,
        name="project_back",
        out_shape=send_shapes(d_project.shape[0] // 4, w_qkv.shape[1]),
        in_specs=in_smem() + in_vmem(2),
        out_specs=in_vmem(5),
        scratch_shapes=[pltpu.VMEM(d_project.shape, jnp.bfloat16)],
        compiler_params=limit(8),
    )(rows_at, d_project, w_qkv)


def weight_kernel(layout, base, spot, which, *refs):
    turned, out = refs[-1], refs[-2]
    more = refs[-3] if spot is not None else None
    count, piece, _ = out.shape
    for i in range(count):
        place = pl.multiple_of(which[base + i] * piece, piece)
        at_ref = column = 0
        for pairs in layout:
            splits = refs[at_ref : at_ref + pairs]
            others = refs[at_ref + pairs : at_ref + 2 * pairs]
            at_ref += 2 * pairs
            length, across = others[0].shape
            for j, split in enumerate(splits):
                turned[:, j * length : (j + 1) * length] = split[:, pl.ds(place, piece)].T
            for at, size in chunks(across, 256):
                part = None
                for j, other in enumerate(others):
                    term = dot(turned[:, j * length : (j + 1) * length], other[:, at : at + size])
                    part = term if part is None else part + term
                cols = slice(column + at, column + at + size)
                if more is not None:
                    part = part + more[spot + i, :, cols].astype(jnp.float32)
                out[i, :, cols] = part.astype(out.dtype)
            column += across


def weight_pieces(which, base, count, groups, more=None, spot=None):
    layout = [len(splits) for splits, _ in groups]
    refs = [ref for splits, others in groups for ref in (*splits, *others)]
    extra = [] if more is None else [more]
    length = groups[0][1][0].shape[0]
    across = sum(others[0].shape[1] for _, others in groups)
    piece = groups[0][0][0].shape[1] // 8
    return pl.pallas_call(
        functools.partial(weight_kernel, layout, base, spot),
        name="weight_pieces",
        out_shape=like((count, piece, across)),
        in_specs=in_smem() + in_vmem(len(refs) + len(extra)),
        out_specs=in_vmem(1)[0],
        scratch_shapes=[pltpu.VMEM((piece, max(layout) * length), jnp.bfloat16)],
        compiler_params=limit(16),
    )(which, *refs, *extra)


def join_kernel(here_outer, here_own, there_outer, there_own, outer, own):
    for here, there, out in ((here_outer, there_outer, outer), (here_own, there_own, own)):
        for at, size in chunks(out.shape[2], 256):
            cols = slice(at, at + size)
            out[0, :, cols] = (
                here[0, :, cols].astype(jnp.float32) + there[0, :, cols].astype(jnp.float32)
            ).astype(jnp.bfloat16)


def join(here, there):
    shape = here[0].shape
    return pl.pallas_call(
        join_kernel,
        name="join",
        out_shape=[like(shape), like(shape)],
        in_specs=in_vmem(4),
        out_specs=in_vmem(2),
        compiler_params=limit(6),
    )(*here, *there)


def hand_kernel(near, far, out):
    for at, size in chunks(out.shape[1], 256):
        cols = slice(at, at + size)
        out[:, cols] = (
            near[0, :, cols].astype(jnp.float32) + far[0, :, cols].astype(jnp.float32)
        ).astype(jnp.bfloat16)


def hand(near, far):
    return pl.pallas_call(
        hand_kernel,
        name="hand",
        out_shape=like(near.shape[1:]),
        in_specs=in_vmem(2),
        out_specs=in_vmem(1)[0],
        compiler_params=limit(6),
    )(near, far)


def finish_kernel(parts, count_inner, inner, *refs):
    count = len(refs) - len(parts)
    here = [ref for ref in refs[:count_inner]]
    outer = [ref for ref in refs[count_inner:count]]

    def total(sources, cols):
        found = None
        for source in sources:
            term = source[0, :, cols] if len(source.shape) == 3 else source[:, cols]
            term = term.astype(jnp.float32)
            found = term if found is None else found + term
        return found

    column = 0
    for (planes, across, turn), out in zip(parts, refs[count:]):
        for c in range(planes):
            for at, size in chunks(across, 256):
                cols = slice(column + at, column + at + size)
                value = jnp.where(inner[0] == 1, total(here, cols), total(outer, cols))
                if turn:
                    out[at : at + size, :] = value.T
                else:
                    out[c, :, at : at + size] = value
            column += across


def finish(inner, here, outer, parts):
    piece = here[0].shape[-2]
    return pl.pallas_call(
        functools.partial(finish_kernel, parts, len(here)),
        name="finish",
        out_shape=[
            like((across, piece) if turn else (planes, piece, across), jnp.float32)
            for planes, across, turn in parts
        ],
        in_specs=in_smem() + in_vmem(len(here) + len(outer)),
        out_specs=in_vmem(len(parts)),
        compiler_params=limit(8),
    )(inner, *here, *outer)


def gains_kernel(chip, *refs):
    sources, out, kept = refs[:4], refs[4], refs[5]
    for back, source in enumerate(sources):
        kept[lax.rem(chip[0] + 4 - back, 4)] = source[...]
    out[...] = (kept[0] + kept[1]) + (kept[2] + kept[3])


def sum_gains(chip, sources):
    return pl.pallas_call(
        gains_kernel,
        name="sum_gains",
        out_shape=like(sources[0].shape, jnp.float32),
        in_specs=in_smem() + in_vmem(4),
        out_specs=in_vmem(1)[0],
        scratch_shapes=[pltpu.VMEM((4, *sources[0].shape), jnp.float32)],
        compiler_params=limit(4),
    )(chip, *sources)


def flips(size, bit):
    return [(i, i ^ bit) for i in range(size)]


def after(value, *earlier):
    return lax.optimization_barrier((value, *earlier))[0]


def over_tensor(values, bit):
    return lax.ppermute(values, "tensor", flips(4, bit))


def gather_near(own):
    return own, over_tensor(own, 1), over_tensor(own, 2)


def gather_far(own, from_x, from_y):
    half = own.shape[0] // 2
    low = over_tensor(from_y[:half], 1)
    high = over_tensor(from_x[half:], 2)
    return [own, from_x, from_y, low, high]


def scatter_far(keep, to_x, to_y, far_low, far_high):
    return keep, *relay(to_x, to_y, over_tensor(far_low, 1), over_tensor(far_high, 2))


def scatter_near(keep, to_x, to_y):
    return keep, over_tensor(to_x, 1), over_tensor(to_y, 2)


def over_cores(values):
    return lax.ppermute(values, "dp", flips(8, 1))


def up_the_line(values, chips):
    return lax.ppermute(values, "dp", [(i, (i + 2 * chips) % 8) for i in range(8)])


def to_inner(values):
    return lax.ppermute(values, "dp", [(0, 2), (1, 3), (6, 4), (7, 5)])


def to_outer(values):
    return lax.ppermute(values, "dp", [(2, 0), (3, 1), (4, 6), (5, 7)])


def over_middle(values):
    return lax.ppermute(values, "dp", [(2, 4), (3, 5), (4, 2), (5, 3)])


class Weight:
    def __init__(self, places, groups):
        self.which_theirs, self.which_mine, self.inner = places
        self.groups = groups

    def sibling_part(self):
        self.sibling_sum = weight_pieces(self.which_theirs, 0, 4, self.groups)
        self.theirs = over_cores(self.sibling_sum)

    def own_part(self, base, count, *earlier):
        more = after(self.theirs, *earlier) if earlier else self.theirs
        return weight_pieces(self.which_mine, base, count, self.groups, more, base)


def sum_flips(values, *steps):
    for axis, size, bit in steps:
        values = values + lax.ppermute(values, axis, flips(size, bit))
    return values


def per_device_square(
    tokens, gain_attn, gain_mlp, w_qkv, w_out, w_gate_up, w_down, cotangent, segment_ids, valid_mask
):
    rows = tokens.shape[0]
    length = segment_ids.shape[0]
    low = jnp.bfloat16
    me = lax.axis_index("tensor")
    order = [me, me ^ 1, me ^ 2, me ^ 3]
    rows_at = jnp.stack([at * rows for at in order] + [order[3] * rows + rows // 2]).astype(jnp.int32)
    index = lax.axis_index("dp")
    place, core = index // 2, index % 2
    line_order = jnp.where(place < 2, jnp.array([3, 2, 0, 1]), jnp.array([0, 1, 3, 2]))
    places = (
        (2 * line_order + 1 - core).astype(jnp.int32),
        (2 * line_order + core).astype(jnp.int32),
        ((place == 1) | (place == 2)).astype(jnp.int32).reshape(1),
    )
    chip = place.astype(jnp.int32).reshape(1)
    gain_one = gain_attn[None, :]
    gain_two = gain_mlp[None, :]

    tokens = after(tokens, rows_at, chip, *places)
    normed = norm(tokens, gain_one)
    near = gather_near(normed)
    cosine, sine, seg_col, valid_col = prepare(
        segment_ids.astype(jnp.float32)[None, :],
        valid_mask.astype(jnp.float32)[None, :],
    )
    near = (near[0], near[1], after(near[2], cosine))
    guest_cot_own = to_inner(cotangent)
    blocks = gather_far(*near)
    cot_near = gather_near(after(cotangent, *blocks))
    normed_all, queries, keys, values = project(
        rows_at, blocks, w_qkv, cosine, sine
    )
    *sent, probs, mixed = attend_square(
        rows_at,
        after(queries, *cot_near, guest_cot_own),
        keys,
        values,
        w_out,
        segment_ids.astype(jnp.float32)[None, :],
        seg_col,
        valid_col,
    )
    guest_cot_near = [to_inner(part) for part in cot_near[1:]]
    keep, to_x, to_y = scatter_far(*sent)
    cot_blocks = gather_far(*(after(part, to_x) for part in cot_near))
    got = scatter_near(keep, to_x, to_y)
    d_hidden, cot_all = back_through_down(
        [after(cot_blocks[0], *guest_cot_near)] + cot_blocks[1:], w_down
    )
    middle, normed_two = make_middle(tokens, after(got[0], cot_all), *got[1:], gain_two)

    near = gather_near(normed_two)
    guest_cot_far = [to_inner(part) for part in cot_blocks[3:]]
    guest_own = to_inner(after(normed_two, *guest_cot_far))
    blocks = gather_far(*near)
    normed_two_all, hidden, d_gate_up = mlp(
        [after(blocks[0], *guest_cot_far)] + blocks[1:], d_hidden, w_gate_up
    )
    guest_near = [to_inner(part) for part in near[1:]]
    guest_far = [to_inner(part) for part in blocks[3:]]
    sent = mlp_back(d_gate_up, w_gate_up)
    keep, to_x, to_y = scatter_far(*sent)
    to_x = after(to_x, guest_own, *guest_near)
    guest_d_hidden, guest_cot_all = back_through_down(
        [after(guest_cot_own, to_x), *guest_cot_near, *guest_cot_far], w_down
    )
    got = scatter_near(keep, to_x, to_y)
    d_middle, gain_two_part, d_middle_low = norm_back(
        cotangent, after(got[0], guest_d_hidden), *got[1:], middle, gain_two, True
    )
    near = gather_near(d_middle_low)
    guest_normed_two, guest_hidden, guest_d_gate_up = mlp(
        [after(guest_own, d_middle_low), *guest_near, *guest_far], guest_d_hidden, w_gate_up
    )
    down = Weight(places, [([cot_all, guest_cot_all], [hidden, guest_hidden])])
    down.sibling_part()
    gate = Weight(
        places,
        [
            (
                [normed_two_all, after(guest_normed_two, down.sibling_sum)],
                [d_gate_up, guest_d_gate_up],
            )
        ],
    )
    gate.sibling_part()
    blocks = gather_far(*near)
    down_outer = down.own_part(0, 1, gate.sibling_sum)
    down_own = down.own_part(1, 1, down_outer)
    gate_outer = gate.own_part(0, 1, down_own)
    gate_own = gate.own_part(1, 1, gate_outer)
    down_outer = over_middle(down_outer)

    d_middle_all, d_project = attend_back_square(
        rows_at,
        blocks,
        w_out,
        after(probs, gate_own, down_outer),
        queries,
        keys,
        values,
        cosine,
        sine,
    )
    down_own = over_middle(down_own)
    gate_outer, gate_own = over_middle(gate_outer), over_middle(gate_own)
    late = Weight(places, [([normed_all], [d_project]), ([d_middle_all], [mixed])])
    late.sibling_part()
    down_near = [down.own_part(2, 1, late.sibling_sum)]
    down_handed = hand(down_near[0], down_outer)
    down_given = to_outer(down_handed)
    late_far = [late.own_part(0, 1, down_handed)]
    late_far += [late.own_part(1, 1, late_far[0])]
    late_arrived = [to_inner(part) for part in late_far]
    sent = project_back(rows_at, after(d_project, late_far[1]), w_qkv)
    keep, to_x, to_y = scatter_far(sent[0], after(sent[1], gate_outer), *sent[2:])
    late_near = [late.own_part(2, 1, to_x, to_y)]
    late_near += [late.own_part(3, 1, late_near[0])]
    late_near_arrived = to_inner(late_near[1])
    got = scatter_near(keep, to_x, to_y)
    gate_near = [gate.own_part(2, 1, late_near[1])]
    gate_handed = hand(gate_near[0], gate_outer)
    gate_given = to_outer(gate_handed)
    gate_near += [gate.own_part(3, 1, gate_handed)]
    down_near += [down.own_part(3, 1, gate_near[1])]
    d_inputs, gain_one_part = norm_back(
        d_middle,
        after(got[0], down_near[1], *late_arrived, down_own, down_given),
        *got[1:],
        tokens,
        gain_one,
        False,
    )
    gains = sum_flips(
        jnp.concatenate([gain_one_part, gain_two_part], axis=0),
        ("dp", 8, 1),
        ("tensor", 4, 1),
        ("tensor", 4, 2),
    )
    late_far[0] = after(late_far[0], gains, gate_own)
    late_outer, late_own = join(late_far, late_arrived)
    sent = through_down(after(hidden, late_own, gate_given), w_down)
    late_outer = over_middle(late_outer)
    late_own = over_middle(after(late_own, late_outer))
    keep, to_x, to_y, *sent = sent
    via_x, via_y = over_tensor(sent[0], 1), over_tensor(sent[1], 2)
    late_handed = hand(after(late_near[0], via_x, via_y), late_outer)
    late_given = to_outer(late_handed)
    to_x, to_y = relay(after(to_x, late_handed), to_y, via_x, via_y)
    gains = [after(gains, late_handed)]
    gains += [up_the_line(gains[0], chips) for chips in (1, 2, 3)]
    keep, got_x, got_y = scatter_near(keep, to_x, to_y)
    output = (middle + keep + got_x.astype(jnp.float32) + got_y.astype(jnp.float32)).astype(low)
    inner = places[2]
    units, wide = w_down.shape[0], w_qkv.shape[2]
    (grad_down,) = finish(
        inner,
        [after(down_near[1], output, late_near_arrived), down_own],
        [down_given],
        [(1, units, True)],
    )
    (grad_gate_up,) = finish(
        inner, [after(gate_near[1], grad_down), gate_own], [gate_given], [(2, units, False)]
    )
    grad_gains = sum_gains(chip, [after(gains[0], grad_gate_up), *gains[1:]])
    grad_qkv, grad_out = finish(
        inner,
        [late_near[1], late_near_arrived, late_own],
        [late_near[0], late_given],
        [(3, wide, False), (1, wide, True)],
    )
    return (
        output,
        d_inputs,
        grad_gains[0],
        grad_gains[1],
        grad_qkv,
        grad_out,
        grad_gate_up,
        grad_down,
    )


def solution(mesh):
    placed = (
        P(("dp", "tensor"), None),
        P(),
        P(),
        P(None, None, "tensor"),
        P("tensor", None),
        P(None, None, "tensor"),
        P("tensor", None),
        P(("dp", "tensor"), None),
        P("dp"),
        P("dp"),
    )
    square = mesh.shape["tensor"] == 4 and mesh.shape["dp"] == 8
    return jax.shard_map(
        per_device_square if square else per_device,
        mesh=mesh,
        in_specs=placed,
        out_specs=(
            P(("dp", "tensor"), None),
            P(("dp", "tensor"), None),
            P(),
            P(),
            P(None, "dp", "tensor"),
            P("tensor", "dp"),
            P(None, "dp", "tensor"),
            P("tensor", "dp"),
        ),
        check_vma=False,
    )
```

```python
import functools
import math

import jax
import jax.numpy as jnp
from jax import lax
from jax.experimental import pallas as pl
from jax.experimental.pallas import tpu as pltpu
from jax.sharding import PartitionSpec as P

HD = 128


EPS = 1e-06
THETA = 10000.0


def rope_tables(places):
    positions = places.astype(jnp.float32)
    freqs = THETA ** (-(jnp.arange(HD // 2).astype(jnp.float32) * 2.0 / HD))
    angles = positions[:, None] * freqs[None, :]
    return (jnp.cos(angles), jnp.sin(angles))


def rotate(values, cosine, sine):
    half = values.shape[-1] // 2
    first = values[..., :half]
    second = values[..., half:]
    cosine = cosine[:, None, :]
    sine = sine[:, None, :]
    return jnp.concatenate(
        [first * cosine - second * sine, second * cosine + first * sine], axis=-1
    )


def block_scores(q_block, keys_rot, start, segments, valid):
    block_rows = q_block.shape[0]
    length = keys_rot.shape[0]
    key_pos = jnp.arange(length)
    row_pos = start + jnp.arange(block_rows)
    row_seg = lax.dynamic_slice_in_dim(segments, start, block_rows, 0)
    scores = jnp.einsum(
        "qhd,khd->hqk", q_block, keys_rot, preferred_element_type=jnp.float32
    ) * HD ** (-0.5)
    allowed = (
        (key_pos[None, :] <= row_pos[:, None])
        & (row_seg[:, None] == segments[None, :])
        & ((valid[None, :] == 1) | (key_pos[None, :] == row_pos[:, None]))
    )
    return jnp.where(allowed[None], scores, -1e30)


def attend(queries, keys_rot, values, segments, valid):
    length = queries.shape[0]
    block_rows = min(512, length)
    count = length // block_rows

    def one_block(index):
        start = index * block_rows
        q_block = lax.dynamic_slice_in_dim(queries, start, block_rows, 0)
        scores = block_scores(q_block, keys_rot, start, segments, valid)
        top = jnp.max(scores, axis=-1, keepdims=True)
        expo = jnp.exp(scores - top)
        total = jnp.sum(expo, axis=-1, keepdims=True)
        probs = (expo / total).astype(jnp.bfloat16)
        result = jnp.einsum("hqk,khd->qhd", probs, values, preferred_element_type=jnp.float32)
        return (result, top[..., 0] + jnp.log(total[..., 0]))

    blocks, log_sums = lax.map(one_block, jnp.arange(count))
    return (blocks.reshape(length, -1), log_sums)


def attend_back(queries, keys_rot, values, d_mixed, log_sums, segments, valid):
    length = queries.shape[0]
    block_rows = min(512, length)
    count = length // block_rows
    scale = HD ** (-0.5)

    def one_block(carry, index):
        d_keys, d_values = carry
        start = index * block_rows
        q_block = lax.dynamic_slice_in_dim(queries, start, block_rows, 0)
        d_block = lax.dynamic_slice_in_dim(d_mixed, start, block_rows, 0)
        scores = block_scores(q_block, keys_rot, start, segments, valid)
        probs = jnp.exp(scores - log_sums[index][..., None])
        d_values = d_values + jnp.einsum(
            "hqk,qhd->khd", probs.astype(jnp.bfloat16), d_block, preferred_element_type=jnp.float32
        )
        d_probs = jnp.einsum("qhd,khd->hqk", d_block, values, preferred_element_type=jnp.float32)
        delta = jnp.sum(d_probs * probs, axis=-1, keepdims=True)
        d_scores = (probs * (d_probs - delta)).astype(jnp.bfloat16)
        d_query = scale * jnp.einsum(
            "hqk,khd->qhd", d_scores, keys_rot, preferred_element_type=jnp.float32
        )
        d_keys = d_keys + scale * jnp.einsum(
            "hqk,qhd->khd", d_scores, q_block, preferred_element_type=jnp.float32
        )
        return ((d_keys, d_values), d_query)

    empty = jnp.zeros(keys_rot.shape, jnp.float32)
    (d_keys, d_values), d_queries = lax.scan(one_block, (empty, empty), jnp.arange(count))
    return (d_queries.reshape(queries.shape), d_keys, d_values)


def per_device(
    tokens, gain_attn, gain_mlp, w_qkv, w_out, w_gate_up, w_down, cotangent, segment_ids, valid_mask
):
    length = segment_ids.shape[0]
    heads_here = w_qkv.shape[2] // HD
    shape3 = (length, heads_here, HD)
    incoming = tokens.astype(jnp.float32)
    gain_one = gain_attn.astype(jnp.float32)
    gain_two = gain_mlp.astype(jnp.float32)
    cosine, sine = rope_tables(jnp.arange(length))
    inv_one = lax.rsqrt(jnp.mean(incoming * incoming, axis=-1, keepdims=True) + EPS)
    normed = (incoming * inv_one * gain_one).astype(jnp.bfloat16)
    normed_all = lax.all_gather(normed, "tensor", axis=0, tiled=True)
    project = jnp.einsum("td,cde->cte", normed_all, w_qkv, preferred_element_type=jnp.float32)
    queries = rotate(project[0].reshape(shape3), cosine, sine).astype(jnp.bfloat16)
    keys_rot = rotate(project[1].reshape(shape3), cosine, sine).astype(jnp.bfloat16)
    values = project[2].reshape(shape3).astype(jnp.bfloat16)
    mixed, log_sums = attend(queries, keys_rot, values, segment_ids, valid_mask)
    mixed = mixed.astype(jnp.bfloat16)
    middle = incoming + lax.psum_scatter(
        jnp.dot(mixed, w_out, preferred_element_type=jnp.float32).astype(jnp.bfloat16),
        "tensor",
        scatter_dimension=0,
        tiled=True,
    ).astype(jnp.float32)
    inv_two = lax.rsqrt(jnp.mean(middle * middle, axis=-1, keepdims=True) + EPS)
    normed_two = (middle * inv_two * gain_two).astype(jnp.bfloat16)
    normed_two_all = lax.all_gather(normed_two, "tensor", axis=0, tiled=True)
    gate = jnp.dot(normed_two_all, w_gate_up[0], preferred_element_type=jnp.float32)
    upper = jnp.dot(normed_two_all, w_gate_up[1], preferred_element_type=jnp.float32)
    sigma = jax.nn.sigmoid(gate)
    hidden = (gate * sigma * upper).astype(jnp.bfloat16)
    result = middle + lax.psum_scatter(
        jnp.dot(hidden, w_down, preferred_element_type=jnp.float32).astype(jnp.bfloat16),
        "tensor",
        scatter_dimension=0,
        tiled=True,
    ).astype(jnp.float32)
    output = result.astype(jnp.bfloat16)
    cot_all = lax.all_gather(cotangent, "tensor", axis=0, tiled=True)
    d_hidden = jnp.einsum("td,fd->tf", cot_all, w_down, preferred_element_type=jnp.float32)
    grad_down = jnp.einsum("tf,td->fd", hidden, cot_all, preferred_element_type=jnp.float32)
    d_upper = (d_hidden * gate * sigma).astype(jnp.bfloat16)
    d_gate = (d_hidden * upper * sigma * (1.0 + gate * (1.0 - sigma))).astype(jnp.bfloat16)
    grad_gate_up = jnp.stack(
        [
            jnp.einsum("td,tf->df", normed_two_all, d_gate, preferred_element_type=jnp.float32),
            jnp.einsum("td,tf->df", normed_two_all, d_upper, preferred_element_type=jnp.float32),
        ]
    )
    d_normed_two = lax.psum_scatter(
        (
            jnp.einsum("tf,df->td", d_gate, w_gate_up[0], preferred_element_type=jnp.float32)
            + jnp.einsum("tf,df->td", d_upper, w_gate_up[1], preferred_element_type=jnp.float32)
        ).astype(jnp.bfloat16),
        "tensor",
        scatter_dimension=0,
        tiled=True,
    ).astype(jnp.float32)
    scaled_two = gain_two * d_normed_two
    d_middle = (
        cotangent.astype(jnp.float32)
        + inv_two * scaled_two
        - middle * inv_two**3 * jnp.mean(scaled_two * middle, axis=-1, keepdims=True)
    )
    grad_gain_two = jnp.sum(d_normed_two * middle * inv_two, axis=0)
    d_middle_all = lax.all_gather(d_middle.astype(jnp.bfloat16), "tensor", axis=0, tiled=True)
    d_mixed = jnp.einsum(
        "td,ed->te", d_middle_all, w_out, preferred_element_type=jnp.float32
    ).astype(jnp.bfloat16)
    grad_out = jnp.einsum("te,td->ed", mixed, d_middle_all, preferred_element_type=jnp.float32)
    d_queries, d_keys, d_values = attend_back(
        queries, keys_rot, values, d_mixed.reshape(shape3), log_sums, segment_ids, valid_mask
    )
    d_project = jnp.stack(
        [
            rotate(d_queries, cosine, -sine).reshape(length, -1),
            rotate(d_keys, cosine, -sine).reshape(length, -1),
            d_values.reshape(length, -1),
        ]
    ).astype(jnp.bfloat16)
    grad_qkv = jnp.einsum("td,cte->cde", normed_all, d_project, preferred_element_type=jnp.float32)
    d_normed = lax.psum_scatter(
        jnp.einsum("cte,cde->td", d_project, w_qkv, preferred_element_type=jnp.float32).astype(
            jnp.bfloat16
        ),
        "tensor",
        scatter_dimension=0,
        tiled=True,
    ).astype(jnp.float32)
    scaled_one = gain_one * d_normed
    d_inputs = (
        d_middle
        + inv_one * scaled_one
        - incoming * inv_one**3 * jnp.mean(scaled_one * incoming, axis=-1, keepdims=True)
    )
    grad_gain_one = jnp.sum(d_normed * incoming * inv_one, axis=0)
    grad_gain_one, grad_gain_two = lax.psum((grad_gain_one, grad_gain_two), ("dp", "tensor"))
    grad_qkv, grad_out, grad_gate_up, grad_down = (
        lax.psum_scatter(
            grad_qkv.astype(jnp.bfloat16), "dp", scatter_dimension=1, tiled=True
        ).astype(jnp.float32),
        lax.psum_scatter(
            grad_out.astype(jnp.bfloat16), "dp", scatter_dimension=1, tiled=True
        ).astype(jnp.float32),
        lax.psum_scatter(
            grad_gate_up.astype(jnp.bfloat16), "dp", scatter_dimension=1, tiled=True
        ).astype(jnp.float32),
        lax.psum_scatter(
            grad_down.astype(jnp.bfloat16), "dp", scatter_dimension=1, tiled=True
        ).astype(jnp.float32),
    )
    return (
        output,
        d_inputs,
        grad_gain_one,
        grad_gain_two,
        grad_qkv,
        grad_out,
        grad_gate_up,
        grad_down,
    )


NT = (((1,), (1,)), ((), ()))
TN = (((0,), (0,)), ((), ()))
MEGA = 1024 * 1024


def chunks(total, step):
    return [(at, min(step, total - at)) for at in range(0, total, step)]


def dot(left, right, dims=None):
    if dims is None:
        return jnp.dot(left, right, preferred_element_type=jnp.float32)
    return lax.dot_general(left, right, dims, preferred_element_type=jnp.float32)


def in_vmem(count):
    return [pl.BlockSpec(memory_space=pltpu.VMEM)] * count


def in_smem():
    return [pl.BlockSpec(memory_space=pltpu.SMEM)]


def like(shape, kind=jnp.bfloat16):
    return jax.ShapeDtypeStruct(shape, kind)


def limit(megabytes):
    return pltpu.CompilerParams(vmem_limit_bytes=megabytes * MEGA)


def starts_of(blocks):
    at, starts = 0, []
    for block in blocks:
        starts.append((at, block.shape[0]))
        at += block.shape[0]
    return starts


def send_shapes(rows, width):
    half = rows // 2
    return [
        like((rows, width), jnp.float32),
        like((rows, width)),
        like((rows, width)),
        like((half, width)),
        like((half, width)),
    ]


def store_parts(part, targets, cols):
    for (start, rows), target in zip(starts_of(targets), targets):
        target[:, cols] = part[start : start + rows].astype(target.dtype)


def norm_kernel(tokens, gain, normed):
    wide = tokens[...].astype(jnp.float32)
    inverse = lax.rsqrt(jnp.mean(wide * wide, axis=-1, keepdims=True) + EPS)
    normed[...] = (wide * inverse * gain[...].astype(jnp.float32)).astype(jnp.bfloat16)


def norm(tokens, gain):
    return pl.pallas_call(
        norm_kernel,
        name="norm",
        out_shape=like(tokens.shape),
        in_specs=in_vmem(2),
        out_specs=in_vmem(1)[0],
        compiler_params=limit(4),
    )(tokens, gain)


def relay_kernel(to_x, to_y, via_x, via_y, next_x, next_y):
    half = via_x.shape[0]
    next_x[:half] = to_x[:half]
    next_x[half:] = (
        to_x[half:].astype(jnp.float32) + via_y[...].astype(jnp.float32)
    ).astype(jnp.bfloat16)
    next_y[:half] = (
        to_y[:half].astype(jnp.float32) + via_x[...].astype(jnp.float32)
    ).astype(jnp.bfloat16)
    next_y[half:] = to_y[half:]


def relay(to_x, to_y, via_x, via_y):
    return pl.pallas_call(
        relay_kernel,
        name="relay",
        out_shape=[like(to_x.shape), like(to_y.shape)],
        in_specs=in_vmem(4),
        out_specs=in_vmem(2),
        compiler_params=limit(4),
    )(to_x, to_y, via_x, via_y)


def middle_kernel(tokens, keep, got_x, got_y, gain, middle, normed):
    total = (
        tokens[...].astype(jnp.float32)
        + keep[...]
        + got_x[...].astype(jnp.float32)
        + got_y[...].astype(jnp.float32)
    )
    middle[...] = total
    inverse = lax.rsqrt(jnp.mean(total * total, axis=-1, keepdims=True) + EPS)
    normed[...] = (total * inverse * gain[...].astype(jnp.float32)).astype(jnp.bfloat16)


def make_middle(tokens, keep, got_x, got_y, gain):
    return pl.pallas_call(
        middle_kernel,
        name="make_middle",
        out_shape=[like(keep.shape, jnp.float32), like(keep.shape)],
        in_specs=in_vmem(5),
        out_specs=in_vmem(2),
        compiler_params=limit(6),
    )(tokens, keep, got_x, got_y, gain)


def norm_back_kernel(base, keep, got_x, got_y, source, gain, *outs):
    d_normed = keep[...] + got_x[...].astype(jnp.float32) + got_y[...].astype(jnp.float32)
    wide = source[...].astype(jnp.float32)
    inverse = lax.rsqrt(jnp.mean(wide * wide, axis=-1, keepdims=True) + EPS)
    scaled = gain[...].astype(jnp.float32) * d_normed
    slope = jnp.mean(scaled * wide, axis=-1, keepdims=True) * inverse * inverse * inverse
    total = base[...].astype(jnp.float32) + inverse * scaled - wide * slope
    outs[0][...] = total
    outs[1][...] = jnp.sum(d_normed * wide * inverse, axis=0, keepdims=True)
    if len(outs) == 3:
        outs[2][...] = total.astype(jnp.bfloat16)


def norm_back(base, keep, got_x, got_y, source, gain, low):
    return pl.pallas_call(
        norm_back_kernel,
        name="norm_back",
        out_shape=[like(keep.shape, jnp.float32), like((1, keep.shape[1]), jnp.float32)]
        + [like(keep.shape)] * low,
        in_specs=in_vmem(6),
        out_specs=in_vmem(2 + low),
        compiler_params=limit(8),
    )(base, keep, got_x, got_y, source, gain)


def prepare_kernel(segments, valid, cosine, sine, seg_col, valid_col):
    length = cosine.shape[0]
    half = HD // 2
    place = lax.broadcasted_iota(jnp.int32, (length, HD), 0).astype(jnp.float32)
    lane = lax.broadcasted_iota(jnp.int32, (length, HD), 1)
    step = jnp.where(lane < half, lane, lane - half).astype(jnp.float32)
    angle = place * jnp.exp(step * (-2.0 / HD * math.log(THETA)))
    cosine[...] = jnp.cos(angle)
    turn = jnp.sin(angle)
    sine[...] = jnp.where(lane < half, -turn, turn)
    seg_col[...] = jnp.broadcast_to(segments[...], (HD, length)).T
    valid_col[...] = jnp.broadcast_to(valid[...], (HD, length)).T


def prepare(segments, valid):
    length = segments.shape[1]
    return pl.pallas_call(
        prepare_kernel,
        name="prepare",
        out_shape=[like((length, HD), jnp.float32)] * 4,
        in_specs=in_vmem(2),
        out_specs=in_vmem(4),
        compiler_params=limit(6),
    )(segments, valid)


def project_kernel(
    rows_at, own, from_x, from_y, low, high, w_qkv, cosine, sine, normed, queries, keys, values
):
    for i, block in enumerate((own, from_x, from_y, low, high)):
        place = pl.multiple_of(rows_at[i], 64)
        normed[pl.ds(place, block.shape[0]), :] = block[...]
    for c, target in enumerate((queries, keys, values)):
        for at, size in chunks(target.shape[1], 2 * HD):
            part = dot(normed[...], w_qkv[c, :, at : at + size])
            for head in range(0, size, HD):
                piece = part[:, head : head + HD]
                if c < 2:
                    piece = piece * cosine[...] + pltpu.roll(piece, HD // 2, 1) * sine[...]
                target[:, at + head : at + head + HD] = piece.astype(jnp.bfloat16)


def project(rows_at, blocks, w_qkv, cosine, sine):
    rows, width = blocks[0].shape
    length = 4 * rows
    wide = w_qkv.shape[2]
    return pl.pallas_call(
        project_kernel,
        name="project",
        out_shape=[like((length, width))] + [like((length, wide))] * 3,
        in_specs=in_smem() + in_vmem(8),
        out_specs=in_vmem(4),
        compiler_params=limit(8),
    )(rows_at, *blocks, w_qkv, cosine, sine)


def attend_kernel(
    rows_at, queries, keys, values, w_out, seg_row, seg_col, valid_col,
    keep, to_x, to_y, far_low, far_high, probs, mixed, bias, joined,
):
    length, wide = queries.shape
    key_at = lax.broadcasted_iota(jnp.int32, (length, length), 0)
    query_at = lax.broadcasted_iota(jnp.int32, (length, length), 1)
    allowed = (
        (key_at <= query_at)
        & (seg_col[:, 0:1] == seg_row[...])
        & ((valid_col[:, 0:1] == 1.0) | (key_at == query_at))
    )
    bias[...] = jnp.where(allowed, 0.0, -1e30)
    for at in range(0, wide, HD):
        head = at // HD
        cols = slice(at, at + HD)
        for q_at, q_size in chunks(length, 256):
            seen = q_at + q_size
            scores = dot(keys[0:seen, cols], queries[q_at:seen, cols], NT)
            scores = scores * HD ** (-0.5) + bias[0:seen, q_at:seen]
            top = jnp.max(scores, axis=0, keepdims=True)
            expo = jnp.exp(scores - top)
            total = jnp.sum(expo, axis=0, keepdims=True)
            chance = (expo * (1.0 / total)).astype(jnp.bfloat16)
            probs[head, 0:seen, q_at:seen] = chance
            result = dot(values[0:seen, cols], chance, TN)
            joined[q_at:seen, cols] = result.T.astype(jnp.bfloat16)
    targets = [keep, to_x, to_y, far_low, far_high]
    for i, (start, size) in enumerate(starts_of(targets)):
        place = pl.multiple_of(rows_at[i], 64)
        mixed[start : start + size, :] = joined[pl.ds(place, size), :]
    for at, size in chunks(w_out.shape[1], 512):
        store_parts(dot(mixed[...], w_out[:, at : at + size]), targets, slice(at, at + size))


def attend_square(rows_at, queries, keys, values, w_out, seg_row, seg_col, valid_col):
    length, wide = queries.shape
    width = w_out.shape[1]
    heads = wide // HD
    return pl.pallas_call(
        attend_kernel,
        name="attend",
        out_shape=send_shapes(length // 4, width)
        + [like((heads, length, length)), like((length, wide))],
        in_specs=in_smem() + in_vmem(7),
        out_specs=in_vmem(7),
        scratch_shapes=[
            pltpu.VMEM((length, length), jnp.float32),
            pltpu.VMEM((length, wide), jnp.bfloat16),
        ],
        compiler_params=limit(8),
    )(rows_at, queries, keys, values, w_out, seg_row, seg_col, valid_col)


def d_hidden_kernel(own, from_x, from_y, low, high, w_down, d_hidden, cot_all):
    blocks = [own, from_x, from_y, low, high]
    for (start, size), block in zip(starts_of(blocks), blocks):
        cot_all[start : start + size, :] = block[...]
    for at, size in chunks(w_down.shape[0], 256):
        d_hidden[:, at : at + size] = dot(cot_all[...], w_down[at : at + size, :], NT)


def back_through_down(blocks, w_down):
    rows, width = blocks[0].shape
    length = 4 * rows
    units = w_down.shape[0]
    return pl.pallas_call(
        d_hidden_kernel,
        name="back_through_down",
        out_shape=[like((length, units), jnp.float32), like((length, width))],
        in_specs=in_vmem(6),
        out_specs=in_vmem(2),
        compiler_params=limit(6),
    )(*blocks, w_down)


def mlp_kernel(
    own, from_x, from_y, low, high, d_hidden, w_gate_up, normed, hidden, d_gate_up
):
    units = w_gate_up.shape[2]
    blocks = [own, from_x, from_y, low, high]
    for (start, size), block in zip(starts_of(blocks), blocks):
        normed[start : start + size, :] = block[...]
    for at, size in chunks(units, 256):
        here = slice(at, at + size)
        gate = dot(normed[...], w_gate_up[0, :, here])
        upper = dot(normed[...], w_gate_up[1, :, here])
        incoming = d_hidden[:, here]
        sigma = 1.0 / (1.0 + jnp.exp(-gate))
        silu = gate * sigma
        hidden[:, here] = (silu * upper).astype(jnp.bfloat16)
        d_gate_up[:, here] = (incoming * upper * sigma * (1.0 + gate * (1.0 - sigma))).astype(
            jnp.bfloat16
        )
        d_gate_up[:, units + at : units + at + size] = (incoming * silu).astype(jnp.bfloat16)


def mlp(blocks, d_hidden, w_gate_up):
    rows, width = blocks[0].shape
    length = 4 * rows
    units = w_gate_up.shape[2]
    return pl.pallas_call(
        mlp_kernel,
        name="mlp",
        out_shape=[like((length, width)), like((length, units)), like((length, 2 * units))],
        in_specs=in_vmem(7),
        out_specs=in_vmem(3),
        compiler_params=limit(8),
    )(*blocks, d_hidden, w_gate_up)


def mlp_back_kernel(d_gate_up, w_gate_up, *targets):
    units = w_gate_up.shape[2]
    for at, size in chunks(w_gate_up.shape[1], 256):
        part = dot(d_gate_up[:, 0:units], w_gate_up[0, at : at + size, :], NT) + dot(
            d_gate_up[:, units : 2 * units], w_gate_up[1, at : at + size, :], NT
        )
        store_parts(part, targets, slice(at, at + size))


def mlp_back(d_gate_up, w_gate_up):
    return pl.pallas_call(
        mlp_back_kernel,
        name="mlp_back",
        out_shape=send_shapes(d_gate_up.shape[0] // 4, w_gate_up.shape[1]),
        in_specs=in_vmem(2),
        out_specs=in_vmem(5),
        compiler_params=limit(6),
    )(d_gate_up, w_gate_up)


def down_kernel(hidden, w_down, *targets):
    for at, size in chunks(w_down.shape[1], 256):
        store_parts(dot(hidden[...], w_down[:, at : at + size]), targets, slice(at, at + size))


def through_down(hidden, w_down):
    return pl.pallas_call(
        down_kernel,
        name="through_down",
        out_shape=send_shapes(hidden.shape[0] // 4, w_down.shape[1]),
        in_specs=in_vmem(2),
        out_specs=in_vmem(5),
        compiler_params=limit(6),
    )(hidden, w_down)


def attend_back_kernel(
    rows_at, own, from_x, from_y, low, high, w_out, probs, queries, keys, values, cosine, sine,
    d_middle, d_project, d_mixed,
):
    length, wide = queries.shape
    blocks = [own, from_x, from_y, low, high]
    starts = starts_of(blocks)
    for (start, size), block in zip(starts, blocks):
        d_middle[start : start + size, :] = block[...]
    for at, size in chunks(wide, 256):
        part = dot(d_middle[...], w_out[at : at + size, :], NT).astype(jnp.bfloat16)
        for i, (start, rows) in enumerate(starts):
            place = pl.multiple_of(rows_at[i], 64)
            d_mixed[pl.ds(place, rows), at : at + size] = part[start : start + rows]
    scale = HD ** (-0.5)

    def back(turned, rows):
        return turned * cosine[rows, :] - pltpu.roll(turned, HD // 2, 1) * sine[rows, :]

    for at in range(0, wide, HD):
        head = at // HD
        cols = slice(at, at + HD)
        d_keys = d_values = None
        for q_at, q_size in reversed(chunks(length, 256)):
            seen = q_at + q_size
            rows = slice(q_at, seen)
            chance = probs[head, 0:seen, rows]
            d_out = d_mixed[rows, cols]
            d_chance = dot(values[0:seen, cols], d_out, NT)
            exact = chance.astype(jnp.float32)
            delta = jnp.sum(d_chance * exact, axis=0, keepdims=True)
            d_scores = (exact * (d_chance - delta)).astype(jnp.bfloat16)
            more_values = dot(chance, d_out)
            more_keys = dot(d_scores, queries[rows, cols])
            d_queries = dot(keys[0:seen, cols], d_scores, TN).T
            d_project[rows, cols] = back(d_queries * scale, rows).astype(jnp.bfloat16)
            if d_keys is None:
                d_keys, d_values = more_keys, more_values
            else:
                d_keys = jnp.concatenate([d_keys[:seen] + more_keys, d_keys[seen:]], axis=0)
                d_values = jnp.concatenate([d_values[:seen] + more_values, d_values[seen:]], axis=0)
        d_project[:, wide + at : wide + at + HD] = back(d_keys * scale, slice(0, length)).astype(
            jnp.bfloat16
        )
        d_project[:, 2 * wide + at : 2 * wide + at + HD] = d_values.astype(jnp.bfloat16)


def attend_back_square(rows_at, blocks, w_out, probs, queries, keys, values, cosine, sine):
    length, wide = queries.shape
    return pl.pallas_call(
        attend_back_kernel,
        name="attend_back",
        out_shape=[like((length, w_out.shape[1])), like((length, 3 * wide))],
        in_specs=in_smem() + in_vmem(12),
        out_specs=in_vmem(2),
        scratch_shapes=[pltpu.VMEM((length, wide), jnp.bfloat16)],
        compiler_params=limit(8),
    )(rows_at, *blocks, w_out, probs, queries, keys, values, cosine, sine)


def project_back_kernel(rows_at, d_project, w_qkv, *refs):
    targets, turned = refs[:5], refs[5]
    wide = w_qkv.shape[2]
    for i, (start, size) in enumerate(starts_of(targets)):
        place = pl.multiple_of(rows_at[i], 64)
        turned[start : start + size, :] = d_project[pl.ds(place, size), :]
    for at, size in chunks(w_qkv.shape[1], 256):
        part = sum(
            dot(turned[:, c * wide : (c + 1) * wide], w_qkv[c, at : at + size, :], NT)
            for c in range(3)
        )
        store_parts(part, targets, slice(at, at + size))


def project_back(rows_at, d_project, w_qkv):
    return pl.pallas_call(
        project_back_kernel,
        name="project_back",
        out_shape=send_shapes(d_project.shape[0] // 4, w_qkv.shape[1]),
        in_specs=in_smem() + in_vmem(2),
        out_specs=in_vmem(5),
        scratch_shapes=[pltpu.VMEM(d_project.shape, jnp.bfloat16)],
        compiler_params=limit(8),
    )(rows_at, d_project, w_qkv)


def weight_kernel(layout, base, spot, which, *refs):
    turned, out = refs[-1], refs[-2]
    more = refs[-3] if spot is not None else None
    count, piece, _ = out.shape
    for i in range(count):
        place = pl.multiple_of(which[base + i] * piece, piece)
        at_ref = column = 0
        for pairs in layout:
            splits = refs[at_ref : at_ref + pairs]
            others = refs[at_ref + pairs : at_ref + 2 * pairs]
            at_ref += 2 * pairs
            length, across = others[0].shape
            for j, split in enumerate(splits):
                turned[:, j * length : (j + 1) * length] = split[:, pl.ds(place, piece)].T
            for at, size in chunks(across, 256):
                part = None
                for j, other in enumerate(others):
                    term = dot(turned[:, j * length : (j + 1) * length], other[:, at : at + size])
                    part = term if part is None else part + term
                cols = slice(column + at, column + at + size)
                if more is not None:
                    part = part + more[spot + i, :, cols].astype(jnp.float32)
                out[i, :, cols] = part.astype(out.dtype)
            column += across


def weight_pieces(which, base, count, groups, more=None, spot=None):
    layout = [len(splits) for splits, _ in groups]
    refs = [ref for splits, others in groups for ref in (*splits, *others)]
    extra = [] if more is None else [more]
    length = groups[0][1][0].shape[0]
    across = sum(others[0].shape[1] for _, others in groups)
    piece = groups[0][0][0].shape[1] // 8
    return pl.pallas_call(
        functools.partial(weight_kernel, layout, base, spot),
        name="weight_pieces",
        out_shape=like((count, piece, across)),
        in_specs=in_smem() + in_vmem(len(refs) + len(extra)),
        out_specs=in_vmem(1)[0],
        scratch_shapes=[pltpu.VMEM((piece, max(layout) * length), jnp.bfloat16)],
        compiler_params=limit(16),
    )(which, *refs, *extra)


def join_kernel(here_outer, here_own, there_outer, there_own, outer, own):
    for here, there, out in ((here_outer, there_outer, outer), (here_own, there_own, own)):
        for at, size in chunks(out.shape[2], 256):
            cols = slice(at, at + size)
            out[0, :, cols] = (
                here[0, :, cols].astype(jnp.float32) + there[0, :, cols].astype(jnp.float32)
            ).astype(jnp.bfloat16)


def join(here, there):
    shape = here[0].shape
    return pl.pallas_call(
        join_kernel,
        name="join",
        out_shape=[like(shape), like(shape)],
        in_specs=in_vmem(4),
        out_specs=in_vmem(2),
        compiler_params=limit(6),
    )(*here, *there)


def hand_kernel(near, far, out):
    for at, size in chunks(out.shape[1], 256):
        cols = slice(at, at + size)
        out[:, cols] = (
            near[0, :, cols].astype(jnp.float32) + far[0, :, cols].astype(jnp.float32)
        ).astype(jnp.bfloat16)


def hand(near, far):
    return pl.pallas_call(
        hand_kernel,
        name="hand",
        out_shape=like(near.shape[1:]),
        in_specs=in_vmem(2),
        out_specs=in_vmem(1)[0],
        compiler_params=limit(6),
    )(near, far)


def finish_kernel(parts, count_inner, inner, *refs):
    count = len(refs) - len(parts)
    here = [ref for ref in refs[:count_inner]]
    outer = [ref for ref in refs[count_inner:count]]

    def total(sources, cols):
        found = None
        for source in sources:
            term = source[0, :, cols] if len(source.shape) == 3 else source[:, cols]
            term = term.astype(jnp.float32)
            found = term if found is None else found + term
        return found

    column = 0
    for (planes, across, turn), out in zip(parts, refs[count:]):
        for c in range(planes):
            for at, size in chunks(across, 256):
                cols = slice(column + at, column + at + size)
                value = jnp.where(inner[0] == 1, total(here, cols), total(outer, cols))
                if turn:
                    out[at : at + size, :] = value.T
                else:
                    out[c, :, at : at + size] = value
            column += across


def finish(inner, here, outer, parts):
    piece = here[0].shape[-2]
    return pl.pallas_call(
        functools.partial(finish_kernel, parts, len(here)),
        name="finish",
        out_shape=[
            like((across, piece) if turn else (planes, piece, across), jnp.float32)
            for planes, across, turn in parts
        ],
        in_specs=in_smem() + in_vmem(len(here) + len(outer)),
        out_specs=in_vmem(len(parts)),
        compiler_params=limit(8),
    )(inner, *here, *outer)


def gains_kernel(chip, *refs):
    sources, out, kept = refs[:4], refs[4], refs[5]
    for back, source in enumerate(sources):
        kept[lax.rem(chip[0] + 4 - back, 4)] = source[...]
    out[...] = (kept[0] + kept[1]) + (kept[2] + kept[3])


def sum_gains(chip, sources):
    return pl.pallas_call(
        gains_kernel,
        name="sum_gains",
        out_shape=like(sources[0].shape, jnp.float32),
        in_specs=in_smem() + in_vmem(4),
        out_specs=in_vmem(1)[0],
        scratch_shapes=[pltpu.VMEM((4, *sources[0].shape), jnp.float32)],
        compiler_params=limit(4),
    )(chip, *sources)


def flips(size, bit):
    return [(i, i ^ bit) for i in range(size)]


def after(value, *earlier):
    return lax.optimization_barrier((value, *earlier))[0]


def over_tensor(values, bit):
    return lax.ppermute(values, "tensor", flips(4, bit))


def gather_near(own):
    return own, over_tensor(own, 1), over_tensor(own, 2)


def gather_far(own, from_x, from_y):
    half = own.shape[0] // 2
    low = over_tensor(from_y[:half], 1)
    high = over_tensor(from_x[half:], 2)
    return [own, from_x, from_y, low, high]


def scatter_far(keep, to_x, to_y, far_low, far_high):
    return keep, *relay(to_x, to_y, over_tensor(far_low, 1), over_tensor(far_high, 2))


def scatter_near(keep, to_x, to_y):
    return keep, over_tensor(to_x, 1), over_tensor(to_y, 2)


def over_cores(values):
    return lax.ppermute(values, "dp", flips(8, 1))


def up_the_line(values, chips):
    return lax.ppermute(values, "dp", [(i, (i + 2 * chips) % 8) for i in range(8)])


def to_inner(values):
    return lax.ppermute(values, "dp", [(0, 2), (1, 3), (6, 4), (7, 5)])


def to_outer(values):
    return lax.ppermute(values, "dp", [(2, 0), (3, 1), (4, 6), (5, 7)])


def over_middle(values):
    return lax.ppermute(values, "dp", [(2, 4), (3, 5), (4, 2), (5, 3)])


class Weight:
    def __init__(self, places, groups):
        self.which_theirs, self.which_mine, self.inner = places
        self.groups = groups

    def sibling_part(self):
        self.sibling_sum = weight_pieces(self.which_theirs, 0, 4, self.groups)
        self.theirs = over_cores(self.sibling_sum)

    def own_part(self, base, count, *earlier):
        more = after(self.theirs, *earlier) if earlier else self.theirs
        return weight_pieces(self.which_mine, base, count, self.groups, more, base)


def sum_flips(values, *steps):
    for axis, size, bit in steps:
        values = values + lax.ppermute(values, axis, flips(size, bit))
    return values


def per_device_square(
    tokens, gain_attn, gain_mlp, w_qkv, w_out, w_gate_up, w_down, cotangent, segment_ids, valid_mask
):
    rows = tokens.shape[0]
    length = segment_ids.shape[0]
    low = jnp.bfloat16
    me = lax.axis_index("tensor")
    order = [me, me ^ 1, me ^ 2, me ^ 3]
    rows_at = jnp.stack([at * rows for at in order] + [order[3] * rows + rows // 2]).astype(jnp.int32)
    index = lax.axis_index("dp")
    place, core = index // 2, index % 2
    line_order = jnp.where(place < 2, jnp.array([3, 2, 0, 1]), jnp.array([0, 1, 3, 2]))
    places = (
        (2 * line_order + 1 - core).astype(jnp.int32),
        (2 * line_order + core).astype(jnp.int32),
        ((place == 1) | (place == 2)).astype(jnp.int32).reshape(1),
    )
    chip = place.astype(jnp.int32).reshape(1)
    gain_one = gain_attn[None, :]
    gain_two = gain_mlp[None, :]

    tokens = after(tokens, rows_at, chip, *places)
    normed = norm(tokens, gain_one)
    near = gather_near(normed)
    cosine, sine, seg_col, valid_col = prepare(
        segment_ids.astype(jnp.float32)[None, :],
        valid_mask.astype(jnp.float32)[None, :],
    )
    near = (near[0], near[1], after(near[2], cosine))
    guest_cot_own = to_inner(cotangent)
    blocks = gather_far(*near)
    cot_near = gather_near(after(cotangent, *blocks))
    normed_all, queries, keys, values = project(
        rows_at, blocks, w_qkv, cosine, sine
    )
    *sent, probs, mixed = attend_square(
        rows_at,
        after(queries, *cot_near, guest_cot_own),
        keys,
        values,
        w_out,
        segment_ids.astype(jnp.float32)[None, :],
        seg_col,
        valid_col,
    )
    guest_cot_near = [to_inner(part) for part in cot_near[1:]]
    keep, to_x, to_y = scatter_far(*sent)
    cot_blocks = gather_far(*(after(part, to_x) for part in cot_near))
    got = scatter_near(keep, to_x, to_y)
    d_hidden, cot_all = back_through_down(
        [after(cot_blocks[0], *guest_cot_near)] + cot_blocks[1:], w_down
    )
    middle, normed_two = make_middle(tokens, after(got[0], cot_all), *got[1:], gain_two)

    near = gather_near(normed_two)
    guest_cot_far = [to_inner(part) for part in cot_blocks[3:]]
    guest_own = to_inner(after(normed_two, *guest_cot_far))
    blocks = gather_far(*near)
    normed_two_all, hidden, d_gate_up = mlp(
        [after(blocks[0], *guest_cot_far)] + blocks[1:], d_hidden, w_gate_up
    )
    guest_near = [to_inner(part) for part in near[1:]]
    guest_far = [to_inner(part) for part in blocks[3:]]
    sent = mlp_back(d_gate_up, w_gate_up)
    keep, to_x, to_y = scatter_far(*sent)
    to_x = after(to_x, guest_own, *guest_near)
    guest_d_hidden, guest_cot_all = back_through_down(
        [after(guest_cot_own, to_x), *guest_cot_near, *guest_cot_far], w_down
    )
    got = scatter_near(keep, to_x, to_y)
    d_middle, gain_two_part, d_middle_low = norm_back(
        cotangent, after(got[0], guest_d_hidden), *got[1:], middle, gain_two, True
    )
    near = gather_near(d_middle_low)
    guest_normed_two, guest_hidden, guest_d_gate_up = mlp(
        [after(guest_own, d_middle_low), *guest_near, *guest_far], guest_d_hidden, w_gate_up
    )
    down = Weight(places, [([cot_all, guest_cot_all], [hidden, guest_hidden])])
    down.sibling_part()
    gate = Weight(
        places,
        [
            (
                [normed_two_all, after(guest_normed_two, down.theirs)],
                [d_gate_up, guest_d_gate_up],
            )
        ],
    )
    gate.sibling_part()
    blocks = gather_far(*near)
    down_outer = down.own_part(0, 1, gate.sibling_sum)
    down_own = down.own_part(1, 1, down_outer)
    gate_outer = gate.own_part(0, 1, down_own)
    gate_own = gate.own_part(1, 1, gate_outer)
    down_outer = over_middle(down_outer)

    d_middle_all, d_project = attend_back_square(
        rows_at,
        blocks,
        w_out,
        after(probs, gate_own),
        queries,
        keys,
        values,
        cosine,
        sine,
    )
    gate_outer = over_middle(gate_outer)
    late = Weight(places, [([normed_all], [d_project]), ([d_middle_all], [mixed])])
    late.groups[0] = ([after(normed_all, down_outer)], [d_project])
    late.sibling_part()
    down_near = [down.own_part(2, 1, late.sibling_sum)]
    down_handed = hand(down_near[0], down_outer)
    down_given = to_outer(down_handed)
    late_far = [late.own_part(0, 1, down_handed)]
    late_far += [late.own_part(1, 1, late_far[0])]
    late_arrived = [to_inner(part) for part in late_far]
    sent = project_back(rows_at, after(d_project, late_far[1]), w_qkv)
    keep, to_x, to_y = scatter_far(*sent)
    gate_own = over_middle(after(gate_own, to_x, to_y))
    down_own = over_middle(after(down_own, to_x, to_y))
    late_near = [late.own_part(2, 1, to_x, to_y)]
    late_near += [late.own_part(3, 1, late_near[0])]
    late_near_arrived = to_inner(late_near[1])
    got = scatter_near(keep, to_x, to_y)
    gate_near = [gate.own_part(2, 1, late_near[1])]
    gate_handed = hand(gate_near[0], gate_outer)
    gate_given = to_outer(gate_handed)
    gate_near += [gate.own_part(3, 1, gate_handed)]
    down_near += [down.own_part(3, 1, gate_near[1])]
    d_inputs, gain_one_part = norm_back(
        d_middle,
        after(got[0], down_near[1], *late_arrived, down_own, down_given, gate_own),
        *got[1:],
        tokens,
        gain_one,
        False,
    )
    late_far[0] = after(late_far[0], d_inputs)
    late_outer, late_own = join(late_far, late_arrived)
    gains = sum_flips(
        after(jnp.concatenate([gain_one_part, gain_two_part], axis=0), late_own),
        ("dp", 8, 1),
        ("tensor", 4, 1),
        ("tensor", 4, 2),
    )
    sent = through_down(after(hidden, gains, gate_given), w_down)
    late_outer = over_middle(late_outer)
    keep, to_x, to_y, *sent = sent
    via_x, via_y = over_tensor(sent[0], 1), over_tensor(sent[1], 2)
    late_own = over_middle(after(late_own, via_x, via_y))
    late_handed = hand(after(late_near[0], via_x, via_y), late_outer)
    late_given = to_outer(late_handed)
    to_x, to_y = relay(after(to_x, late_handed), to_y, via_x, via_y)
    gains = [after(gains, late_handed)]
    gains += [up_the_line(gains[0], chips) for chips in (1, 2, 3)]
    keep, got_x, got_y = scatter_near(keep, to_x, to_y)
    output = (middle + keep + got_x.astype(jnp.float32) + got_y.astype(jnp.float32)).astype(low)
    inner = places[2]
    units, wide = w_down.shape[0], w_qkv.shape[2]
    (grad_down,) = finish(
        inner,
        [after(down_near[1], output, late_near_arrived), down_own],
        [down_given],
        [(1, units, True)],
    )
    (grad_gate_up,) = finish(
        inner, [after(gate_near[1], grad_down), gate_own], [gate_given], [(2, units, False)]
    )
    grad_gains = sum_gains(chip, [after(gains[0], grad_gate_up), *gains[1:]])
    grad_qkv, grad_out = finish(
        inner,
        [late_near[1], late_near_arrived, late_own],
        [late_near[0], late_given],
        [(3, wide, False), (1, wide, True)],
    )
    return (
        output,
        d_inputs,
        grad_gains[0],
        grad_gains[1],
        grad_qkv,
        grad_out,
        grad_gate_up,
        grad_down,
    )


def solution(mesh):
    placed = (
        P(("dp", "tensor"), None),
        P(),
        P(),
        P(None, None, "tensor"),
        P("tensor", None),
        P(None, None, "tensor"),
        P("tensor", None),
        P(("dp", "tensor"), None),
        P("dp"),
        P("dp"),
    )
    square = mesh.shape["tensor"] == 4 and mesh.shape["dp"] == 8
    return jax.shard_map(
        per_device_square if square else per_device,
        mesh=mesh,
        in_specs=placed,
        out_specs=(
            P(("dp", "tensor"), None),
            P(("dp", "tensor"), None),
            P(),
            P(),
            P(None, "dp", "tensor"),
            P("tensor", "dp"),
            P(None, "dp", "tensor"),
            P("tensor", "dp"),
        ),
        check_vma=False,
    )
```

```python
import functools
import math

import jax
import jax.numpy as jnp
from jax import lax
from jax.experimental import pallas as pl
from jax.experimental.pallas import tpu as pltpu
from jax.sharding import PartitionSpec as P

HD = 128


EPS = 1e-06
THETA = 10000.0


def rope_tables(places):
    positions = places.astype(jnp.float32)
    freqs = THETA ** (-(jnp.arange(HD // 2).astype(jnp.float32) * 2.0 / HD))
    angles = positions[:, None] * freqs[None, :]
    return (jnp.cos(angles), jnp.sin(angles))


def rotate(values, cosine, sine):
    half = values.shape[-1] // 2
    first = values[..., :half]
    second = values[..., half:]
    cosine = cosine[:, None, :]
    sine = sine[:, None, :]
    return jnp.concatenate(
        [first * cosine - second * sine, second * cosine + first * sine], axis=-1
    )


def block_scores(q_block, keys_rot, start, segments, valid):
    block_rows = q_block.shape[0]
    length = keys_rot.shape[0]
    key_pos = jnp.arange(length)
    row_pos = start + jnp.arange(block_rows)
    row_seg = lax.dynamic_slice_in_dim(segments, start, block_rows, 0)
    scores = jnp.einsum(
        "qhd,khd->hqk", q_block, keys_rot, preferred_element_type=jnp.float32
    ) * HD ** (-0.5)
    allowed = (
        (key_pos[None, :] <= row_pos[:, None])
        & (row_seg[:, None] == segments[None, :])
        & ((valid[None, :] == 1) | (key_pos[None, :] == row_pos[:, None]))
    )
    return jnp.where(allowed[None], scores, -1e30)


def attend(queries, keys_rot, values, segments, valid):
    length = queries.shape[0]
    block_rows = min(512, length)
    count = length // block_rows

    def one_block(index):
        start = index * block_rows
        q_block = lax.dynamic_slice_in_dim(queries, start, block_rows, 0)
        scores = block_scores(q_block, keys_rot, start, segments, valid)
        top = jnp.max(scores, axis=-1, keepdims=True)
        expo = jnp.exp(scores - top)
        total = jnp.sum(expo, axis=-1, keepdims=True)
        probs = (expo / total).astype(jnp.bfloat16)
        result = jnp.einsum("hqk,khd->qhd", probs, values, preferred_element_type=jnp.float32)
        return (result, top[..., 0] + jnp.log(total[..., 0]))

    blocks, log_sums = lax.map(one_block, jnp.arange(count))
    return (blocks.reshape(length, -1), log_sums)


def attend_back(queries, keys_rot, values, d_mixed, log_sums, segments, valid):
    length = queries.shape[0]
    block_rows = min(512, length)
    count = length // block_rows
    scale = HD ** (-0.5)

    def one_block(carry, index):
        d_keys, d_values = carry
        start = index * block_rows
        q_block = lax.dynamic_slice_in_dim(queries, start, block_rows, 0)
        d_block = lax.dynamic_slice_in_dim(d_mixed, start, block_rows, 0)
        scores = block_scores(q_block, keys_rot, start, segments, valid)
        probs = jnp.exp(scores - log_sums[index][..., None])
        d_values = d_values + jnp.einsum(
            "hqk,qhd->khd", probs.astype(jnp.bfloat16), d_block, preferred_element_type=jnp.float32
        )
        d_probs = jnp.einsum("qhd,khd->hqk", d_block, values, preferred_element_type=jnp.float32)
        delta = jnp.sum(d_probs * probs, axis=-1, keepdims=True)
        d_scores = (probs * (d_probs - delta)).astype(jnp.bfloat16)
        d_query = scale * jnp.einsum(
            "hqk,khd->qhd", d_scores, keys_rot, preferred_element_type=jnp.float32
        )
        d_keys = d_keys + scale * jnp.einsum(
            "hqk,qhd->khd", d_scores, q_block, preferred_element_type=jnp.float32
        )
        return ((d_keys, d_values), d_query)

    empty = jnp.zeros(keys_rot.shape, jnp.float32)
    (d_keys, d_values), d_queries = lax.scan(one_block, (empty, empty), jnp.arange(count))
    return (d_queries.reshape(queries.shape), d_keys, d_values)


def per_device(
    tokens, gain_attn, gain_mlp, w_qkv, w_out, w_gate_up, w_down, cotangent, segment_ids, valid_mask
):
    length = segment_ids.shape[0]
    heads_here = w_qkv.shape[2] // HD
    shape3 = (length, heads_here, HD)
    incoming = tokens.astype(jnp.float32)
    gain_one = gain_attn.astype(jnp.float32)
    gain_two = gain_mlp.astype(jnp.float32)
    cosine, sine = rope_tables(jnp.arange(length))
    inv_one = lax.rsqrt(jnp.mean(incoming * incoming, axis=-1, keepdims=True) + EPS)
    normed = (incoming * inv_one * gain_one).astype(jnp.bfloat16)
    normed_all = lax.all_gather(normed, "tensor", axis=0, tiled=True)
    project = jnp.einsum("td,cde->cte", normed_all, w_qkv, preferred_element_type=jnp.float32)
    queries = rotate(project[0].reshape(shape3), cosine, sine).astype(jnp.bfloat16)
    keys_rot = rotate(project[1].reshape(shape3), cosine, sine).astype(jnp.bfloat16)
    values = project[2].reshape(shape3).astype(jnp.bfloat16)
    mixed, log_sums = attend(queries, keys_rot, values, segment_ids, valid_mask)
    mixed = mixed.astype(jnp.bfloat16)
    middle = incoming + lax.psum_scatter(
        jnp.dot(mixed, w_out, preferred_element_type=jnp.float32).astype(jnp.bfloat16),
        "tensor",
        scatter_dimension=0,
        tiled=True,
    ).astype(jnp.float32)
    inv_two = lax.rsqrt(jnp.mean(middle * middle, axis=-1, keepdims=True) + EPS)
    normed_two = (middle * inv_two * gain_two).astype(jnp.bfloat16)
    normed_two_all = lax.all_gather(normed_two, "tensor", axis=0, tiled=True)
    gate = jnp.dot(normed_two_all, w_gate_up[0], preferred_element_type=jnp.float32)
    upper = jnp.dot(normed_two_all, w_gate_up[1], preferred_element_type=jnp.float32)
    sigma = jax.nn.sigmoid(gate)
    hidden = (gate * sigma * upper).astype(jnp.bfloat16)
    result = middle + lax.psum_scatter(
        jnp.dot(hidden, w_down, preferred_element_type=jnp.float32).astype(jnp.bfloat16),
        "tensor",
        scatter_dimension=0,
        tiled=True,
    ).astype(jnp.float32)
    output = result.astype(jnp.bfloat16)
    cot_all = lax.all_gather(cotangent, "tensor", axis=0, tiled=True)
    d_hidden = jnp.einsum("td,fd->tf", cot_all, w_down, preferred_element_type=jnp.float32)
    grad_down = jnp.einsum("tf,td->fd", hidden, cot_all, preferred_element_type=jnp.float32)
    d_upper = (d_hidden * gate * sigma).astype(jnp.bfloat16)
    d_gate = (d_hidden * upper * sigma * (1.0 + gate * (1.0 - sigma))).astype(jnp.bfloat16)
    grad_gate_up = jnp.stack(
        [
            jnp.einsum("td,tf->df", normed_two_all, d_gate, preferred_element_type=jnp.float32),
            jnp.einsum("td,tf->df", normed_two_all, d_upper, preferred_element_type=jnp.float32),
        ]
    )
    d_normed_two = lax.psum_scatter(
        (
            jnp.einsum("tf,df->td", d_gate, w_gate_up[0], preferred_element_type=jnp.float32)
            + jnp.einsum("tf,df->td", d_upper, w_gate_up[1], preferred_element_type=jnp.float32)
        ).astype(jnp.bfloat16),
        "tensor",
        scatter_dimension=0,
        tiled=True,
    ).astype(jnp.float32)
    scaled_two = gain_two * d_normed_two
    d_middle = (
        cotangent.astype(jnp.float32)
        + inv_two * scaled_two
        - middle * inv_two**3 * jnp.mean(scaled_two * middle, axis=-1, keepdims=True)
    )
    grad_gain_two = jnp.sum(d_normed_two * middle * inv_two, axis=0)
    d_middle_all = lax.all_gather(d_middle.astype(jnp.bfloat16), "tensor", axis=0, tiled=True)
    d_mixed = jnp.einsum(
        "td,ed->te", d_middle_all, w_out, preferred_element_type=jnp.float32
    ).astype(jnp.bfloat16)
    grad_out = jnp.einsum("te,td->ed", mixed, d_middle_all, preferred_element_type=jnp.float32)
    d_queries, d_keys, d_values = attend_back(
        queries, keys_rot, values, d_mixed.reshape(shape3), log_sums, segment_ids, valid_mask
    )
    d_project = jnp.stack(
        [
            rotate(d_queries, cosine, -sine).reshape(length, -1),
            rotate(d_keys, cosine, -sine).reshape(length, -1),
            d_values.reshape(length, -1),
        ]
    ).astype(jnp.bfloat16)
    grad_qkv = jnp.einsum("td,cte->cde", normed_all, d_project, preferred_element_type=jnp.float32)
    d_normed = lax.psum_scatter(
        jnp.einsum("cte,cde->td", d_project, w_qkv, preferred_element_type=jnp.float32).astype(
            jnp.bfloat16
        ),
        "tensor",
        scatter_dimension=0,
        tiled=True,
    ).astype(jnp.float32)
    scaled_one = gain_one * d_normed
    d_inputs = (
        d_middle
        + inv_one * scaled_one
        - incoming * inv_one**3 * jnp.mean(scaled_one * incoming, axis=-1, keepdims=True)
    )
    grad_gain_one = jnp.sum(d_normed * incoming * inv_one, axis=0)
    grad_gain_one, grad_gain_two = lax.psum((grad_gain_one, grad_gain_two), ("dp", "tensor"))
    grad_qkv, grad_out, grad_gate_up, grad_down = (
        lax.psum_scatter(
            grad_qkv.astype(jnp.bfloat16), "dp", scatter_dimension=1, tiled=True
        ).astype(jnp.float32),
        lax.psum_scatter(
            grad_out.astype(jnp.bfloat16), "dp", scatter_dimension=1, tiled=True
        ).astype(jnp.float32),
        lax.psum_scatter(
            grad_gate_up.astype(jnp.bfloat16), "dp", scatter_dimension=1, tiled=True
        ).astype(jnp.float32),
        lax.psum_scatter(
            grad_down.astype(jnp.bfloat16), "dp", scatter_dimension=1, tiled=True
        ).astype(jnp.float32),
    )
    return (
        output,
        d_inputs,
        grad_gain_one,
        grad_gain_two,
        grad_qkv,
        grad_out,
        grad_gate_up,
        grad_down,
    )


NT = (((1,), (1,)), ((), ()))
TN = (((0,), (0,)), ((), ()))
MEGA = 1024 * 1024


def chunks(total, step):
    return [(at, min(step, total - at)) for at in range(0, total, step)]


def dot(left, right, dims=None):
    if dims is None:
        return jnp.dot(left, right, preferred_element_type=jnp.float32)
    return lax.dot_general(left, right, dims, preferred_element_type=jnp.float32)


def in_vmem(count):
    return [pl.BlockSpec(memory_space=pltpu.VMEM)] * count


def in_smem():
    return [pl.BlockSpec(memory_space=pltpu.SMEM)]


def like(shape, kind=jnp.bfloat16):
    return jax.ShapeDtypeStruct(shape, kind)


def limit(megabytes):
    return pltpu.CompilerParams(vmem_limit_bytes=megabytes * MEGA)


def starts_of(blocks):
    at, starts = 0, []
    for block in blocks:
        starts.append((at, block.shape[0]))
        at += block.shape[0]
    return starts


def send_shapes(rows, width):
    half = rows // 2
    return [
        like((rows, width), jnp.float32),
        like((rows, width)),
        like((rows, width)),
        like((half, width)),
        like((half, width)),
    ]


def store_parts(part, targets, cols):
    for (start, rows), target in zip(starts_of(targets), targets):
        target[:, cols] = part[start : start + rows].astype(target.dtype)


def norm_kernel(tokens, gain, normed):
    wide = tokens[...].astype(jnp.float32)
    inverse = lax.rsqrt(jnp.mean(wide * wide, axis=-1, keepdims=True) + EPS)
    normed[...] = (wide * inverse * gain[...].astype(jnp.float32)).astype(jnp.bfloat16)


def norm(tokens, gain):
    return pl.pallas_call(
        norm_kernel,
        name="norm",
        out_shape=like(tokens.shape),
        in_specs=in_vmem(2),
        out_specs=in_vmem(1)[0],
        compiler_params=limit(4),
    )(tokens, gain)


def relay_kernel(to_x, to_y, via_x, via_y, next_x, next_y):
    half = via_x.shape[0]
    next_x[:half] = to_x[:half]
    next_x[half:] = (
        to_x[half:].astype(jnp.float32) + via_y[...].astype(jnp.float32)
    ).astype(jnp.bfloat16)
    next_y[:half] = (
        to_y[:half].astype(jnp.float32) + via_x[...].astype(jnp.float32)
    ).astype(jnp.bfloat16)
    next_y[half:] = to_y[half:]


def relay(to_x, to_y, via_x, via_y):
    return pl.pallas_call(
        relay_kernel,
        name="relay",
        out_shape=[like(to_x.shape), like(to_y.shape)],
        in_specs=in_vmem(4),
        out_specs=in_vmem(2),
        compiler_params=limit(4),
    )(to_x, to_y, via_x, via_y)


def middle_kernel(tokens, keep, got_x, got_y, gain, middle, normed):
    total = (
        tokens[...].astype(jnp.float32)
        + keep[...]
        + got_x[...].astype(jnp.float32)
        + got_y[...].astype(jnp.float32)
    )
    middle[...] = total
    inverse = lax.rsqrt(jnp.mean(total * total, axis=-1, keepdims=True) + EPS)
    normed[...] = (total * inverse * gain[...].astype(jnp.float32)).astype(jnp.bfloat16)


def make_middle(tokens, keep, got_x, got_y, gain):
    return pl.pallas_call(
        middle_kernel,
        name="make_middle",
        out_shape=[like(keep.shape, jnp.float32), like(keep.shape)],
        in_specs=in_vmem(5),
        out_specs=in_vmem(2),
        compiler_params=limit(6),
    )(tokens, keep, got_x, got_y, gain)


def norm_back_kernel(base, keep, got_x, got_y, source, gain, *outs):
    d_normed = keep[...] + got_x[...].astype(jnp.float32) + got_y[...].astype(jnp.float32)
    wide = source[...].astype(jnp.float32)
    inverse = lax.rsqrt(jnp.mean(wide * wide, axis=-1, keepdims=True) + EPS)
    scaled = gain[...].astype(jnp.float32) * d_normed
    slope = jnp.mean(scaled * wide, axis=-1, keepdims=True) * inverse * inverse * inverse
    total = base[...].astype(jnp.float32) + inverse * scaled - wide * slope
    outs[0][...] = total
    outs[1][...] = jnp.sum(d_normed * wide * inverse, axis=0, keepdims=True)
    if len(outs) == 3:
        outs[2][...] = total.astype(jnp.bfloat16)


def norm_back(base, keep, got_x, got_y, source, gain, low):
    return pl.pallas_call(
        norm_back_kernel,
        name="norm_back",
        out_shape=[like(keep.shape, jnp.float32), like((1, keep.shape[1]), jnp.float32)]
        + [like(keep.shape)] * low,
        in_specs=in_vmem(6),
        out_specs=in_vmem(2 + low),
        compiler_params=limit(8),
    )(base, keep, got_x, got_y, source, gain)


def prepare_kernel(segments, valid, cosine, sine, seg_col, valid_col):
    length = cosine.shape[0]
    half = HD // 2
    place = lax.broadcasted_iota(jnp.int32, (length, HD), 0).astype(jnp.float32)
    lane = lax.broadcasted_iota(jnp.int32, (length, HD), 1)
    step = jnp.where(lane < half, lane, lane - half).astype(jnp.float32)
    angle = place * jnp.exp(step * (-2.0 / HD * math.log(THETA)))
    cosine[...] = jnp.cos(angle)
    turn = jnp.sin(angle)
    sine[...] = jnp.where(lane < half, -turn, turn)
    seg_col[...] = jnp.broadcast_to(segments[...], (HD, length)).T
    valid_col[...] = jnp.broadcast_to(valid[...], (HD, length)).T


def prepare(segments, valid):
    length = segments.shape[1]
    return pl.pallas_call(
        prepare_kernel,
        name="prepare",
        out_shape=[like((length, HD), jnp.float32)] * 4,
        in_specs=in_vmem(2),
        out_specs=in_vmem(4),
        compiler_params=limit(6),
    )(segments, valid)


def project_kernel(
    rows_at, own, from_x, from_y, low, high, w_qkv, cosine, sine, normed, queries, keys, values
):
    for i, block in enumerate((own, from_x, from_y, low, high)):
        place = pl.multiple_of(rows_at[i], 64)
        normed[pl.ds(place, block.shape[0]), :] = block[...]
    for c, target in enumerate((queries, keys, values)):
        for at, size in chunks(target.shape[1], 2 * HD):
            part = dot(normed[...], w_qkv[c, :, at : at + size])
            for head in range(0, size, HD):
                piece = part[:, head : head + HD]
                if c < 2:
                    piece = piece * cosine[...] + pltpu.roll(piece, HD // 2, 1) * sine[...]
                target[:, at + head : at + head + HD] = piece.astype(jnp.bfloat16)


def project(rows_at, blocks, w_qkv, cosine, sine):
    rows, width = blocks[0].shape
    length = 4 * rows
    wide = w_qkv.shape[2]
    return pl.pallas_call(
        project_kernel,
        name="project",
        out_shape=[like((length, width))] + [like((length, wide))] * 3,
        in_specs=in_smem() + in_vmem(8),
        out_specs=in_vmem(4),
        compiler_params=limit(8),
    )(rows_at, *blocks, w_qkv, cosine, sine)


def attend_kernel(
    rows_at, queries, keys, values, w_out, seg_row, seg_col, valid_col,
    keep, to_x, to_y, far_low, far_high, probs, mixed, bias, joined,
):
    length, wide = queries.shape
    key_at = lax.broadcasted_iota(jnp.int32, (length, length), 0)
    query_at = lax.broadcasted_iota(jnp.int32, (length, length), 1)
    allowed = (
        (key_at <= query_at)
        & (seg_col[:, 0:1] == seg_row[...])
        & ((valid_col[:, 0:1] == 1.0) | (key_at == query_at))
    )
    bias[...] = jnp.where(allowed, 0.0, -1e30)
    for at in range(0, wide, HD):
        head = at // HD
        cols = slice(at, at + HD)
        for q_at, q_size in chunks(length, 256):
            seen = q_at + q_size
            scores = dot(keys[0:seen, cols], queries[q_at:seen, cols], NT)
            scores = scores * HD ** (-0.5) + bias[0:seen, q_at:seen]
            top = jnp.max(scores, axis=0, keepdims=True)
            expo = jnp.exp(scores - top)
            total = jnp.sum(expo, axis=0, keepdims=True)
            chance = (expo * (1.0 / total)).astype(jnp.bfloat16)
            probs[head, 0:seen, q_at:seen] = chance
            result = dot(values[0:seen, cols], chance, TN)
            joined[q_at:seen, cols] = result.T.astype(jnp.bfloat16)
    targets = [keep, to_x, to_y, far_low, far_high]
    for i, (start, size) in enumerate(starts_of(targets)):
        place = pl.multiple_of(rows_at[i], 64)
        mixed[start : start + size, :] = joined[pl.ds(place, size), :]
    for at, size in chunks(w_out.shape[1], 512):
        store_parts(dot(mixed[...], w_out[:, at : at + size]), targets, slice(at, at + size))


def attend_square(rows_at, queries, keys, values, w_out, seg_row, seg_col, valid_col):
    length, wide = queries.shape
    width = w_out.shape[1]
    heads = wide // HD
    return pl.pallas_call(
        attend_kernel,
        name="attend",
        out_shape=send_shapes(length // 4, width)
        + [like((heads, length, length)), like((length, wide))],
        in_specs=in_smem() + in_vmem(7),
        out_specs=in_vmem(7),
        scratch_shapes=[
            pltpu.VMEM((length, length), jnp.float32),
            pltpu.VMEM((length, wide), jnp.bfloat16),
        ],
        compiler_params=limit(8),
    )(rows_at, queries, keys, values, w_out, seg_row, seg_col, valid_col)


def d_hidden_kernel(own, from_x, from_y, low, high, w_down, d_hidden, cot_all):
    blocks = [own, from_x, from_y, low, high]
    for (start, size), block in zip(starts_of(blocks), blocks):
        cot_all[start : start + size, :] = block[...]
    for at, size in chunks(w_down.shape[0], 256):
        d_hidden[:, at : at + size] = dot(cot_all[...], w_down[at : at + size, :], NT)


def back_through_down(blocks, w_down):
    rows, width = blocks[0].shape
    length = 4 * rows
    units = w_down.shape[0]
    return pl.pallas_call(
        d_hidden_kernel,
        name="back_through_down",
        out_shape=[like((length, units), jnp.float32), like((length, width))],
        in_specs=in_vmem(6),
        out_specs=in_vmem(2),
        compiler_params=limit(6),
    )(*blocks, w_down)


def mlp_kernel(
    own, from_x, from_y, low, high, d_hidden, w_gate_up, normed, hidden, d_gate_up
):
    units = w_gate_up.shape[2]
    blocks = [own, from_x, from_y, low, high]
    for (start, size), block in zip(starts_of(blocks), blocks):
        normed[start : start + size, :] = block[...]
    for at, size in chunks(units, 256):
        here = slice(at, at + size)
        gate = dot(normed[...], w_gate_up[0, :, here])
        upper = dot(normed[...], w_gate_up[1, :, here])
        incoming = d_hidden[:, here]
        sigma = 1.0 / (1.0 + jnp.exp(-gate))
        silu = gate * sigma
        hidden[:, here] = (silu * upper).astype(jnp.bfloat16)
        d_gate_up[:, here] = (incoming * upper * sigma * (1.0 + gate * (1.0 - sigma))).astype(
            jnp.bfloat16
        )
        d_gate_up[:, units + at : units + at + size] = (incoming * silu).astype(jnp.bfloat16)


def mlp(blocks, d_hidden, w_gate_up):
    rows, width = blocks[0].shape
    length = 4 * rows
    units = w_gate_up.shape[2]
    return pl.pallas_call(
        mlp_kernel,
        name="mlp",
        out_shape=[like((length, width)), like((length, units)), like((length, 2 * units))],
        in_specs=in_vmem(7),
        out_specs=in_vmem(3),
        compiler_params=limit(8),
    )(*blocks, d_hidden, w_gate_up)


def mlp_back_kernel(d_gate_up, w_gate_up, *targets):
    units = w_gate_up.shape[2]
    for at, size in chunks(w_gate_up.shape[1], 256):
        part = dot(d_gate_up[:, 0:units], w_gate_up[0, at : at + size, :], NT) + dot(
            d_gate_up[:, units : 2 * units], w_gate_up[1, at : at + size, :], NT
        )
        store_parts(part, targets, slice(at, at + size))


def mlp_back(d_gate_up, w_gate_up):
    return pl.pallas_call(
        mlp_back_kernel,
        name="mlp_back",
        out_shape=send_shapes(d_gate_up.shape[0] // 4, w_gate_up.shape[1]),
        in_specs=in_vmem(2),
        out_specs=in_vmem(5),
        compiler_params=limit(6),
    )(d_gate_up, w_gate_up)


def down_kernel(hidden, w_down, *targets):
    for at, size in chunks(w_down.shape[1], 256):
        store_parts(dot(hidden[...], w_down[:, at : at + size]), targets, slice(at, at + size))


def through_down(hidden, w_down):
    return pl.pallas_call(
        down_kernel,
        name="through_down",
        out_shape=send_shapes(hidden.shape[0] // 4, w_down.shape[1]),
        in_specs=in_vmem(2),
        out_specs=in_vmem(5),
        compiler_params=limit(6),
    )(hidden, w_down)


def attend_back_kernel(
    rows_at, own, from_x, from_y, low, high, w_out, probs, queries, keys, values, cosine, sine,
    d_middle, d_project, d_mixed,
):
    length, wide = queries.shape
    blocks = [own, from_x, from_y, low, high]
    starts = starts_of(blocks)
    for (start, size), block in zip(starts, blocks):
        d_middle[start : start + size, :] = block[...]
    for at, size in chunks(wide, 256):
        part = dot(d_middle[...], w_out[at : at + size, :], NT).astype(jnp.bfloat16)
        for i, (start, rows) in enumerate(starts):
            place = pl.multiple_of(rows_at[i], 64)
            d_mixed[pl.ds(place, rows), at : at + size] = part[start : start + rows]
    scale = HD ** (-0.5)

    def back(turned, rows):
        return turned * cosine[rows, :] - pltpu.roll(turned, HD // 2, 1) * sine[rows, :]

    for at in range(0, wide, HD):
        head = at // HD
        cols = slice(at, at + HD)
        d_keys = d_values = None
        for q_at, q_size in reversed(chunks(length, 256)):
            seen = q_at + q_size
            rows = slice(q_at, seen)
            chance = probs[head, 0:seen, rows]
            d_out = d_mixed[rows, cols]
            d_chance = dot(values[0:seen, cols], d_out, NT)
            exact = chance.astype(jnp.float32)
            delta = jnp.sum(d_chance * exact, axis=0, keepdims=True)
            d_scores = (exact * (d_chance - delta)).astype(jnp.bfloat16)
            more_values = dot(chance, d_out)
            more_keys = dot(d_scores, queries[rows, cols])
            d_queries = dot(keys[0:seen, cols], d_scores, TN).T
            d_project[rows, cols] = back(d_queries * scale, rows).astype(jnp.bfloat16)
            if d_keys is None:
                d_keys, d_values = more_keys, more_values
            else:
                d_keys = jnp.concatenate([d_keys[:seen] + more_keys, d_keys[seen:]], axis=0)
                d_values = jnp.concatenate([d_values[:seen] + more_values, d_values[seen:]], axis=0)
        d_project[:, wide + at : wide + at + HD] = back(d_keys * scale, slice(0, length)).astype(
            jnp.bfloat16
        )
        d_project[:, 2 * wide + at : 2 * wide + at + HD] = d_values.astype(jnp.bfloat16)


def attend_back_square(rows_at, blocks, w_out, probs, queries, keys, values, cosine, sine):
    length, wide = queries.shape
    return pl.pallas_call(
        attend_back_kernel,
        name="attend_back",
        out_shape=[like((length, w_out.shape[1])), like((length, 3 * wide))],
        in_specs=in_smem() + in_vmem(12),
        out_specs=in_vmem(2),
        scratch_shapes=[pltpu.VMEM((length, wide), jnp.bfloat16)],
        compiler_params=limit(8),
    )(rows_at, *blocks, w_out, probs, queries, keys, values, cosine, sine)


def project_back_kernel(rows_at, d_project, w_qkv, *refs):
    targets, turned = refs[:5], refs[5]
    wide = w_qkv.shape[2]
    for i, (start, size) in enumerate(starts_of(targets)):
        place = pl.multiple_of(rows_at[i], 64)
        turned[start : start + size, :] = d_project[pl.ds(place, size), :]
    for at, size in chunks(w_qkv.shape[1], 256):
        part = sum(
            dot(turned[:, c * wide : (c + 1) * wide], w_qkv[c, at : at + size, :], NT)
            for c in range(3)
        )
        store_parts(part, targets, slice(at, at + size))


def project_back(rows_at, d_project, w_qkv):
    return pl.pallas_call(
        project_back_kernel,
        name="project_back",
        out_shape=send_shapes(d_project.shape[0] // 4, w_qkv.shape[1]),
        in_specs=in_smem() + in_vmem(2),
        out_specs=in_vmem(5),
        scratch_shapes=[pltpu.VMEM(d_project.shape, jnp.bfloat16)],
        compiler_params=limit(8),
    )(rows_at, d_project, w_qkv)


def weight_kernel(layout, base, spot, which, *refs):
    turned, out = refs[-1], refs[-2]
    more = refs[-3] if spot is not None else None
    count, piece, _ = out.shape
    for i in range(count):
        place = pl.multiple_of(which[base + i] * piece, piece)
        at_ref = column = 0
        for pairs in layout:
            splits = refs[at_ref : at_ref + pairs]
            others = refs[at_ref + pairs : at_ref + 2 * pairs]
            at_ref += 2 * pairs
            length, across = others[0].shape
            for j, split in enumerate(splits):
                turned[:, j * length : (j + 1) * length] = split[:, pl.ds(place, piece)].T
            for at, size in chunks(across, 256):
                part = None
                for j, other in enumerate(others):
                    term = dot(turned[:, j * length : (j + 1) * length], other[:, at : at + size])
                    part = term if part is None else part + term
                cols = slice(column + at, column + at + size)
                if more is not None:
                    part = part + more[spot + i, :, cols].astype(jnp.float32)
                out[i, :, cols] = part.astype(out.dtype)
            column += across


def weight_pieces(which, base, count, groups, more=None, spot=None):
    layout = [len(splits) for splits, _ in groups]
    refs = [ref for splits, others in groups for ref in (*splits, *others)]
    extra = [] if more is None else [more]
    length = groups[0][1][0].shape[0]
    across = sum(others[0].shape[1] for _, others in groups)
    piece = groups[0][0][0].shape[1] // 8
    return pl.pallas_call(
        functools.partial(weight_kernel, layout, base, spot),
        name="weight_pieces",
        out_shape=like((count, piece, across)),
        in_specs=in_smem() + in_vmem(len(refs) + len(extra)),
        out_specs=in_vmem(1)[0],
        scratch_shapes=[pltpu.VMEM((piece, max(layout) * length), jnp.bfloat16)],
        compiler_params=limit(16),
    )(which, *refs, *extra)


def join_kernel(here_outer, here_own, there_outer, there_own, outer, own):
    for here, there, out in ((here_outer, there_outer, outer), (here_own, there_own, own)):
        for at, size in chunks(out.shape[2], 256):
            cols = slice(at, at + size)
            out[0, :, cols] = (
                here[0, :, cols].astype(jnp.float32) + there[0, :, cols].astype(jnp.float32)
            ).astype(jnp.bfloat16)


def join(here, there):
    shape = here[0].shape
    return pl.pallas_call(
        join_kernel,
        name="join",
        out_shape=[like(shape), like(shape)],
        in_specs=in_vmem(4),
        out_specs=in_vmem(2),
        compiler_params=limit(6),
    )(*here, *there)


def hand_kernel(near, far, out):
    for at, size in chunks(out.shape[1], 256):
        cols = slice(at, at + size)
        out[:, cols] = (
            near[0, :, cols].astype(jnp.float32) + far[0, :, cols].astype(jnp.float32)
        ).astype(jnp.bfloat16)


def hand(near, far):
    return pl.pallas_call(
        hand_kernel,
        name="hand",
        out_shape=like(near.shape[1:]),
        in_specs=in_vmem(2),
        out_specs=in_vmem(1)[0],
        compiler_params=limit(6),
    )(near, far)


def finish_kernel(parts, count_inner, inner, *refs):
    count = len(refs) - len(parts)
    here = [ref for ref in refs[:count_inner]]
    outer = [ref for ref in refs[count_inner:count]]

    def total(sources, cols):
        found = None
        for source in sources:
            term = source[0, :, cols] if len(source.shape) == 3 else source[:, cols]
            term = term.astype(jnp.float32)
            found = term if found is None else found + term
        return found

    column = 0
    for (planes, across, turn), out in zip(parts, refs[count:]):
        for c in range(planes):
            for at, size in chunks(across, 256):
                cols = slice(column + at, column + at + size)
                value = jnp.where(inner[0] == 1, total(here, cols), total(outer, cols))
                if turn:
                    out[at : at + size, :] = value.T
                else:
                    out[c, :, at : at + size] = value
            column += across


def finish(inner, here, outer, parts):
    piece = here[0].shape[-2]
    return pl.pallas_call(
        functools.partial(finish_kernel, parts, len(here)),
        name="finish",
        out_shape=[
            like((across, piece) if turn else (planes, piece, across), jnp.float32)
            for planes, across, turn in parts
        ],
        in_specs=in_smem() + in_vmem(len(here) + len(outer)),
        out_specs=in_vmem(len(parts)),
        compiler_params=limit(8),
    )(inner, *here, *outer)


def gains_kernel(chip, *refs):
    sources, out, kept = refs[:4], refs[4], refs[5]
    for back, source in enumerate(sources):
        kept[lax.rem(chip[0] + 4 - back, 4)] = source[...]
    out[...] = (kept[0] + kept[1]) + (kept[2] + kept[3])


def sum_gains(chip, sources):
    return pl.pallas_call(
        gains_kernel,
        name="sum_gains",
        out_shape=like(sources[0].shape, jnp.float32),
        in_specs=in_smem() + in_vmem(4),
        out_specs=in_vmem(1)[0],
        scratch_shapes=[pltpu.VMEM((4, *sources[0].shape), jnp.float32)],
        compiler_params=limit(4),
    )(chip, *sources)


def flips(size, bit):
    return [(i, i ^ bit) for i in range(size)]


def after(value, *earlier):
    return lax.optimization_barrier((value, *earlier))[0]


def over_tensor(values, bit):
    return lax.ppermute(values, "tensor", flips(4, bit))


def gather_near(own):
    return own, over_tensor(own, 1), over_tensor(own, 2)


def gather_far(own, from_x, from_y):
    half = own.shape[0] // 2
    low = over_tensor(from_y[:half], 1)
    high = over_tensor(from_x[half:], 2)
    return [own, from_x, from_y, low, high]


def scatter_far(keep, to_x, to_y, far_low, far_high):
    return keep, *relay(to_x, to_y, over_tensor(far_low, 1), over_tensor(far_high, 2))


def scatter_near(keep, to_x, to_y):
    return keep, over_tensor(to_x, 1), over_tensor(to_y, 2)


def over_cores(values):
    return lax.ppermute(values, "dp", flips(8, 1))


def up_the_line(values, chips):
    return lax.ppermute(values, "dp", [(i, (i + 2 * chips) % 8) for i in range(8)])


def to_inner(values):
    return lax.ppermute(values, "dp", [(0, 2), (1, 3), (6, 4), (7, 5)])


def to_outer(values):
    return lax.ppermute(values, "dp", [(2, 0), (3, 1), (4, 6), (5, 7)])


def over_middle(values):
    return lax.ppermute(values, "dp", [(2, 4), (3, 5), (4, 2), (5, 3)])


class Weight:
    def __init__(self, places, groups):
        self.which_theirs, self.which_mine, self.inner = places
        self.groups = groups

    def sibling_part(self):
        self.sibling_sum = weight_pieces(self.which_theirs, 0, 4, self.groups)
        self.theirs = over_cores(self.sibling_sum)

    def own_part(self, base, count, *earlier):
        more = after(self.theirs, *earlier) if earlier else self.theirs
        return weight_pieces(self.which_mine, base, count, self.groups, more, base)


def sum_flips(values, *steps):
    for axis, size, bit in steps:
        values = values + lax.ppermute(values, axis, flips(size, bit))
    return values


def per_device_square(
    tokens, gain_attn, gain_mlp, w_qkv, w_out, w_gate_up, w_down, cotangent, segment_ids, valid_mask
):
    rows = tokens.shape[0]
    length = segment_ids.shape[0]
    low = jnp.bfloat16
    me = lax.axis_index("tensor")
    order = [me, me ^ 1, me ^ 2, me ^ 3]
    rows_at = jnp.stack([at * rows for at in order] + [order[3] * rows + rows // 2]).astype(jnp.int32)
    index = lax.axis_index("dp")
    place, core = index // 2, index % 2
    line_order = jnp.where(place < 2, jnp.array([3, 2, 0, 1]), jnp.array([0, 1, 3, 2]))
    places = (
        (2 * line_order + 1 - core).astype(jnp.int32),
        (2 * line_order + core).astype(jnp.int32),
        ((place == 1) | (place == 2)).astype(jnp.int32).reshape(1),
    )
    chip = place.astype(jnp.int32).reshape(1)
    gain_one = gain_attn[None, :]
    gain_two = gain_mlp[None, :]

    tokens = after(tokens, rows_at, chip, *places)
    normed = norm(tokens, gain_one)
    near = gather_near(normed)
    cosine, sine, seg_col, valid_col = prepare(
        segment_ids.astype(jnp.float32)[None, :],
        valid_mask.astype(jnp.float32)[None, :],
    )
    near = (near[0], near[1], after(near[2], cosine))
    guest_cot_own = to_inner(cotangent)
    blocks = gather_far(*near)
    cot_near = gather_near(after(cotangent, *blocks))
    normed_all, queries, keys, values = project(
        rows_at, blocks, w_qkv, cosine, sine
    )
    *sent, probs, mixed = attend_square(
        rows_at,
        after(queries, *cot_near, guest_cot_own),
        keys,
        values,
        w_out,
        segment_ids.astype(jnp.float32)[None, :],
        seg_col,
        valid_col,
    )
    guest_cot_near = [to_inner(part) for part in cot_near[1:]]
    keep, to_x, to_y = scatter_far(*sent)
    cot_blocks = gather_far(*(after(part, to_x) for part in cot_near))
    got = scatter_near(keep, to_x, to_y)
    d_hidden, cot_all = back_through_down(
        [after(cot_blocks[0], *guest_cot_near)] + cot_blocks[1:], w_down
    )
    middle, normed_two = make_middle(tokens, after(got[0], cot_all), *got[1:], gain_two)

    near = gather_near(normed_two)
    guest_cot_far = [to_inner(part) for part in cot_blocks[3:]]
    guest_own = to_inner(after(normed_two, *guest_cot_far))
    blocks = gather_far(*near)
    normed_two_all, hidden, d_gate_up = mlp(
        [after(blocks[0], *guest_cot_far)] + blocks[1:], d_hidden, w_gate_up
    )
    guest_near = [to_inner(part) for part in near[1:]]
    guest_far = [to_inner(part) for part in blocks[3:]]
    sent = mlp_back(d_gate_up, w_gate_up)
    keep, to_x, to_y = scatter_far(*sent)
    to_x = after(to_x, guest_own, *guest_near)
    guest_d_hidden, guest_cot_all = back_through_down(
        [after(guest_cot_own, to_x), *guest_cot_near, *guest_cot_far], w_down
    )
    got = scatter_near(keep, to_x, to_y)
    d_middle, gain_two_part, d_middle_low = norm_back(
        cotangent, after(got[0], guest_d_hidden), *got[1:], middle, gain_two, True
    )
    near = gather_near(d_middle_low)
    guest_normed_two, guest_hidden, guest_d_gate_up = mlp(
        [after(guest_own, d_middle_low), *guest_near, *guest_far], guest_d_hidden, w_gate_up
    )
    down = Weight(places, [([cot_all, guest_cot_all], [hidden, guest_hidden])])
    down.sibling_part()
    gate = Weight(
        places,
        [
            (
                [normed_two_all, after(guest_normed_two, down.theirs)],
                [d_gate_up, guest_d_gate_up],
            )
        ],
    )
    gate.sibling_part()
    blocks = gather_far(*near)
    down_outer = down.own_part(0, 1, gate.sibling_sum)
    down_own = down.own_part(1, 1, down_outer)
    gate_outer = gate.own_part(0, 1, down_own)
    gate_own = gate.own_part(1, 1, gate_outer)
    down_outer = over_middle(down_outer)

    d_middle_all, d_project = attend_back_square(
        rows_at,
        blocks,
        w_out,
        after(probs, gate_own),
        queries,
        keys,
        values,
        cosine,
        sine,
    )
    gate_outer = over_middle(gate_outer)
    late = Weight(places, [([normed_all], [d_project]), ([d_middle_all], [mixed])])
    late.groups[0] = ([after(normed_all, down_outer)], [d_project])
    late.sibling_part()
    down_near = [down.own_part(2, 1, late.sibling_sum)]
    down_handed = hand(down_near[0], down_outer)
    down_given = to_outer(down_handed)
    late_far = [late.own_part(0, 1, down_handed)]
    late_far += [late.own_part(1, 1, late_far[0])]
    late_arrived = [to_inner(part) for part in late_far]
    sent = project_back(rows_at, after(d_project, late_far[1]), w_qkv)
    keep, to_x, to_y = scatter_far(*sent)
    gate_own = over_middle(after(gate_own, to_x, to_y))
    down_own = over_middle(after(down_own, to_x, to_y))
    late_near = [late.own_part(2, 1, to_x, to_y)]
    late_near += [late.own_part(3, 1, late_near[0])]
    late_near_arrived = to_inner(late_near[1])
    got = scatter_near(keep, to_x, to_y)
    gate_near = [gate.own_part(2, 1, late_near[1])]
    gate_handed = hand(gate_near[0], gate_outer)
    gate_given = to_outer(gate_handed)
    gate_near += [gate.own_part(3, 1, gate_handed)]
    down_near += [down.own_part(3, 1, gate_near[1])]
    d_inputs, gain_one_part = norm_back(
        d_middle,
        after(got[0], down_near[1], down_given, late_arrived[0]),
        *got[1:],
        tokens,
        gain_one,
        False,
    )
    late_far[0] = after(late_far[0], d_inputs, gate_own, down_own)
    late_outer, late_own = join(late_far, late_arrived)
    gains = sum_flips(
        after(jnp.concatenate([gain_one_part, gain_two_part], axis=0), late_own),
        ("dp", 8, 1),
        ("tensor", 4, 1),
        ("tensor", 4, 2),
    )
    sent = through_down(after(hidden, gains, gate_given), w_down)
    late_outer = over_middle(late_outer)
    keep, to_x, to_y, *sent = sent
    via_x, via_y = over_tensor(sent[0], 1), over_tensor(sent[1], 2)
    late_own = over_middle(after(late_own, via_x, via_y))
    late_handed = hand(after(late_near[0], via_x, via_y), late_outer)
    late_given = to_outer(late_handed)
    to_x, to_y = relay(after(to_x, late_handed), to_y, via_x, via_y)
    gains = [after(gains, late_handed)]
    gains += [up_the_line(gains[0], chips) for chips in (1, 2, 3)]
    keep, got_x, got_y = scatter_near(keep, to_x, to_y)
    output = (middle + keep + got_x.astype(jnp.float32) + got_y.astype(jnp.float32)).astype(low)
    inner = places[2]
    units, wide = w_down.shape[0], w_qkv.shape[2]
    (grad_down,) = finish(
        inner,
        [after(down_near[1], output, late_near_arrived), down_own],
        [down_given],
        [(1, units, True)],
    )
    (grad_gate_up,) = finish(
        inner, [after(gate_near[1], grad_down), gate_own], [gate_given], [(2, units, False)]
    )
    grad_gains = sum_gains(chip, [after(gains[0], grad_gate_up), *gains[1:]])
    grad_qkv, grad_out = finish(
        inner,
        [late_near[1], late_near_arrived, late_own],
        [late_near[0], late_given],
        [(3, wide, False), (1, wide, True)],
    )
    return (
        output,
        d_inputs,
        grad_gains[0],
        grad_gains[1],
        grad_qkv,
        grad_out,
        grad_gate_up,
        grad_down,
    )


def solution(mesh):
    placed = (
        P(("dp", "tensor"), None),
        P(),
        P(),
        P(None, None, "tensor"),
        P("tensor", None),
        P(None, None, "tensor"),
        P("tensor", None),
        P(("dp", "tensor"), None),
        P("dp"),
        P("dp"),
    )
    square = mesh.shape["tensor"] == 4 and mesh.shape["dp"] == 8
    return jax.shard_map(
        per_device_square if square else per_device,
        mesh=mesh,
        in_specs=placed,
        out_specs=(
            P(("dp", "tensor"), None),
            P(("dp", "tensor"), None),
            P(),
            P(),
            P(None, "dp", "tensor"),
            P("tensor", "dp"),
            P(None, "dp", "tensor"),
            P("tensor", "dp"),
        ),
        check_vma=False,
    )
```

```python
import functools
import math

import jax
import jax.numpy as jnp
from jax import lax
from jax.experimental import pallas as pl
from jax.experimental.pallas import tpu as pltpu
from jax.sharding import PartitionSpec as P

HD = 128


EPS = 1e-06
THETA = 10000.0


def rope_tables(places):
    positions = places.astype(jnp.float32)
    freqs = THETA ** (-(jnp.arange(HD // 2).astype(jnp.float32) * 2.0 / HD))
    angles = positions[:, None] * freqs[None, :]
    return (jnp.cos(angles), jnp.sin(angles))


def rotate(values, cosine, sine):
    half = values.shape[-1] // 2
    first = values[..., :half]
    second = values[..., half:]
    cosine = cosine[:, None, :]
    sine = sine[:, None, :]
    return jnp.concatenate(
        [first * cosine - second * sine, second * cosine + first * sine], axis=-1
    )


def block_scores(q_block, keys_rot, start, segments, valid):
    block_rows = q_block.shape[0]
    length = keys_rot.shape[0]
    key_pos = jnp.arange(length)
    row_pos = start + jnp.arange(block_rows)
    row_seg = lax.dynamic_slice_in_dim(segments, start, block_rows, 0)
    scores = jnp.einsum(
        "qhd,khd->hqk", q_block, keys_rot, preferred_element_type=jnp.float32
    ) * HD ** (-0.5)
    allowed = (
        (key_pos[None, :] <= row_pos[:, None])
        & (row_seg[:, None] == segments[None, :])
        & ((valid[None, :] == 1) | (key_pos[None, :] == row_pos[:, None]))
    )
    return jnp.where(allowed[None], scores, -1e30)


def attend(queries, keys_rot, values, segments, valid):
    length = queries.shape[0]
    block_rows = min(512, length)
    count = length // block_rows

    def one_block(index):
        start = index * block_rows
        q_block = lax.dynamic_slice_in_dim(queries, start, block_rows, 0)
        scores = block_scores(q_block, keys_rot, start, segments, valid)
        top = jnp.max(scores, axis=-1, keepdims=True)
        expo = jnp.exp(scores - top)
        total = jnp.sum(expo, axis=-1, keepdims=True)
        probs = (expo / total).astype(jnp.bfloat16)
        result = jnp.einsum("hqk,khd->qhd", probs, values, preferred_element_type=jnp.float32)
        return (result, top[..., 0] + jnp.log(total[..., 0]))

    blocks, log_sums = lax.map(one_block, jnp.arange(count))
    return (blocks.reshape(length, -1), log_sums)


def attend_back(queries, keys_rot, values, d_mixed, log_sums, segments, valid):
    length = queries.shape[0]
    block_rows = min(512, length)
    count = length // block_rows
    scale = HD ** (-0.5)

    def one_block(carry, index):
        d_keys, d_values = carry
        start = index * block_rows
        q_block = lax.dynamic_slice_in_dim(queries, start, block_rows, 0)
        d_block = lax.dynamic_slice_in_dim(d_mixed, start, block_rows, 0)
        scores = block_scores(q_block, keys_rot, start, segments, valid)
        probs = jnp.exp(scores - log_sums[index][..., None])
        d_values = d_values + jnp.einsum(
            "hqk,qhd->khd", probs.astype(jnp.bfloat16), d_block, preferred_element_type=jnp.float32
        )
        d_probs = jnp.einsum("qhd,khd->hqk", d_block, values, preferred_element_type=jnp.float32)
        delta = jnp.sum(d_probs * probs, axis=-1, keepdims=True)
        d_scores = (probs * (d_probs - delta)).astype(jnp.bfloat16)
        d_query = scale * jnp.einsum(
            "hqk,khd->qhd", d_scores, keys_rot, preferred_element_type=jnp.float32
        )
        d_keys = d_keys + scale * jnp.einsum(
            "hqk,qhd->khd", d_scores, q_block, preferred_element_type=jnp.float32
        )
        return ((d_keys, d_values), d_query)

    empty = jnp.zeros(keys_rot.shape, jnp.float32)
    (d_keys, d_values), d_queries = lax.scan(one_block, (empty, empty), jnp.arange(count))
    return (d_queries.reshape(queries.shape), d_keys, d_values)


def per_device(
    tokens, gain_attn, gain_mlp, w_qkv, w_out, w_gate_up, w_down, cotangent, segment_ids, valid_mask
):
    length = segment_ids.shape[0]
    heads_here = w_qkv.shape[2] // HD
    shape3 = (length, heads_here, HD)
    incoming = tokens.astype(jnp.float32)
    gain_one = gain_attn.astype(jnp.float32)
    gain_two = gain_mlp.astype(jnp.float32)
    cosine, sine = rope_tables(jnp.arange(length))
    inv_one = lax.rsqrt(jnp.mean(incoming * incoming, axis=-1, keepdims=True) + EPS)
    normed = (incoming * inv_one * gain_one).astype(jnp.bfloat16)
    normed_all = lax.all_gather(normed, "tensor", axis=0, tiled=True)
    project = jnp.einsum("td,cde->cte", normed_all, w_qkv, preferred_element_type=jnp.float32)
    queries = rotate(project[0].reshape(shape3), cosine, sine).astype(jnp.bfloat16)
    keys_rot = rotate(project[1].reshape(shape3), cosine, sine).astype(jnp.bfloat16)
    values = project[2].reshape(shape3).astype(jnp.bfloat16)
    mixed, log_sums = attend(queries, keys_rot, values, segment_ids, valid_mask)
    mixed = mixed.astype(jnp.bfloat16)
    middle = incoming + lax.psum_scatter(
        jnp.dot(mixed, w_out, preferred_element_type=jnp.float32).astype(jnp.bfloat16),
        "tensor",
        scatter_dimension=0,
        tiled=True,
    ).astype(jnp.float32)
    inv_two = lax.rsqrt(jnp.mean(middle * middle, axis=-1, keepdims=True) + EPS)
    normed_two = (middle * inv_two * gain_two).astype(jnp.bfloat16)
    normed_two_all = lax.all_gather(normed_two, "tensor", axis=0, tiled=True)
    gate = jnp.dot(normed_two_all, w_gate_up[0], preferred_element_type=jnp.float32)
    upper = jnp.dot(normed_two_all, w_gate_up[1], preferred_element_type=jnp.float32)
    sigma = jax.nn.sigmoid(gate)
    hidden = (gate * sigma * upper).astype(jnp.bfloat16)
    result = middle + lax.psum_scatter(
        jnp.dot(hidden, w_down, preferred_element_type=jnp.float32).astype(jnp.bfloat16),
        "tensor",
        scatter_dimension=0,
        tiled=True,
    ).astype(jnp.float32)
    output = result.astype(jnp.bfloat16)
    cot_all = lax.all_gather(cotangent, "tensor", axis=0, tiled=True)
    d_hidden = jnp.einsum("td,fd->tf", cot_all, w_down, preferred_element_type=jnp.float32)
    grad_down = jnp.einsum("tf,td->fd", hidden, cot_all, preferred_element_type=jnp.float32)
    d_upper = (d_hidden * gate * sigma).astype(jnp.bfloat16)
    d_gate = (d_hidden * upper * sigma * (1.0 + gate * (1.0 - sigma))).astype(jnp.bfloat16)
    grad_gate_up = jnp.stack(
        [
            jnp.einsum("td,tf->df", normed_two_all, d_gate, preferred_element_type=jnp.float32),
            jnp.einsum("td,tf->df", normed_two_all, d_upper, preferred_element_type=jnp.float32),
        ]
    )
    d_normed_two = lax.psum_scatter(
        (
            jnp.einsum("tf,df->td", d_gate, w_gate_up[0], preferred_element_type=jnp.float32)
            + jnp.einsum("tf,df->td", d_upper, w_gate_up[1], preferred_element_type=jnp.float32)
        ).astype(jnp.bfloat16),
        "tensor",
        scatter_dimension=0,
        tiled=True,
    ).astype(jnp.float32)
    scaled_two = gain_two * d_normed_two
    d_middle = (
        cotangent.astype(jnp.float32)
        + inv_two * scaled_two
        - middle * inv_two**3 * jnp.mean(scaled_two * middle, axis=-1, keepdims=True)
    )
    grad_gain_two = jnp.sum(d_normed_two * middle * inv_two, axis=0)
    d_middle_all = lax.all_gather(d_middle.astype(jnp.bfloat16), "tensor", axis=0, tiled=True)
    d_mixed = jnp.einsum(
        "td,ed->te", d_middle_all, w_out, preferred_element_type=jnp.float32
    ).astype(jnp.bfloat16)
    grad_out = jnp.einsum("te,td->ed", mixed, d_middle_all, preferred_element_type=jnp.float32)
    d_queries, d_keys, d_values = attend_back(
        queries, keys_rot, values, d_mixed.reshape(shape3), log_sums, segment_ids, valid_mask
    )
    d_project = jnp.stack(
        [
            rotate(d_queries, cosine, -sine).reshape(length, -1),
            rotate(d_keys, cosine, -sine).reshape(length, -1),
            d_values.reshape(length, -1),
        ]
    ).astype(jnp.bfloat16)
    grad_qkv = jnp.einsum("td,cte->cde", normed_all, d_project, preferred_element_type=jnp.float32)
    d_normed = lax.psum_scatter(
        jnp.einsum("cte,cde->td", d_project, w_qkv, preferred_element_type=jnp.float32).astype(
            jnp.bfloat16
        ),
        "tensor",
        scatter_dimension=0,
        tiled=True,
    ).astype(jnp.float32)
    scaled_one = gain_one * d_normed
    d_inputs = (
        d_middle
        + inv_one * scaled_one
        - incoming * inv_one**3 * jnp.mean(scaled_one * incoming, axis=-1, keepdims=True)
    )
    grad_gain_one = jnp.sum(d_normed * incoming * inv_one, axis=0)
    grad_gain_one, grad_gain_two = lax.psum((grad_gain_one, grad_gain_two), ("dp", "tensor"))
    grad_qkv, grad_out, grad_gate_up, grad_down = (
        lax.psum_scatter(
            grad_qkv.astype(jnp.bfloat16), "dp", scatter_dimension=1, tiled=True
        ).astype(jnp.float32),
        lax.psum_scatter(
            grad_out.astype(jnp.bfloat16), "dp", scatter_dimension=1, tiled=True
        ).astype(jnp.float32),
        lax.psum_scatter(
            grad_gate_up.astype(jnp.bfloat16), "dp", scatter_dimension=1, tiled=True
        ).astype(jnp.float32),
        lax.psum_scatter(
            grad_down.astype(jnp.bfloat16), "dp", scatter_dimension=1, tiled=True
        ).astype(jnp.float32),
    )
    return (
        output,
        d_inputs,
        grad_gain_one,
        grad_gain_two,
        grad_qkv,
        grad_out,
        grad_gate_up,
        grad_down,
    )


NT = (((1,), (1,)), ((), ()))
TN = (((0,), (0,)), ((), ()))
MEGA = 1024 * 1024


def chunks(total, step):
    return [(at, min(step, total - at)) for at in range(0, total, step)]


def dot(left, right, dims=None):
    if dims is None:
        return jnp.dot(left, right, preferred_element_type=jnp.float32)
    return lax.dot_general(left, right, dims, preferred_element_type=jnp.float32)


def in_vmem(count):
    return [pl.BlockSpec(memory_space=pltpu.VMEM)] * count


def in_smem():
    return [pl.BlockSpec(memory_space=pltpu.SMEM)]


def like(shape, kind=jnp.bfloat16):
    return jax.ShapeDtypeStruct(shape, kind)


def limit(megabytes):
    return pltpu.CompilerParams(vmem_limit_bytes=megabytes * MEGA)


def starts_of(blocks):
    at, starts = 0, []
    for block in blocks:
        starts.append((at, block.shape[0]))
        at += block.shape[0]
    return starts


def send_shapes(rows, width):
    half = rows // 2
    return [
        like((rows, width), jnp.float32),
        like((rows, width)),
        like((rows, width)),
        like((half, width)),
        like((half, width)),
    ]


def store_parts(part, targets, cols):
    for (start, rows), target in zip(starts_of(targets), targets):
        target[:, cols] = part[start : start + rows].astype(target.dtype)


def norm_kernel(tokens, gain, normed):
    wide = tokens[...].astype(jnp.float32)
    inverse = lax.rsqrt(jnp.mean(wide * wide, axis=-1, keepdims=True) + EPS)
    normed[...] = (wide * inverse * gain[...].astype(jnp.float32)).astype(jnp.bfloat16)


def norm(tokens, gain):
    return pl.pallas_call(
        norm_kernel,
        name="norm",
        out_shape=like(tokens.shape),
        in_specs=in_vmem(2),
        out_specs=in_vmem(1)[0],
        compiler_params=limit(4),
    )(tokens, gain)


def relay_kernel(to_x, to_y, via_x, via_y, next_x, next_y):
    half = via_x.shape[0]
    next_x[:half] = to_x[:half]
    next_x[half:] = (
        to_x[half:].astype(jnp.float32) + via_y[...].astype(jnp.float32)
    ).astype(jnp.bfloat16)
    next_y[:half] = (
        to_y[:half].astype(jnp.float32) + via_x[...].astype(jnp.float32)
    ).astype(jnp.bfloat16)
    next_y[half:] = to_y[half:]


def relay(to_x, to_y, via_x, via_y):
    return pl.pallas_call(
        relay_kernel,
        name="relay",
        out_shape=[like(to_x.shape), like(to_y.shape)],
        in_specs=in_vmem(4),
        out_specs=in_vmem(2),
        compiler_params=limit(4),
    )(to_x, to_y, via_x, via_y)


def middle_kernel(tokens, keep, got_x, got_y, gain, middle, normed):
    total = (
        tokens[...].astype(jnp.float32)
        + keep[...]
        + got_x[...].astype(jnp.float32)
        + got_y[...].astype(jnp.float32)
    )
    middle[...] = total
    inverse = lax.rsqrt(jnp.mean(total * total, axis=-1, keepdims=True) + EPS)
    normed[...] = (total * inverse * gain[...].astype(jnp.float32)).astype(jnp.bfloat16)


def make_middle(tokens, keep, got_x, got_y, gain):
    return pl.pallas_call(
        middle_kernel,
        name="make_middle",
        out_shape=[like(keep.shape, jnp.float32), like(keep.shape)],
        in_specs=in_vmem(5),
        out_specs=in_vmem(2),
        compiler_params=limit(6),
    )(tokens, keep, got_x, got_y, gain)


def norm_back_kernel(base, keep, got_x, got_y, source, gain, *outs):
    d_normed = keep[...] + got_x[...].astype(jnp.float32) + got_y[...].astype(jnp.float32)
    wide = source[...].astype(jnp.float32)
    inverse = lax.rsqrt(jnp.mean(wide * wide, axis=-1, keepdims=True) + EPS)
    scaled = gain[...].astype(jnp.float32) * d_normed
    slope = jnp.mean(scaled * wide, axis=-1, keepdims=True) * inverse * inverse * inverse
    total = base[...].astype(jnp.float32) + inverse * scaled - wide * slope
    outs[0][...] = total
    outs[1][...] = jnp.sum(d_normed * wide * inverse, axis=0, keepdims=True)
    if len(outs) == 3:
        outs[2][...] = total.astype(jnp.bfloat16)


def norm_back(base, keep, got_x, got_y, source, gain, low):
    return pl.pallas_call(
        norm_back_kernel,
        name="norm_back",
        out_shape=[like(keep.shape, jnp.float32), like((1, keep.shape[1]), jnp.float32)]
        + [like(keep.shape)] * low,
        in_specs=in_vmem(6),
        out_specs=in_vmem(2 + low),
        compiler_params=limit(8),
    )(base, keep, got_x, got_y, source, gain)


def prepare_kernel(segments, valid, cosine, sine, seg_col, valid_col):
    length = cosine.shape[0]
    half = HD // 2
    place = lax.broadcasted_iota(jnp.int32, (length, HD), 0).astype(jnp.float32)
    lane = lax.broadcasted_iota(jnp.int32, (length, HD), 1)
    step = jnp.where(lane < half, lane, lane - half).astype(jnp.float32)
    angle = place * jnp.exp(step * (-2.0 / HD * math.log(THETA)))
    cosine[...] = jnp.cos(angle)
    turn = jnp.sin(angle)
    sine[...] = jnp.where(lane < half, -turn, turn)
    seg_col[...] = jnp.broadcast_to(segments[...], (HD, length)).T
    valid_col[...] = jnp.broadcast_to(valid[...], (HD, length)).T


def prepare(segments, valid):
    length = segments.shape[1]
    return pl.pallas_call(
        prepare_kernel,
        name="prepare",
        out_shape=[like((length, HD), jnp.float32)] * 4,
        in_specs=in_vmem(2),
        out_specs=in_vmem(4),
        compiler_params=limit(6),
    )(segments, valid)


def project_kernel(
    rows_at, own, from_x, from_y, low, high, w_qkv, cosine, sine, normed, queries, keys, values
):
    for i, block in enumerate((own, from_x, from_y, low, high)):
        place = pl.multiple_of(rows_at[i], 64)
        normed[pl.ds(place, block.shape[0]), :] = block[...]
    for c, target in enumerate((queries, keys, values)):
        for at, size in chunks(target.shape[1], 2 * HD):
            part = dot(normed[...], w_qkv[c, :, at : at + size])
            for head in range(0, size, HD):
                piece = part[:, head : head + HD]
                if c < 2:
                    piece = piece * cosine[...] + pltpu.roll(piece, HD // 2, 1) * sine[...]
                target[:, at + head : at + head + HD] = piece.astype(jnp.bfloat16)


def project(rows_at, blocks, w_qkv, cosine, sine):
    rows, width = blocks[0].shape
    length = 4 * rows
    wide = w_qkv.shape[2]
    return pl.pallas_call(
        project_kernel,
        name="project",
        out_shape=[like((length, width))] + [like((length, wide))] * 3,
        in_specs=in_smem() + in_vmem(8),
        out_specs=in_vmem(4),
        compiler_params=limit(8),
    )(rows_at, *blocks, w_qkv, cosine, sine)


def attend_kernel(
    rows_at, queries, keys, values, w_out, seg_row, seg_col, valid_col,
    keep, to_x, to_y, far_low, far_high, probs, mixed, bias, joined,
):
    length, wide = queries.shape
    key_at = lax.broadcasted_iota(jnp.int32, (length, length), 0)
    query_at = lax.broadcasted_iota(jnp.int32, (length, length), 1)
    allowed = (
        (key_at <= query_at)
        & (seg_col[:, 0:1] == seg_row[...])
        & ((valid_col[:, 0:1] == 1.0) | (key_at == query_at))
    )
    bias[...] = jnp.where(allowed, 0.0, -1e30)
    for at in range(0, wide, HD):
        head = at // HD
        cols = slice(at, at + HD)
        for q_at, q_size in chunks(length, 256):
            seen = q_at + q_size
            scores = dot(keys[0:seen, cols], queries[q_at:seen, cols], NT)
            scores = scores * HD ** (-0.5) + bias[0:seen, q_at:seen]
            top = jnp.max(scores, axis=0, keepdims=True)
            expo = jnp.exp(scores - top)
            total = jnp.sum(expo, axis=0, keepdims=True)
            chance = (expo * (1.0 / total)).astype(jnp.bfloat16)
            probs[head, 0:seen, q_at:seen] = chance
            result = dot(values[0:seen, cols], chance, TN)
            joined[q_at:seen, cols] = result.T.astype(jnp.bfloat16)
    targets = [keep, to_x, to_y, far_low, far_high]
    for i, (start, size) in enumerate(starts_of(targets)):
        place = pl.multiple_of(rows_at[i], 64)
        mixed[start : start + size, :] = joined[pl.ds(place, size), :]
    for at, size in chunks(w_out.shape[1], 512):
        store_parts(dot(mixed[...], w_out[:, at : at + size]), targets, slice(at, at + size))


def attend_square(rows_at, queries, keys, values, w_out, seg_row, seg_col, valid_col):
    length, wide = queries.shape
    width = w_out.shape[1]
    heads = wide // HD
    return pl.pallas_call(
        attend_kernel,
        name="attend",
        out_shape=send_shapes(length // 4, width)
        + [like((heads, length, length)), like((length, wide))],
        in_specs=in_smem() + in_vmem(7),
        out_specs=in_vmem(7),
        scratch_shapes=[
            pltpu.VMEM((length, length), jnp.float32),
            pltpu.VMEM((length, wide), jnp.bfloat16),
        ],
        compiler_params=limit(8),
    )(rows_at, queries, keys, values, w_out, seg_row, seg_col, valid_col)


def d_hidden_kernel(own, from_x, from_y, low, high, w_down, d_hidden, cot_all):
    blocks = [own, from_x, from_y, low, high]
    for (start, size), block in zip(starts_of(blocks), blocks):
        cot_all[start : start + size, :] = block[...]
    for at, size in chunks(w_down.shape[0], 256):
        d_hidden[:, at : at + size] = dot(cot_all[...], w_down[at : at + size, :], NT)


def back_through_down(blocks, w_down):
    rows, width = blocks[0].shape
    length = 4 * rows
    units = w_down.shape[0]
    return pl.pallas_call(
        d_hidden_kernel,
        name="back_through_down",
        out_shape=[like((length, units), jnp.float32), like((length, width))],
        in_specs=in_vmem(6),
        out_specs=in_vmem(2),
        compiler_params=limit(6),
    )(*blocks, w_down)


def mlp_kernel(
    own, from_x, from_y, low, high, d_hidden, w_gate_up, normed, hidden, d_gate_up
):
    units = w_gate_up.shape[2]
    blocks = [own, from_x, from_y, low, high]
    for (start, size), block in zip(starts_of(blocks), blocks):
        normed[start : start + size, :] = block[...]
    for at, size in chunks(units, 256):
        here = slice(at, at + size)
        gate = dot(normed[...], w_gate_up[0, :, here])
        upper = dot(normed[...], w_gate_up[1, :, here])
        incoming = d_hidden[:, here]
        sigma = 1.0 / (1.0 + jnp.exp(-gate))
        silu = gate * sigma
        hidden[:, here] = (silu * upper).astype(jnp.bfloat16)
        d_gate_up[:, here] = (incoming * upper * sigma * (1.0 + gate * (1.0 - sigma))).astype(
            jnp.bfloat16
        )
        d_gate_up[:, units + at : units + at + size] = (incoming * silu).astype(jnp.bfloat16)


def mlp(blocks, d_hidden, w_gate_up):
    rows, width = blocks[0].shape
    length = 4 * rows
    units = w_gate_up.shape[2]
    return pl.pallas_call(
        mlp_kernel,
        name="mlp",
        out_shape=[like((length, width)), like((length, units)), like((length, 2 * units))],
        in_specs=in_vmem(7),
        out_specs=in_vmem(3),
        compiler_params=limit(8),
    )(*blocks, d_hidden, w_gate_up)


def mlp_back_kernel(d_gate_up, w_gate_up, *targets):
    units = w_gate_up.shape[2]
    for at, size in chunks(w_gate_up.shape[1], 256):
        part = dot(d_gate_up[:, 0:units], w_gate_up[0, at : at + size, :], NT) + dot(
            d_gate_up[:, units : 2 * units], w_gate_up[1, at : at + size, :], NT
        )
        store_parts(part, targets, slice(at, at + size))


def mlp_back(d_gate_up, w_gate_up):
    return pl.pallas_call(
        mlp_back_kernel,
        name="mlp_back",
        out_shape=send_shapes(d_gate_up.shape[0] // 4, w_gate_up.shape[1]),
        in_specs=in_vmem(2),
        out_specs=in_vmem(5),
        compiler_params=limit(6),
    )(d_gate_up, w_gate_up)


def down_kernel(hidden, w_down, *targets):
    for at, size in chunks(w_down.shape[1], 256):
        store_parts(dot(hidden[...], w_down[:, at : at + size]), targets, slice(at, at + size))


def through_down(hidden, w_down):
    return pl.pallas_call(
        down_kernel,
        name="through_down",
        out_shape=send_shapes(hidden.shape[0] // 4, w_down.shape[1]),
        in_specs=in_vmem(2),
        out_specs=in_vmem(5),
        compiler_params=limit(6),
    )(hidden, w_down)


def attend_back_kernel(
    rows_at, own, from_x, from_y, low, high, w_out, probs, queries, keys, values, cosine, sine,
    d_middle, d_project, d_mixed,
):
    length, wide = queries.shape
    blocks = [own, from_x, from_y, low, high]
    starts = starts_of(blocks)
    for (start, size), block in zip(starts, blocks):
        d_middle[start : start + size, :] = block[...]
    for at, size in chunks(wide, 256):
        part = dot(d_middle[...], w_out[at : at + size, :], NT).astype(jnp.bfloat16)
        for i, (start, rows) in enumerate(starts):
            place = pl.multiple_of(rows_at[i], 64)
            d_mixed[pl.ds(place, rows), at : at + size] = part[start : start + rows]
    scale = HD ** (-0.5)

    def back(turned, rows):
        return turned * cosine[rows, :] - pltpu.roll(turned, HD // 2, 1) * sine[rows, :]

    for at in range(0, wide, HD):
        head = at // HD
        cols = slice(at, at + HD)
        d_keys = d_values = None
        for q_at, q_size in reversed(chunks(length, 256)):
            seen = q_at + q_size
            rows = slice(q_at, seen)
            chance = probs[head, 0:seen, rows]
            d_out = d_mixed[rows, cols]
            d_chance = dot(values[0:seen, cols], d_out, NT)
            exact = chance.astype(jnp.float32)
            delta = jnp.sum(d_chance * exact, axis=0, keepdims=True)
            d_scores = (exact * (d_chance - delta)).astype(jnp.bfloat16)
            more_values = dot(chance, d_out)
            more_keys = dot(d_scores, queries[rows, cols])
            d_queries = dot(keys[0:seen, cols], d_scores, TN).T
            d_project[rows, cols] = back(d_queries * scale, rows).astype(jnp.bfloat16)
            if d_keys is None:
                d_keys, d_values = more_keys, more_values
            else:
                d_keys = jnp.concatenate([d_keys[:seen] + more_keys, d_keys[seen:]], axis=0)
                d_values = jnp.concatenate([d_values[:seen] + more_values, d_values[seen:]], axis=0)
        d_project[:, wide + at : wide + at + HD] = back(d_keys * scale, slice(0, length)).astype(
            jnp.bfloat16
        )
        d_project[:, 2 * wide + at : 2 * wide + at + HD] = d_values.astype(jnp.bfloat16)


def attend_back_square(rows_at, blocks, w_out, probs, queries, keys, values, cosine, sine):
    length, wide = queries.shape
    return pl.pallas_call(
        attend_back_kernel,
        name="attend_back",
        out_shape=[like((length, w_out.shape[1])), like((length, 3 * wide))],
        in_specs=in_smem() + in_vmem(12),
        out_specs=in_vmem(2),
        scratch_shapes=[pltpu.VMEM((length, wide), jnp.bfloat16)],
        compiler_params=limit(8),
    )(rows_at, *blocks, w_out, probs, queries, keys, values, cosine, sine)


def project_back_kernel(rows_at, d_project, w_qkv, *refs):
    targets, turned = refs[:5], refs[5]
    wide = w_qkv.shape[2]
    for i, (start, size) in enumerate(starts_of(targets)):
        place = pl.multiple_of(rows_at[i], 64)
        turned[start : start + size, :] = d_project[pl.ds(place, size), :]
    for at, size in chunks(w_qkv.shape[1], 256):
        part = sum(
            dot(turned[:, c * wide : (c + 1) * wide], w_qkv[c, at : at + size, :], NT)
            for c in range(3)
        )
        store_parts(part, targets, slice(at, at + size))


def project_back(rows_at, d_project, w_qkv):
    return pl.pallas_call(
        project_back_kernel,
        name="project_back",
        out_shape=send_shapes(d_project.shape[0] // 4, w_qkv.shape[1]),
        in_specs=in_smem() + in_vmem(2),
        out_specs=in_vmem(5),
        scratch_shapes=[pltpu.VMEM(d_project.shape, jnp.bfloat16)],
        compiler_params=limit(8),
    )(rows_at, d_project, w_qkv)


def weight_kernel(layout, base, spot, which, *refs):
    turned, out = refs[-1], refs[-2]
    more = refs[-3] if spot is not None else None
    count, piece, _ = out.shape
    for i in range(count):
        place = pl.multiple_of(which[base + i] * piece, piece)
        at_ref = column = 0
        for pairs in layout:
            splits = refs[at_ref : at_ref + pairs]
            others = refs[at_ref + pairs : at_ref + 2 * pairs]
            at_ref += 2 * pairs
            length, across = others[0].shape
            for j, split in enumerate(splits):
                turned[:, j * length : (j + 1) * length] = split[:, pl.ds(place, piece)].T
            for at, size in chunks(across, 256):
                part = None
                for j, other in enumerate(others):
                    term = dot(turned[:, j * length : (j + 1) * length], other[:, at : at + size])
                    part = term if part is None else part + term
                cols = slice(column + at, column + at + size)
                if more is not None:
                    part = part + more[spot + i, :, cols].astype(jnp.float32)
                out[i, :, cols] = part.astype(out.dtype)
            column += across


def weight_pieces(which, base, count, groups, more=None, spot=None):
    layout = [len(splits) for splits, _ in groups]
    refs = [ref for splits, others in groups for ref in (*splits, *others)]
    extra = [] if more is None else [more]
    length = groups[0][1][0].shape[0]
    across = sum(others[0].shape[1] for _, others in groups)
    piece = groups[0][0][0].shape[1] // 8
    return pl.pallas_call(
        functools.partial(weight_kernel, layout, base, spot),
        name="weight_pieces",
        out_shape=like((count, piece, across)),
        in_specs=in_smem() + in_vmem(len(refs) + len(extra)),
        out_specs=in_vmem(1)[0],
        scratch_shapes=[pltpu.VMEM((piece, max(layout) * length), jnp.bfloat16)],
        compiler_params=limit(16),
    )(which, *refs, *extra)


def join_kernel(here_outer, here_own, there_outer, there_own, outer, own):
    for here, there, out in ((here_outer, there_outer, outer), (here_own, there_own, own)):
        for at, size in chunks(out.shape[2], 256):
            cols = slice(at, at + size)
            out[0, :, cols] = (
                here[0, :, cols].astype(jnp.float32) + there[0, :, cols].astype(jnp.float32)
            ).astype(jnp.bfloat16)


def join(here, there):
    shape = here[0].shape
    return pl.pallas_call(
        join_kernel,
        name="join",
        out_shape=[like(shape), like(shape)],
        in_specs=in_vmem(4),
        out_specs=in_vmem(2),
        compiler_params=limit(6),
    )(*here, *there)


def hand_kernel(near, far, out):
    for at, size in chunks(out.shape[1], 256):
        cols = slice(at, at + size)
        out[:, cols] = (
            near[0, :, cols].astype(jnp.float32) + far[0, :, cols].astype(jnp.float32)
        ).astype(jnp.bfloat16)


def hand(near, far):
    return pl.pallas_call(
        hand_kernel,
        name="hand",
        out_shape=like(near.shape[1:]),
        in_specs=in_vmem(2),
        out_specs=in_vmem(1)[0],
        compiler_params=limit(6),
    )(near, far)


def finish_kernel(parts, count_inner, inner, *refs):
    count = len(refs) - len(parts)
    here = [ref for ref in refs[:count_inner]]
    outer = [ref for ref in refs[count_inner:count]]

    def total(sources, cols):
        found = None
        for source in sources:
            term = source[0, :, cols] if len(source.shape) == 3 else source[:, cols]
            term = term.astype(jnp.float32)
            found = term if found is None else found + term
        return found

    column = 0
    for (planes, across, turn), out in zip(parts, refs[count:]):
        for c in range(planes):
            for at, size in chunks(across, 256):
                cols = slice(column + at, column + at + size)
                value = jnp.where(inner[0] == 1, total(here, cols), total(outer, cols))
                if turn:
                    out[at : at + size, :] = value.T
                else:
                    out[c, :, at : at + size] = value
            column += across


def finish(inner, here, outer, parts):
    piece = here[0].shape[-2]
    return pl.pallas_call(
        functools.partial(finish_kernel, parts, len(here)),
        name="finish",
        out_shape=[
            like((across, piece) if turn else (planes, piece, across), jnp.float32)
            for planes, across, turn in parts
        ],
        in_specs=in_smem() + in_vmem(len(here) + len(outer)),
        out_specs=in_vmem(len(parts)),
        compiler_params=limit(8),
    )(inner, *here, *outer)


def gains_kernel(chip, *refs):
    sources, out, kept = refs[:4], refs[4], refs[5]
    for back, source in enumerate(sources):
        kept[lax.rem(chip[0] + 4 - back, 4)] = source[...]
    out[...] = (kept[0] + kept[1]) + (kept[2] + kept[3])


def sum_gains(chip, sources):
    return pl.pallas_call(
        gains_kernel,
        name="sum_gains",
        out_shape=like(sources[0].shape, jnp.float32),
        in_specs=in_smem() + in_vmem(4),
        out_specs=in_vmem(1)[0],
        scratch_shapes=[pltpu.VMEM((4, *sources[0].shape), jnp.float32)],
        compiler_params=limit(4),
    )(chip, *sources)


def flips(size, bit):
    return [(i, i ^ bit) for i in range(size)]


def after(value, *earlier):
    return lax.optimization_barrier((value, *earlier))[0]


def over_tensor(values, bit):
    return lax.ppermute(values, "tensor", flips(4, bit))


def gather_near(own):
    return own, over_tensor(own, 1), over_tensor(own, 2)


def gather_far(own, from_x, from_y):
    half = own.shape[0] // 2
    low = over_tensor(from_y[:half], 1)
    high = over_tensor(from_x[half:], 2)
    return [own, from_x, from_y, low, high]


def scatter_far(keep, to_x, to_y, far_low, far_high):
    return keep, *relay(to_x, to_y, over_tensor(far_low, 1), over_tensor(far_high, 2))


def scatter_near(keep, to_x, to_y):
    return keep, over_tensor(to_x, 1), over_tensor(to_y, 2)


def over_cores(values):
    return lax.ppermute(values, "dp", flips(8, 1))


def up_the_line(values, chips):
    return lax.ppermute(values, "dp", [(i, (i + 2 * chips) % 8) for i in range(8)])


def to_inner(values):
    return lax.ppermute(values, "dp", [(0, 2), (1, 3), (6, 4), (7, 5)])


def to_outer(values):
    return lax.ppermute(values, "dp", [(2, 0), (3, 1), (4, 6), (5, 7)])


def over_middle(values):
    return lax.ppermute(values, "dp", [(2, 4), (3, 5), (4, 2), (5, 3)])


class Weight:
    def __init__(self, places, groups):
        self.which_theirs, self.which_mine, self.inner = places
        self.groups = groups
        self.theirs = None
        self.halves = {}

    def sibling_part(self):
        self.sibling_sum = weight_pieces(self.which_theirs, 0, 4, self.groups)
        self.theirs = over_cores(self.sibling_sum)

    def sibling_half(self, base, groups):
        found = weight_pieces(self.which_theirs, base, 2, groups)
        self.halves[base] = over_cores(found)
        return found

    def own_part(self, base, count, *earlier):
        spot = base
        more = self.theirs
        if self.halves:
            more, spot = self.halves[base // 2 * 2], base % 2
        if earlier:
            more = after(more, *earlier)
        return weight_pieces(self.which_mine, base, count, self.groups, more, spot)


def sum_flips(values, *steps):
    for axis, size, bit in steps:
        values = values + lax.ppermute(values, axis, flips(size, bit))
    return values


def per_device_square(
    tokens, gain_attn, gain_mlp, w_qkv, w_out, w_gate_up, w_down, cotangent, segment_ids, valid_mask
):
    rows = tokens.shape[0]
    length = segment_ids.shape[0]
    low = jnp.bfloat16
    me = lax.axis_index("tensor")
    order = [me, me ^ 1, me ^ 2, me ^ 3]
    rows_at = jnp.stack([at * rows for at in order] + [order[3] * rows + rows // 2]).astype(jnp.int32)
    index = lax.axis_index("dp")
    place, core = index // 2, index % 2
    line_order = jnp.where(place < 2, jnp.array([3, 2, 0, 1]), jnp.array([0, 1, 3, 2]))
    places = (
        (2 * line_order + 1 - core).astype(jnp.int32),
        (2 * line_order + core).astype(jnp.int32),
        ((place == 1) | (place == 2)).astype(jnp.int32).reshape(1),
    )
    chip = place.astype(jnp.int32).reshape(1)
    gain_one = gain_attn[None, :]
    gain_two = gain_mlp[None, :]

    tokens = after(tokens, rows_at, chip, *places)
    normed = norm(tokens, gain_one)
    near = gather_near(normed)
    cosine, sine, seg_col, valid_col = prepare(
        segment_ids.astype(jnp.float32)[None, :],
        valid_mask.astype(jnp.float32)[None, :],
    )
    near = (near[0], near[1], after(near[2], cosine))
    guest_cot_own = to_inner(cotangent)
    blocks = gather_far(*near)
    cot_near = gather_near(after(cotangent, *blocks))
    normed_all, queries, keys, values = project(
        rows_at, blocks, w_qkv, cosine, sine
    )
    *sent, probs, mixed = attend_square(
        rows_at,
        after(queries, *cot_near, guest_cot_own),
        keys,
        values,
        w_out,
        segment_ids.astype(jnp.float32)[None, :],
        seg_col,
        valid_col,
    )
    guest_cot_near = [to_inner(part) for part in cot_near[1:]]
    keep, to_x, to_y = scatter_far(*sent)
    cot_blocks = gather_far(*(after(part, to_x) for part in cot_near))
    got = scatter_near(keep, to_x, to_y)
    d_hidden, cot_all = back_through_down(
        [after(cot_blocks[0], *guest_cot_near)] + cot_blocks[1:], w_down
    )
    middle, normed_two = make_middle(tokens, after(got[0], cot_all), *got[1:], gain_two)

    near = gather_near(normed_two)
    guest_cot_far = [to_inner(part) for part in cot_blocks[3:]]
    guest_own = to_inner(after(normed_two, *guest_cot_far))
    blocks = gather_far(*near)
    normed_two_all, hidden, d_gate_up = mlp(
        [after(blocks[0], *guest_cot_far)] + blocks[1:], d_hidden, w_gate_up
    )
    guest_near = [to_inner(part) for part in near[1:]]
    guest_far = [to_inner(part) for part in blocks[3:]]
    sent = mlp_back(d_gate_up, w_gate_up)
    keep, to_x, to_y = scatter_far(*sent)
    to_x = after(to_x, guest_own, *guest_near)
    guest_d_hidden, guest_cot_all = back_through_down(
        [after(guest_cot_own, to_x), *guest_cot_near, *guest_cot_far], w_down
    )
    got = scatter_near(keep, to_x, to_y)
    d_middle, gain_two_part, d_middle_low = norm_back(
        cotangent, after(got[0], guest_d_hidden), *got[1:], middle, gain_two, True
    )
    near = gather_near(d_middle_low)
    guest_normed_two, guest_hidden, guest_d_gate_up = mlp(
        [after(guest_own, d_middle_low), *guest_near, *guest_far], guest_d_hidden, w_gate_up
    )
    down = Weight(places, [([cot_all, guest_cot_all], [hidden, guest_hidden])])
    down.sibling_part()
    splits, others = [normed_two_all, guest_normed_two], [d_gate_up, guest_d_gate_up]
    gate = Weight(places, [(splits, others)])
    first = gate.sibling_half(0, [([splits[0], after(splits[1], down.theirs)], others)])
    down_outer = down.own_part(0, 1, first)
    second = gate.sibling_half(2, [([splits[0], after(splits[1], down_outer, *near)], others)])
    blocks = gather_far(*near)
    down_own = down.own_part(1, 1, second)
    down_outer = over_middle(down_outer)
    gate_outer = gate.own_part(0, 1, down_own, *blocks[3:])
    gate_own = gate.own_part(1, 1, gate_outer)

    d_middle_all, d_project = attend_back_square(
        rows_at,
        blocks,
        w_out,
        after(probs, gate_own),
        queries,
        keys,
        values,
        cosine,
        sine,
    )
    gate_outer = over_middle(gate_outer)
    late = Weight(places, [([normed_all], [d_project]), ([d_middle_all], [mixed])])
    late.groups[0] = ([after(normed_all, down_outer)], [d_project])
    late.sibling_part()
    down_near = [down.own_part(2, 1, late.sibling_sum)]
    down_handed = hand(down_near[0], down_outer)
    down_given = to_outer(down_handed)
    late_far = [late.own_part(0, 1, down_handed)]
    late_far += [late.own_part(1, 1, late_far[0])]
    late_arrived = [to_inner(part) for part in late_far]
    sent = project_back(rows_at, after(d_project, late_far[1]), w_qkv)
    keep, to_x, to_y = scatter_far(*sent)
    gate_own = over_middle(after(gate_own, to_x, to_y))
    down_own = over_middle(after(down_own, to_x, to_y))
    late_near = [late.own_part(2, 1, to_x, to_y)]
    late_near += [late.own_part(3, 1, late_near[0])]
    late_near_arrived = to_inner(late_near[1])
    got = scatter_near(keep, to_x, to_y)
    gate_near = [gate.own_part(2, 1, late_near[1])]
    gate_handed = hand(gate_near[0], gate_outer)
    gate_given = to_outer(gate_handed)
    gate_near += [gate.own_part(3, 1, gate_handed)]
    down_near += [down.own_part(3, 1, gate_near[1])]
    d_inputs, gain_one_part = norm_back(
        d_middle,
        after(got[0], down_near[1], down_given, late_arrived[0]),
        *got[1:],
        tokens,
        gain_one,
        False,
    )
    late_far[0] = after(late_far[0], d_inputs, gate_own, down_own)
    late_outer, late_own = join(late_far, late_arrived)
    gains = sum_flips(
        after(jnp.concatenate([gain_one_part, gain_two_part], axis=0), late_own),
        ("dp", 8, 1),
        ("tensor", 4, 1),
        ("tensor", 4, 2),
    )
    sent = through_down(after(hidden, gains, gate_given), w_down)
    late_outer = over_middle(late_outer)
    keep, to_x, to_y, *sent = sent
    via_x, via_y = over_tensor(sent[0], 1), over_tensor(sent[1], 2)
    late_own = over_middle(after(late_own, via_x, via_y))
    late_handed = hand(after(late_near[0], via_x, via_y), late_outer)
    late_given = to_outer(late_handed)
    to_x, to_y = relay(after(to_x, late_handed, late_near_arrived), to_y, via_x, via_y)
    gains = [after(gains, late_handed)]
    gains += [up_the_line(gains[0], chips) for chips in (1, 2, 3)]
    keep, got_x, got_y = scatter_near(keep, to_x, to_y)
    output = (middle + keep + got_x.astype(jnp.float32) + got_y.astype(jnp.float32)).astype(low)
    inner = places[2]
    units, wide = w_down.shape[0], w_qkv.shape[2]
    (grad_down,) = finish(
        inner,
        [after(down_near[1], output, late_near_arrived), down_own],
        [down_given],
        [(1, units, True)],
    )
    (grad_gate_up,) = finish(
        inner, [after(gate_near[1], grad_down), gate_own], [gate_given], [(2, units, False)]
    )
    grad_gains = sum_gains(chip, [after(gains[0], grad_gate_up), *gains[1:]])
    grad_qkv, grad_out = finish(
        inner,
        [late_near[1], late_near_arrived, late_own],
        [late_near[0], late_given],
        [(3, wide, False), (1, wide, True)],
    )
    return (
        output,
        d_inputs,
        grad_gains[0],
        grad_gains[1],
        grad_qkv,
        grad_out,
        grad_gate_up,
        grad_down,
    )


def solution(mesh):
    placed = (
        P(("dp", "tensor"), None),
        P(),
        P(),
        P(None, None, "tensor"),
        P("tensor", None),
        P(None, None, "tensor"),
        P("tensor", None),
        P(("dp", "tensor"), None),
        P("dp"),
        P("dp"),
    )
    square = mesh.shape["tensor"] == 4 and mesh.shape["dp"] == 8
    return jax.shard_map(
        per_device_square if square else per_device,
        mesh=mesh,
        in_specs=placed,
        out_specs=(
            P(("dp", "tensor"), None),
            P(("dp", "tensor"), None),
            P(),
            P(),
            P(None, "dp", "tensor"),
            P("tensor", "dp"),
            P(None, "dp", "tensor"),
            P("tensor", "dp"),
        ),
        check_vma=False,
    )
```

```python
import functools
import math

import jax
import jax.numpy as jnp
from jax import lax
from jax.experimental import pallas as pl
from jax.experimental.pallas import tpu as pltpu
from jax.sharding import PartitionSpec as P

HD = 128


EPS = 1e-06
THETA = 10000.0


def rope_tables(places):
    positions = places.astype(jnp.float32)
    freqs = THETA ** (-(jnp.arange(HD // 2).astype(jnp.float32) * 2.0 / HD))
    angles = positions[:, None] * freqs[None, :]
    return (jnp.cos(angles), jnp.sin(angles))


def rotate(values, cosine, sine):
    half = values.shape[-1] // 2
    first = values[..., :half]
    second = values[..., half:]
    cosine = cosine[:, None, :]
    sine = sine[:, None, :]
    return jnp.concatenate(
        [first * cosine - second * sine, second * cosine + first * sine], axis=-1
    )


def block_scores(q_block, keys_rot, start, segments, valid):
    block_rows = q_block.shape[0]
    length = keys_rot.shape[0]
    key_pos = jnp.arange(length)
    row_pos = start + jnp.arange(block_rows)
    row_seg = lax.dynamic_slice_in_dim(segments, start, block_rows, 0)
    scores = jnp.einsum(
        "qhd,khd->hqk", q_block, keys_rot, preferred_element_type=jnp.float32
    ) * HD ** (-0.5)
    allowed = (
        (key_pos[None, :] <= row_pos[:, None])
        & (row_seg[:, None] == segments[None, :])
        & ((valid[None, :] == 1) | (key_pos[None, :] == row_pos[:, None]))
    )
    return jnp.where(allowed[None], scores, -1e30)


def attend(queries, keys_rot, values, segments, valid):
    length = queries.shape[0]
    block_rows = min(512, length)
    count = length // block_rows

    def one_block(index):
        start = index * block_rows
        q_block = lax.dynamic_slice_in_dim(queries, start, block_rows, 0)
        scores = block_scores(q_block, keys_rot, start, segments, valid)
        top = jnp.max(scores, axis=-1, keepdims=True)
        expo = jnp.exp(scores - top)
        total = jnp.sum(expo, axis=-1, keepdims=True)
        probs = (expo / total).astype(jnp.bfloat16)
        result = jnp.einsum("hqk,khd->qhd", probs, values, preferred_element_type=jnp.float32)
        return (result, top[..., 0] + jnp.log(total[..., 0]))

    blocks, log_sums = lax.map(one_block, jnp.arange(count))
    return (blocks.reshape(length, -1), log_sums)


def attend_back(queries, keys_rot, values, d_mixed, log_sums, segments, valid):
    length = queries.shape[0]
    block_rows = min(512, length)
    count = length // block_rows
    scale = HD ** (-0.5)

    def one_block(carry, index):
        d_keys, d_values = carry
        start = index * block_rows
        q_block = lax.dynamic_slice_in_dim(queries, start, block_rows, 0)
        d_block = lax.dynamic_slice_in_dim(d_mixed, start, block_rows, 0)
        scores = block_scores(q_block, keys_rot, start, segments, valid)
        probs = jnp.exp(scores - log_sums[index][..., None])
        d_values = d_values + jnp.einsum(
            "hqk,qhd->khd", probs.astype(jnp.bfloat16), d_block, preferred_element_type=jnp.float32
        )
        d_probs = jnp.einsum("qhd,khd->hqk", d_block, values, preferred_element_type=jnp.float32)
        delta = jnp.sum(d_probs * probs, axis=-1, keepdims=True)
        d_scores = (probs * (d_probs - delta)).astype(jnp.bfloat16)
        d_query = scale * jnp.einsum(
            "hqk,khd->qhd", d_scores, keys_rot, preferred_element_type=jnp.float32
        )
        d_keys = d_keys + scale * jnp.einsum(
            "hqk,qhd->khd", d_scores, q_block, preferred_element_type=jnp.float32
        )
        return ((d_keys, d_values), d_query)

    empty = jnp.zeros(keys_rot.shape, jnp.float32)
    (d_keys, d_values), d_queries = lax.scan(one_block, (empty, empty), jnp.arange(count))
    return (d_queries.reshape(queries.shape), d_keys, d_values)


def per_device(
    tokens, gain_attn, gain_mlp, w_qkv, w_out, w_gate_up, w_down, cotangent, segment_ids, valid_mask
):
    length = segment_ids.shape[0]
    heads_here = w_qkv.shape[2] // HD
    shape3 = (length, heads_here, HD)
    incoming = tokens.astype(jnp.float32)
    gain_one = gain_attn.astype(jnp.float32)
    gain_two = gain_mlp.astype(jnp.float32)
    cosine, sine = rope_tables(jnp.arange(length))
    inv_one = lax.rsqrt(jnp.mean(incoming * incoming, axis=-1, keepdims=True) + EPS)
    normed = (incoming * inv_one * gain_one).astype(jnp.bfloat16)
    normed_all = lax.all_gather(normed, "tensor", axis=0, tiled=True)
    project = jnp.einsum("td,cde->cte", normed_all, w_qkv, preferred_element_type=jnp.float32)
    queries = rotate(project[0].reshape(shape3), cosine, sine).astype(jnp.bfloat16)
    keys_rot = rotate(project[1].reshape(shape3), cosine, sine).astype(jnp.bfloat16)
    values = project[2].reshape(shape3).astype(jnp.bfloat16)
    mixed, log_sums = attend(queries, keys_rot, values, segment_ids, valid_mask)
    mixed = mixed.astype(jnp.bfloat16)
    middle = incoming + lax.psum_scatter(
        jnp.dot(mixed, w_out, preferred_element_type=jnp.float32).astype(jnp.bfloat16),
        "tensor",
        scatter_dimension=0,
        tiled=True,
    ).astype(jnp.float32)
    inv_two = lax.rsqrt(jnp.mean(middle * middle, axis=-1, keepdims=True) + EPS)
    normed_two = (middle * inv_two * gain_two).astype(jnp.bfloat16)
    normed_two_all = lax.all_gather(normed_two, "tensor", axis=0, tiled=True)
    gate = jnp.dot(normed_two_all, w_gate_up[0], preferred_element_type=jnp.float32)
    upper = jnp.dot(normed_two_all, w_gate_up[1], preferred_element_type=jnp.float32)
    sigma = jax.nn.sigmoid(gate)
    hidden = (gate * sigma * upper).astype(jnp.bfloat16)
    result = middle + lax.psum_scatter(
        jnp.dot(hidden, w_down, preferred_element_type=jnp.float32).astype(jnp.bfloat16),
        "tensor",
        scatter_dimension=0,
        tiled=True,
    ).astype(jnp.float32)
    output = result.astype(jnp.bfloat16)
    cot_all = lax.all_gather(cotangent, "tensor", axis=0, tiled=True)
    d_hidden = jnp.einsum("td,fd->tf", cot_all, w_down, preferred_element_type=jnp.float32)
    grad_down = jnp.einsum("tf,td->fd", hidden, cot_all, preferred_element_type=jnp.float32)
    d_upper = (d_hidden * gate * sigma).astype(jnp.bfloat16)
    d_gate = (d_hidden * upper * sigma * (1.0 + gate * (1.0 - sigma))).astype(jnp.bfloat16)
    grad_gate_up = jnp.stack(
        [
            jnp.einsum("td,tf->df", normed_two_all, d_gate, preferred_element_type=jnp.float32),
            jnp.einsum("td,tf->df", normed_two_all, d_upper, preferred_element_type=jnp.float32),
        ]
    )
    d_normed_two = lax.psum_scatter(
        (
            jnp.einsum("tf,df->td", d_gate, w_gate_up[0], preferred_element_type=jnp.float32)
            + jnp.einsum("tf,df->td", d_upper, w_gate_up[1], preferred_element_type=jnp.float32)
        ).astype(jnp.bfloat16),
        "tensor",
        scatter_dimension=0,
        tiled=True,
    ).astype(jnp.float32)
    scaled_two = gain_two * d_normed_two
    d_middle = (
        cotangent.astype(jnp.float32)
        + inv_two * scaled_two
        - middle * inv_two**3 * jnp.mean(scaled_two * middle, axis=-1, keepdims=True)
    )
    grad_gain_two = jnp.sum(d_normed_two * middle * inv_two, axis=0)
    d_middle_all = lax.all_gather(d_middle.astype(jnp.bfloat16), "tensor", axis=0, tiled=True)
    d_mixed = jnp.einsum(
        "td,ed->te", d_middle_all, w_out, preferred_element_type=jnp.float32
    ).astype(jnp.bfloat16)
    grad_out = jnp.einsum("te,td->ed", mixed, d_middle_all, preferred_element_type=jnp.float32)
    d_queries, d_keys, d_values = attend_back(
        queries, keys_rot, values, d_mixed.reshape(shape3), log_sums, segment_ids, valid_mask
    )
    d_project = jnp.stack(
        [
            rotate(d_queries, cosine, -sine).reshape(length, -1),
            rotate(d_keys, cosine, -sine).reshape(length, -1),
            d_values.reshape(length, -1),
        ]
    ).astype(jnp.bfloat16)
    grad_qkv = jnp.einsum("td,cte->cde", normed_all, d_project, preferred_element_type=jnp.float32)
    d_normed = lax.psum_scatter(
        jnp.einsum("cte,cde->td", d_project, w_qkv, preferred_element_type=jnp.float32).astype(
            jnp.bfloat16
        ),
        "tensor",
        scatter_dimension=0,
        tiled=True,
    ).astype(jnp.float32)
    scaled_one = gain_one * d_normed
    d_inputs = (
        d_middle
        + inv_one * scaled_one
        - incoming * inv_one**3 * jnp.mean(scaled_one * incoming, axis=-1, keepdims=True)
    )
    grad_gain_one = jnp.sum(d_normed * incoming * inv_one, axis=0)
    grad_gain_one, grad_gain_two = lax.psum((grad_gain_one, grad_gain_two), ("dp", "tensor"))
    grad_qkv, grad_out, grad_gate_up, grad_down = (
        lax.psum_scatter(
            grad_qkv.astype(jnp.bfloat16), "dp", scatter_dimension=1, tiled=True
        ).astype(jnp.float32),
        lax.psum_scatter(
            grad_out.astype(jnp.bfloat16), "dp", scatter_dimension=1, tiled=True
        ).astype(jnp.float32),
        lax.psum_scatter(
            grad_gate_up.astype(jnp.bfloat16), "dp", scatter_dimension=1, tiled=True
        ).astype(jnp.float32),
        lax.psum_scatter(
            grad_down.astype(jnp.bfloat16), "dp", scatter_dimension=1, tiled=True
        ).astype(jnp.float32),
    )
    return (
        output,
        d_inputs,
        grad_gain_one,
        grad_gain_two,
        grad_qkv,
        grad_out,
        grad_gate_up,
        grad_down,
    )


NT = (((1,), (1,)), ((), ()))
TN = (((0,), (0,)), ((), ()))
MEGA = 1024 * 1024


def chunks(total, step):
    return [(at, min(step, total - at)) for at in range(0, total, step)]


def dot(left, right, dims=None):
    if dims is None:
        return jnp.dot(left, right, preferred_element_type=jnp.float32)
    return lax.dot_general(left, right, dims, preferred_element_type=jnp.float32)


def in_vmem(count):
    return [pl.BlockSpec(memory_space=pltpu.VMEM)] * count


def in_smem():
    return [pl.BlockSpec(memory_space=pltpu.SMEM)]


def like(shape, kind=jnp.bfloat16):
    return jax.ShapeDtypeStruct(shape, kind)


def limit(megabytes):
    return pltpu.CompilerParams(vmem_limit_bytes=megabytes * MEGA)


def starts_of(blocks):
    at, starts = 0, []
    for block in blocks:
        starts.append((at, block.shape[0]))
        at += block.shape[0]
    return starts


def send_shapes(rows, width):
    half = rows // 2
    return [
        like((rows, width), jnp.float32),
        like((rows, width)),
        like((rows, width)),
        like((half, width)),
        like((half, width)),
    ]


def store_parts(part, targets, cols):
    for (start, rows), target in zip(starts_of(targets), targets):
        target[:, cols] = part[start : start + rows].astype(target.dtype)


def norm_kernel(tokens, gain, normed):
    wide = tokens[...].astype(jnp.float32)
    inverse = lax.rsqrt(jnp.mean(wide * wide, axis=-1, keepdims=True) + EPS)
    normed[...] = (wide * inverse * gain[...].astype(jnp.float32)).astype(jnp.bfloat16)


def norm(tokens, gain):
    return pl.pallas_call(
        norm_kernel,
        name="norm",
        out_shape=like(tokens.shape),
        in_specs=in_vmem(2),
        out_specs=in_vmem(1)[0],
        compiler_params=limit(4),
    )(tokens, gain)


def relay_kernel(to_x, to_y, via_x, via_y, next_x, next_y):
    half = via_x.shape[0]
    next_x[:half] = to_x[:half]
    next_x[half:] = (
        to_x[half:].astype(jnp.float32) + via_y[...].astype(jnp.float32)
    ).astype(jnp.bfloat16)
    next_y[:half] = (
        to_y[:half].astype(jnp.float32) + via_x[...].astype(jnp.float32)
    ).astype(jnp.bfloat16)
    next_y[half:] = to_y[half:]


def relay(to_x, to_y, via_x, via_y):
    return pl.pallas_call(
        relay_kernel,
        name="relay",
        out_shape=[like(to_x.shape), like(to_y.shape)],
        in_specs=in_vmem(4),
        out_specs=in_vmem(2),
        compiler_params=limit(4),
    )(to_x, to_y, via_x, via_y)


def middle_kernel(tokens, keep, got_x, got_y, gain, middle, normed):
    total = (
        tokens[...].astype(jnp.float32)
        + keep[...]
        + got_x[...].astype(jnp.float32)
        + got_y[...].astype(jnp.float32)
    )
    middle[...] = total
    inverse = lax.rsqrt(jnp.mean(total * total, axis=-1, keepdims=True) + EPS)
    normed[...] = (total * inverse * gain[...].astype(jnp.float32)).astype(jnp.bfloat16)


def make_middle(tokens, keep, got_x, got_y, gain):
    return pl.pallas_call(
        middle_kernel,
        name="make_middle",
        out_shape=[like(keep.shape, jnp.float32), like(keep.shape)],
        in_specs=in_vmem(5),
        out_specs=in_vmem(2),
        compiler_params=limit(6),
    )(tokens, keep, got_x, got_y, gain)


def norm_back_kernel(base, keep, got_x, got_y, source, gain, *outs):
    d_normed = keep[...] + got_x[...].astype(jnp.float32) + got_y[...].astype(jnp.float32)
    wide = source[...].astype(jnp.float32)
    inverse = lax.rsqrt(jnp.mean(wide * wide, axis=-1, keepdims=True) + EPS)
    scaled = gain[...].astype(jnp.float32) * d_normed
    slope = jnp.mean(scaled * wide, axis=-1, keepdims=True) * inverse * inverse * inverse
    total = base[...].astype(jnp.float32) + inverse * scaled - wide * slope
    outs[0][...] = total
    outs[1][...] = jnp.sum(d_normed * wide * inverse, axis=0, keepdims=True)
    if len(outs) == 3:
        outs[2][...] = total.astype(jnp.bfloat16)


def norm_back(base, keep, got_x, got_y, source, gain, low):
    return pl.pallas_call(
        norm_back_kernel,
        name="norm_back",
        out_shape=[like(keep.shape, jnp.float32), like((1, keep.shape[1]), jnp.float32)]
        + [like(keep.shape)] * low,
        in_specs=in_vmem(6),
        out_specs=in_vmem(2 + low),
        compiler_params=limit(8),
    )(base, keep, got_x, got_y, source, gain)


def prepare_kernel(segments, valid, cosine, sine, seg_col, valid_col):
    length = cosine.shape[0]
    half = HD // 2
    place = lax.broadcasted_iota(jnp.int32, (length, HD), 0).astype(jnp.float32)
    lane = lax.broadcasted_iota(jnp.int32, (length, HD), 1)
    step = jnp.where(lane < half, lane, lane - half).astype(jnp.float32)
    angle = place * jnp.exp(step * (-2.0 / HD * math.log(THETA)))
    cosine[...] = jnp.cos(angle)
    turn = jnp.sin(angle)
    sine[...] = jnp.where(lane < half, -turn, turn)
    seg_col[...] = jnp.broadcast_to(segments[...], (HD, length)).T
    valid_col[...] = jnp.broadcast_to(valid[...], (HD, length)).T


def prepare(segments, valid):
    length = segments.shape[1]
    return pl.pallas_call(
        prepare_kernel,
        name="prepare",
        out_shape=[like((length, HD), jnp.float32)] * 4,
        in_specs=in_vmem(2),
        out_specs=in_vmem(4),
        compiler_params=limit(6),
    )(segments, valid)


def project_kernel(
    rows_at, own, from_x, from_y, low, high, w_qkv, cosine, sine, normed, queries, keys, values
):
    for i, block in enumerate((own, from_x, from_y, low, high)):
        place = pl.multiple_of(rows_at[i], 64)
        normed[pl.ds(place, block.shape[0]), :] = block[...]
    for c, target in enumerate((queries, keys, values)):
        for at, size in chunks(target.shape[1], 2 * HD):
            part = dot(normed[...], w_qkv[c, :, at : at + size])
            for head in range(0, size, HD):
                piece = part[:, head : head + HD]
                if c < 2:
                    piece = piece * cosine[...] + pltpu.roll(piece, HD // 2, 1) * sine[...]
                target[:, at + head : at + head + HD] = piece.astype(jnp.bfloat16)


def project(rows_at, blocks, w_qkv, cosine, sine):
    rows, width = blocks[0].shape
    length = 4 * rows
    wide = w_qkv.shape[2]
    return pl.pallas_call(
        project_kernel,
        name="project",
        out_shape=[like((length, width))] + [like((length, wide))] * 3,
        in_specs=in_smem() + in_vmem(8),
        out_specs=in_vmem(4),
        compiler_params=limit(8),
    )(rows_at, *blocks, w_qkv, cosine, sine)


def attend_kernel(
    rows_at, queries, keys, values, w_out, seg_row, seg_col, valid_col,
    keep, to_x, to_y, far_low, far_high, probs, mixed, bias, joined,
):
    length, wide = queries.shape
    key_at = lax.broadcasted_iota(jnp.int32, (length, length), 0)
    query_at = lax.broadcasted_iota(jnp.int32, (length, length), 1)
    allowed = (
        (key_at <= query_at)
        & (seg_col[:, 0:1] == seg_row[...])
        & ((valid_col[:, 0:1] == 1.0) | (key_at == query_at))
    )
    bias[...] = jnp.where(allowed, 0.0, -1e30)
    for at in range(0, wide, HD):
        head = at // HD
        cols = slice(at, at + HD)
        for q_at, q_size in chunks(length, 256):
            seen = q_at + q_size
            scores = dot(keys[0:seen, cols], queries[q_at:seen, cols], NT)
            scores = scores * HD ** (-0.5) + bias[0:seen, q_at:seen]
            top = jnp.max(scores, axis=0, keepdims=True)
            expo = jnp.exp(scores - top)
            total = jnp.sum(expo, axis=0, keepdims=True)
            chance = (expo * (1.0 / total)).astype(jnp.bfloat16)
            probs[head, 0:seen, q_at:seen] = chance
            result = dot(values[0:seen, cols], chance, TN)
            joined[q_at:seen, cols] = result.T.astype(jnp.bfloat16)
    targets = [keep, to_x, to_y, far_low, far_high]
    for i, (start, size) in enumerate(starts_of(targets)):
        place = pl.multiple_of(rows_at[i], 64)
        mixed[start : start + size, :] = joined[pl.ds(place, size), :]
    for at, size in chunks(w_out.shape[1], 512):
        store_parts(dot(mixed[...], w_out[:, at : at + size]), targets, slice(at, at + size))


def attend_square(rows_at, queries, keys, values, w_out, seg_row, seg_col, valid_col):
    length, wide = queries.shape
    width = w_out.shape[1]
    heads = wide // HD
    return pl.pallas_call(
        attend_kernel,
        name="attend",
        out_shape=send_shapes(length // 4, width)
        + [like((heads, length, length)), like((length, wide))],
        in_specs=in_smem() + in_vmem(7),
        out_specs=in_vmem(7),
        scratch_shapes=[
            pltpu.VMEM((length, length), jnp.float32),
            pltpu.VMEM((length, wide), jnp.bfloat16),
        ],
        compiler_params=limit(8),
    )(rows_at, queries, keys, values, w_out, seg_row, seg_col, valid_col)


def d_hidden_kernel(own, from_x, from_y, low, high, w_down, d_hidden, cot_all):
    blocks = [own, from_x, from_y, low, high]
    for (start, size), block in zip(starts_of(blocks), blocks):
        cot_all[start : start + size, :] = block[...]
    for at, size in chunks(w_down.shape[0], 256):
        d_hidden[:, at : at + size] = dot(cot_all[...], w_down[at : at + size, :], NT)


def back_through_down(blocks, w_down):
    rows, width = blocks[0].shape
    length = 4 * rows
    units = w_down.shape[0]
    return pl.pallas_call(
        d_hidden_kernel,
        name="back_through_down",
        out_shape=[like((length, units), jnp.float32), like((length, width))],
        in_specs=in_vmem(6),
        out_specs=in_vmem(2),
        compiler_params=limit(6),
    )(*blocks, w_down)


def mlp_kernel(
    own, from_x, from_y, low, high, d_hidden, w_gate_up, normed, hidden, d_gate_up
):
    units = w_gate_up.shape[2]
    blocks = [own, from_x, from_y, low, high]
    for (start, size), block in zip(starts_of(blocks), blocks):
        normed[start : start + size, :] = block[...]
    for at, size in chunks(units, 256):
        here = slice(at, at + size)
        gate = dot(normed[...], w_gate_up[0, :, here])
        upper = dot(normed[...], w_gate_up[1, :, here])
        incoming = d_hidden[:, here]
        sigma = 1.0 / (1.0 + jnp.exp(-gate))
        silu = gate * sigma
        hidden[:, here] = (silu * upper).astype(jnp.bfloat16)
        d_gate_up[:, here] = (incoming * upper * sigma * (1.0 + gate * (1.0 - sigma))).astype(
            jnp.bfloat16
        )
        d_gate_up[:, units + at : units + at + size] = (incoming * silu).astype(jnp.bfloat16)


def mlp(blocks, d_hidden, w_gate_up):
    rows, width = blocks[0].shape
    length = 4 * rows
    units = w_gate_up.shape[2]
    return pl.pallas_call(
        mlp_kernel,
        name="mlp",
        out_shape=[like((length, width)), like((length, units)), like((length, 2 * units))],
        in_specs=in_vmem(7),
        out_specs=in_vmem(3),
        compiler_params=limit(8),
    )(*blocks, d_hidden, w_gate_up)


def mlp_back_kernel(d_gate_up, w_gate_up, *targets):
    units = w_gate_up.shape[2]
    for at, size in chunks(w_gate_up.shape[1], 256):
        part = dot(d_gate_up[:, 0:units], w_gate_up[0, at : at + size, :], NT) + dot(
            d_gate_up[:, units : 2 * units], w_gate_up[1, at : at + size, :], NT
        )
        store_parts(part, targets, slice(at, at + size))


def mlp_back(d_gate_up, w_gate_up):
    return pl.pallas_call(
        mlp_back_kernel,
        name="mlp_back",
        out_shape=send_shapes(d_gate_up.shape[0] // 4, w_gate_up.shape[1]),
        in_specs=in_vmem(2),
        out_specs=in_vmem(5),
        compiler_params=limit(6),
    )(d_gate_up, w_gate_up)


def down_kernel(hidden, w_down, *targets):
    for at, size in chunks(w_down.shape[1], 256):
        store_parts(dot(hidden[...], w_down[:, at : at + size]), targets, slice(at, at + size))


def through_down(hidden, w_down):
    return pl.pallas_call(
        down_kernel,
        name="through_down",
        out_shape=send_shapes(hidden.shape[0] // 4, w_down.shape[1]),
        in_specs=in_vmem(2),
        out_specs=in_vmem(5),
        compiler_params=limit(6),
    )(hidden, w_down)


def attend_back_kernel(
    rows_at, own, from_x, from_y, low, high, w_out, probs, queries, keys, values, cosine, sine,
    d_middle, d_project, d_mixed,
):
    length, wide = queries.shape
    blocks = [own, from_x, from_y, low, high]
    starts = starts_of(blocks)
    for (start, size), block in zip(starts, blocks):
        d_middle[start : start + size, :] = block[...]
    for at, size in chunks(wide, 256):
        part = dot(d_middle[...], w_out[at : at + size, :], NT).astype(jnp.bfloat16)
        for i, (start, rows) in enumerate(starts):
            place = pl.multiple_of(rows_at[i], 64)
            d_mixed[pl.ds(place, rows), at : at + size] = part[start : start + rows]
    scale = HD ** (-0.5)

    def back(turned, rows):
        return turned * cosine[rows, :] - pltpu.roll(turned, HD // 2, 1) * sine[rows, :]

    for at in range(0, wide, HD):
        head = at // HD
        cols = slice(at, at + HD)
        d_keys = d_values = None
        for q_at, q_size in reversed(chunks(length, 256)):
            seen = q_at + q_size
            rows = slice(q_at, seen)
            chance = probs[head, 0:seen, rows]
            d_out = d_mixed[rows, cols]
            d_chance = dot(values[0:seen, cols], d_out, NT)
            exact = chance.astype(jnp.float32)
            delta = jnp.sum(d_chance * exact, axis=0, keepdims=True)
            d_scores = (exact * (d_chance - delta)).astype(jnp.bfloat16)
            more_values = dot(chance, d_out)
            more_keys = dot(d_scores, queries[rows, cols])
            d_queries = dot(keys[0:seen, cols], d_scores, TN).T
            d_project[rows, cols] = back(d_queries * scale, rows).astype(jnp.bfloat16)
            if d_keys is None:
                d_keys, d_values = more_keys, more_values
            else:
                d_keys = jnp.concatenate([d_keys[:seen] + more_keys, d_keys[seen:]], axis=0)
                d_values = jnp.concatenate([d_values[:seen] + more_values, d_values[seen:]], axis=0)
        d_project[:, wide + at : wide + at + HD] = back(d_keys * scale, slice(0, length)).astype(
            jnp.bfloat16
        )
        d_project[:, 2 * wide + at : 2 * wide + at + HD] = d_values.astype(jnp.bfloat16)


def attend_back_square(rows_at, blocks, w_out, probs, queries, keys, values, cosine, sine):
    length, wide = queries.shape
    return pl.pallas_call(
        attend_back_kernel,
        name="attend_back",
        out_shape=[like((length, w_out.shape[1])), like((length, 3 * wide))],
        in_specs=in_smem() + in_vmem(12),
        out_specs=in_vmem(2),
        scratch_shapes=[pltpu.VMEM((length, wide), jnp.bfloat16)],
        compiler_params=limit(8),
    )(rows_at, *blocks, w_out, probs, queries, keys, values, cosine, sine)


def project_back_kernel(rows_at, d_project, w_qkv, *refs):
    targets, turned = refs[:5], refs[5]
    wide = w_qkv.shape[2]
    for i, (start, size) in enumerate(starts_of(targets)):
        place = pl.multiple_of(rows_at[i], 64)
        turned[start : start + size, :] = d_project[pl.ds(place, size), :]
    for at, size in chunks(w_qkv.shape[1], 256):
        part = sum(
            dot(turned[:, c * wide : (c + 1) * wide], w_qkv[c, at : at + size, :], NT)
            for c in range(3)
        )
        store_parts(part, targets, slice(at, at + size))


def project_back(rows_at, d_project, w_qkv):
    return pl.pallas_call(
        project_back_kernel,
        name="project_back",
        out_shape=send_shapes(d_project.shape[0] // 4, w_qkv.shape[1]),
        in_specs=in_smem() + in_vmem(2),
        out_specs=in_vmem(5),
        scratch_shapes=[pltpu.VMEM(d_project.shape, jnp.bfloat16)],
        compiler_params=limit(8),
    )(rows_at, d_project, w_qkv)


def weight_kernel(layout, base, spot, which, *refs):
    turned, out = refs[-1], refs[-2]
    more = refs[-3] if spot is not None else None
    count, piece, _ = out.shape
    for i in range(count):
        place = pl.multiple_of(which[base + i] * piece, piece)
        at_ref = column = 0
        for pairs in layout:
            splits = refs[at_ref : at_ref + pairs]
            others = refs[at_ref + pairs : at_ref + 2 * pairs]
            at_ref += 2 * pairs
            length, across = others[0].shape
            for j, split in enumerate(splits):
                turned[:, j * length : (j + 1) * length] = split[:, pl.ds(place, piece)].T
            for at, size in chunks(across, 256):
                part = None
                for j, other in enumerate(others):
                    term = dot(turned[:, j * length : (j + 1) * length], other[:, at : at + size])
                    part = term if part is None else part + term
                cols = slice(column + at, column + at + size)
                if more is not None:
                    part = part + more[spot + i, :, cols].astype(jnp.float32)
                out[i, :, cols] = part.astype(out.dtype)
            column += across


def weight_pieces(which, base, count, groups, more=None, spot=None):
    layout = [len(splits) for splits, _ in groups]
    refs = [ref for splits, others in groups for ref in (*splits, *others)]
    extra = [] if more is None else [more]
    length = groups[0][1][0].shape[0]
    across = sum(others[0].shape[1] for _, others in groups)
    piece = groups[0][0][0].shape[1] // 8
    return pl.pallas_call(
        functools.partial(weight_kernel, layout, base, spot),
        name="weight_pieces",
        out_shape=like((count, piece, across)),
        in_specs=in_smem() + in_vmem(len(refs) + len(extra)),
        out_specs=in_vmem(1)[0],
        scratch_shapes=[pltpu.VMEM((piece, max(layout) * length), jnp.bfloat16)],
        compiler_params=limit(16),
    )(which, *refs, *extra)


def join_kernel(here_outer, here_own, there_outer, there_own, outer, own):
    for here, there, out in ((here_outer, there_outer, outer), (here_own, there_own, own)):
        for at, size in chunks(out.shape[2], 256):
            cols = slice(at, at + size)
            out[0, :, cols] = (
                here[0, :, cols].astype(jnp.float32) + there[0, :, cols].astype(jnp.float32)
            ).astype(jnp.bfloat16)


def join(here, there):
    shape = here[0].shape
    return pl.pallas_call(
        join_kernel,
        name="join",
        out_shape=[like(shape), like(shape)],
        in_specs=in_vmem(4),
        out_specs=in_vmem(2),
        compiler_params=limit(6),
    )(*here, *there)


def hand_kernel(near, far, out):
    for at, size in chunks(out.shape[1], 256):
        cols = slice(at, at + size)
        out[:, cols] = (
            near[0, :, cols].astype(jnp.float32) + far[0, :, cols].astype(jnp.float32)
        ).astype(jnp.bfloat16)


def hand(near, far):
    return pl.pallas_call(
        hand_kernel,
        name="hand",
        out_shape=like(near.shape[1:]),
        in_specs=in_vmem(2),
        out_specs=in_vmem(1)[0],
        compiler_params=limit(6),
    )(near, far)


def finish_kernel(parts, count_inner, inner, *refs):
    count = len(refs) - len(parts)
    here = [ref for ref in refs[:count_inner]]
    outer = [ref for ref in refs[count_inner:count]]

    def total(sources, cols):
        found = None
        for source in sources:
            term = source[0, :, cols] if len(source.shape) == 3 else source[:, cols]
            term = term.astype(jnp.float32)
            found = term if found is None else found + term
        return found

    column = 0
    for (planes, across, turn), out in zip(parts, refs[count:]):
        for c in range(planes):
            for at, size in chunks(across, 256):
                cols = slice(column + at, column + at + size)
                value = jnp.where(inner[0] == 1, total(here, cols), total(outer, cols))
                if turn:
                    out[at : at + size, :] = value.T
                else:
                    out[c, :, at : at + size] = value
            column += across


def finish(inner, here, outer, parts):
    piece = here[0].shape[-2]
    return pl.pallas_call(
        functools.partial(finish_kernel, parts, len(here)),
        name="finish",
        out_shape=[
            like((across, piece) if turn else (planes, piece, across), jnp.float32)
            for planes, across, turn in parts
        ],
        in_specs=in_smem() + in_vmem(len(here) + len(outer)),
        out_specs=in_vmem(len(parts)),
        compiler_params=limit(8),
    )(inner, *here, *outer)


def gains_kernel(chip, *refs):
    sources, out, kept = refs[:4], refs[4], refs[5]
    for back, source in enumerate(sources):
        kept[lax.rem(chip[0] + 4 - back, 4)] = source[...]
    out[...] = (kept[0] + kept[1]) + (kept[2] + kept[3])


def sum_gains(chip, sources):
    return pl.pallas_call(
        gains_kernel,
        name="sum_gains",
        out_shape=like(sources[0].shape, jnp.float32),
        in_specs=in_smem() + in_vmem(4),
        out_specs=in_vmem(1)[0],
        scratch_shapes=[pltpu.VMEM((4, *sources[0].shape), jnp.float32)],
        compiler_params=limit(4),
    )(chip, *sources)


def flips(size, bit):
    return [(i, i ^ bit) for i in range(size)]


def after(value, *earlier):
    return lax.optimization_barrier((value, *earlier))[0]


def over_tensor(values, bit):
    return lax.ppermute(values, "tensor", flips(4, bit))


def gather_near(own):
    return own, over_tensor(own, 1), over_tensor(own, 2)


def gather_far(own, from_x, from_y):
    half = own.shape[0] // 2
    low = over_tensor(from_y[:half], 1)
    high = over_tensor(from_x[half:], 2)
    return [own, from_x, from_y, low, high]


def scatter_far(keep, to_x, to_y, far_low, far_high):
    return keep, *relay(to_x, to_y, over_tensor(far_low, 1), over_tensor(far_high, 2))


def scatter_near(keep, to_x, to_y):
    return keep, over_tensor(to_x, 1), over_tensor(to_y, 2)


def over_cores(values):
    return lax.ppermute(values, "dp", flips(8, 1))


def up_the_line(values, chips):
    return lax.ppermute(values, "dp", [(i, (i + 2 * chips) % 8) for i in range(8)])


def to_inner(values):
    return lax.ppermute(values, "dp", [(0, 2), (1, 3), (6, 4), (7, 5)])


def to_outer(values):
    return lax.ppermute(values, "dp", [(2, 0), (3, 1), (4, 6), (5, 7)])


def over_middle(values):
    return lax.ppermute(values, "dp", [(2, 4), (3, 5), (4, 2), (5, 3)])


class Weight:
    def __init__(self, places, groups):
        self.which_theirs, self.which_mine, self.inner = places
        self.groups = groups

    def sibling_part(self):
        self.sibling_sum = weight_pieces(self.which_theirs, 0, 4, self.groups)
        self.theirs = over_cores(self.sibling_sum)

    def own_part(self, base, count, *earlier):
        more = after(self.theirs, *earlier) if earlier else self.theirs
        return weight_pieces(self.which_mine, base, count, self.groups, more, base)


def sum_flips(values, *steps):
    for axis, size, bit in steps:
        values = values + lax.ppermute(values, axis, flips(size, bit))
    return values


def per_device_square(
    tokens, gain_attn, gain_mlp, w_qkv, w_out, w_gate_up, w_down, cotangent, segment_ids, valid_mask
):
    rows = tokens.shape[0]
    length = segment_ids.shape[0]
    low = jnp.bfloat16
    me = lax.axis_index("tensor")
    order = [me, me ^ 1, me ^ 2, me ^ 3]
    rows_at = jnp.stack([at * rows for at in order] + [order[3] * rows + rows // 2]).astype(jnp.int32)
    index = lax.axis_index("dp")
    place, core = index // 2, index % 2
    line_order = jnp.where(place < 2, jnp.array([3, 2, 0, 1]), jnp.array([0, 1, 3, 2]))
    places = (
        (2 * line_order + 1 - core).astype(jnp.int32),
        (2 * line_order + core).astype(jnp.int32),
        ((place == 1) | (place == 2)).astype(jnp.int32).reshape(1),
    )
    chip = place.astype(jnp.int32).reshape(1)
    gain_one = gain_attn[None, :]
    gain_two = gain_mlp[None, :]

    tokens = after(tokens, rows_at, chip, *places)
    normed = norm(tokens, gain_one)
    near = gather_near(normed)
    cosine, sine, seg_col, valid_col = prepare(
        segment_ids.astype(jnp.float32)[None, :],
        valid_mask.astype(jnp.float32)[None, :],
    )
    near = (near[0], near[1], after(near[2], cosine))
    guest_cot_own = to_inner(cotangent)
    blocks = gather_far(*near)
    cot_near = gather_near(after(cotangent, *blocks))
    normed_all, queries, keys, values = project(
        rows_at, blocks, w_qkv, cosine, sine
    )
    *sent, probs, mixed = attend_square(
        rows_at,
        after(queries, *cot_near, guest_cot_own),
        keys,
        values,
        w_out,
        segment_ids.astype(jnp.float32)[None, :],
        seg_col,
        valid_col,
    )
    guest_cot_near = [to_inner(part) for part in cot_near[1:]]
    keep, to_x, to_y = scatter_far(*sent)
    cot_blocks = gather_far(*(after(part, to_x) for part in cot_near))
    got = scatter_near(keep, to_x, to_y)
    d_hidden, cot_all = back_through_down(
        [after(cot_blocks[0], *guest_cot_near)] + cot_blocks[1:], w_down
    )
    middle, normed_two = make_middle(tokens, after(got[0], cot_all), *got[1:], gain_two)

    near = gather_near(normed_two)
    guest_cot_far = [to_inner(part) for part in cot_blocks[3:]]
    guest_own = to_inner(after(normed_two, *guest_cot_far))
    blocks = gather_far(*near)
    normed_two_all, hidden, d_gate_up = mlp(
        [after(blocks[0], *guest_cot_far)] + blocks[1:], d_hidden, w_gate_up
    )
    guest_near = [to_inner(part) for part in near[1:]]
    guest_far = [to_inner(part) for part in blocks[3:]]
    sent = mlp_back(d_gate_up, w_gate_up)
    keep, to_x, to_y = scatter_far(*sent)
    to_x = after(to_x, guest_own, *guest_near)
    guest_d_hidden, guest_cot_all = back_through_down(
        [after(guest_cot_own, to_x), *guest_cot_near, *guest_cot_far], w_down
    )
    got = scatter_near(keep, to_x, to_y)
    d_middle, gain_two_part, d_middle_low = norm_back(
        cotangent, after(got[0], guest_d_hidden), *got[1:], middle, gain_two, True
    )
    near = gather_near(d_middle_low)
    guest_normed_two, guest_hidden, guest_d_gate_up = mlp(
        [after(guest_own, d_middle_low), *guest_near, *guest_far], guest_d_hidden, w_gate_up
    )
    down = Weight(places, [([cot_all, guest_cot_all], [hidden, guest_hidden])])
    down.sibling_part()
    gate = Weight(
        places,
        [
            (
                [normed_two_all, after(guest_normed_two, down.theirs)],
                [d_gate_up, guest_d_gate_up],
            )
        ],
    )
    gate.sibling_part()
    blocks = gather_far(*near)
    down_outer = down.own_part(0, 1, gate.sibling_sum)
    down_own = down.own_part(1, 1, down_outer)
    gate_outer = gate.own_part(0, 1, down_own)
    gate_own = gate.own_part(1, 1, gate_outer)
    down_outer = over_middle(down_outer)

    d_middle_all, d_project = attend_back_square(
        rows_at,
        blocks,
        w_out,
        after(probs, gate_own),
        queries,
        keys,
        values,
        cosine,
        sine,
    )
    gate_outer = over_middle(gate_outer)
    late = Weight(places, [([normed_all], [d_project]), ([d_middle_all], [mixed])])
    late.groups[0] = ([after(normed_all, down_outer)], [d_project])
    late.sibling_part()
    down_near = [down.own_part(2, 1, late.sibling_sum)]
    down_handed = hand(down_near[0], down_outer)
    down_given = to_outer(down_handed)
    late_far = [late.own_part(0, 1, down_handed)]
    late_far += [late.own_part(1, 1, late_far[0])]
    late_arrived = [to_inner(part) for part in late_far]
    sent = project_back(rows_at, after(d_project, late_far[1]), w_qkv)
    keep, to_x, to_y = scatter_far(*sent)
    gate_own = over_middle(after(gate_own, to_x, to_y))
    late_near = [late.own_part(2, 1, to_x, to_y)]
    late_near += [late.own_part(3, 1, late_near[0])]
    late_near_arrived = to_inner(late_near[1])
    got = scatter_near(keep, to_x, to_y)
    gate_near = [gate.own_part(2, 1, late_near[1])]
    gate_handed = hand(gate_near[0], gate_outer)
    gate_given = to_outer(gate_handed)
    gate_near += [gate.own_part(3, 1, gate_handed)]
    down_near += [down.own_part(3, 1, gate_near[1])]
    down_own = over_middle(after(down_own, down_near[1]))
    d_inputs, gain_one_part = norm_back(
        d_middle,
        after(got[0], down_near[1], down_given, late_arrived[0]),
        *got[1:],
        tokens,
        gain_one,
        False,
    )
    late_far[0] = after(late_far[0], d_inputs, gate_own, down_own)
    late_outer, late_own = join(late_far, late_arrived)
    gains = sum_flips(
        after(jnp.concatenate([gain_one_part, gain_two_part], axis=0), late_own),
        ("dp", 8, 1),
        ("tensor", 4, 1),
        ("tensor", 4, 2),
    )
    sent = through_down(after(hidden, gains, gate_given), w_down)
    late_outer = over_middle(late_outer)
    keep, to_x, to_y, *sent = sent
    via_x, via_y = over_tensor(sent[0], 1), over_tensor(sent[1], 2)
    late_own = over_middle(after(late_own, via_x, via_y))
    late_handed = hand(after(late_near[0], via_x, via_y), late_outer)
    late_given = to_outer(late_handed)
    to_x, to_y = relay(after(to_x, late_handed), to_y, via_x, via_y)
    gains = [after(gains, late_handed)]
    gains += [up_the_line(gains[0], chips) for chips in (1, 2, 3)]
    keep, got_x, got_y = scatter_near(keep, to_x, to_y)
    output = (middle + keep + got_x.astype(jnp.float32) + got_y.astype(jnp.float32)).astype(low)
    inner = places[2]
    units, wide = w_down.shape[0], w_qkv.shape[2]
    (grad_down,) = finish(
        inner,
        [after(down_near[1], output, late_near_arrived), down_own],
        [down_given],
        [(1, units, True)],
    )
    (grad_gate_up,) = finish(
        inner, [after(gate_near[1], grad_down), gate_own], [gate_given], [(2, units, False)]
    )
    grad_gains = sum_gains(chip, [after(gains[0], grad_gate_up), *gains[1:]])
    grad_qkv, grad_out = finish(
        inner,
        [late_near[1], late_near_arrived, late_own],
        [late_near[0], late_given],
        [(3, wide, False), (1, wide, True)],
    )
    return (
        output,
        d_inputs,
        grad_gains[0],
        grad_gains[1],
        grad_qkv,
        grad_out,
        grad_gate_up,
        grad_down,
    )


def solution(mesh):
    placed = (
        P(("dp", "tensor"), None),
        P(),
        P(),
        P(None, None, "tensor"),
        P("tensor", None),
        P(None, None, "tensor"),
        P("tensor", None),
        P(("dp", "tensor"), None),
        P("dp"),
        P("dp"),
    )
    square = mesh.shape["tensor"] == 4 and mesh.shape["dp"] == 8
    return jax.shard_map(
        per_device_square if square else per_device,
        mesh=mesh,
        in_specs=placed,
        out_specs=(
            P(("dp", "tensor"), None),
            P(("dp", "tensor"), None),
            P(),
            P(),
            P(None, "dp", "tensor"),
            P("tensor", "dp"),
            P(None, "dp", "tensor"),
            P("tensor", "dp"),
        ),
        check_vma=False,
    )
```

```python
import functools
import math

import jax
import jax.numpy as jnp
from jax import lax
from jax.experimental import pallas as pl
from jax.experimental.pallas import tpu as pltpu
from jax.sharding import PartitionSpec as P

HD = 128


EPS = 1e-06
THETA = 10000.0


def rope_tables(places):
    positions = places.astype(jnp.float32)
    freqs = THETA ** (-(jnp.arange(HD // 2).astype(jnp.float32) * 2.0 / HD))
    angles = positions[:, None] * freqs[None, :]
    return (jnp.cos(angles), jnp.sin(angles))


def rotate(values, cosine, sine):
    half = values.shape[-1] // 2
    first = values[..., :half]
    second = values[..., half:]
    cosine = cosine[:, None, :]
    sine = sine[:, None, :]
    return jnp.concatenate(
        [first * cosine - second * sine, second * cosine + first * sine], axis=-1
    )


def block_scores(q_block, keys_rot, start, segments, valid):
    block_rows = q_block.shape[0]
    length = keys_rot.shape[0]
    key_pos = jnp.arange(length)
    row_pos = start + jnp.arange(block_rows)
    row_seg = lax.dynamic_slice_in_dim(segments, start, block_rows, 0)
    scores = jnp.einsum(
        "qhd,khd->hqk", q_block, keys_rot, preferred_element_type=jnp.float32
    ) * HD ** (-0.5)
    allowed = (
        (key_pos[None, :] <= row_pos[:, None])
        & (row_seg[:, None] == segments[None, :])
        & ((valid[None, :] == 1) | (key_pos[None, :] == row_pos[:, None]))
    )
    return jnp.where(allowed[None], scores, -1e30)


def attend(queries, keys_rot, values, segments, valid):
    length = queries.shape[0]
    block_rows = min(512, length)
    count = length // block_rows

    def one_block(index):
        start = index * block_rows
        q_block = lax.dynamic_slice_in_dim(queries, start, block_rows, 0)
        scores = block_scores(q_block, keys_rot, start, segments, valid)
        top = jnp.max(scores, axis=-1, keepdims=True)
        expo = jnp.exp(scores - top)
        total = jnp.sum(expo, axis=-1, keepdims=True)
        probs = (expo / total).astype(jnp.bfloat16)
        result = jnp.einsum("hqk,khd->qhd", probs, values, preferred_element_type=jnp.float32)
        return (result, top[..., 0] + jnp.log(total[..., 0]))

    blocks, log_sums = lax.map(one_block, jnp.arange(count))
    return (blocks.reshape(length, -1), log_sums)


def attend_back(queries, keys_rot, values, d_mixed, log_sums, segments, valid):
    length = queries.shape[0]
    block_rows = min(512, length)
    count = length // block_rows
    scale = HD ** (-0.5)

    def one_block(carry, index):
        d_keys, d_values = carry
        start = index * block_rows
        q_block = lax.dynamic_slice_in_dim(queries, start, block_rows, 0)
        d_block = lax.dynamic_slice_in_dim(d_mixed, start, block_rows, 0)
        scores = block_scores(q_block, keys_rot, start, segments, valid)
        probs = jnp.exp(scores - log_sums[index][..., None])
        d_values = d_values + jnp.einsum(
            "hqk,qhd->khd", probs.astype(jnp.bfloat16), d_block, preferred_element_type=jnp.float32
        )
        d_probs = jnp.einsum("qhd,khd->hqk", d_block, values, preferred_element_type=jnp.float32)
        delta = jnp.sum(d_probs * probs, axis=-1, keepdims=True)
        d_scores = (probs * (d_probs - delta)).astype(jnp.bfloat16)
        d_query = scale * jnp.einsum(
            "hqk,khd->qhd", d_scores, keys_rot, preferred_element_type=jnp.float32
        )
        d_keys = d_keys + scale * jnp.einsum(
            "hqk,qhd->khd", d_scores, q_block, preferred_element_type=jnp.float32
        )
        return ((d_keys, d_values), d_query)

    empty = jnp.zeros(keys_rot.shape, jnp.float32)
    (d_keys, d_values), d_queries = lax.scan(one_block, (empty, empty), jnp.arange(count))
    return (d_queries.reshape(queries.shape), d_keys, d_values)


def per_device(
    tokens, gain_attn, gain_mlp, w_qkv, w_out, w_gate_up, w_down, cotangent, segment_ids, valid_mask
):
    length = segment_ids.shape[0]
    heads_here = w_qkv.shape[2] // HD
    shape3 = (length, heads_here, HD)
    incoming = tokens.astype(jnp.float32)
    gain_one = gain_attn.astype(jnp.float32)
    gain_two = gain_mlp.astype(jnp.float32)
    cosine, sine = rope_tables(jnp.arange(length))
    inv_one = lax.rsqrt(jnp.mean(incoming * incoming, axis=-1, keepdims=True) + EPS)
    normed = (incoming * inv_one * gain_one).astype(jnp.bfloat16)
    normed_all = lax.all_gather(normed, "tensor", axis=0, tiled=True)
    project = jnp.einsum("td,cde->cte", normed_all, w_qkv, preferred_element_type=jnp.float32)
    queries = rotate(project[0].reshape(shape3), cosine, sine).astype(jnp.bfloat16)
    keys_rot = rotate(project[1].reshape(shape3), cosine, sine).astype(jnp.bfloat16)
    values = project[2].reshape(shape3).astype(jnp.bfloat16)
    mixed, log_sums = attend(queries, keys_rot, values, segment_ids, valid_mask)
    mixed = mixed.astype(jnp.bfloat16)
    middle = incoming + lax.psum_scatter(
        jnp.dot(mixed, w_out, preferred_element_type=jnp.float32).astype(jnp.bfloat16),
        "tensor",
        scatter_dimension=0,
        tiled=True,
    ).astype(jnp.float32)
    inv_two = lax.rsqrt(jnp.mean(middle * middle, axis=-1, keepdims=True) + EPS)
    normed_two = (middle * inv_two * gain_two).astype(jnp.bfloat16)
    normed_two_all = lax.all_gather(normed_two, "tensor", axis=0, tiled=True)
    gate = jnp.dot(normed_two_all, w_gate_up[0], preferred_element_type=jnp.float32)
    upper = jnp.dot(normed_two_all, w_gate_up[1], preferred_element_type=jnp.float32)
    sigma = jax.nn.sigmoid(gate)
    hidden = (gate * sigma * upper).astype(jnp.bfloat16)
    result = middle + lax.psum_scatter(
        jnp.dot(hidden, w_down, preferred_element_type=jnp.float32).astype(jnp.bfloat16),
        "tensor",
        scatter_dimension=0,
        tiled=True,
    ).astype(jnp.float32)
    output = result.astype(jnp.bfloat16)
    cot_all = lax.all_gather(cotangent, "tensor", axis=0, tiled=True)
    d_hidden = jnp.einsum("td,fd->tf", cot_all, w_down, preferred_element_type=jnp.float32)
    grad_down = jnp.einsum("tf,td->fd", hidden, cot_all, preferred_element_type=jnp.float32)
    d_upper = (d_hidden * gate * sigma).astype(jnp.bfloat16)
    d_gate = (d_hidden * upper * sigma * (1.0 + gate * (1.0 - sigma))).astype(jnp.bfloat16)
    grad_gate_up = jnp.stack(
        [
            jnp.einsum("td,tf->df", normed_two_all, d_gate, preferred_element_type=jnp.float32),
            jnp.einsum("td,tf->df", normed_two_all, d_upper, preferred_element_type=jnp.float32),
        ]
    )
    d_normed_two = lax.psum_scatter(
        (
            jnp.einsum("tf,df->td", d_gate, w_gate_up[0], preferred_element_type=jnp.float32)
            + jnp.einsum("tf,df->td", d_upper, w_gate_up[1], preferred_element_type=jnp.float32)
        ).astype(jnp.bfloat16),
        "tensor",
        scatter_dimension=0,
        tiled=True,
    ).astype(jnp.float32)
    scaled_two = gain_two * d_normed_two
    d_middle = (
        cotangent.astype(jnp.float32)
        + inv_two * scaled_two
        - middle * inv_two**3 * jnp.mean(scaled_two * middle, axis=-1, keepdims=True)
    )
    grad_gain_two = jnp.sum(d_normed_two * middle * inv_two, axis=0)
    d_middle_all = lax.all_gather(d_middle.astype(jnp.bfloat16), "tensor", axis=0, tiled=True)
    d_mixed = jnp.einsum(
        "td,ed->te", d_middle_all, w_out, preferred_element_type=jnp.float32
    ).astype(jnp.bfloat16)
    grad_out = jnp.einsum("te,td->ed", mixed, d_middle_all, preferred_element_type=jnp.float32)
    d_queries, d_keys, d_values = attend_back(
        queries, keys_rot, values, d_mixed.reshape(shape3), log_sums, segment_ids, valid_mask
    )
    d_project = jnp.stack(
        [
            rotate(d_queries, cosine, -sine).reshape(length, -1),
            rotate(d_keys, cosine, -sine).reshape(length, -1),
            d_values.reshape(length, -1),
        ]
    ).astype(jnp.bfloat16)
    grad_qkv = jnp.einsum("td,cte->cde", normed_all, d_project, preferred_element_type=jnp.float32)
    d_normed = lax.psum_scatter(
        jnp.einsum("cte,cde->td", d_project, w_qkv, preferred_element_type=jnp.float32).astype(
            jnp.bfloat16
        ),
        "tensor",
        scatter_dimension=0,
        tiled=True,
    ).astype(jnp.float32)
    scaled_one = gain_one * d_normed
    d_inputs = (
        d_middle
        + inv_one * scaled_one
        - incoming * inv_one**3 * jnp.mean(scaled_one * incoming, axis=-1, keepdims=True)
    )
    grad_gain_one = jnp.sum(d_normed * incoming * inv_one, axis=0)
    grad_gain_one, grad_gain_two = lax.psum((grad_gain_one, grad_gain_two), ("dp", "tensor"))
    grad_qkv, grad_out, grad_gate_up, grad_down = (
        lax.psum_scatter(
            grad_qkv.astype(jnp.bfloat16), "dp", scatter_dimension=1, tiled=True
        ).astype(jnp.float32),
        lax.psum_scatter(
            grad_out.astype(jnp.bfloat16), "dp", scatter_dimension=1, tiled=True
        ).astype(jnp.float32),
        lax.psum_scatter(
            grad_gate_up.astype(jnp.bfloat16), "dp", scatter_dimension=1, tiled=True
        ).astype(jnp.float32),
        lax.psum_scatter(
            grad_down.astype(jnp.bfloat16), "dp", scatter_dimension=1, tiled=True
        ).astype(jnp.float32),
    )
    return (
        output,
        d_inputs,
        grad_gain_one,
        grad_gain_two,
        grad_qkv,
        grad_out,
        grad_gate_up,
        grad_down,
    )


NT = (((1,), (1,)), ((), ()))
TN = (((0,), (0,)), ((), ()))
MEGA = 1024 * 1024


def chunks(total, step):
    return [(at, min(step, total - at)) for at in range(0, total, step)]


def dot(left, right, dims=None):
    if dims is None:
        return jnp.dot(left, right, preferred_element_type=jnp.float32)
    return lax.dot_general(left, right, dims, preferred_element_type=jnp.float32)


def in_vmem(count):
    return [pl.BlockSpec(memory_space=pltpu.VMEM)] * count


def in_smem():
    return [pl.BlockSpec(memory_space=pltpu.SMEM)]


def like(shape, kind=jnp.bfloat16):
    return jax.ShapeDtypeStruct(shape, kind)


def limit(megabytes):
    return pltpu.CompilerParams(vmem_limit_bytes=megabytes * MEGA)


def starts_of(blocks):
    at, starts = 0, []
    for block in blocks:
        starts.append((at, block.shape[0]))
        at += block.shape[0]
    return starts


def send_shapes(rows, width):
    half = rows // 2
    return [
        like((rows, width), jnp.float32),
        like((rows, width)),
        like((rows, width)),
        like((half, width)),
        like((half, width)),
    ]


def store_parts(part, targets, cols):
    for (start, rows), target in zip(starts_of(targets), targets):
        target[:, cols] = part[start : start + rows].astype(target.dtype)


def norm_kernel(tokens, gain, normed):
    wide = tokens[...].astype(jnp.float32)
    inverse = lax.rsqrt(jnp.mean(wide * wide, axis=-1, keepdims=True) + EPS)
    normed[...] = (wide * inverse * gain[...].astype(jnp.float32)).astype(jnp.bfloat16)


def norm(tokens, gain):
    return pl.pallas_call(
        norm_kernel,
        name="norm",
        out_shape=like(tokens.shape),
        in_specs=in_vmem(2),
        out_specs=in_vmem(1)[0],
        compiler_params=limit(4),
    )(tokens, gain)


def relay_kernel(to_x, to_y, via_x, via_y, next_x, next_y):
    half = via_x.shape[0]
    next_x[:half] = to_x[:half]
    next_x[half:] = (
        to_x[half:].astype(jnp.float32) + via_y[...].astype(jnp.float32)
    ).astype(jnp.bfloat16)
    next_y[:half] = (
        to_y[:half].astype(jnp.float32) + via_x[...].astype(jnp.float32)
    ).astype(jnp.bfloat16)
    next_y[half:] = to_y[half:]


def relay(to_x, to_y, via_x, via_y):
    return pl.pallas_call(
        relay_kernel,
        name="relay",
        out_shape=[like(to_x.shape), like(to_y.shape)],
        in_specs=in_vmem(4),
        out_specs=in_vmem(2),
        compiler_params=limit(4),
    )(to_x, to_y, via_x, via_y)


def middle_kernel(tokens, keep, got_x, got_y, gain, middle, normed):
    total = (
        tokens[...].astype(jnp.float32)
        + keep[...]
        + got_x[...].astype(jnp.float32)
        + got_y[...].astype(jnp.float32)
    )
    middle[...] = total
    inverse = lax.rsqrt(jnp.mean(total * total, axis=-1, keepdims=True) + EPS)
    normed[...] = (total * inverse * gain[...].astype(jnp.float32)).astype(jnp.bfloat16)


def make_middle(tokens, keep, got_x, got_y, gain):
    return pl.pallas_call(
        middle_kernel,
        name="make_middle",
        out_shape=[like(keep.shape, jnp.float32), like(keep.shape)],
        in_specs=in_vmem(5),
        out_specs=in_vmem(2),
        compiler_params=limit(6),
    )(tokens, keep, got_x, got_y, gain)


def norm_back_kernel(base, keep, got_x, got_y, source, gain, *outs):
    d_normed = keep[...] + got_x[...].astype(jnp.float32) + got_y[...].astype(jnp.float32)
    wide = source[...].astype(jnp.float32)
    inverse = lax.rsqrt(jnp.mean(wide * wide, axis=-1, keepdims=True) + EPS)
    scaled = gain[...].astype(jnp.float32) * d_normed
    slope = jnp.mean(scaled * wide, axis=-1, keepdims=True) * inverse * inverse * inverse
    total = base[...].astype(jnp.float32) + inverse * scaled - wide * slope
    outs[0][...] = total
    outs[1][...] = jnp.sum(d_normed * wide * inverse, axis=0, keepdims=True)
    if len(outs) == 3:
        outs[2][...] = total.astype(jnp.bfloat16)


def norm_back(base, keep, got_x, got_y, source, gain, low):
    return pl.pallas_call(
        norm_back_kernel,
        name="norm_back",
        out_shape=[like(keep.shape, jnp.float32), like((1, keep.shape[1]), jnp.float32)]
        + [like(keep.shape)] * low,
        in_specs=in_vmem(6),
        out_specs=in_vmem(2 + low),
        compiler_params=limit(8),
    )(base, keep, got_x, got_y, source, gain)


def prepare_kernel(segments, valid, cosine, sine, seg_col, valid_col):
    length = cosine.shape[0]
    half = HD // 2
    place = lax.broadcasted_iota(jnp.int32, (length, HD), 0).astype(jnp.float32)
    lane = lax.broadcasted_iota(jnp.int32, (length, HD), 1)
    step = jnp.where(lane < half, lane, lane - half).astype(jnp.float32)
    angle = place * jnp.exp(step * (-2.0 / HD * math.log(THETA)))
    cosine[...] = jnp.cos(angle)
    turn = jnp.sin(angle)
    sine[...] = jnp.where(lane < half, -turn, turn)
    seg_col[...] = jnp.broadcast_to(segments[...], (HD, length)).T
    valid_col[...] = jnp.broadcast_to(valid[...], (HD, length)).T


def prepare(segments, valid):
    length = segments.shape[1]
    return pl.pallas_call(
        prepare_kernel,
        name="prepare",
        out_shape=[like((length, HD), jnp.float32)] * 4,
        in_specs=in_vmem(2),
        out_specs=in_vmem(4),
        compiler_params=limit(6),
    )(segments, valid)


def project_kernel(
    rows_at, own, from_x, from_y, low, high, w_qkv, cosine, sine, normed, queries, keys, values
):
    for i, block in enumerate((own, from_x, from_y, low, high)):
        place = pl.multiple_of(rows_at[i], 64)
        normed[pl.ds(place, block.shape[0]), :] = block[...]
    for c, target in enumerate((queries, keys, values)):
        for at, size in chunks(target.shape[1], 2 * HD):
            part = dot(normed[...], w_qkv[c, :, at : at + size])
            for head in range(0, size, HD):
                piece = part[:, head : head + HD]
                if c < 2:
                    piece = piece * cosine[...] + pltpu.roll(piece, HD // 2, 1) * sine[...]
                target[:, at + head : at + head + HD] = piece.astype(jnp.bfloat16)


def project(rows_at, blocks, w_qkv, cosine, sine):
    rows, width = blocks[0].shape
    length = 4 * rows
    wide = w_qkv.shape[2]
    return pl.pallas_call(
        project_kernel,
        name="project",
        out_shape=[like((length, width))] + [like((length, wide))] * 3,
        in_specs=in_smem() + in_vmem(8),
        out_specs=in_vmem(4),
        compiler_params=limit(8),
    )(rows_at, *blocks, w_qkv, cosine, sine)


def attend_kernel(
    rows_at, queries, keys, values, w_out, seg_row, seg_col, valid_col,
    keep, to_x, to_y, far_low, far_high, probs, mixed, bias, joined,
):
    length, wide = queries.shape
    key_at = lax.broadcasted_iota(jnp.int32, (length, length), 0)
    query_at = lax.broadcasted_iota(jnp.int32, (length, length), 1)
    allowed = (
        (key_at <= query_at)
        & (seg_col[:, 0:1] == seg_row[...])
        & ((valid_col[:, 0:1] == 1.0) | (key_at == query_at))
    )
    bias[...] = jnp.where(allowed, 0.0, -1e30)
    for at in range(0, wide, HD):
        head = at // HD
        cols = slice(at, at + HD)
        for q_at, q_size in chunks(length, 256):
            seen = q_at + q_size
            scores = dot(keys[0:seen, cols], queries[q_at:seen, cols], NT)
            scores = scores * HD ** (-0.5) + bias[0:seen, q_at:seen]
            top = jnp.max(scores, axis=0, keepdims=True)
            expo = jnp.exp(scores - top)
            total = jnp.sum(expo, axis=0, keepdims=True)
            chance = (expo * (1.0 / total)).astype(jnp.bfloat16)
            probs[head, 0:seen, q_at:seen] = chance
            result = dot(values[0:seen, cols], chance, TN)
            joined[q_at:seen, cols] = result.T.astype(jnp.bfloat16)
    targets = [keep, to_x, to_y, far_low, far_high]
    for i, (start, size) in enumerate(starts_of(targets)):
        place = pl.multiple_of(rows_at[i], 64)
        mixed[start : start + size, :] = joined[pl.ds(place, size), :]
    for at, size in chunks(w_out.shape[1], 512):
        store_parts(dot(mixed[...], w_out[:, at : at + size]), targets, slice(at, at + size))


def attend_square(rows_at, queries, keys, values, w_out, seg_row, seg_col, valid_col):
    length, wide = queries.shape
    width = w_out.shape[1]
    heads = wide // HD
    return pl.pallas_call(
        attend_kernel,
        name="attend",
        out_shape=send_shapes(length // 4, width)
        + [like((heads, length, length)), like((length, wide))],
        in_specs=in_smem() + in_vmem(7),
        out_specs=in_vmem(7),
        scratch_shapes=[
            pltpu.VMEM((length, length), jnp.float32),
            pltpu.VMEM((length, wide), jnp.bfloat16),
        ],
        compiler_params=limit(8),
    )(rows_at, queries, keys, values, w_out, seg_row, seg_col, valid_col)


def d_hidden_kernel(own, from_x, from_y, low, high, w_down, d_hidden, cot_all):
    blocks = [own, from_x, from_y, low, high]
    for (start, size), block in zip(starts_of(blocks), blocks):
        cot_all[start : start + size, :] = block[...]
    for at, size in chunks(w_down.shape[0], 256):
        d_hidden[:, at : at + size] = dot(cot_all[...], w_down[at : at + size, :], NT)


def back_through_down(blocks, w_down):
    rows, width = blocks[0].shape
    length = 4 * rows
    units = w_down.shape[0]
    return pl.pallas_call(
        d_hidden_kernel,
        name="back_through_down",
        out_shape=[like((length, units), jnp.float32), like((length, width))],
        in_specs=in_vmem(6),
        out_specs=in_vmem(2),
        compiler_params=limit(6),
    )(*blocks, w_down)


def mlp_kernel(
    own, from_x, from_y, low, high, d_hidden, w_gate_up, normed, hidden, d_gate_up
):
    units = w_gate_up.shape[2]
    blocks = [own, from_x, from_y, low, high]
    for (start, size), block in zip(starts_of(blocks), blocks):
        normed[start : start + size, :] = block[...]
    for at, size in chunks(units, 256):
        here = slice(at, at + size)
        gate = dot(normed[...], w_gate_up[0, :, here])
        upper = dot(normed[...], w_gate_up[1, :, here])
        incoming = d_hidden[:, here]
        sigma = 1.0 / (1.0 + jnp.exp(-gate))
        silu = gate * sigma
        hidden[:, here] = (silu * upper).astype(jnp.bfloat16)
        d_gate_up[:, here] = (incoming * upper * sigma * (1.0 + gate * (1.0 - sigma))).astype(
            jnp.bfloat16
        )
        d_gate_up[:, units + at : units + at + size] = (incoming * silu).astype(jnp.bfloat16)


def mlp(blocks, d_hidden, w_gate_up):
    rows, width = blocks[0].shape
    length = 4 * rows
    units = w_gate_up.shape[2]
    return pl.pallas_call(
        mlp_kernel,
        name="mlp",
        out_shape=[like((length, width)), like((length, units)), like((length, 2 * units))],
        in_specs=in_vmem(7),
        out_specs=in_vmem(3),
        compiler_params=limit(8),
    )(*blocks, d_hidden, w_gate_up)


def mlp_back_kernel(d_gate_up, w_gate_up, *targets):
    units = w_gate_up.shape[2]
    for at, size in chunks(w_gate_up.shape[1], 256):
        part = dot(d_gate_up[:, 0:units], w_gate_up[0, at : at + size, :], NT) + dot(
            d_gate_up[:, units : 2 * units], w_gate_up[1, at : at + size, :], NT
        )
        store_parts(part, targets, slice(at, at + size))


def mlp_back(d_gate_up, w_gate_up):
    return pl.pallas_call(
        mlp_back_kernel,
        name="mlp_back",
        out_shape=send_shapes(d_gate_up.shape[0] // 4, w_gate_up.shape[1]),
        in_specs=in_vmem(2),
        out_specs=in_vmem(5),
        compiler_params=limit(6),
    )(d_gate_up, w_gate_up)


def down_kernel(hidden, w_down, *targets):
    for at, size in chunks(w_down.shape[1], 256):
        store_parts(dot(hidden[...], w_down[:, at : at + size]), targets, slice(at, at + size))


def through_down(hidden, w_down):
    return pl.pallas_call(
        down_kernel,
        name="through_down",
        out_shape=send_shapes(hidden.shape[0] // 4, w_down.shape[1]),
        in_specs=in_vmem(2),
        out_specs=in_vmem(5),
        compiler_params=limit(6),
    )(hidden, w_down)


def attend_back_kernel(
    rows_at, own, from_x, from_y, low, high, w_out, probs, queries, keys, values, cosine, sine,
    d_middle, d_project, d_mixed,
):
    length, wide = queries.shape
    blocks = [own, from_x, from_y, low, high]
    starts = starts_of(blocks)
    for (start, size), block in zip(starts, blocks):
        d_middle[start : start + size, :] = block[...]
    for at, size in chunks(wide, 256):
        part = dot(d_middle[...], w_out[at : at + size, :], NT).astype(jnp.bfloat16)
        for i, (start, rows) in enumerate(starts):
            place = pl.multiple_of(rows_at[i], 64)
            d_mixed[pl.ds(place, rows), at : at + size] = part[start : start + rows]
    scale = HD ** (-0.5)

    def back(turned, rows):
        return turned * cosine[rows, :] - pltpu.roll(turned, HD // 2, 1) * sine[rows, :]

    for at in range(0, wide, HD):
        head = at // HD
        cols = slice(at, at + HD)
        d_keys = d_values = None
        for q_at, q_size in reversed(chunks(length, 256)):
            seen = q_at + q_size
            rows = slice(q_at, seen)
            chance = probs[head, 0:seen, rows]
            d_out = d_mixed[rows, cols]
            d_chance = dot(values[0:seen, cols], d_out, NT)
            exact = chance.astype(jnp.float32)
            delta = jnp.sum(d_chance * exact, axis=0, keepdims=True)
            d_scores = (exact * (d_chance - delta)).astype(jnp.bfloat16)
            more_values = dot(chance, d_out)
            more_keys = dot(d_scores, queries[rows, cols])
            d_queries = dot(keys[0:seen, cols], d_scores, TN).T
            d_project[rows, cols] = back(d_queries * scale, rows).astype(jnp.bfloat16)
            if d_keys is None:
                d_keys, d_values = more_keys, more_values
            else:
                d_keys = jnp.concatenate([d_keys[:seen] + more_keys, d_keys[seen:]], axis=0)
                d_values = jnp.concatenate([d_values[:seen] + more_values, d_values[seen:]], axis=0)
        d_project[:, wide + at : wide + at + HD] = back(d_keys * scale, slice(0, length)).astype(
            jnp.bfloat16
        )
        d_project[:, 2 * wide + at : 2 * wide + at + HD] = d_values.astype(jnp.bfloat16)


def attend_back_square(rows_at, blocks, w_out, probs, queries, keys, values, cosine, sine):
    length, wide = queries.shape
    return pl.pallas_call(
        attend_back_kernel,
        name="attend_back",
        out_shape=[like((length, w_out.shape[1])), like((length, 3 * wide))],
        in_specs=in_smem() + in_vmem(12),
        out_specs=in_vmem(2),
        scratch_shapes=[pltpu.VMEM((length, wide), jnp.bfloat16)],
        compiler_params=limit(8),
    )(rows_at, *blocks, w_out, probs, queries, keys, values, cosine, sine)


def project_back_kernel(rows_at, d_project, w_qkv, *refs):
    targets, turned = refs[:5], refs[5]
    wide = w_qkv.shape[2]
    for i, (start, size) in enumerate(starts_of(targets)):
        place = pl.multiple_of(rows_at[i], 64)
        turned[start : start + size, :] = d_project[pl.ds(place, size), :]
    for at, size in chunks(w_qkv.shape[1], 256):
        part = sum(
            dot(turned[:, c * wide : (c + 1) * wide], w_qkv[c, at : at + size, :], NT)
            for c in range(3)
        )
        store_parts(part, targets, slice(at, at + size))


def project_back(rows_at, d_project, w_qkv):
    return pl.pallas_call(
        project_back_kernel,
        name="project_back",
        out_shape=send_shapes(d_project.shape[0] // 4, w_qkv.shape[1]),
        in_specs=in_smem() + in_vmem(2),
        out_specs=in_vmem(5),
        scratch_shapes=[pltpu.VMEM(d_project.shape, jnp.bfloat16)],
        compiler_params=limit(8),
    )(rows_at, d_project, w_qkv)


def weight_kernel(layout, base, spot, which, *refs):
    turned, out = refs[-1], refs[-2]
    more = refs[-3] if spot is not None else None
    count, piece, _ = out.shape
    for i in range(count):
        place = pl.multiple_of(which[base + i] * piece, piece)
        at_ref = column = 0
        for pairs in layout:
            splits = refs[at_ref : at_ref + pairs]
            others = refs[at_ref + pairs : at_ref + 2 * pairs]
            at_ref += 2 * pairs
            length, across = others[0].shape
            for j, split in enumerate(splits):
                turned[:, j * length : (j + 1) * length] = split[:, pl.ds(place, piece)].T
            for at, size in chunks(across, 256):
                part = None
                for j, other in enumerate(others):
                    term = dot(turned[:, j * length : (j + 1) * length], other[:, at : at + size])
                    part = term if part is None else part + term
                cols = slice(column + at, column + at + size)
                if more is not None:
                    part = part + more[spot + i, :, cols].astype(jnp.float32)
                out[i, :, cols] = part.astype(out.dtype)
            column += across


def weight_pieces(which, base, count, groups, more=None, spot=None):
    layout = [len(splits) for splits, _ in groups]
    refs = [ref for splits, others in groups for ref in (*splits, *others)]
    extra = [] if more is None else [more]
    length = groups[0][1][0].shape[0]
    across = sum(others[0].shape[1] for _, others in groups)
    piece = groups[0][0][0].shape[1] // 8
    return pl.pallas_call(
        functools.partial(weight_kernel, layout, base, spot),
        name="weight_pieces",
        out_shape=like((count, piece, across)),
        in_specs=in_smem() + in_vmem(len(refs) + len(extra)),
        out_specs=in_vmem(1)[0],
        scratch_shapes=[pltpu.VMEM((piece, max(layout) * length), jnp.bfloat16)],
        compiler_params=limit(16),
    )(which, *refs, *extra)


def join_kernel(here_outer, here_own, there_outer, there_own, outer, own):
    for here, there, out in ((here_outer, there_outer, outer), (here_own, there_own, own)):
        for at, size in chunks(out.shape[2], 256):
            cols = slice(at, at + size)
            out[0, :, cols] = (
                here[0, :, cols].astype(jnp.float32) + there[0, :, cols].astype(jnp.float32)
            ).astype(jnp.bfloat16)


def join(here, there):
    shape = here[0].shape
    return pl.pallas_call(
        join_kernel,
        name="join",
        out_shape=[like(shape), like(shape)],
        in_specs=in_vmem(4),
        out_specs=in_vmem(2),
        compiler_params=limit(6),
    )(*here, *there)


def hand_kernel(near, far, out):
    for at, size in chunks(out.shape[1], 256):
        cols = slice(at, at + size)
        out[:, cols] = (
            near[0, :, cols].astype(jnp.float32) + far[0, :, cols].astype(jnp.float32)
        ).astype(jnp.bfloat16)


def hand(near, far):
    return pl.pallas_call(
        hand_kernel,
        name="hand",
        out_shape=like(near.shape[1:]),
        in_specs=in_vmem(2),
        out_specs=in_vmem(1)[0],
        compiler_params=limit(6),
    )(near, far)


def finish_kernel(parts, count_inner, inner, *refs):
    count = len(refs) - len(parts)
    here = [ref for ref in refs[:count_inner]]
    outer = [ref for ref in refs[count_inner:count]]

    def total(sources, cols):
        found = None
        for source in sources:
            term = source[0, :, cols] if len(source.shape) == 3 else source[:, cols]
            term = term.astype(jnp.float32)
            found = term if found is None else found + term
        return found

    column = 0
    for (planes, across, turn), out in zip(parts, refs[count:]):
        for c in range(planes):
            for at, size in chunks(across, 256):
                cols = slice(column + at, column + at + size)
                value = jnp.where(inner[0] == 1, total(here, cols), total(outer, cols))
                if turn:
                    out[at : at + size, :] = value.T
                else:
                    out[c, :, at : at + size] = value
            column += across


def finish(inner, here, outer, parts):
    piece = here[0].shape[-2]
    return pl.pallas_call(
        functools.partial(finish_kernel, parts, len(here)),
        name="finish",
        out_shape=[
            like((across, piece) if turn else (planes, piece, across), jnp.float32)
            for planes, across, turn in parts
        ],
        in_specs=in_smem() + in_vmem(len(here) + len(outer)),
        out_specs=in_vmem(len(parts)),
        compiler_params=limit(8),
    )(inner, *here, *outer)


def gains_kernel(chip, *refs):
    sources, out, kept = refs[:4], refs[4], refs[5]
    for back, source in enumerate(sources):
        kept[lax.rem(chip[0] + 4 - back, 4)] = source[...]
    out[...] = (kept[0] + kept[1]) + (kept[2] + kept[3])


def sum_gains(chip, sources):
    return pl.pallas_call(
        gains_kernel,
        name="sum_gains",
        out_shape=like(sources[0].shape, jnp.float32),
        in_specs=in_smem() + in_vmem(4),
        out_specs=in_vmem(1)[0],
        scratch_shapes=[pltpu.VMEM((4, *sources[0].shape), jnp.float32)],
        compiler_params=limit(4),
    )(chip, *sources)


def flips(size, bit):
    return [(i, i ^ bit) for i in range(size)]


def after(value, *earlier):
    return lax.optimization_barrier((value, *earlier))[0]


def over_tensor(values, bit):
    return lax.ppermute(values, "tensor", flips(4, bit))


def gather_near(own):
    return own, over_tensor(own, 1), over_tensor(own, 2)


def gather_far(own, from_x, from_y):
    half = own.shape[0] // 2
    low = over_tensor(from_y[:half], 1)
    high = over_tensor(from_x[half:], 2)
    return [own, from_x, from_y, low, high]


def scatter_far(keep, to_x, to_y, far_low, far_high):
    return keep, *relay(to_x, to_y, over_tensor(far_low, 1), over_tensor(far_high, 2))


def scatter_near(keep, to_x, to_y):
    return keep, over_tensor(to_x, 1), over_tensor(to_y, 2)


def over_cores(values):
    return lax.ppermute(values, "dp", flips(8, 1))


def up_the_line(values, chips):
    return lax.ppermute(values, "dp", [(i, (i + 2 * chips) % 8) for i in range(8)])


def to_inner(values):
    return lax.ppermute(values, "dp", [(0, 2), (1, 3), (6, 4), (7, 5)])


def to_outer(values):
    return lax.ppermute(values, "dp", [(2, 0), (3, 1), (4, 6), (5, 7)])


def over_middle(values):
    return lax.ppermute(values, "dp", [(2, 4), (3, 5), (4, 2), (5, 3)])


class Weight:
    def __init__(self, places, groups):
        self.which_theirs, self.which_mine, self.inner = places
        self.groups = groups

    def sibling_part(self):
        self.sibling_sum = weight_pieces(self.which_theirs, 0, 4, self.groups)
        self.theirs = over_cores(self.sibling_sum)

    def own_part(self, base, count, *earlier):
        more = after(self.theirs, *earlier) if earlier else self.theirs
        return weight_pieces(self.which_mine, base, count, self.groups, more, base)


def sum_flips(values, *steps):
    for axis, size, bit in steps:
        values = values + lax.ppermute(values, axis, flips(size, bit))
    return values


def per_device_square(
    tokens, gain_attn, gain_mlp, w_qkv, w_out, w_gate_up, w_down, cotangent, segment_ids, valid_mask
):
    rows = tokens.shape[0]
    length = segment_ids.shape[0]
    low = jnp.bfloat16
    me = lax.axis_index("tensor")
    order = [me, me ^ 1, me ^ 2, me ^ 3]
    rows_at = jnp.stack([at * rows for at in order] + [order[3] * rows + rows // 2]).astype(jnp.int32)
    index = lax.axis_index("dp")
    place, core = index // 2, index % 2
    line_order = jnp.where(place < 2, jnp.array([3, 2, 0, 1]), jnp.array([0, 1, 3, 2]))
    places = (
        (2 * line_order + 1 - core).astype(jnp.int32),
        (2 * line_order + core).astype(jnp.int32),
        ((place == 1) | (place == 2)).astype(jnp.int32).reshape(1),
    )
    chip = place.astype(jnp.int32).reshape(1)
    gain_one = gain_attn[None, :]
    gain_two = gain_mlp[None, :]

    tokens = after(tokens, rows_at, chip, *places)
    normed = norm(tokens, gain_one)
    near = gather_near(normed)
    cosine, sine, seg_col, valid_col = prepare(
        segment_ids.astype(jnp.float32)[None, :],
        valid_mask.astype(jnp.float32)[None, :],
    )
    near = (near[0], near[1], after(near[2], cosine))
    guest_cot_own = to_inner(cotangent)
    blocks = gather_far(*near)
    cot_near = gather_near(after(cotangent, *blocks))
    normed_all, queries, keys, values = project(
        rows_at, blocks, w_qkv, cosine, sine
    )
    *sent, probs, mixed = attend_square(
        rows_at,
        after(queries, *cot_near, guest_cot_own),
        keys,
        values,
        w_out,
        segment_ids.astype(jnp.float32)[None, :],
        seg_col,
        valid_col,
    )
    guest_cot_near = [to_inner(part) for part in cot_near[1:]]
    keep, to_x, to_y = scatter_far(*sent)
    cot_blocks = gather_far(*(after(part, to_x) for part in cot_near))
    got = scatter_near(keep, to_x, to_y)
    d_hidden, cot_all = back_through_down(
        [after(cot_blocks[0], *guest_cot_near)] + cot_blocks[1:], w_down
    )
    middle, normed_two = make_middle(tokens, after(got[0], cot_all), *got[1:], gain_two)

    near = gather_near(normed_two)
    guest_cot_far = [to_inner(part) for part in cot_blocks[3:]]
    guest_own = to_inner(after(normed_two, *guest_cot_far))
    blocks = gather_far(*near)
    normed_two_all, hidden, d_gate_up = mlp(
        [after(blocks[0], *guest_cot_far)] + blocks[1:], d_hidden, w_gate_up
    )
    guest_near = [to_inner(part) for part in near[1:]]
    guest_far = [to_inner(part) for part in blocks[3:]]
    sent = mlp_back(d_gate_up, w_gate_up)
    keep, to_x, to_y = scatter_far(*sent)
    to_x = after(to_x, guest_own, *guest_near)
    guest_d_hidden, guest_cot_all = back_through_down(
        [after(guest_cot_own, to_x), *guest_cot_near, *guest_cot_far], w_down
    )
    got = scatter_near(keep, to_x, to_y)
    d_middle, gain_two_part, d_middle_low = norm_back(
        cotangent, after(got[0], guest_d_hidden), *got[1:], middle, gain_two, True
    )
    near = gather_near(d_middle_low)
    guest_normed_two, guest_hidden, guest_d_gate_up = mlp(
        [after(guest_own, d_middle_low), *guest_near, *guest_far], guest_d_hidden, w_gate_up
    )
    down = Weight(places, [([cot_all, guest_cot_all], [hidden, guest_hidden])])
    down.sibling_part()
    gate = Weight(
        places,
        [
            (
                [normed_two_all, after(guest_normed_two, down.theirs)],
                [d_gate_up, guest_d_gate_up],
            )
        ],
    )
    gate.sibling_part()
    blocks = gather_far(*near)
    down_outer = down.own_part(0, 1, gate.sibling_sum)
    down_own = down.own_part(1, 1, down_outer)
    gate_outer = gate.own_part(0, 1, down_own)
    gate_own = gate.own_part(1, 1, gate_outer)
    down_outer = over_middle(down_outer)

    d_middle_all, d_project = attend_back_square(
        rows_at,
        blocks,
        w_out,
        after(probs, gate_own),
        queries,
        keys,
        values,
        cosine,
        sine,
    )
    gate_outer = over_middle(gate_outer)
    late = Weight(places, [([normed_all], [d_project]), ([d_middle_all], [mixed])])
    late.groups[0] = ([after(normed_all, down_outer)], [d_project])
    late.sibling_part()
    down_near = [down.own_part(2, 1, late.sibling_sum)]
    down_handed = hand(down_near[0], down_outer)
    down_given = to_outer(down_handed)
    late_far = [late.own_part(0, 1, down_handed)]
    late_far += [late.own_part(1, 1, late_far[0])]
    late_arrived = [to_inner(part) for part in late_far]
    sent = project_back(rows_at, after(d_project, late_far[1]), w_qkv)
    keep, to_x, to_y = scatter_far(*sent)
    gate_own = over_middle(after(gate_own, to_x, to_y))
    late_near = [late.own_part(2, 1, to_x, to_y)]
    late_near += [late.own_part(3, 1, late_near[0])]
    late_near_arrived = to_inner(late_near[1])
    got = scatter_near(keep, to_x, to_y)
    gate_near = [gate.own_part(2, 1, late_near[1])]
    gate_handed = hand(gate_near[0], gate_outer)
    gate_given = to_outer(gate_handed)
    gate_near += [gate.own_part(3, 1, gate_handed)]
    down_near += [down.own_part(3, 1, gate_near[1])]
    down_own = over_middle(after(down_own, down_near[1]))
    d_inputs, gain_one_part = norm_back(
        d_middle,
        after(got[0], down_near[1], down_given, late_arrived[0]),
        *got[1:],
        tokens,
        gain_one,
        False,
    )
    late_far[0] = after(late_far[0], d_inputs, gate_own)
    late_outer, late_own = join(late_far, late_arrived)
    gains = sum_flips(
        after(jnp.concatenate([gain_one_part, gain_two_part], axis=0), late_own),
        ("dp", 8, 1),
        ("tensor", 4, 1),
        ("tensor", 4, 2),
    )
    sent = through_down(after(hidden, gains, gate_given), w_down)
    late_outer = over_middle(late_outer)
    keep, to_x, to_y, *sent = sent
    via_x, via_y = over_tensor(sent[0], 1), over_tensor(sent[1], 2)
    late_own = over_middle(after(late_own, via_x, via_y))
    late_handed = hand(after(late_near[0], via_x, via_y, down_own), late_outer)
    late_given = to_outer(late_handed)
    to_x, to_y = relay(after(to_x, late_handed), to_y, via_x, via_y)
    gains = [after(gains, late_handed)]
    gains += [up_the_line(gains[0], chips) for chips in (1, 2, 3)]
    keep, got_x, got_y = scatter_near(keep, to_x, to_y)
    output = (middle + keep + got_x.astype(jnp.float32) + got_y.astype(jnp.float32)).astype(low)
    inner = places[2]
    units, wide = w_down.shape[0], w_qkv.shape[2]
    (grad_down,) = finish(
        inner,
        [after(down_near[1], output, late_near_arrived), down_own],
        [down_given],
        [(1, units, True)],
    )
    (grad_gate_up,) = finish(
        inner, [after(gate_near[1], grad_down), gate_own], [gate_given], [(2, units, False)]
    )
    grad_gains = sum_gains(chip, [after(gains[0], grad_gate_up), *gains[1:]])
    grad_qkv, grad_out = finish(
        inner,
        [late_near[1], late_near_arrived, late_own],
        [late_near[0], late_given],
        [(3, wide, False), (1, wide, True)],
    )
    return (
        output,
        d_inputs,
        grad_gains[0],
        grad_gains[1],
        grad_qkv,
        grad_out,
        grad_gate_up,
        grad_down,
    )


def solution(mesh):
    placed = (
        P(("dp", "tensor"), None),
        P(),
        P(),
        P(None, None, "tensor"),
        P("tensor", None),
        P(None, None, "tensor"),
        P("tensor", None),
        P(("dp", "tensor"), None),
        P("dp"),
        P("dp"),
    )
    square = mesh.shape["tensor"] == 4 and mesh.shape["dp"] == 8
    return jax.shard_map(
        per_device_square if square else per_device,
        mesh=mesh,
        in_specs=placed,
        out_specs=(
            P(("dp", "tensor"), None),
            P(("dp", "tensor"), None),
            P(),
            P(),
            P(None, "dp", "tensor"),
            P("tensor", "dp"),
            P(None, "dp", "tensor"),
            P("tensor", "dp"),
        ),
        check_vma=False,
    )
```
